32 devices in a mesh: gx: 4 (over z), gy: 2 (over x), gz: 4 (over y, core).
Axes of the slice: x: 2, y: 2, z: 4, core: 2. Of those that a mesh axis runs over, the one named last changes fastest.
Arguments:
- load_currents: float32 [24, 16, 32, 256], P(None, 'gz', 'gx', 'gy')
- cond_rows: float32 [16, 32, 256], P('gz', 'gx', 'gy'), may hold values from 0.5 to 2
- cond_cols: float32 [16, 32, 256], P('gz', 'gx', 'gy'), may hold values from 0.5 to 2
- cond_vias: float32 [16, 32, 256], P('gz', 'gx', 'gy'), may hold values from 0.5 to 2
- ground: float32 [16, 32, 256], P('gz', 'gx', 'gy'), may hold values from 0.02 to 0.5
- via_offset: int32 [16], replicated, may hold values from -1 to 1, as said below
Outputs:
- basis_q: float32 [96, 16, 32, 256], P(None, 'gz', 'gx', 'gy')
- factor_r: float32 [96, 96], replicated
The draws below stay inside these ranges and needn't reach their ends.
Inputs may be any that keep to these rules, and one draw needn't show every extreme that they name: `via_offset`: in every aligned group of three layers (layers 3 k, 3 k + 1, 3 k + 2) the offsets -1, 0 and 1 appear once each.
All inputs are finite; a program needn't handle non-finite values.
Results may differ from the reference program's by a relative error of at most 0.0003.
Values sent between devices are 32-bit elements; how exact they have to be, the bound alone decides.
No kernel may reach another device: no remote copies, remote signals or barrier semaphores. Data moves between devices by JAX's collectives and lax.ppermute only.
A program may use at most 64 MiB of HBM per device.

```python
import math
import jax
import jax.numpy as jnp
from jax import lax

NRHS = 24
POWERS = 4
NZ = 16
NX = 32
NY = 256


def draw_load_currents(key, part):
    noise_key = jax.random.fold_in(key, 11)
    column_key = jax.random.fold_in(key, 12)
    shape = (NRHS, NZ, NX, NY)
    columns = jnp.exp(jax.random.uniform(column_key, (NRHS, 1, 1, 1), jnp.float32) * jnp.log(10.0))
    row_rise = 1.0 + 2.0 * jnp.arange(NX, dtype=jnp.float32) / max(NX - 1, 1)
    layer_rise = 1.0 + jnp.arange(NZ, dtype=jnp.float32) / NZ
    base = jax.random.normal(noise_key, shape, jnp.float32)
    return base * columns * row_rise[None, None, :, None] * layer_rise[None, :, None, None]


def draw_via_offset(key, part):
    start_key = jax.random.fold_in(key, 21)
    group_count = (NZ + 2) // 3
    starts = jax.random.randint(start_key, (group_count,), 0, 3, jnp.int32)
    layer_ids = jnp.arange(NZ, dtype=jnp.int32)
    group_ids = layer_ids // 3
    chosen = jnp.sum(jnp.where(group_ids[:, None] == jnp.arange(group_count, dtype=jnp.int32)[None, :], starts[None, :], 0), axis=1)
    return ((layer_ids + chosen) % 3 - 1).astype(jnp.int32)


def block_levels(own_key, shape, split, least, top_value):
    def one(dim, shards_of):
        steps = jax.random.uniform(jax.random.fold_in(jax.random.fold_in(own_key, 6), dim), (shards_of,), jnp.float32, least / len(split), top_value / len(split))
        return jnp.repeat(jnp.exp(steps), shape[dim] // shards_of).reshape((-1,) + (1,) * (len(shape) - dim - 1))

    loudness = one(*split[0])
    for cut in split[1:]:
        loudness = loudness * one(*cut)
    return loudness


def setup_inputs(seed: int = 0) -> dict:
    seeds = jax.random.split(jax.random.key(seed), 7)
    load_currents = draw_load_currents(jax.random.fold_in(seeds[6], 71), 0)
    cond_rows = jnp.clip(jnp.exp(math.log(2.0) - 1.3862944 * jax.random.uniform(seeds[1], (NZ, NX, NY), jnp.float32) ** block_levels(seeds[1], (NZ, NX, NY), ((0, 4), (1, 4), (2, 2)), -0.2, 0.2)), 0.5, 2.0)
    cond_cols = jnp.clip(jnp.exp(math.log(2.0) - 1.3862944 * jax.random.uniform(seeds[2], (NZ, NX, NY), jnp.float32) ** block_levels(seeds[2], (NZ, NX, NY), ((0, 4), (1, 4), (2, 2)), -0.2, 0.2)), 0.5, 2.0)
    cond_vias = jnp.clip(jnp.exp(math.log(2.0) - 1.3862944 * jax.random.uniform(seeds[3], (NZ, NX, NY), jnp.float32) ** block_levels(seeds[3], (NZ, NX, NY), ((0, 4), (1, 4), (2, 2)), -0.2, 0.2)), 0.5, 2.0)
    ground = jnp.clip(jnp.exp(math.log(0.5) - 3.218876 * jax.random.uniform(seeds[4], (NZ, NX, NY), jnp.float32) ** block_levels(seeds[4], (NZ, NX, NY), ((0, 4), (1, 4), (2, 2)), -0.2, 0.2)), 0.02, 0.5)
    via_offset = draw_via_offset(jax.random.fold_in(seeds[6], 71), 0)
    return dict(load_currents=load_currents, cond_rows=cond_rows, cond_cols=cond_cols, cond_vias=cond_vias, ground=ground, via_offset=via_offset)


newton_shifts = (15.4, 0.6, 11.7, 4.3)
basis_scale = 0.125

def pick_above(widened, offsets, width):
    lower = widened[..., 0:width]
    middle = widened[..., 1:width + 1]
    upper = widened[..., 2:width + 2]
    shift = offsets[None, :, None, None]
    return jnp.where(shift < 0, lower, jnp.where(shift > 0, upper, middle))

def pick_below(padded, offsets, width):
    lower = padded[..., 0:width]
    middle = padded[..., 1:width + 1]
    upper = padded[..., 2:width + 2]
    shift = offsets[None, :, None, None]
    return jnp.where(shift < 0, upper, jnp.where(shift > 0, lower, middle))

def conduct(field, cond_rows, cond_cols, cond_vias, ground, offsets):
    width = field.shape[3]
    flux_rows = cond_rows[None, :, :-1, :] * (field[:, :, :-1, :] - field[:, :, 1:, :])
    flux_cols = cond_cols[None, :, :, :-1] * (field[:, :, :, :-1] - field[:, :, :, 1:])
    widened = jnp.pad(field[:, 1:], ((0, 0), (0, 0), (0, 0), (1, 1)))
    above = pick_above(widened, offsets[:-1], width)
    flux_vias = cond_vias[None, :-1] * (field[:, :-1] - above)
    padded_flux = jnp.pad(flux_vias, ((0, 0), (0, 0), (0, 0), (1, 1)))
    incoming = pick_below(padded_flux, offsets[:-1], width)
    core = field[:, 1:-1, 1:-1, 1:-1]
    result = ground[None, 1:-1, 1:-1, 1:-1] * core
    result = result + flux_rows[:, 1:-1, 1:, 1:-1] - flux_rows[:, 1:-1, :-1, 1:-1]
    result = result + flux_cols[:, 1:-1, 1:-1, 1:] - flux_cols[:, 1:-1, 1:-1, :-1]
    result = result + flux_vias[:, 1:, 1:-1, 1:-1] - incoming[:, :-1, 1:-1, 1:-1]
    return result

def reference(load_currents, cond_rows, cond_cols, cond_vias, ground, via_offset):
    layers, rows, cols = ground.shape
    row_pos = jnp.arange(rows, dtype=jnp.int32)
    col_pos = jnp.arange(cols, dtype=jnp.int32)
    layer_pos = jnp.arange(layers, dtype=jnp.int32)
    rows_eff = jnp.where((row_pos < rows - 1)[None, :, None], cond_rows, 0.0)
    cols_eff = jnp.where((col_pos < cols - 1)[None, None, :], cond_cols, 0.0)
    target = col_pos[None, :] + via_offset[:, None]
    via_ok = (target >= 0) & (target < cols) & (layer_pos < layers - 1)[:, None]
    vias_eff = jnp.where(via_ok[:, None, :], cond_vias, 0.0)
    pad3 = ((1, 1), (1, 1), (1, 1))
    rows_pad = jnp.pad(rows_eff, pad3)
    cols_pad = jnp.pad(cols_eff, pad3)
    vias_pad = jnp.pad(vias_eff, pad3)
    ground_pad = jnp.pad(ground, pad3)
    offsets = jnp.pad(via_offset, (1, 1)).astype(jnp.int32)
    current = load_currents
    blocks = []
    for level in range(POWERS):
        padded = jnp.pad(current, ((0, 0), (1, 1), (1, 1), (1, 1)))
        image = conduct(padded, rows_pad, cols_pad, vias_pad, ground_pad, offsets)
        current = (image - newton_shifts[level] * current) * basis_scale
        blocks.append(current)
    basis = jnp.stack(blocks).reshape(POWERS * NRHS, layers * rows * cols)
    count = layers * rows * cols
    gram = jnp.dot(basis, basis.T, precision=lax.Precision.HIGHEST) / count
    lower = jnp.linalg.cholesky(gram)
    basis_q = jax.scipy.linalg.solve_triangular(lower, basis, lower=True)
    return (basis_q.reshape(POWERS * NRHS, layers, rows, cols), lower.T)
```

```python
import functools

import jax
import jax.numpy as jnp
from jax import lax
from jax.experimental import pallas as pl
from jax.experimental.pallas import tpu as pltpu
from jax.sharding import PartitionSpec as P

NRHS = 24
POWERS = 4


newton_shifts = (15.4, 0.6, 11.7, 4.3)
basis_scale = 0.125


def shifted(value, axis, steps):
    count = lax.axis_size(axis)
    initial, last = (max(0, -steps), min(count, count - steps))
    return lax.ppermute(value, axis, [(source, source + steps) for source in range(initial, last)])


def extended(value, sides, width):
    for axis, dim in sides:
        size, length = (lax.axis_size(axis), value.shape[dim])
        up = [(i, (i + 1) % size) for i in range(size - 1)]
        down = [(j, i) for i, j in up]
        last = lax.slice_in_dim(value, length - width, length, axis=dim)
        initial = lax.slice_in_dim(value, 0, width, axis=dim)
        before = lax.ppermute(last, axis, up)
        after = lax.ppermute(initial, axis, down)
        value = jnp.concatenate([before, value, after], axis=dim)
    return value


def pick_above(widened, offsets, width):
    lower = widened[..., 0:width]
    middle = widened[..., 1 : width + 1]
    upper = widened[..., 2 : width + 2]
    shift = offsets[None, :, None, None]
    return jnp.where(shift < 0, lower, jnp.where(shift > 0, upper, middle))


def pick_below(padded, offsets, width):
    lower = padded[..., 0:width]
    middle = padded[..., 1 : width + 1]
    upper = padded[..., 2 : width + 2]
    shift = offsets[None, :, None, None]
    return jnp.where(shift < 0, upper, jnp.where(shift > 0, lower, middle))


def conduct(field, cond_rows, cond_cols, cond_vias, ground, offsets):
    width = field.shape[3]
    flux_rows = cond_rows[None, :, :-1, :] * (field[:, :, :-1, :] - field[:, :, 1:, :])
    flux_cols = cond_cols[None, :, :, :-1] * (field[:, :, :, :-1] - field[:, :, :, 1:])
    widened = jnp.pad(field[:, 1:], ((0, 0), (0, 0), (0, 0), (1, 1)))
    above = pick_above(widened, offsets[:-1], width)
    flux_vias = cond_vias[None, :-1] * (field[:, :-1] - above)
    padded_flux = jnp.pad(flux_vias, ((0, 0), (0, 0), (0, 0), (1, 1)))
    incoming = pick_below(padded_flux, offsets[:-1], width)
    core = field[:, 1:-1, 1:-1, 1:-1]
    result = ground[None, 1:-1, 1:-1, 1:-1] * core
    result = result + flux_rows[:, 1:-1, 1:, 1:-1] - flux_rows[:, 1:-1, :-1, 1:-1]
    result = result + flux_cols[:, 1:-1, 1:-1, 1:] - flux_cols[:, 1:-1, 1:-1, :-1]
    result = result + flux_vias[:, 1:, 1:-1, 1:-1] - incoming[:, :-1, 1:-1, 1:-1]
    return result


def layer_offsets(via_offset, first_layer, count):
    layer_ids = first_layer + jnp.arange(count, dtype=jnp.int32)
    table_ids = jnp.arange(via_offset.shape[0], dtype=jnp.int32)
    matches = layer_ids[:, None] == table_ids[None, :]
    return jnp.sum(jnp.where(matches, via_offset[None, :], 0), axis=1)


def eliminate(tiles, order, step):
    width = tiles[0].shape[1]
    lane = lax.broadcasted_iota(jnp.int32, (8, width), 1)
    sub = lax.broadcasted_iota(jnp.int32, (8, width), 0)
    spread = lambda value: jnp.broadcast_to(value, (8, width))
    for first in range(0, order, step):
        home, base = first // 8, first % 8
        panel = tiles[home]
        entry = {}
        for i in range(step):
            for j in range(i, step):
                entry[i, j] = spread(panel[base + i : base + i + 1, first + j : first + j + 1])
        rows = [spread(panel[base + i : base + i + 1, :]) for i in range(step)]
        inverse = []
        done = []
        for i in range(step):
            row = rows[i]
            if i:
                row = jnp.where((lane >= first) & (lane < first + i), 0.0, row)
            factors = []
            for j in range(i):
                factor = entry[j, i] * inverse[j]
                factors.append(factor)
            for j in range(i):
                source = jnp.where(lane == first + j, 1.0, done[j])
                if i - j > 1:
                    source = jnp.where((lane > first + j) & (lane < first + i), 0.0, source)
                row = row - factors[j] * source
                for m in range(i, step):
                    entry[i, m] = entry[i, m] - factors[j] * entry[j, m]
            inverse.append(1.0 / entry[i, i])
            done.append(row)
        sources = []
        for j in range(step):
            source = jnp.where(lane == first + j, 1.0, done[j])
            if j < step - 1:
                source = jnp.where((lane > first + j) & (lane < first + step), 0.0, source)
            sources.append(source)
        inside = (lane >= first) & (lane < first + step)
        for t in range(home, order // 8):
            if t == home and base + step == 8:
                fresh = tiles[t]
            else:
                columns = [spread(tiles[t][:, first + j : first + j + 1]) for j in range(step)]
                fresh = jnp.where(inside, 0.0, tiles[t])
                for j in range(step):
                    factor = columns[j] * inverse[j]
                    fresh = fresh - factor * sources[j]
                    for m in range(j + 1, step):
                        columns[m] = columns[m] - factor * entry[j, m]
            if t == home:
                fresh = jnp.where(sub < base + step, tiles[t], fresh)
                for j in range(step):
                    fresh = jnp.where(sub == base + j, done[j], fresh)
            tiles[t] = fresh
    return tiles


def factor_kernel(parts_ref, upper_ref, inverse_ref, *, step):
    order = upper_ref.shape[0]
    tiles = []
    for t in range(order // 8):
        total = parts_ref[0, 8 * t : 8 * t + 8, :]
        for part in range(1, parts_ref.shape[0]):
            total = total + parts_ref[part, 8 * t : 8 * t + 8, :]
        tiles.append(total)
    tiles = eliminate(tiles, order, step)
    lane = lax.broadcasted_iota(jnp.int32, (8, order), 1)
    sub = lax.broadcasted_iota(jnp.int32, (8, order), 0)
    for t in range(order // 8):
        row = sub + 8 * t
        pivot = jnp.sum(jnp.where(lane == row, tiles[t], 0.0), axis=1, keepdims=True)
        scale = 1.0 / jnp.sqrt(pivot)
        upper_ref[8 * t : 8 * t + 8, :] = jnp.where(lane >= row, tiles[t] * scale, 0.0)
        inverse_ref[8 * t : 8 * t + 8, :] = jnp.where(lane < row, tiles[t], jnp.where(lane == row, 1.0, 0.0)) * scale


def factor(parts):
    order = parts.shape[1]
    shape = jax.ShapeDtypeStruct((order, order), jnp.float32)
    return pl.pallas_call(
        functools.partial(factor_kernel, step=4),
        out_shape=(shape, shape),
        in_specs=[pl.BlockSpec(memory_space=pltpu.VMEM)],
        out_specs=(pl.BlockSpec(memory_space=pltpu.VMEM),) * 2,
        compiler_params=pltpu.CompilerParams(vmem_limit_bytes=32 * 1024 * 1024),
        name="factor",
    )(parts)


def local(load_currents, cond_rows, cond_cols, cond_vias, ground, via_offset):
    layers, rows, cols = ground.shape
    total_layers = via_offset.shape[0]
    total_rows = rows * lax.axis_size("gx")
    total_cols = cols * lax.axis_size("gy")
    first_layer = lax.axis_index("gz") * layers
    first_row = lax.axis_index("gx") * rows
    first_col = lax.axis_index("gy") * cols
    row_pos = first_row + jnp.arange(rows, dtype=jnp.int32)
    col_pos = first_col + jnp.arange(cols, dtype=jnp.int32)
    layer_pos = first_layer + jnp.arange(layers, dtype=jnp.int32)
    own_offsets = layer_offsets(via_offset, first_layer, layers)
    rows_eff = jnp.where((row_pos < total_rows - 1)[None, :, None], cond_rows, 0.0)
    cols_eff = jnp.where((col_pos < total_cols - 1)[None, None, :], cond_cols, 0.0)
    target = col_pos[None, :] + own_offsets[:, None]
    via_ok = (target >= 0) & (target < total_cols) & (layer_pos < total_layers - 1)[:, None]
    vias_eff = jnp.where(via_ok[:, None, :], cond_vias, 0.0)
    blocks = []
    row_edge = shifted(rows_eff[:, rows - 1 :, :], "gx", 1)
    rows_pad = jnp.pad(jnp.concatenate([row_edge, rows_eff], axis=1), ((1, 1), (0, 1), (1, 1)))
    via_edge = shifted(vias_eff[layers - 1 :], "gz", 1)
    vias_ext = jnp.concatenate([via_edge, vias_eff], axis=0)
    cols_ext = jnp.concatenate([jnp.zeros((1, rows, cols), jnp.float32), cols_eff], axis=0)
    sides = extended(jnp.stack([cols_ext, vias_ext]), (("gy", 3),), 1)
    cols_pad = jnp.pad(sides[0], ((0, 1), (1, 1), (0, 0)))
    vias_pad = jnp.pad(sides[1], ((0, 1), (1, 1), (0, 0)))
    ground_pad = jnp.pad(ground, ((1, 1), (1, 1), (1, 1)))
    offsets = layer_offsets(via_offset, first_layer - 1, layers + 2)
    current = load_currents
    for level in range(POWERS):
        padded = extended(current, (("gx", 2), ("gy", 3), ("gz", 1)), 1)
        image = conduct(padded, rows_pad, cols_pad, vias_pad, ground_pad, offsets)
        current = (image - newton_shifts[level] * current) * basis_scale
        blocks.append(current)
    basis = jnp.stack(blocks).reshape(POWERS * NRHS, layers * rows * cols)
    count = layers * rows * cols * lax.axis_size("gx") * lax.axis_size("gy") * lax.axis_size("gz")
    gram_local = jnp.dot(basis, basis.T, precision=lax.Precision.HIGHEST) / count
    parts = lax.all_gather(gram_local, ("gx", "gy", "gz"))
    upper, inverse = factor(parts)
    basis_q = jnp.dot(inverse, basis, precision=lax.Precision.HIGHEST)
    return (basis_q.reshape(POWERS * NRHS, layers, rows, cols), upper)


def solution(mesh):
    in_specs = (
        P(None, "gz", "gx", "gy"),
        P("gz", "gx", "gy"),
        P("gz", "gx", "gy"),
        P("gz", "gx", "gy"),
        P("gz", "gx", "gy"),
        P(),
    )
    out_specs = (P(None, "gz", "gx", "gy"), P())
    return jax.shard_map(local, mesh=mesh, in_specs=in_specs, out_specs=out_specs, check_vma=False)
```

```python
import functools

import jax
import jax.numpy as jnp
from jax import lax
from jax.experimental import pallas as pl
from jax.experimental.pallas import tpu as pltpu
from jax.sharding import PartitionSpec as P

POWERS = 4


newton_shifts = (15.4, 0.6, 11.7, 4.3)
basis_scale = 0.125

VMEM = pl.BlockSpec(memory_space=pltpu.VMEM)
SMEM = pl.BlockSpec(memory_space=pltpu.SMEM)
PARAMS = pltpu.CompilerParams(vmem_limit_bytes=40 * 1024 * 1024)


def positions(shape):
    sub = lax.broadcasted_iota(jnp.int32, shape, 0)
    lane = lax.broadcasted_iota(jnp.int32, shape, 1)
    return sub, lane


def edges_kernel(load_ref, rows_ref, cols_ref, vias_ref, ground_ref, offset_ref, coef_ref, *strip_refs):
    fields, layers, rows, cols = load_ref.shape
    depth = POWERS
    total_layers = offset_ref.shape[0]
    gx, gy, gz = (lax.axis_index(name) for name in ("gx", "gy", "gz"))
    last_row = jnp.where(gx == lax.axis_size("gx") - 1, rows - 1, rows)
    last_col = jnp.where(gy == lax.axis_size("gy") - 1, cols - 1, cols)
    sub, lane = positions((rows, cols))
    for l in range(layers):
        layer = gz * layers + l
        shift = offset_ref[layer]
        target = gy * cols + lane + shift
        via_ok = (target >= 0) & (target < cols * lax.axis_size("gy"))
        via_ok = via_ok & (jnp.broadcast_to(layer, lane.shape) < total_layers - 1)
        coef_ref[0, l] = jnp.where(sub == last_row, 0.0, rows_ref[l])
        coef_ref[1, l] = jnp.where(lane == last_col, 0.0, cols_ref[l])
        coef_ref[2, l] = jnp.where(via_ok, vias_ref[l], 0.0)
        coef_ref[3, l] = ground_ref[l]
    planes = fields + coef_ref.shape[0]
    if len(strip_refs) == 1:
        starts = [jnp.where(gy == 0, depth, 0)]
    else:
        starts = [depth, 0]
    for l in range(layers):
        for strip_ref, start in zip(strip_refs, starts):
            total = jnp.zeros((rows, cols), jnp.float32)
            for f in range(planes):
                tile = load_ref[f, l] if f < fields else coef_ref[f - fields, l]
                moved = pltpu.roll(tile, start + depth * f, 1)
                total = jnp.where((lane >= depth * f) & (lane < depth * f + depth), moved, total)
            strip_ref[l] = total


def pack_kernel(load_ref, coef_ref, *refs, pair):
    strip_refs = refs[: 1 if pair else 2]
    block_ref, next_ref, prev_ref, pp_ref, pm_ref, mp_ref, mm_ref = refs[len(strip_refs) :]
    fields, layers, rows, cols = load_ref.shape
    half = rows // 2
    sub, lane = positions((rows, cols))

    def emit(q, x):
        swapped = [pltpu.roll(tile, half, 0) for tile in x]
        for l in range(layers):
            block_ref[q, l] = x[l]
        for t in range(layers // 2):
            next_ref[q, t] = jnp.where(sub >= half, x[2 * t], swapped[2 * t + 1])
            prev_ref[q, t] = jnp.where(sub < half, x[2 * t], swapped[2 * t + 1])
        for up, (after, before) in ((True, (pp_ref, mp_ref)), (False, (pm_ref, mm_ref))):
            one, two, three = (3, 2, 1) if up else (0, 1, 2)
            after[q] = jnp.where(
                sub > half, x[one], jnp.where(sub == half, pltpu.roll(x[three], half + 1, 0), swapped[two])
            )
            before[q] = jnp.where(
                sub < half - 1, x[one], jnp.where(sub == half - 1, pltpu.roll(x[three], half - 1, 0), swapped[two])
            )

    @pl.loop(0, fields)
    def _(f):
        emit(f, [load_ref[f, l] for l in range(layers)])

    for c in range(coef_ref.shape[0]):
        emit(fields + c, [coef_ref[c, l] for l in range(layers)])
    gy = lax.axis_index("gy")
    for side in range(2):
        tiles = []
        for l in range(layers):
            if pair:
                mine = jnp.broadcast_to(gy, (rows, cols)) == 1 - side
                tiles.append(jnp.where(mine, strip_refs[0][l], 0.0))
            else:
                tiles.append(strip_refs[side][l])
        emit(fields + coef_ref.shape[0] + side, tiles)


def powers_kernel(
    own_ref, below_ref, above_ref, after_ref, before_ref, bp_ref, bn_ref, ap_ref, an_ref, offset_ref,
    basis_ref, gram_ref, strips, coef, field,
):
    planes, layers, rows, cols = own_ref.shape
    fields = planes - 6
    depth = POWERS
    half = rows // 2
    order = depth * fields
    total_layers = offset_ref.shape[0]
    high = layers + 2 * depth
    sub, lane = positions((rows, cols))
    first_layer = lax.axis_index("gz") * layers
    zero = jnp.zeros((rows, cols), jnp.float32)

    skew = {depth: jnp.int32(0)}

    def offset(e):
        layer = first_layer + e - depth
        inside = (layer >= 0) & (layer < total_layers)
        return jnp.where(inside, offset_ref[jnp.clip(layer, 0, total_layers - 1)], 0)

    for e in range(depth, high - 1):
        skew[e + 1] = skew[e] + offset(e)
    for e in range(depth - 1, -1, -1):
        skew[e] = skew[e + 1] - offset(e)

    def assemble(q, e):
        if depth <= e < depth + layers:
            l = e - depth
            t = l // 2
            if l % 2 == 0:
                return own_ref[q, l], jnp.where(sub < half, before_ref[q, t], after_ref[q, t])
            return own_ref[q, l], pltpu.roll(jnp.where(sub >= half, before_ref[q, t], after_ref[q, t]), half, 0)
        if e < depth:
            distance, home, tile_p, tile_n = depth - e, below_ref[q, e], bp_ref, bn_ref
        else:
            distance, home, tile_p, tile_n = e - depth - layers + 1, above_ref[q, e - depth - layers], ap_ref, an_ref
        if distance == depth:
            return home, zero
        shift_p, shift_n = {1: (0, 0), 2: (half, half), 3: (half - 1, half + 1)}[distance]
        prev = pltpu.roll(tile_p[q], shift_p, 0) if shift_p else tile_p[q]
        following = pltpu.roll(tile_n[q], shift_n, 0) if shift_n else tile_n[q]
        return home, jnp.where(sub < half, following, prev)

    for side in range(2):
        for e in range(high):
            pieces = assemble(planes - 2 + side, e)
            for rt in range(2):
                strips[side, e, rt] = pieces[rt]

    left_lane = lane >= cols - depth
    right_lane = lane < depth

    def load_plane(q, e, put):
        pieces = assemble(q, e)
        c = skew[e]
        kept = (lane + c >= 0) & (lane + c < cols)
        for rt in range(2):
            if rt == 1 and (e == 0 or e == high - 1):
                continue
            near = pieces[rt]
            left = pltpu.roll(strips[0, e, rt], lax.rem(2 * cols - depth * (q + 1), cols), 1)
            right = pltpu.roll(strips[1, e, rt], lax.rem(2 * cols - depth * q, cols), 1)
            far = jnp.where(right_lane, right, jnp.where(left_lane, left, 0.0))
            if e != depth:
                shift = lax.rem(cols - c, cols)
                near, far = pltpu.roll(near, shift, 1), pltpu.roll(far, shift, 1)
                near, far = jnp.where(kept, near, far), jnp.where(kept, far, near)
            put(e, rt, 0, near)
            put(e, rt, 1, far)

    def left_of(tiles):
        turned = [pltpu.roll(tile, 1, 1) for tile in tiles]
        return [jnp.where(lane == 0, turned[1 - i], turned[i]) for i in range(2)]

    def right_of(tiles):
        turned = [pltpu.roll(tile, cols - 1, 1) for tile in tiles]
        return [jnp.where(lane == cols - 1, turned[1 - i], turned[i]) for i in range(2)]

    def up_of(tiles):
        turned = [pltpu.roll(tile, 1, 0) for tile in tiles]
        return [jnp.where(sub == 0, turned[1 - i], turned[i]) for i in range(2)]

    def down_of(tiles):
        turned = [pltpu.roll(tile, rows - 1, 0) for tile in tiles]
        return [jnp.where(sub == rows - 1, turned[1 - i], turned[i]) for i in range(2)]

    for c in range(4):
        for e in range(high):

            def put(e, rt, ct, value, c=c):
                coef[c, e, rt, ct] = value * basis_scale

            load_plane(jnp.int32(fields + c), e, put)
    for e in range(1, high - 1):
        for rt in range(2):
            for ct in range(2):
                down = coef[0, e, rt, ct]
                up = up_of([coef[0, e, i, ct] for i in range(2)])[rt]
                right = coef[1, e, rt, ct]
                left = left_of([coef[1, e, rt, i] for i in range(2)])[ct]
                upper = coef[2, e, rt, ct]
                lower = coef[2, e - 1, rt, ct] if not (rt == 1 and e == 1) else zero
                coef[4, e, rt, ct] = up
                coef[5, e, rt, ct] = left
                coef[6, e, rt, ct] = coef[3, e, rt, ct] + down + up + right + left + upper + lower

    @pl.loop(0, fields)
    def _(f):
        for e in range(high):

            def put(e, rt, ct, value):
                field[0, e, rt, ct] = value

            load_plane(f, e, put)
        for k in range(1, depth + 1):
            reach = depth - k
            for e in range(depth - reach, depth + layers + reach):
                distance = max(depth - e, e - depth - layers + 1, 0)
                for rt in range(2 if distance < reach else 1):
                    centre = [field[k - 1, e, rt, ct] for ct in range(2)]
                    lefts, rights = left_of(centre), right_of(centre)
                    for ct in range(2):
                        column = [field[k - 1, e, i, ct] for i in range(2)]
                        up, down = up_of(column)[rt], down_of(column)[rt]
                        value = (coef[6, e, rt, ct] - newton_shifts[k - 1] * basis_scale) * centre[ct]
                        value = value - (coef[0, e, rt, ct] * down + coef[4, e, rt, ct] * up)
                        value = value - (coef[1, e, rt, ct] * rights[ct] + coef[5, e, rt, ct] * lefts[ct])
                        value = value - coef[2, e, rt, ct] * field[k - 1, e + 1, rt, ct]
                        value = value - coef[2, e - 1, rt, ct] * field[k - 1, e - 1, rt, ct]
                        field[k, e, rt, ct] = value
            for l in range(layers):
                e = depth + l
                near, far = field[k, e, 0, 0], field[k, e, 0, 1]
                if l:
                    c = skew[e]
                    shift = lax.rem(cols + c, cols)
                    kept = (lane - c >= 0) & (lane - c < cols)
                    near = jnp.where(kept, pltpu.roll(near, shift, 1), pltpu.roll(far, shift, 1))
                basis_ref[pl.ds(l * rows * order + (k - 1) * fields + f, rows, stride=order), :] = near

    gram_ref[...] = jnp.zeros_like(gram_ref)

    @pl.loop(0, layers * rows // 2)
    def _(i):
        start = pl.multiple_of(i * 2 * order, 8)
        middle = pl.multiple_of(i * 2 * order + order, 8)
        wide = jnp.concatenate([basis_ref[pl.ds(start, order), :], basis_ref[pl.ds(middle, order), :]], axis=1)
        gram_ref[...] += lax.dot_general(
            wide, wide, (((1,), (1,)), ((), ())),
            precision=lax.Precision.HIGHEST, preferred_element_type=jnp.float32,
        )


def eliminate(tiles, order, step):
    width = tiles[0].shape[1]
    lane = lax.broadcasted_iota(jnp.int32, (8, width), 1)
    sub = lax.broadcasted_iota(jnp.int32, (8, width), 0)
    spread = lambda value: jnp.broadcast_to(value, (8, width))
    for first in range(0, order, step):
        home, base = first // 8, first % 8
        panel = tiles[home]
        entry = {}
        for i in range(step):
            for j in range(i, step):
                entry[i, j] = spread(panel[base + i : base + i + 1, first + j : first + j + 1])
        rows = [spread(panel[base + i : base + i + 1, :]) for i in range(step)]
        inverse = []
        done = []
        for i in range(step):
            row = rows[i]
            if i:
                row = jnp.where((lane >= first) & (lane < first + i), 0.0, row)
            factors = []
            for j in range(i):
                factor = entry[j, i] * inverse[j]
                factors.append(factor)
            for j in range(i):
                source = jnp.where(lane == first + j, 1.0, done[j])
                if i - j > 1:
                    source = jnp.where((lane > first + j) & (lane < first + i), 0.0, source)
                row = row - factors[j] * source
                for m in range(i, step):
                    entry[i, m] = entry[i, m] - factors[j] * entry[j, m]
            inverse.append(1.0 / entry[i, i])
            done.append(row)
        sources = []
        for j in range(step):
            source = jnp.where(lane == first + j, 1.0, done[j])
            if j < step - 1:
                source = jnp.where((lane > first + j) & (lane < first + step), 0.0, source)
            sources.append(source)
        inside = (lane >= first) & (lane < first + step)
        for t in range(home, order // 8):
            if t == home and base + step == 8:
                fresh = tiles[t]
            else:
                columns = [spread(tiles[t][:, first + j : first + j + 1]) for j in range(step)]
                fresh = jnp.where(inside, 0.0, tiles[t])
                for j in range(step):
                    factor = columns[j] * inverse[j]
                    fresh = fresh - factor * sources[j]
                    for m in range(j + 1, step):
                        columns[m] = columns[m] - factor * entry[j, m]
            if t == home:
                fresh = jnp.where(sub < base + step, tiles[t], fresh)
                for j in range(step):
                    fresh = jnp.where(sub == base + j, done[j], fresh)
            tiles[t] = fresh
    return tiles


def finish_kernel(*refs, parts, count, step):
    part_refs, basis_ref, upper_ref, out_ref = refs[:parts], refs[parts], refs[parts + 1], refs[parts + 2]
    order = upper_ref.shape[0]
    points = basis_ref.shape[0] // order
    tiles = []
    for t in range(order // 8):
        pieces = [ref[8 * t : 8 * t + 8, :] for ref in part_refs]
        tiles.append(together(pieces) / count)
    tiles = eliminate(tiles, order, step)
    lane = lax.broadcasted_iota(jnp.int32, (8, order), 1)
    sub = lax.broadcasted_iota(jnp.int32, (8, order), 0)
    inverse = []
    for t in range(order // 8):
        row = sub + 8 * t
        pivot = jnp.sum(jnp.where(lane == row, tiles[t], 0.0), axis=1, keepdims=True)
        scale = 1.0 / jnp.sqrt(pivot)
        upper_ref[8 * t : 8 * t + 8, :] = jnp.where(lane >= row, tiles[t] * scale, 0.0)
        inverse.append(jnp.where(lane < row, tiles[t], jnp.where(lane == row, 1.0, 0.0)) * scale)
    inverse = jnp.concatenate(inverse, axis=0)
    for i in range(points // 2):
        start = 2 * i * order
        wide = jnp.concatenate(
            [basis_ref[start : start + order, :], basis_ref[start + order : start + 2 * order, :]], axis=1
        )
        out = jnp.dot(inverse, wide, precision=lax.Precision.HIGHEST, preferred_element_type=jnp.float32)
        cols = basis_ref.shape[1]
        out_ref[pl.ds(2 * i, order, stride=points), :] = out[:, :cols]
        out_ref[pl.ds(2 * i + 1, order, stride=points), :] = out[:, cols:]


def together(pieces):
    while len(pieces) > 1:
        half = len(pieces) // 2
        pieces = [pieces[i] + pieces[i + half] for i in range(half)]
    return pieces[0]


def gathered(value, axis):
    size = lax.axis_size(axis)
    return [value] + [
        lax.ppermute(value, axis, [((i + step) % size, i) for i in range(size)]) for step in range(1, size)
    ]


def summed(value, axis):
    size = lax.axis_size(axis)
    if size <= 4:
        return together(gathered(value, axis))
    step = 1
    while step < size:
        value = value + lax.ppermute(value, axis, [(i, i ^ step) for i in range(size)])
        step *= 2
    return value


def sent(value, steps):
    axes = tuple(steps)
    sizes = [lax.axis_size(name) for name in axes]
    pairs = []
    if len(axes) == 1:
        pairs = [(i, i + steps[axes[0]]) for i in range(sizes[0]) if 0 <= i + steps[axes[0]] < sizes[0]]
        return lax.ppermute(value, axes[0], pairs)
    for i in range(sizes[0]):
        for j in range(sizes[1]):
            m, n = i + steps[axes[0]], j + steps[axes[1]]
            if 0 <= m < sizes[0] and 0 <= n < sizes[1]:
                pairs.append((i * sizes[1] + j, m * sizes[1] + n))
    return lax.ppermute(value, axes, pairs)


def local(load_currents, cond_rows, cond_cols, cond_vias, ground, via_offset):
    fields, layers, rows, cols = load_currents.shape
    assert layers == POWERS and rows == 2 * POWERS and (fields + 4) * POWERS <= cols
    float_of = lambda *shape: jax.ShapeDtypeStruct(shape, jnp.float32)
    pair = lax.axis_size("gy") == 2
    sides = 1 if pair else 2
    coef, *edges = pl.pallas_call(
        edges_kernel,
        out_shape=(float_of(4, layers, rows, cols),) + (float_of(layers, rows, cols),) * sides,
        in_specs=[VMEM] * 5 + [SMEM],
        out_specs=(VMEM,) * (1 + sides),
        compiler_params=PARAMS,
        name="edges",
    )(load_currents, cond_rows, cond_cols, cond_vias, ground, via_offset)
    if pair:
        strips = [lax.ppermute(edges[0], "gy", [(0, 1), (1, 0)])]
    else:
        strips = [sent(edges[0], {"gy": 1}), sent(edges[1], {"gy": -1})]
    planes = fields + 6
    whole, half, corner = (float_of(planes, n, rows, cols) for n in (layers, layers // 2, 1))
    corner = float_of(planes, rows, cols)
    block, to_next, to_prev, pp, pm, mp, mm = pl.pallas_call(
        functools.partial(pack_kernel, pair=pair),
        out_shape=(whole, half, half, corner, corner, corner, corner),
        in_specs=[VMEM] * (2 + sides),
        out_specs=(VMEM,) * 7,
        compiler_params=PARAMS,
        name="pack",
    )(load_currents, coef, *strips)
    below = sent(block, {"gz": 1})
    above = sent(block, {"gz": -1})
    after = sent(to_next, {"gx": 1})
    before = sent(to_prev, {"gx": -1})
    bp = sent(pp, {"gx": 1, "gz": 1})
    ap = sent(pm, {"gx": 1, "gz": -1})
    bn = sent(mp, {"gx": -1, "gz": 1})
    an = sent(mm, {"gx": -1, "gz": -1})
    order = POWERS * fields
    points = layers * rows
    high = layers + 2 * POWERS
    basis, gram = pl.pallas_call(
        powers_kernel,
        out_shape=(float_of(points * order, cols), float_of(order, order)),
        in_specs=[VMEM] * 9 + [SMEM],
        out_specs=(VMEM, VMEM),
        scratch_shapes=[
            pltpu.VMEM((2, high, 2, rows, cols), jnp.float32),
            pltpu.VMEM((7, high, 2, 2, rows, cols), jnp.float32),
            pltpu.VMEM((POWERS + 1, high, 2, 2, rows, cols), jnp.float32),
        ],
        compiler_params=PARAMS,
        name="powers",
    )(block, below, above, after, before, bp, bn, ap, an, via_offset)
    count = points * cols * lax.axis_size("gx") * lax.axis_size("gy") * lax.axis_size("gz")
    gram = summed(gram, "gy")
    gram = summed(gram, "gx")
    parts = gathered(gram, "gz") if lax.axis_size("gz") in (2, 4) else [summed(gram, "gz")]
    upper, basis_q = pl.pallas_call(
        functools.partial(finish_kernel, parts=len(parts), count=float(count), step=4),
        out_shape=(float_of(order, order), float_of(order * points, cols)),
        in_specs=[VMEM] * (len(parts) + 1),
        out_specs=(VMEM, VMEM),
        compiler_params=PARAMS,
        name="finish",
    )(*parts, basis)
    return basis_q.reshape(order, layers, rows, cols), upper


def solution(mesh):
    in_specs = (
        P(None, "gz", "gx", "gy"),
        P("gz", "gx", "gy"),
        P("gz", "gx", "gy"),
        P("gz", "gx", "gy"),
        P("gz", "gx", "gy"),
        P(),
    )
    out_specs = (P(None, "gz", "gx", "gy"), P())
    return jax.shard_map(local, mesh=mesh, in_specs=in_specs, out_specs=out_specs, check_vma=False)
```

```python
import functools

import jax
import jax.numpy as jnp
from jax import lax
from jax.experimental import pallas as pl
from jax.experimental.pallas import tpu as pltpu
from jax.sharding import PartitionSpec as P

POWERS = 4


newton_shifts = (15.4, 0.6, 11.7, 4.3)
basis_scale = 0.125

VMEM = pl.BlockSpec(memory_space=pltpu.VMEM)
SMEM = pl.BlockSpec(memory_space=pltpu.SMEM)
ANY = pl.BlockSpec(memory_space=pl.ANY)
PARAMS = pltpu.CompilerParams(vmem_limit_bytes=40 * 1024 * 1024)

COEFS = 4
TOP = 2 * POWERS
HOME = TOP + POWERS


def positions(shape):
    sub = lax.broadcasted_iota(jnp.int32, shape, 0)
    lane = lax.broadcasted_iota(jnp.int32, shape, 1)
    return sub, lane


def edges_kernel(
    load_ref, rows_ref, cols_ref, vias_ref, ground_ref, offset_ref, block_ref, shift_ref, *refs, pair
):
    strip_refs, (staged, sems) = refs[:-2], refs[-2:]
    planes, layers, rows, cols = block_ref.shape
    fields = load_ref.shape[0]
    depth = POWERS
    group = 2 * depth
    per_tile = cols // group
    tiles = strip_refs[0].shape[0]
    total_layers = offset_ref.shape[0]
    copies = [
        pltpu.make_async_copy(ref, staged.at[i], sems.at[i])
        for i, ref in enumerate((rows_ref, cols_ref, vias_ref, ground_ref))
    ]
    copies.append(pltpu.make_async_copy(load_ref, block_ref.at[pl.ds(0, fields)], sems.at[COEFS]))
    for copy in copies:
        copy.start()
    gx, gy, gz = (lax.axis_index(name) for name in ("gx", "gy", "gz"))
    last_row = jnp.where(gx == lax.axis_size("gx") - 1, rows - 1, rows)
    last_col = jnp.where(gy == lax.axis_size("gy") - 1, cols - 1, cols)
    sub, lane = positions((rows, cols))
    for e in range(shift_ref.shape[0]):
        layer = gz * layers + e - depth
        inside = (layer >= 0) & (layer < total_layers)
        value = jnp.where(inside, offset_ref[jnp.clip(layer, 0, total_layers - 1)], 0)
        shift_ref[e] = jnp.broadcast_to(value, (rows, cols))
    for copy in copies:
        copy.wait()
    for l in range(layers):
        layer = gz * layers + l
        target = gy * cols + lane + shift_ref[depth + l]
        via_ok = (target >= 0) & (target < cols * lax.axis_size("gy"))
        via_ok = via_ok & (jnp.broadcast_to(layer, lane.shape) < total_layers - 1)
        block_ref[fields, l] = jnp.where(sub == last_row, 0.0, staged[0, l])
        block_ref[fields + 1, l] = jnp.where(lane == last_col, 0.0, staged[1, l])
        block_ref[fields + 2, l] = jnp.where(via_ok, staged[2, l], 0.0)
        block_ref[fields + 3, l] = staged[3, l]
    ahead = lax.rem(lane + group // 4, group)
    for l in range(layers):
        for t in range(tiles):
            low = jnp.zeros((rows, cols), jnp.float32)
            high = jnp.zeros((rows, cols), jnp.float32)
            for f in range(min(per_tile, fields + COEFS - t * per_tile)):
                tile = block_ref[t * per_tile + f, l]
                start = group * f
                mine = (lane >= start) & (lane < start + group)
                low = jnp.where(mine, pltpu.roll(tile, (start + depth) % cols, 1), low)
                mine = lax.rem(lane + depth // 2, cols)
                mine = (mine >= start) & (mine < start + group)
                high = jnp.where(mine, pltpu.roll(tile, (start + depth // 2) % cols, 1), high)
            block_ref[fields + COEFS + t, l] = low
            block_ref[fields + COEFS + tiles + t, l] = high
            if pair:
                strip_refs[0][t, l] = jnp.where(jnp.broadcast_to(gy, (rows, cols)) == 0, low, high)
            else:
                strip_refs[0][t, l] = low
                strip_refs[1][t, l] = high


def rows_kernel(block_ref, *refs, pair, fields):
    count = 1 if pair else 2
    strip_refs = refs[:count]
    strips_ref, next_ref, prev_ref = refs[count:]
    planes, layers, rows, cols = block_ref.shape
    depth = POWERS
    group = 2 * depth
    half = rows // 2
    tiles = strip_refs[0].shape[0]
    sub, lane = positions((rows, cols))
    outer_low = lax.rem(lane, group) < depth
    outer_high = lax.rem(lane + depth // 2, group) >= depth
    gy = jnp.broadcast_to(lax.axis_index("gy"), (rows, cols))
    for t in range(tiles):
        for l in range(layers):
            if pair:
                got = strip_refs[0][t, l]
                low, high = jnp.where(gy == 1, got, 0.0), jnp.where(gy == 0, got, 0.0)
            else:
                low, high = strip_refs[0][t, l], strip_refs[1][t, l]
            start = fields + COEFS
            strips_ref[t, l] = jnp.where(outer_low, low, block_ref[start + t, l])
            strips_ref[tiles + t, l] = jnp.where(outer_high, high, block_ref[start + tiles + t, l])

    def emit(q, source, p):
        for t in range(layers // 2):
            x, y = source[p, 2 * t], source[p, 2 * t + 1]
            turned = pltpu.roll(y, half, 0)
            next_ref[q, t] = jnp.where(sub >= half, x, turned)
            prev_ref[q, t] = jnp.where(sub < half, x, turned)

    @pl.loop(0, fields + COEFS, unroll=4)
    def _(q):
        emit(q, block_ref, q)

    for p in range(2 * tiles):
        emit(fields + COEFS + p, strips_ref, p)


def layers_kernel(block_ref, strips_ref, after_ref, before_ref, up_ref, down_ref, *, fields):
    planes, layers, rows, cols = block_ref.shape
    half = rows // 2
    sub, lane = positions((rows, cols))

    def emit(q, source, p):
        low, high = [], []
        for l in range(layers):
            tile = source[p, l]
            up_ref[q, l] = tile
            down_ref[q, l] = tile
            t = l // 2
            low.append(pltpu.roll(after_ref[q, t], half, 0) if l % 2 == 0 else after_ref[q, t])
            high.append(pltpu.roll(before_ref[q, t], half, 0) if l % 2 == 0 else before_ref[q, t])
        for ref, (one, two, three) in ((up_ref, (3, 2, 1)), (down_ref, (0, 1, 2))):
            ref[q, layers] = jnp.where(
                sub < half,
                low[one],
                jnp.where(sub >= half + 2, pltpu.roll(low[two], half, 0), pltpu.roll(low[three], 1, 0)),
            )
            ref[q, layers + 1] = jnp.where(
                sub >= half,
                high[one],
                jnp.where(sub < half - 2, pltpu.roll(high[two], half, 0), pltpu.roll(high[three], rows - 1, 0)),
            )

    @pl.loop(0, fields + COEFS, unroll=2)
    def _(q):
        emit(q, block_ref, q)

    for p in range(planes - fields - COEFS):
        emit(fields + COEFS + p, strips_ref, p)


def powers_kernel(
    block_ref, strips_ref, after_ref, before_ref, below_ref, above_ref, shift_ref,
    basis_ref, gram_ref, raw, coef, strip, field, *, fields, together,
):
    planes, layers, rows, cols = block_ref.shape
    depth = POWERS
    half = rows // 2
    group = 2 * depth
    per_tile = cols // group
    tiles = strips_ref.shape[0] // 2
    order = depth * fields
    high = layers + 2 * depth
    sub, lane = positions((rows, cols))
    base = fields + COEFS

    def clear(ref, lead):
        @pl.loop(0, lead)
        def _(i):
            for e in range(high):
                ref[i, e] = jnp.zeros(ref.shape[2:], jnp.float32)

    clear(raw, COEFS)
    for part in range(coef.shape[0]):
        clear(coef.at[part], coef.shape[1])
    for part in range(strip.shape[0]):
        clear(strip.at[part], strip.shape[1])
    for part in range(field.shape[0]):
        clear(field.at[part], field.shape[1])

    def assemble(q, source, p, out):
        end = HOME + rows
        for l in range(layers):
            e, t = depth + l, l // 2
            out[e, HOME:end, :] = source[p, l]
            a = half if l % 2 == 0 else 0
            out[e, TOP:HOME, :] = after_ref[q, t, a : a + half, :]
            b = 0 if l % 2 == 0 else half
            out[e, end : end + depth, :] = before_ref[q, t, b : b + half, :]
        for ref, first, distances in ((below_ref, 0, (4, 3, 2, 1)), (above_ref, depth + layers, (1, 2, 3, 4))):
            for i, distance in enumerate(distances):
                e = first + i
                out[e, HOME:end, :] = ref[q, i]
                if distance == 1:
                    out[e, HOME - 3 : HOME, :] = ref[q, layers, 1:4, :]
                    out[e, end : end + 3, :] = ref[q, layers + 1, 4:7, :]
                elif distance == 2:
                    out[e, HOME - 2 : HOME, :] = ref[q, layers, 6:8, :]
                    out[e, end : end + 2, :] = ref[q, layers + 1, 0:2, :]
                elif distance == 3:
                    out[e, HOME - 1 : HOME, :] = ref[q, layers, 4:5, :]
                    out[e, end : end + 1, :] = ref[q, layers + 1, 3:4, :]

    def sides(source, e, row, edge):
        centre = source[e, row : row + rows, :]
        left, right = pltpu.roll(centre, 1, 1), pltpu.roll(centre, cols - 1, 1)
        if edge is not None:
            ref, turn = edge
            outer = pltpu.roll(ref[e, row : row + rows, :], turn, 1)
            left = jnp.where(lane == 0, outer, left)
            right = jnp.where(lane == cols - 1, outer, right)
        return left, centre, right

    def from_above(seen, e):
        left, centre, right = seen
        shift = shift_ref[e]
        return jnp.where(shift == 0, centre, jnp.where(shift > 0, right, left))

    def from_below(seen, e):
        left, centre, right = seen
        shift = shift_ref[e]
        return jnp.where(shift == 0, centre, jnp.where(shift > 0, left, right))

    def turn_of(q):
        return lax.rem(2 * cols - group * lax.rem(q, per_tile) - depth + 1, cols)

    def prepare(part, edge_of):
        both = (TOP, TOP + rows)
        for e in range(1, high - 1):
            for row in both:
                here = slice(row, row + rows)
                down, right, upper = (raw[c, e, here, :] for c in range(3))
                up = raw[0, e, row - 1 : row - 1 + rows, :]
                left = sides(raw.at[1], e, row, edge_of(1))[0]
                lower = from_below(sides(raw.at[2], e - 1, row, edge_of(2)), e - 1)
                coef[part, 0, e, here, :] = down
                coef[part, 1, e, here, :] = right
                coef[part, 2, e, here, :] = upper
                coef[part, 3, e, here, :] = left
                coef[part, 4, e, here, :] = lower
                coef[part, 5, e, here, :] = raw[3, e, here, :] + down + up + right + left + upper + lower

    def advance(part, members, k):
        reach = depth - k
        theta = newton_shifts[k - 1] * basis_scale
        seen = {}

        def look(m, e, row):
            if (m, e, row) not in seen:
                seen[m, e, row] = sides(members[m][0].at[k - 1], e, row, members[m][1](k - 1))
            return seen[m, e, row]

        work = [(e, row) for e in range(depth - reach + 1, depth + layers + reach - 1) for row in (TOP, TOP + rows)]
        work = sorted(work, key=lambda item: item[1]) if reach else []
        ends = range(depth, depth + layers) if not reach else (depth - reach, depth + layers + reach - 1)
        work = work + [(e, HOME) for e in ends]
        for e, row in work:
            here = slice(row, row + rows)
            down, right, upper, left, lower, diagonal = (coef[part, c, e, here, :] for c in range(6))
            up = coef[part, 0, e, row - 1 : row - 1 + rows, :]
            diagonal = diagonal - theta
            for m, (buffers, _) in enumerate(members):
                lefts, centre, rights = look(m, e, row)
                value = diagonal * centre
                value = value - (
                    down * buffers[k - 1, e, row + 1 : row + 1 + rows, :]
                    + up * buffers[k - 1, e, row - 1 : row - 1 + rows, :]
                )
                value = value - (right * rights + left * lefts)
                value = value - upper * from_above(look(m, e + 1, row), e)
                value = value - lower * from_below(look(m, e - 1, row), e - 1)
                buffers[k, e, here, :] = value

    for p in range(2 * tiles):
        assemble(base + p, strips_ref, p, strip.at[p].at[0])
    for side in range(2):
        for c in range(COEFS):
            t, member = divmod(fields + c, per_tile)
            start = group * member - (depth // 2 if side else 0)
            mine = (lane >= start) & (lane < start + group)
            for e in range(high):
                for row in (TOP, TOP + rows):
                    value = jnp.where(mine, strip[side * tiles + t, 0, e, row : row + rows, :], 0.0)
                    width = group
                    while width < cols:
                        value = value + pltpu.roll(value, width, 1)
                        width *= 2
                    raw[c, e, row : row + rows, :] = value * basis_scale
        prepare(1 + side, lambda c: None)
        for k in range(1, depth):
            advance(1 + side, [(strip.at[side * tiles + t], lambda k: None) for t in range(tiles)], k)
    border = lax.rem(lane, group) == depth - 1
    for t in range(tiles):
        for k in range(depth):
            for e in range(high):
                for row in (TOP, TOP + rows):
                    here = slice(row, row + rows)
                    strip[t, k, e, here, :] = jnp.where(
                        border, strip[t, k, e, here, :], strip[tiles + t, k, e, here, :]
                    )

    for c in range(COEFS):
        assemble(fields + c, block_ref, fields + c, raw.at[c])
    for c in range(COEFS):
        for e in range(high):
            for row in (TOP, TOP + rows):
                raw[c, e, row : row + rows, :] = raw[c, e, row : row + rows, :] * basis_scale

    def edge_of(c):
        q = fields + c
        return scaled.at[q // per_tile], (2 * cols - group * (q % per_tile) - depth + 1) % cols

    scaled = field.at[0]
    for t in sorted({(fields + c) // per_tile for c in (1, 2)}):
        for e in range(high):
            for row in (TOP, TOP + rows):
                here = slice(row, row + rows)
                scaled[t, e, here, :] = strip[t, 0, e, here, :] * basis_scale
    prepare(0, edge_of)

    @pl.loop(0, fields // together)
    def _(i):
        members = []
        for m in range(together):
            f = i * together + m
            assemble(f, block_ref, f, field.at[m].at[0])
            edge = functools.partial(
                lambda k, t, turn: (strip.at[t].at[k], turn), t=lax.div(f, per_tile), turn=turn_of(f)
            )
            members.append((field.at[m], edge))
        for k in range(1, depth + 1):
            advance(0, members, k)
            for m in range(together):
                f = i * together + m
                for l in range(layers):
                    tile = field[m, k, depth + l, HOME : HOME + rows, :]
                    basis_ref[pl.ds(l * rows * order + (k - 1) * fields + f, rows, stride=order), :] = tile

    total = jnp.zeros((order, order), jnp.float32)
    for i in range(layers * rows // 2):
        start = 2 * i * order
        wide = jnp.concatenate(
            [basis_ref[start : start + order, :], basis_ref[start + order : start + 2 * order, :]], axis=1
        )
        total = total + lax.dot_general(
            wide, wide, (((1,), (1,)), ((), ())),
            precision=lax.Precision.HIGHEST, preferred_element_type=jnp.float32,
        )
    gram_ref[...] = total


def eliminate(tiles, order, step):
    width = tiles[0].shape[1]
    lane = lax.broadcasted_iota(jnp.int32, (8, width), 1)
    sub = lax.broadcasted_iota(jnp.int32, (8, width), 0)
    spread = lambda value: jnp.broadcast_to(value, (8, width))
    for first in range(0, order, step):
        home, base = first // 8, first % 8
        panel = tiles[home]
        entry = {}
        for i in range(step):
            for j in range(i, step):
                entry[i, j] = spread(panel[base + i : base + i + 1, first + j : first + j + 1])
        rows = [spread(panel[base + i : base + i + 1, :]) for i in range(step)]
        inverse = []
        done = []
        for i in range(step):
            row = rows[i]
            if i:
                row = jnp.where((lane >= first) & (lane < first + i), 0.0, row)
            factors = []
            for j in range(i):
                factor = entry[j, i] * inverse[j]
                factors.append(factor)
            for j in range(i):
                source = jnp.where(lane == first + j, 1.0, done[j])
                if i - j > 1:
                    source = jnp.where((lane > first + j) & (lane < first + i), 0.0, source)
                row = row - factors[j] * source
                for m in range(i, step):
                    entry[i, m] = entry[i, m] - factors[j] * entry[j, m]
            inverse.append(1.0 / entry[i, i])
            done.append(row)
        sources = []
        for j in range(step):
            source = jnp.where(lane == first + j, 1.0, done[j])
            if j < step - 1:
                source = jnp.where((lane > first + j) & (lane < first + step), 0.0, source)
            sources.append(source)
        inside = (lane >= first) & (lane < first + step)
        for t in range(home, order // 8):
            if t == home and base + step == 8:
                fresh = tiles[t]
            else:
                columns = [spread(tiles[t][:, first + j : first + j + 1]) for j in range(step)]
                fresh = jnp.where(inside, 0.0, tiles[t])
                for j in range(step):
                    factor = columns[j] * inverse[j]
                    fresh = fresh - factor * sources[j]
                    for m in range(j + 1, step):
                        columns[m] = columns[m] - factor * entry[j, m]
            if t == home:
                fresh = jnp.where(sub < base + step, tiles[t], fresh)
                for j in range(step):
                    fresh = jnp.where(sub == base + j, done[j], fresh)
            tiles[t] = fresh
    return tiles


def finish_kernel(*refs, parts, count, step):
    part_refs, basis_ref, upper_ref, out_ref = refs[:parts], refs[parts], refs[parts + 1], refs[parts + 2]
    order = upper_ref.shape[0]
    points = basis_ref.shape[0] // order
    tiles = []
    for t in range(order // 8):
        pieces = [ref[8 * t : 8 * t + 8, :] for ref in part_refs]
        tiles.append(folded(pieces) / count)
    tiles = eliminate(tiles, order, step)
    lane = lax.broadcasted_iota(jnp.int32, (8, order), 1)
    sub = lax.broadcasted_iota(jnp.int32, (8, order), 0)
    inverse = []
    for t in range(order // 8):
        row = sub + 8 * t
        pivot = jnp.sum(jnp.where(lane == row, tiles[t], 0.0), axis=1, keepdims=True)
        scale = 1.0 / jnp.sqrt(pivot)
        upper_ref[8 * t : 8 * t + 8, :] = jnp.where(lane >= row, tiles[t] * scale, 0.0)
        inverse.append(jnp.where(lane < row, tiles[t], jnp.where(lane == row, 1.0, 0.0)) * scale)
    inverse = jnp.concatenate(inverse, axis=0)
    for i in range(points // 2):
        start = 2 * i * order
        wide = jnp.concatenate(
            [basis_ref[start : start + order, :], basis_ref[start + order : start + 2 * order, :]], axis=1
        )
        out = jnp.dot(inverse, wide, precision=lax.Precision.HIGHEST, preferred_element_type=jnp.float32)
        cols = basis_ref.shape[1]
        out_ref[pl.ds(2 * i, order, stride=points), :] = out[:, :cols]
        out_ref[pl.ds(2 * i + 1, order, stride=points), :] = out[:, cols:]


def folded(pieces):
    while len(pieces) > 1:
        half = len(pieces) // 2
        pieces = [pieces[i] + pieces[i + half] for i in range(half)]
    return pieces[0]


def gathered(value, axis):
    size = lax.axis_size(axis)
    return [value] + [
        lax.ppermute(value, axis, [((i + step) % size, i) for i in range(size)]) for step in range(1, size)
    ]


def summed(value, axis):
    size = lax.axis_size(axis)
    if size <= 4:
        return folded(gathered(value, axis))
    step = 1
    while step < size:
        value = value + lax.ppermute(value, axis, [(i, i ^ step) for i in range(size)])
        step *= 2
    return value


def sent(value, steps):
    axes = tuple(steps)
    sizes = [lax.axis_size(name) for name in axes]
    pairs = []
    if len(axes) == 1:
        pairs = [(i, i + steps[axes[0]]) for i in range(sizes[0]) if 0 <= i + steps[axes[0]] < sizes[0]]
        return lax.ppermute(value, axes[0], pairs)
    for i in range(sizes[0]):
        for j in range(sizes[1]):
            m, n = i + steps[axes[0]], j + steps[axes[1]]
            if 0 <= m < sizes[0] and 0 <= n < sizes[1]:
                pairs.append((i * sizes[1] + j, m * sizes[1] + n))
    return lax.ppermute(value, axes, pairs)


def local(load_currents, cond_rows, cond_cols, cond_vias, ground, via_offset):
    fields, layers, rows, cols = load_currents.shape
    assert layers == POWERS and rows == 2 * POWERS and (fields + 4) * POWERS <= cols
    float_of = lambda *shape: jax.ShapeDtypeStruct(shape, jnp.float32)
    pair = lax.axis_size("gy") == 2
    sides = 1 if pair else 2
    group = 2 * POWERS
    tiles = -(-(fields + COEFS) * group // cols)
    planes = fields + COEFS + 2 * tiles
    high = layers + 2 * POWERS
    block, shifts, *edges = pl.pallas_call(
        functools.partial(edges_kernel, pair=pair),
        out_shape=(
            float_of(planes, layers, rows, cols),
            jax.ShapeDtypeStruct((high, rows, cols), jnp.int32),
        )
        + (float_of(tiles, layers, rows, cols),) * sides,
        in_specs=[ANY] * 5 + [SMEM],
        out_specs=(VMEM,) * (2 + sides),
        scratch_shapes=[
            pltpu.VMEM((COEFS, layers, rows, cols), jnp.float32),
            pltpu.SemaphoreType.DMA((COEFS + 1,)),
        ],
        compiler_params=PARAMS,
        name="edges",
    )(load_currents, cond_rows, cond_cols, cond_vias, ground, via_offset)
    if pair:
        strips = [lax.ppermute(edges[0], "gy", [(0, 1), (1, 0)])]
    else:
        strips = [sent(edges[0], {"gy": 1}), sent(edges[1], {"gy": -1})]
    joined, to_next, to_prev = pl.pallas_call(
        functools.partial(rows_kernel, pair=pair, fields=fields),
        out_shape=(float_of(2 * tiles, layers, rows, cols),) + (float_of(planes, layers // 2, rows, cols),) * 2,
        in_specs=[VMEM] * (1 + sides),
        out_specs=(VMEM,) * 3,
        compiler_params=PARAMS,
        name="rows",
    )(block, *strips)
    after = sent(to_next, {"gx": 1})
    before = sent(to_prev, {"gx": -1})
    to_above, to_below = pl.pallas_call(
        functools.partial(layers_kernel, fields=fields),
        out_shape=(float_of(planes, layers + 2, rows, cols),) * 2,
        in_specs=[VMEM] * 4,
        out_specs=(VMEM,) * 2,
        compiler_params=PARAMS,
        name="layers",
    )(block, joined, after, before)
    below = sent(to_above, {"gz": 1})
    above = sent(to_below, {"gz": -1})
    order = POWERS * fields
    points = layers * rows
    together = 2 if fields % 2 == 0 else 1
    tall = 4 * rows
    basis, gram = pl.pallas_call(
        functools.partial(powers_kernel, fields=fields, together=together),
        out_shape=(float_of(points * order, cols), float_of(order, order)),
        in_specs=[VMEM] * 7,
        out_specs=(VMEM, VMEM),
        scratch_shapes=[
            pltpu.VMEM((COEFS, high, tall, cols), jnp.float32),
            pltpu.VMEM((3, 6, high, tall, cols), jnp.float32),
            pltpu.VMEM((2 * tiles, POWERS, high, tall, cols), jnp.float32),
            pltpu.VMEM((max(together, 1), POWERS + 1, high, tall, cols), jnp.float32),
        ],
        compiler_params=PARAMS,
        name="powers",
    )(block, joined, after, before, below, above, shifts)
    count = points * cols * lax.axis_size("gx") * lax.axis_size("gy") * lax.axis_size("gz")
    gram = summed(gram, "gy")
    gram = summed(gram, "gx")
    parts = gathered(gram, "gz") if lax.axis_size("gz") in (2, 4) else [summed(gram, "gz")]
    upper, basis_q = pl.pallas_call(
        functools.partial(finish_kernel, parts=len(parts), count=float(count), step=4),
        out_shape=(float_of(order, order), float_of(order * points, cols)),
        in_specs=[VMEM] * (len(parts) + 1),
        out_specs=(VMEM, VMEM),
        compiler_params=PARAMS,
        name="finish",
    )(*parts, basis)
    return basis_q.reshape(order, layers, rows, cols), upper


def solution(mesh):
    in_specs = (
        P(None, "gz", "gx", "gy"),
        P("gz", "gx", "gy"),
        P("gz", "gx", "gy"),
        P("gz", "gx", "gy"),
        P("gz", "gx", "gy"),
        P(),
    )
    out_specs = (P(None, "gz", "gx", "gy"), P())
    return jax.shard_map(local, mesh=mesh, in_specs=in_specs, out_specs=out_specs, check_vma=False)
```

```python
import functools

import jax
import jax.numpy as jnp
from jax import lax
from jax.experimental import pallas as pl
from jax.experimental.pallas import tpu as pltpu
from jax.sharding import PartitionSpec as P

POWERS = 4


newton_shifts = (15.4, 0.6, 11.7, 4.3)
basis_scale = 0.125

VMEM = pl.BlockSpec(memory_space=pltpu.VMEM)
SMEM = pl.BlockSpec(memory_space=pltpu.SMEM)
HBM = pl.BlockSpec(memory_space=pltpu.HBM)
PARAMS = pltpu.CompilerParams(vmem_limit_bytes=48 * 1024 * 1024)

COEFS = 4
TILE = 8
CORNERS = ((1, 3), (1, 2), (1, 1), (2, 2), (2, 1), (3, 1))


def positions(shape):
    sub = lax.broadcasted_iota(jnp.int32, shape, 0)
    lane = lax.broadcasted_iota(jnp.int32, shape, 1)
    return sub, lane


def edges_kernel(
    load_ref, rows_ref, cols_ref, vias_ref, ground_ref, offset_ref, block_ref, shift_ref, edge_ref, fields_in, coefs_in, sems
):
    slabs, planes, cols = block_ref.shape
    fields = load_ref.shape[0] // slabs
    layers, rows, _ = rows_ref.shape
    depth = POWERS
    group = 2 * depth
    total_layers = offset_ref.shape[0]
    copies = [
        pltpu.make_async_copy(ref, coefs_in.at[i], sems.at[i])
        for i, ref in enumerate((rows_ref, cols_ref, vias_ref, ground_ref))
    ]
    copies.append(pltpu.make_async_copy(load_ref, fields_in, sems.at[COEFS]))
    for copy in copies:
        copy.start()
    gx, gy, gz = (lax.axis_index(name) for name in ("gx", "gy", "gz"))
    last_row = jnp.where(gx == lax.axis_size("gx") - 1, rows - 1, rows)
    last_col = jnp.where(gy == lax.axis_size("gy") - 1, cols - 1, cols)
    sub, lane = positions((TILE, cols))
    for e in range(shift_ref.shape[0]):
        layer = gz * layers + e - depth
        inside = (layer >= 0) & (layer < total_layers)
        value = jnp.where(inside, offset_ref[jnp.clip(layer, 0, total_layers - 1)], 0)
        shift_ref[e] = jnp.broadcast_to(value, (TILE, cols))
    for copy in copies:
        copy.wait()
    for l in range(layers):
        layer = gz * layers + l
        target = gy * cols + lane + shift_ref[depth + l]
        via_ok = (target >= 0) & (target < cols * lax.axis_size("gy"))
        via_ok = via_ok & (jnp.broadcast_to(layer, lane.shape) < total_layers - 1)
        four = (
            jnp.where(sub == last_row, 0.0, coefs_in[0, l]),
            jnp.where(lane == last_col, 0.0, coefs_in[1, l]),
            jnp.where(via_ok, coefs_in[2, l], 0.0),
            coefs_in[3, l],
        )
        for r in range(rows):
            slab = l * rows + r
            for f in range(0, fields, TILE):
                block_ref[slab, f : f + TILE, :] = fields_in[pl.ds(f * slabs + slab, TILE, stride=slabs), :]
            value = jnp.zeros((TILE, cols), jnp.float32)
            for c in range(COEFS):
                value = jnp.where(sub == c, jnp.broadcast_to(four[c][r : r + 1, :], (TILE, cols)), value)
            block_ref[slab, fields : fields + TILE, :] = value
    for t in range(layers // 2):
        for f in range(0, planes, TILE):
            total = jnp.zeros((TILE, cols), jnp.float32)
            for i in range(2 * rows):
                moved = pltpu.roll(block_ref[2 * t * rows + i, f : f + TILE, :], (group * i + depth) % cols, 1)
                total = jnp.where((lane >= group * i) & (lane < group * i + group), moved, total)
            edge_ref[t, f : f + TILE, :] = total


def rows_kernel(block_ref, edge_ref, *refs, pair):
    count = 1 if pair else 2
    got_refs = refs[:count]
    strips_ref, next_ref, prev_ref = refs[count:]
    slabs, planes, cols = block_ref.shape
    layers = strips_ref.shape[0]
    rows = slabs // layers
    depth = POWERS
    half = rows // 2
    turn = half * 2 * depth
    _, lane = positions((TILE, cols))
    low_part = lax.rem(lane, 2 * depth) < depth
    first = lane < cols // 2
    early = lax.rem(lane, cols // 2) < turn
    gy = jnp.broadcast_to(lax.axis_index("gy"), (TILE, cols))
    for f in range(0, planes, TILE):
        here = slice(f, f + TILE)
        strips = []
        for t in range(layers // 2):
            own = edge_ref[t, here, :]
            if pair:
                got = got_refs[0][t, here, :]
                before, after = jnp.where(gy == 1, got, 0.0), jnp.where(gy == 0, got, 0.0)
            else:
                before, after = got_refs[0][t, here, :], got_refs[1][t, here, :]
            low, high = jnp.where(low_part, before, own), jnp.where(low_part, own, after)
            strips.append(jnp.where(first, low, pltpu.roll(high, cols // 2, 1)))
            strips.append(jnp.where(first, pltpu.roll(low, cols // 2, 1), high))
        for l in range(layers):
            strips_ref[l, here, :] = strips[l]
        for t in range(layers // 2):
            one, two = strips[2 * t], strips[2 * t + 1]
            next_ref[layers * half + t, here, :] = jnp.where(early, pltpu.roll(two, cols - turn, 1), one)
            prev_ref[layers * half + t, here, :] = jnp.where(early, one, pltpu.roll(two, turn, 1))

    @pl.loop(0, layers)
    def _(l):
        for i in range(half):
            for f in range(0, planes, TILE):
                here = slice(f, f + TILE)
                next_ref[l * half + i, here, :] = block_ref[l * rows + half + i, here, :]
                prev_ref[l * half + i, here, :] = block_ref[l * rows + i, here, :]


def layers_kernel(strips_ref, after_ref, before_ref, wide_ref, up_ref, down_ref):
    layers, planes, cols = strips_ref.shape
    half = (after_ref.shape[0] - layers // 2) // layers
    turn = half * 2 * POWERS
    _, lane = positions((TILE, cols))
    head, tail = lane < turn, lane >= cols - turn
    count = len(CORNERS)
    for f in range(0, planes, TILE):
        here = slice(f, f + TILE)
        for l in range(layers):
            t = layers * half + l // 2
            own, prev, following = strips_ref[l, here, :], after_ref[t, here, :], before_ref[t, here, :]
            odd = l % 2
            shifts = (
                (turn, 0 if odd else cols - turn, 2 * turn if odd else cols - turn),
                (cols - turn, 2 * turn if odd else turn, 0 if odd else turn),
            )
            for side in range(2):
                moved = [
                    pltpu.roll(x, s, 1) if s else x for x, s in zip((own, prev, following), shifts[side])
                ]
                value = jnp.where(head, moved[1], jnp.where(tail, moved[2], moved[0]))
                wide_ref[side, l, here, :] = value
                up_ref[2 * count + side * layers + l, here, :] = value
                down_ref[2 * count + side * layers + l, here, :] = value
        for i, (dz, dx) in enumerate(CORNERS):
            for ref, l in ((up_ref, layers - dz), (down_ref, dz - 1)):
                ref[i, here, :] = after_ref[l * half + half - dx, here, :]
                ref[count + i, here, :] = before_ref[l * half + dx - 1, here, :]


def powers_kernel(
    block_ref, after_ref, before_ref, wide_ref, below_ref, above_ref, corner_below_ref, corner_above_ref, shift_ref,
    basis_ref, gram_ref, start_ref, power_ref, coef_ref, strip_ref, strip_coef_ref, border_ref, *, fields, rows,
):
    slabs, planes, cols = block_ref.shape
    layers = slabs // rows
    depth = POWERS
    half = rows // 2
    group = 2 * depth
    order = depth * fields
    high = layers + 2 * depth
    count = len(CORNERS)
    tiles = range(0, fields, TILE)
    _, lane = positions((TILE, cols))

    def copy_slab(e, row, ref, slab):
        for f in range(0, planes, TILE):
            start_ref[e, row, f : f + TILE, :] = ref[slab, f : f + TILE, :]

    @pl.loop(0, rows)
    def _(r):
        for l in range(layers):
            copy_slab(depth + l, depth + r, block_ref, l * rows + r)
            copy_slab(l, depth + r, below_ref, l * rows + r)
            copy_slab(depth + layers + l, depth + r, above_ref, l * rows + r)

    @pl.loop(0, half)
    def _(i):
        for l in range(layers):
            copy_slab(depth + l, i, after_ref, l * half + i)
            copy_slab(depth + l, depth + rows + i, before_ref, l * half + i)

    for i, (dz, dx) in enumerate(CORNERS):
        for ref, e in ((corner_below_ref, depth - dz), (corner_above_ref, depth + layers - 1 + dz)):
            copy_slab(e, depth - dx, ref, i)
            copy_slab(e, depth + rows - 1 + dx, ref, count + i)

    def wide(side, e):
        if e < depth:
            return corner_below_ref.at[2 * count + side * layers + e]
        if e < depth + layers:
            return wide_ref.at[side, e - depth]
        return corner_above_ref.at[2 * count + side * layers + e - depth - layers]

    def masks(e):
        shift = shift_ref[e]
        return shift == 0, shift > 0

    def from_above(seen, mask):
        left, centre, right = seen
        return jnp.where(mask[0], centre, jnp.where(mask[1], right, left))

    def from_below(seen, mask):
        left, centre, right = seen
        return jnp.where(mask[0], centre, jnp.where(mask[1], left, right))

    def around(tile):
        return pltpu.roll(tile, 1, 1), tile, pltpu.roll(tile, cols - 1, 1)

    def spread(tile, c):
        return jnp.broadcast_to(tile[c : c + 1, :], (TILE, cols))

    def put_factors(put, tile, row_above, seen, seen_below, mask):
        down, right, upper, ground = (spread(tile, c) for c in range(COEFS))
        up = spread(row_above, 0)
        left = spread(seen[0], 1)
        lower = from_below([spread(x, 2) for x in seen_below], mask)
        diagonal = ground + down + up + right + left + upper + lower
        for i, value in enumerate((down, up, right, left, upper, lower, diagonal)):
            put(i, value * basis_scale)

    def step(factors, theta, seen, up, down, above, below):
        value = (factors[6] - theta) * seen[1]
        value = value - (factors[0] * down + factors[1] * up)
        value = value - (factors[2] * seen[2] + factors[3] * seen[0])
        return value - (factors[4] * above + factors[5] * below)

    thetas = [shift * basis_scale for shift in newton_shifts]

    for side in range(2):
        for e in range(high):
            for f in tiles:
                strip_ref[side, 0, e, f : f + TILE, :] = wide(side, e)[f : f + TILE, :]
        raw = [wide(side, e)[fields : fields + TILE, :] for e in range(high)]
        seen = [around(tile) for tile in raw]
        for e in range(1, high - 1):

            def put(i, value, side=side, e=e):
                strip_coef_ref[side, i, e] = value

            put_factors(put, raw[e], pltpu.roll(raw[e], group, 1), seen[e], seen[e - 1], masks(e - 1))

    @pl.loop(0, 2)
    def _(side):
        for k in range(1, depth):
            reach = depth - k
            looks = {}

            def look(e, f, k=k, looks=looks):
                if (e, f) not in looks:
                    looks[e, f] = around(strip_ref[side, k - 1, e, f : f + TILE, :])
                return looks[e, f]

            for e in range(depth - reach, depth + layers + reach):
                factors = [strip_coef_ref[side, i, e] for i in range(7)]
                over, under = masks(e), masks(e - 1)
                for f in tiles:
                    here = look(e, f)
                    strip_ref[side, k, e, f : f + TILE, :] = step(
                        factors,
                        thetas[k - 1],
                        here,
                        pltpu.roll(here[1], group, 1),
                        pltpu.roll(here[1], cols - group, 1),
                        from_above(look(e + 1, f), over),
                        from_below(look(e - 1, f), under),
                    )

    own = lax.rem(lane, group) == depth - 1

    @pl.loop(0, high)
    def _(e):
        for k in range(depth):
            for f in tiles:
                here = slice(f, f + TILE)
                border_ref[k, e, here, :] = jnp.where(
                    own, strip_ref[0, k, e, here, :], pltpu.roll(strip_ref[1, k, e, here, :], cols - 2, 1)
                )

    for e in range(high):
        sides = [wide(side, e)[fields : fields + TILE, :] for side in range(2)]
        border_ref[0, e, fields : fields + TILE, :] = jnp.where(own, sides[0], pltpu.roll(sides[1], cols - 2, 1))

    leftmost, rightmost = lane == 0, lane == cols - 1

    def looked(k, e, row, f):
        here = slice(f, f + TILE)
        tile = start_ref[e, row, here, :] if k == 0 else power_ref[k - 1, e, row, here, :]
        turn = lax.rem(2 * cols - group * row - depth + 1, cols)
        outer = pltpu.roll(border_ref[k, e, here, :], turn, 1)
        left, _, right = around(tile)
        return jnp.where(leftmost, outer, left), tile, jnp.where(rightmost, outer, right)

    def by_rows(reach, body):
        @pl.loop(0, rows)
        def _(r):
            body(depth + r, depth - reach, depth + layers + reach)

        for dx in range(1, reach + 1):

            @pl.loop(0, 2)
            def _(side, dx=dx):
                row = jnp.where(side == 0, depth - dx, depth + rows - 1 + dx)
                body(row, depth - reach + dx, depth + layers + reach - dx)

    def factors_of_row(row, first, last):
        seen = {e: looked(0, e, row, fields) for e in range(first - 1, last)}
        for e in range(first, last):

            def put(i, value, e=e):
                coef_ref[i, e, row] = value

            above_row = start_ref[e, row - 1, fields : fields + TILE, :]
            put_factors(put, seen[e][1], above_row, seen[e], seen[e - 1], masks(e - 1))

    by_rows(depth - 1, factors_of_row)

    for k in range(1, depth + 1):

        def advance(row, first, last, k=k):
            source = start_ref if k == 1 else power_ref.at[k - 2]
            below = {f: from_below(looked(k - 1, first - 1, row, f), masks(first - 1)) for f in tiles}
            centre = {f: looked(k - 1, first, row, f) for f in tiles}
            for e in range(first, last):
                factors = [coef_ref[i, e, row] for i in range(7)]
                mask = masks(e)
                for f in tiles:
                    here = slice(f, f + TILE)
                    upper = looked(k - 1, e + 1, row, f)
                    value = step(
                        factors,
                        thetas[k - 1],
                        centre[f],
                        source[e, row - 1, here, :],
                        source[e, row + 1, here, :],
                        from_above(upper, mask),
                        below[f],
                    )
                    below[f], centre[f] = from_below(centre[f], mask), upper
                    if k < depth:
                        power_ref[k - 1, e, row, here, :] = value
                    if first == depth - (depth - k) and depth <= e < depth + layers:
                        slab = (e - depth) * rows + row - depth
                        place = pl.multiple_of(slab * order + (k - 1) * fields + f, TILE)
                        basis_ref[pl.ds(place, TILE), :] = value

        by_rows(depth - k, advance)

    total = jnp.zeros((order, order), jnp.float32)
    for i in range(slabs // 2):
        begin = 2 * i * order
        pair = jnp.concatenate(
            [basis_ref[begin : begin + order, :], basis_ref[begin + order : begin + 2 * order, :]], axis=1
        )
        total = total + lax.dot_general(
            pair, pair, (((1,), (1,)), ((), ())),
            precision=lax.Precision.HIGHEST, preferred_element_type=jnp.float32,
        )
    gram_ref[...] = total


def eliminate(tiles, order, step):
    width = tiles[0].shape[1]
    lane = lax.broadcasted_iota(jnp.int32, (8, width), 1)
    sub = lax.broadcasted_iota(jnp.int32, (8, width), 0)
    spread = lambda value: jnp.broadcast_to(value, (8, width))
    for first in range(0, order, step):
        home, base = first // 8, first % 8
        panel = tiles[home]
        entry = {}
        for i in range(step):
            for j in range(i, step):
                entry[i, j] = spread(panel[base + i : base + i + 1, first + j : first + j + 1])
        rows = [spread(panel[base + i : base + i + 1, :]) for i in range(step)]
        inverse = []
        done = []
        for i in range(step):
            row = rows[i]
            if i:
                row = jnp.where((lane >= first) & (lane < first + i), 0.0, row)
            factors = []
            for j in range(i):
                factor = entry[j, i] * inverse[j]
                factors.append(factor)
            for j in range(i):
                source = jnp.where(lane == first + j, 1.0, done[j])
                if i - j > 1:
                    source = jnp.where((lane > first + j) & (lane < first + i), 0.0, source)
                row = row - factors[j] * source
                for m in range(i, step):
                    entry[i, m] = entry[i, m] - factors[j] * entry[j, m]
            inverse.append(1.0 / entry[i, i])
            done.append(row)
        sources = []
        for j in range(step):
            source = jnp.where(lane == first + j, 1.0, done[j])
            if j < step - 1:
                source = jnp.where((lane > first + j) & (lane < first + step), 0.0, source)
            sources.append(source)
        inside = (lane >= first) & (lane < first + step)
        for t in range(home, order // 8):
            if t == home and base + step == 8:
                fresh = tiles[t]
            else:
                columns = [spread(tiles[t][:, first + j : first + j + 1]) for j in range(step)]
                fresh = jnp.where(inside, 0.0, tiles[t])
                for j in range(step):
                    factor = columns[j] * inverse[j]
                    fresh = fresh - factor * sources[j]
                    for m in range(j + 1, step):
                        columns[m] = columns[m] - factor * entry[j, m]
            if t == home:
                fresh = jnp.where(sub < base + step, tiles[t], fresh)
                for j in range(step):
                    fresh = jnp.where(sub == base + j, done[j], fresh)
            tiles[t] = fresh
    return tiles


def finish_kernel(*refs, parts, count, step):
    part_refs, basis_ref, upper_ref, out_ref = refs[:parts], refs[parts], refs[parts + 1], refs[parts + 2]
    order = upper_ref.shape[0]
    points = basis_ref.shape[0] // order
    tiles = []
    for t in range(order // 8):
        pieces = [ref[8 * t : 8 * t + 8, :] for ref in part_refs]
        tiles.append(folded(pieces) / count)
    tiles = eliminate(tiles, order, step)
    lane = lax.broadcasted_iota(jnp.int32, (8, order), 1)
    sub = lax.broadcasted_iota(jnp.int32, (8, order), 0)
    inverse = []
    for t in range(order // 8):
        row = sub + 8 * t
        pivot = jnp.sum(jnp.where(lane == row, tiles[t], 0.0), axis=1, keepdims=True)
        scale = 1.0 / jnp.sqrt(pivot)
        upper_ref[8 * t : 8 * t + 8, :] = jnp.where(lane >= row, tiles[t] * scale, 0.0)
        inverse.append(jnp.where(lane < row, tiles[t], jnp.where(lane == row, 1.0, 0.0)) * scale)
    inverse = jnp.concatenate(inverse, axis=0)
    for i in range(points // 2):
        start = 2 * i * order
        wide = jnp.concatenate(
            [basis_ref[start : start + order, :], basis_ref[start + order : start + 2 * order, :]], axis=1
        )
        out = jnp.dot(inverse, wide, precision=lax.Precision.HIGHEST, preferred_element_type=jnp.float32)
        cols = basis_ref.shape[1]
        out_ref[pl.ds(2 * i, order, stride=points), :] = out[:, :cols]
        out_ref[pl.ds(2 * i + 1, order, stride=points), :] = out[:, cols:]


def folded(pieces):
    while len(pieces) > 1:
        half = len(pieces) // 2
        pieces = [pieces[i] + pieces[i + half] for i in range(half)]
    return pieces[0]


def gathered(value, axis):
    size = lax.axis_size(axis)
    return [value] + [
        lax.ppermute(value, axis, [((i + step) % size, i) for i in range(size)]) for step in range(1, size)
    ]


def summed(value, axis):
    size = lax.axis_size(axis)
    if size <= 4:
        return folded(gathered(value, axis))
    step = 1
    while step < size:
        value = value + lax.ppermute(value, axis, [(i, i ^ step) for i in range(size)])
        step *= 2
    return value


def sent(value, steps):
    axes = tuple(steps)
    sizes = [lax.axis_size(name) for name in axes]
    pairs = []
    if len(axes) == 1:
        pairs = [(i, i + steps[axes[0]]) for i in range(sizes[0]) if 0 <= i + steps[axes[0]] < sizes[0]]
        return lax.ppermute(value, axes[0], pairs)
    for i in range(sizes[0]):
        for j in range(sizes[1]):
            m, n = i + steps[axes[0]], j + steps[axes[1]]
            if 0 <= m < sizes[0] and 0 <= n < sizes[1]:
                pairs.append((i * sizes[1] + j, m * sizes[1] + n))
    return lax.ppermute(value, axes, pairs)


def local(load_currents, cond_rows, cond_cols, cond_vias, ground, via_offset):
    fields, layers, rows, cols = load_currents.shape
    depth = POWERS
    assert layers == depth and rows == 2 * depth and cols == 4 * depth * rows and fields % TILE == 0
    float_of = lambda *shape: jax.ShapeDtypeStruct(shape, jnp.float32)
    pair = lax.axis_size("gy") == 2
    planes = fields + TILE
    slabs = layers * rows
    high = layers + 2 * depth
    tall = rows + 2 * depth
    count = len(CORNERS)
    block, shifts, edge = pl.pallas_call(
        edges_kernel,
        out_shape=(
            float_of(slabs, planes, cols),
            jax.ShapeDtypeStruct((high, TILE, cols), jnp.int32),
            float_of(layers // 2, planes, cols),
        ),
        in_specs=[HBM] * 5 + [SMEM],
        out_specs=(VMEM,) * 3,
        scratch_shapes=[
            pltpu.VMEM((fields * slabs, cols), jnp.float32),
            pltpu.VMEM((COEFS, layers, rows, cols), jnp.float32),
            pltpu.SemaphoreType.DMA((COEFS + 1,)),
        ],
        compiler_params=PARAMS,
        name="edges",
    )(load_currents.reshape(fields * slabs, cols), cond_rows, cond_cols, cond_vias, ground, via_offset)
    below = sent(block, {"gz": 1})
    above = sent(block, {"gz": -1})
    if pair:
        got = [lax.ppermute(edge, "gy", [(0, 1), (1, 0)])]
    else:
        got = [sent(edge, {"gy": 1}), sent(edge, {"gy": -1})]
    strips, to_next, to_prev = pl.pallas_call(
        functools.partial(rows_kernel, pair=pair),
        out_shape=(float_of(layers, planes, cols),) + (float_of(slabs // 2 + layers // 2, planes, cols),) * 2,
        in_specs=[VMEM] * (2 + len(got)),
        out_specs=(VMEM,) * 3,
        compiler_params=PARAMS,
        name="rows",
    )(block, edge, *got)
    after = sent(to_next, {"gx": 1})
    before = sent(to_prev, {"gx": -1})
    wide, to_above, to_below = pl.pallas_call(
        layers_kernel,
        out_shape=(float_of(2, layers, planes, cols),) + (float_of(2 * count + 2 * layers, planes, cols),) * 2,
        in_specs=[VMEM] * 3,
        out_specs=(VMEM,) * 3,
        compiler_params=PARAMS,
        name="layers",
    )(strips, after, before)
    corner_below = sent(to_above, {"gz": 1})
    corner_above = sent(to_below, {"gz": -1})
    order = depth * fields
    points = slabs
    basis, gram = pl.pallas_call(
        functools.partial(powers_kernel, fields=fields, rows=rows),
        out_shape=(float_of(points * order, cols), float_of(order, order)),
        in_specs=[VMEM] * 9,
        out_specs=(VMEM, VMEM),
        scratch_shapes=[
            pltpu.VMEM((high, tall, planes, cols), jnp.float32),
            pltpu.VMEM((depth - 1, high, tall, fields, cols), jnp.float32),
            pltpu.VMEM((7, high, tall, TILE, cols), jnp.float32),
            pltpu.VMEM((2, depth, high, fields, cols), jnp.float32),
            pltpu.VMEM((2, 7, high, TILE, cols), jnp.float32),
            pltpu.VMEM((depth, high, planes, cols), jnp.float32),
        ],
        compiler_params=PARAMS,
        name="powers",
    )(block, after, before, wide, below, above, corner_below, corner_above, shifts)
    count = points * cols * lax.axis_size("gx") * lax.axis_size("gy") * lax.axis_size("gz")
    gram = summed(gram, "gy")
    gram = summed(gram, "gx")
    parts = gathered(gram, "gz") if lax.axis_size("gz") in (2, 4) else [summed(gram, "gz")]
    upper, basis_q = pl.pallas_call(
        functools.partial(finish_kernel, parts=len(parts), count=float(count), step=4),
        out_shape=(float_of(order, order), float_of(order * points, cols)),
        in_specs=[VMEM] * (len(parts) + 1),
        out_specs=(VMEM, VMEM),
        compiler_params=PARAMS,
        name="finish",
    )(*parts, basis)
    return basis_q.reshape(order, layers, rows, cols), upper


def solution(mesh):
    in_specs = (
        P(None, "gz", "gx", "gy"),
        P("gz", "gx", "gy"),
        P("gz", "gx", "gy"),
        P("gz", "gx", "gy"),
        P("gz", "gx", "gy"),
        P(),
    )
    out_specs = (P(None, "gz", "gx", "gy"), P())
    return jax.shard_map(local, mesh=mesh, in_specs=in_specs, out_specs=out_specs, check_vma=False)
```

```python
import functools

import jax
import jax.numpy as jnp
from jax import lax
from jax.experimental import pallas as pl
from jax.experimental.pallas import tpu as pltpu
from jax.sharding import PartitionSpec as P

POWERS = 4


newton_shifts = (15.4, 0.6, 11.7, 4.3)
basis_scale = 0.125

VMEM = pl.BlockSpec(memory_space=pltpu.VMEM)
SMEM = pl.BlockSpec(memory_space=pltpu.SMEM)
HBM = pl.BlockSpec(memory_space=pltpu.HBM)
PARAMS = pltpu.CompilerParams(vmem_limit_bytes=48 * 1024 * 1024)

COEFS = 4
TILE = 8
CORNERS = ((1, 3), (1, 2), (1, 1), (2, 2), (2, 1), (3, 1))


def positions(shape):
    sub = lax.broadcasted_iota(jnp.int32, shape, 0)
    lane = lax.broadcasted_iota(jnp.int32, shape, 1)
    return sub, lane


def edges_kernel(
    load_ref, rows_ref, cols_ref, vias_ref, ground_ref, offset_ref, block_ref, shift_ref, edge_ref, fields_in, coefs_in, sems
):
    slabs, planes, cols = block_ref.shape
    fields = load_ref.shape[0] // slabs
    layers, rows, _ = rows_ref.shape
    depth = POWERS
    group = 2 * depth
    total_layers = offset_ref.shape[0]
    copies = [
        pltpu.make_async_copy(ref, coefs_in.at[i], sems.at[i])
        for i, ref in enumerate((rows_ref, cols_ref, vias_ref, ground_ref))
    ]
    copies.append(pltpu.make_async_copy(load_ref, fields_in, sems.at[COEFS]))
    for copy in copies:
        copy.start()
    gx, gy, gz = (lax.axis_index(name) for name in ("gx", "gy", "gz"))
    last_row = jnp.where(gx == lax.axis_size("gx") - 1, rows - 1, rows)
    last_col = jnp.where(gy == lax.axis_size("gy") - 1, cols - 1, cols)
    sub, lane = positions((TILE, cols))
    for e in range(shift_ref.shape[0]):
        layer = gz * layers + e - depth
        inside = (layer >= 0) & (layer < total_layers)
        value = jnp.where(inside, offset_ref[jnp.clip(layer, 0, total_layers - 1)], 0)
        shift_ref[e] = jnp.broadcast_to(value, (TILE, cols))
    for copy in copies:
        copy.wait()
    for l in range(layers):
        layer = gz * layers + l
        target = gy * cols + lane + shift_ref[depth + l]
        via_ok = (target >= 0) & (target < cols * lax.axis_size("gy"))
        via_ok = via_ok & (jnp.broadcast_to(layer, lane.shape) < total_layers - 1)
        four = (
            jnp.where(sub == last_row, 0.0, coefs_in[0, l]),
            jnp.where(lane == last_col, 0.0, coefs_in[1, l]),
            jnp.where(via_ok, coefs_in[2, l], 0.0),
            coefs_in[3, l],
        )
        for r in range(rows):
            slab = l * rows + r
            for f in range(0, fields, TILE):
                block_ref[slab, f : f + TILE, :] = fields_in[pl.ds(f * slabs + slab, TILE, stride=slabs), :]
            value = jnp.zeros((TILE, cols), jnp.float32)
            for c in range(COEFS):
                value = jnp.where(sub == c, jnp.broadcast_to(four[c][r : r + 1, :], (TILE, cols)), value)
            block_ref[slab, fields : fields + TILE, :] = value
    for t in range(layers // 2):
        for f in range(0, planes, TILE):
            total = jnp.zeros((TILE, cols), jnp.float32)
            for i in range(2 * rows):
                moved = pltpu.roll(block_ref[2 * t * rows + i, f : f + TILE, :], (group * i + depth) % cols, 1)
                total = jnp.where((lane >= group * i) & (lane < group * i + group), moved, total)
            edge_ref[t, f : f + TILE, :] = total


def rows_kernel(block_ref, edge_ref, *refs, pair):
    count = 1 if pair else 2
    got_refs = refs[:count]
    strips_ref, next_ref, prev_ref = refs[count:]
    slabs, planes, cols = block_ref.shape
    layers = strips_ref.shape[0]
    rows = slabs // layers
    depth = POWERS
    half = rows // 2
    turn = half * 2 * depth
    _, lane = positions((TILE, cols))
    low_part = lax.rem(lane, 2 * depth) < depth
    first = lane < cols // 2
    early = lax.rem(lane, cols // 2) < turn
    gy = jnp.broadcast_to(lax.axis_index("gy"), (TILE, cols))
    for f in range(0, planes, TILE):
        here = slice(f, f + TILE)
        strips = []
        for t in range(layers // 2):
            own = edge_ref[t, here, :]
            if pair:
                got = got_refs[0][t, here, :]
                before, after = jnp.where(gy == 1, got, 0.0), jnp.where(gy == 0, got, 0.0)
            else:
                before, after = got_refs[0][t, here, :], got_refs[1][t, here, :]
            low, high = jnp.where(low_part, before, own), jnp.where(low_part, own, after)
            strips.append(jnp.where(first, low, pltpu.roll(high, cols // 2, 1)))
            strips.append(jnp.where(first, pltpu.roll(low, cols // 2, 1), high))
        for l in range(layers):
            strips_ref[l, here, :] = strips[l]
        for t in range(layers // 2):
            one, two = strips[2 * t], strips[2 * t + 1]
            next_ref[layers * half + t, here, :] = jnp.where(early, pltpu.roll(two, cols - turn, 1), one)
            prev_ref[layers * half + t, here, :] = jnp.where(early, one, pltpu.roll(two, turn, 1))

    @pl.loop(0, layers)
    def _(l):
        for i in range(half):
            for f in range(0, planes, TILE):
                here = slice(f, f + TILE)
                next_ref[l * half + i, here, :] = block_ref[l * rows + half + i, here, :]
                prev_ref[l * half + i, here, :] = block_ref[l * rows + i, here, :]


def layers_kernel(strips_ref, after_ref, before_ref, wide_ref, up_ref, down_ref):
    layers, planes, cols = strips_ref.shape
    half = (after_ref.shape[0] - layers // 2) // layers
    turn = half * 2 * POWERS
    _, lane = positions((TILE, cols))
    head, tail = lane < turn, lane >= cols - turn
    count = len(CORNERS)
    for f in range(0, planes, TILE):
        here = slice(f, f + TILE)
        for l in range(layers):
            t = layers * half + l // 2
            own, prev, following = strips_ref[l, here, :], after_ref[t, here, :], before_ref[t, here, :]
            odd = l % 2
            shifts = (
                (turn, 0 if odd else cols - turn, 2 * turn if odd else cols - turn),
                (cols - turn, 2 * turn if odd else turn, 0 if odd else turn),
            )
            for side in range(2):
                moved = [
                    pltpu.roll(x, s, 1) if s else x for x, s in zip((own, prev, following), shifts[side])
                ]
                value = jnp.where(head, moved[1], jnp.where(tail, moved[2], moved[0]))
                wide_ref[side, l, here, :] = value
                up_ref[2 * count + side * layers + l, here, :] = value
                down_ref[2 * count + side * layers + l, here, :] = value
        for i, (dz, dx) in enumerate(CORNERS):
            for ref, l in ((up_ref, layers - dz), (down_ref, dz - 1)):
                ref[i, here, :] = after_ref[l * half + half - dx, here, :]
                ref[count + i, here, :] = before_ref[l * half + dx - 1, here, :]


def powers_kernel(
    block_ref, after_ref, before_ref, wide_ref, below_ref, above_ref, corner_below_ref, corner_above_ref, shift_ref,
    basis_ref, gram_ref, start_ref, power_ref, coef_ref, strip_ref, strip_coef_ref, border_ref, *, fields, rows,
):
    slabs, planes, cols = block_ref.shape
    layers = slabs // rows
    depth = POWERS
    half = rows // 2
    group = 2 * depth
    order = depth * fields
    high = layers + 2 * depth
    count = len(CORNERS)
    tiles = range(0, fields, TILE)
    _, lane = positions((TILE, cols))

    def copy_slab(e, row, ref, slab):
        for f in range(0, planes, TILE):
            start_ref[e, row, f : f + TILE, :] = ref[slab, f : f + TILE, :]

    @pl.loop(0, rows)
    def _(r):
        for l in range(layers):
            copy_slab(depth + l, depth + r, block_ref, l * rows + r)
            copy_slab(l, depth + r, below_ref, l * rows + r)
            copy_slab(depth + layers + l, depth + r, above_ref, l * rows + r)

    @pl.loop(0, half)
    def _(i):
        for l in range(layers):
            copy_slab(depth + l, i, after_ref, l * half + i)
            copy_slab(depth + l, depth + rows + i, before_ref, l * half + i)

    for i, (dz, dx) in enumerate(CORNERS):
        for ref, e in ((corner_below_ref, depth - dz), (corner_above_ref, depth + layers - 1 + dz)):
            copy_slab(e, depth - dx, ref, i)
            copy_slab(e, depth + rows - 1 + dx, ref, count + i)

    def wide(side, e):
        if e < depth:
            return corner_below_ref.at[2 * count + side * layers + e]
        if e < depth + layers:
            return wide_ref.at[side, e - depth]
        return corner_above_ref.at[2 * count + side * layers + e - depth - layers]

    def masks(e):
        shift = shift_ref[e]
        return shift == 0, shift > 0

    def from_above(seen, mask):
        left, centre, right = seen
        return jnp.where(mask[0], centre, jnp.where(mask[1], right, left))

    def from_below(seen, mask):
        left, centre, right = seen
        return jnp.where(mask[0], centre, jnp.where(mask[1], left, right))

    def around(tile):
        return pltpu.roll(tile, 1, 1), tile, pltpu.roll(tile, cols - 1, 1)

    def spread(tile, c):
        return jnp.broadcast_to(tile[c : c + 1, :], (TILE, cols))

    def put_factors(put, tile, row_above, seen, seen_below, mask):
        down, right, upper, ground = (spread(tile, c) for c in range(COEFS))
        up = spread(row_above, 0)
        left = spread(seen[0], 1)
        lower = from_below([spread(x, 2) for x in seen_below], mask)
        diagonal = ground + down + up + right + left + upper + lower
        for i, value in enumerate((down, up, right, left, upper, lower, diagonal)):
            put(i, value * basis_scale)

    def step(factors, theta, seen, up, down, above, below):
        value = (factors[6] - theta) * seen[1]
        value = value - (factors[0] * down + factors[1] * up)
        value = value - (factors[2] * seen[2] + factors[3] * seen[0])
        return value - (factors[4] * above + factors[5] * below)

    thetas = [shift * basis_scale for shift in newton_shifts]

    for side in range(2):
        for e in range(high):
            for f in tiles:
                strip_ref[side, 0, e, f : f + TILE, :] = wide(side, e)[f : f + TILE, :]
        raw = [wide(side, e)[fields : fields + TILE, :] for e in range(high)]
        seen = [around(tile) for tile in raw]
        for e in range(1, high - 1):

            def put(i, value, side=side, e=e):
                strip_coef_ref[side, i, e] = value

            put_factors(put, raw[e], pltpu.roll(raw[e], group, 1), seen[e], seen[e - 1], masks(e - 1))

    @pl.loop(0, 2)
    def _(side):
        for k in range(1, depth):
            reach = depth - k
            looks = {}

            def look(e, f, k=k, looks=looks):
                if (e, f) not in looks:
                    looks[e, f] = around(strip_ref[side, k - 1, e, f : f + TILE, :])
                return looks[e, f]

            for e in range(depth - reach, depth + layers + reach):
                factors = [strip_coef_ref[side, i, e] for i in range(7)]
                over, under = masks(e), masks(e - 1)
                for f in tiles:
                    here = look(e, f)
                    strip_ref[side, k, e, f : f + TILE, :] = step(
                        factors,
                        thetas[k - 1],
                        here,
                        pltpu.roll(here[1], group, 1),
                        pltpu.roll(here[1], cols - group, 1),
                        from_above(look(e + 1, f), over),
                        from_below(look(e - 1, f), under),
                    )

    own = lax.rem(lane, group) == depth - 1

    @pl.loop(0, high)
    def _(e):
        for k in range(depth):
            for f in tiles:
                here = slice(f, f + TILE)
                border_ref[k, e, here, :] = jnp.where(
                    own, strip_ref[0, k, e, here, :], pltpu.roll(strip_ref[1, k, e, here, :], cols - 2, 1)
                )

    for e in range(high):
        sides = [wide(side, e)[fields : fields + TILE, :] for side in range(2)]
        border_ref[0, e, fields : fields + TILE, :] = jnp.where(own, sides[0], pltpu.roll(sides[1], cols - 2, 1))

    leftmost, rightmost = lane == 0, lane == cols - 1

    def looked(k, e, row, f):
        here = slice(f, f + TILE)
        tile = start_ref[e, row, here, :] if k == 0 else power_ref[k - 1, e, row, here, :]
        turn = lax.rem(2 * cols - group * row - depth + 1, cols)
        outer = pltpu.roll(border_ref[k, e, here, :], turn, 1)
        left, _, right = around(tile)
        return jnp.where(leftmost, outer, left), tile, jnp.where(rightmost, outer, right)

    def by_rows(reach, body):
        @pl.loop(0, rows)
        def _(r):
            body(depth + r, depth - reach, depth + layers + reach)

        for dx in range(1, reach + 1):

            @pl.loop(0, 2)
            def _(side, dx=dx):
                row = jnp.where(side == 0, depth - dx, depth + rows - 1 + dx)
                body(row, depth - reach + dx, depth + layers + reach - dx)

    def factors_of_row(row, first, last):
        seen = {e: looked(0, e, row, fields) for e in range(first - 1, last)}
        for e in range(first, last):

            def put(i, value, e=e):
                coef_ref[i, e, row] = value

            above_row = start_ref[e, row - 1, fields : fields + TILE, :]
            put_factors(put, seen[e][1], above_row, seen[e], seen[e - 1], masks(e - 1))

    by_rows(depth - 1, factors_of_row)

    for k in range(1, depth + 1):

        def advance(row, first, last, k=k):
            source = start_ref if k == 1 else power_ref.at[k - 2]
            below = {f: from_below(looked(k - 1, first - 1, row, f), masks(first - 1)) for f in tiles}
            centre = {f: looked(k - 1, first, row, f) for f in tiles}
            for e in range(first, last):
                factors = [coef_ref[i, e, row] for i in range(7)]
                mask = masks(e)
                for f in tiles:
                    here = slice(f, f + TILE)
                    upper = looked(k - 1, e + 1, row, f)
                    value = step(
                        factors,
                        thetas[k - 1],
                        centre[f],
                        source[e, row - 1, here, :],
                        source[e, row + 1, here, :],
                        from_above(upper, mask),
                        below[f],
                    )
                    below[f], centre[f] = from_below(centre[f], mask), upper
                    if k < depth:
                        power_ref[k - 1, e, row, here, :] = value
                    if first == depth - (depth - k) and depth <= e < depth + layers:
                        slab = (e - depth) * rows + row - depth
                        place = pl.multiple_of(slab * order + (k - 1) * fields + f, TILE)
                        basis_ref[pl.ds(place, TILE), :] = value

        by_rows(depth - k, advance)

    total = jnp.zeros((order, order), jnp.float32)
    for i in range(slabs // 2):
        begin = 2 * i * order
        pair = jnp.concatenate(
            [basis_ref[begin : begin + order, :], basis_ref[begin + order : begin + 2 * order, :]], axis=1
        )
        total = total + lax.dot_general(
            pair, pair, (((1,), (1,)), ((), ())),
            precision=lax.Precision.HIGHEST, preferred_element_type=jnp.float32,
        )
    gram_ref[...] = jnp.concatenate([total, jnp.zeros((order, cols - order), jnp.float32)], axis=1)


def eliminate(tiles, order, step):
    width = tiles[0].shape[1]
    lane = lax.broadcasted_iota(jnp.int32, (8, width), 1)
    sub = lax.broadcasted_iota(jnp.int32, (8, width), 0)
    spread = lambda value: jnp.broadcast_to(value, (8, width))
    for first in range(0, order, step):
        home, base = first // 8, first % 8
        panel = tiles[home]
        entry = {}
        for i in range(step):
            for j in range(i, step):
                entry[i, j] = spread(panel[base + i : base + i + 1, first + j : first + j + 1])
        rows = [spread(panel[base + i : base + i + 1, :]) for i in range(step)]
        inverse = []
        done = []
        for i in range(step):
            row = rows[i]
            if i:
                row = jnp.where((lane >= first) & (lane < first + i), 0.0, row)
            factors = []
            for j in range(i):
                factor = entry[j, i] * inverse[j]
                factors.append(factor)
            for j in range(i):
                source = jnp.where(lane == first + j, 1.0, done[j])
                if i - j > 1:
                    source = jnp.where((lane > first + j) & (lane < first + i), 0.0, source)
                row = row - factors[j] * source
                for m in range(i, step):
                    entry[i, m] = entry[i, m] - factors[j] * entry[j, m]
            inverse.append(1.0 / entry[i, i])
            done.append(row)
        sources = []
        for j in range(step):
            source = jnp.where(lane == first + j, 1.0, done[j])
            if j < step - 1:
                source = jnp.where((lane > first + j) & (lane < first + step), 0.0, source)
            sources.append(source)
        inside = (lane >= first) & (lane < first + step)
        for t in range(home, order // 8):
            if t == home and base + step == 8:
                fresh = tiles[t]
            else:
                columns = [spread(tiles[t][:, first + j : first + j + 1]) for j in range(step)]
                fresh = jnp.where(inside, 0.0, tiles[t])
                for j in range(step):
                    factor = columns[j] * inverse[j]
                    fresh = fresh - factor * sources[j]
                    for m in range(j + 1, step):
                        columns[m] = columns[m] - factor * entry[j, m]
            if t == home:
                fresh = jnp.where(sub < base + step, tiles[t], fresh)
                for j in range(step):
                    fresh = jnp.where(sub == base + j, done[j], fresh)
            tiles[t] = fresh
    return tiles


def finish_kernel(*refs, parts, count, step):
    part_refs, basis_ref, upper_ref, out_ref = refs[:parts], refs[parts], refs[parts + 1], refs[parts + 2]
    order = upper_ref.shape[0]
    points = basis_ref.shape[0] // order
    tiles = []
    for t in range(order // 8):
        pieces = [ref[8 * t : 8 * t + 8, :order] for ref in part_refs]
        tiles.append(folded(pieces) / count)
    tiles = eliminate(tiles, order, step)
    lane = lax.broadcasted_iota(jnp.int32, (8, order), 1)
    sub = lax.broadcasted_iota(jnp.int32, (8, order), 0)
    inverse = []
    for t in range(order // 8):
        row = sub + 8 * t
        pivot = jnp.sum(jnp.where(lane == row, tiles[t], 0.0), axis=1, keepdims=True)
        scale = 1.0 / jnp.sqrt(pivot)
        upper_ref[8 * t : 8 * t + 8, :] = jnp.where(lane >= row, tiles[t] * scale, 0.0)
        inverse.append(jnp.where(lane < row, tiles[t], jnp.where(lane == row, 1.0, 0.0)) * scale)
    inverse = jnp.concatenate(inverse, axis=0)
    for i in range(points // 2):
        start = 2 * i * order
        wide = jnp.concatenate(
            [basis_ref[start : start + order, :], basis_ref[start + order : start + 2 * order, :]], axis=1
        )
        out = jnp.dot(inverse, wide, precision=lax.Precision.HIGHEST, preferred_element_type=jnp.float32)
        cols = basis_ref.shape[1]
        out_ref[pl.ds(2 * i, order, stride=points), :] = out[:, :cols]
        out_ref[pl.ds(2 * i + 1, order, stride=points), :] = out[:, cols:]


def folded(pieces):
    while len(pieces) > 1:
        half = len(pieces) // 2
        pieces = [pieces[i] + pieces[i + half] for i in range(half)]
    return pieces[0]


def gathered(value, axis):
    size = lax.axis_size(axis)
    return [value] + [
        lax.ppermute(value, axis, [((i + step) % size, i) for i in range(size)]) for step in range(1, size)
    ]


def summed(value, axis):
    size = lax.axis_size(axis)
    if size <= 4:
        return folded(gathered(value, axis))
    step = 1
    while step < size:
        value = value + lax.ppermute(value, axis, [(i, i ^ step) for i in range(size)])
        step *= 2
    return value


def sent(value, steps):
    axes = tuple(steps)
    sizes = [lax.axis_size(name) for name in axes]
    pairs = []
    if len(axes) == 1:
        pairs = [(i, i + steps[axes[0]]) for i in range(sizes[0]) if 0 <= i + steps[axes[0]] < sizes[0]]
        return lax.ppermute(value, axes[0], pairs)
    for i in range(sizes[0]):
        for j in range(sizes[1]):
            m, n = i + steps[axes[0]], j + steps[axes[1]]
            if 0 <= m < sizes[0] and 0 <= n < sizes[1]:
                pairs.append((i * sizes[1] + j, m * sizes[1] + n))
    return lax.ppermute(value, axes, pairs)


def local(load_currents, cond_rows, cond_cols, cond_vias, ground, via_offset):
    fields, layers, rows, cols = load_currents.shape
    depth = POWERS
    assert layers == depth and rows == 2 * depth and cols == 4 * depth * rows and fields % TILE == 0
    float_of = lambda *shape: jax.ShapeDtypeStruct(shape, jnp.float32)
    pair = lax.axis_size("gy") == 2
    planes = fields + TILE
    slabs = layers * rows
    high = layers + 2 * depth
    tall = rows + 2 * depth
    count = len(CORNERS)
    block, shifts, edge = pl.pallas_call(
        edges_kernel,
        out_shape=(
            float_of(slabs, planes, cols),
            jax.ShapeDtypeStruct((high, TILE, cols), jnp.int32),
            float_of(layers // 2, planes, cols),
        ),
        in_specs=[HBM] * 5 + [SMEM],
        out_specs=(VMEM,) * 3,
        scratch_shapes=[
            pltpu.VMEM((fields * slabs, cols), jnp.float32),
            pltpu.VMEM((COEFS, layers, rows, cols), jnp.float32),
            pltpu.SemaphoreType.DMA((COEFS + 1,)),
        ],
        compiler_params=PARAMS,
        name="edges",
    )(load_currents.reshape(fields * slabs, cols), cond_rows, cond_cols, cond_vias, ground, via_offset)
    below = sent(block, {"gz": 1})
    above = sent(block, {"gz": -1})
    if pair:
        got = [lax.ppermute(edge, "gy", [(0, 1), (1, 0)])]
    else:
        got = [sent(edge, {"gy": 1}), sent(edge, {"gy": -1})]
    strips, to_next, to_prev = pl.pallas_call(
        functools.partial(rows_kernel, pair=pair),
        out_shape=(float_of(layers, planes, cols),) + (float_of(slabs // 2 + layers // 2, planes, cols),) * 2,
        in_specs=[VMEM] * (2 + len(got)),
        out_specs=(VMEM,) * 3,
        compiler_params=PARAMS,
        name="rows",
    )(block, edge, *got)
    after = sent(to_next, {"gx": 1})
    before = sent(to_prev, {"gx": -1})
    wide, to_above, to_below = pl.pallas_call(
        layers_kernel,
        out_shape=(float_of(2, layers, planes, cols),) + (float_of(2 * count + 2 * layers, planes, cols),) * 2,
        in_specs=[VMEM] * 3,
        out_specs=(VMEM,) * 3,
        compiler_params=PARAMS,
        name="layers",
    )(strips, after, before)
    corner_below = sent(to_above, {"gz": 1})
    corner_above = sent(to_below, {"gz": -1})
    order = depth * fields
    points = slabs
    basis, gram = pl.pallas_call(
        functools.partial(powers_kernel, fields=fields, rows=rows),
        out_shape=(float_of(points * order, cols), float_of(order, cols)),
        in_specs=[VMEM] * 9,
        out_specs=(VMEM, VMEM),
        scratch_shapes=[
            pltpu.VMEM((high, tall, planes, cols), jnp.float32),
            pltpu.VMEM((depth - 1, high, tall, fields, cols), jnp.float32),
            pltpu.VMEM((7, high, tall, TILE, cols), jnp.float32),
            pltpu.VMEM((2, depth, high, fields, cols), jnp.float32),
            pltpu.VMEM((2, 7, high, TILE, cols), jnp.float32),
            pltpu.VMEM((depth, high, planes, cols), jnp.float32),
        ],
        compiler_params=PARAMS,
        name="powers",
    )(block, after, before, wide, below, above, corner_below, corner_above, shifts)
    count = points * cols * lax.axis_size("gx") * lax.axis_size("gy") * lax.axis_size("gz")
    axes = ("gx", "gy", "gz")
    devices = 1
    for name in axes:
        devices *= lax.axis_size(name)
    if order % devices == 0:
        share = jnp.sum(lax.all_to_all(gram.reshape(devices, order // devices, cols), axes, 0, 0), axis=0)
        spread = jnp.broadcast_to(share[None], (devices,) + share.shape)
        parts = [lax.all_to_all(spread, axes, 0, 0).reshape(order, cols)]
    else:
        parts = [summed(summed(summed(gram, "gy"), "gx"), "gz")]
    upper, basis_q = pl.pallas_call(
        functools.partial(finish_kernel, parts=len(parts), count=float(count), step=4),
        out_shape=(float_of(order, order), float_of(order * points, cols)),
        in_specs=[VMEM] * (len(parts) + 1),
        out_specs=(VMEM, VMEM),
        compiler_params=PARAMS,
        name="finish",
    )(*parts, basis)
    return basis_q.reshape(order, layers, rows, cols), upper


def solution(mesh):
    in_specs = (
        P(None, "gz", "gx", "gy"),
        P("gz", "gx", "gy"),
        P("gz", "gx", "gy"),
        P("gz", "gx", "gy"),
        P("gz", "gx", "gy"),
        P(),
    )
    out_specs = (P(None, "gz", "gx", "gy"), P())
    return jax.shard_map(local, mesh=mesh, in_specs=in_specs, out_specs=out_specs, check_vma=False)
```

```python
import functools

import jax
import jax.numpy as jnp
from jax import lax
from jax.experimental import pallas as pl
from jax.experimental.pallas import tpu as pltpu
from jax.sharding import PartitionSpec as P

POWERS = 4


newton_shifts = (15.4, 0.6, 11.7, 4.3)
basis_scale = 0.125

VMEM = pl.BlockSpec(memory_space=pltpu.VMEM)
SMEM = pl.BlockSpec(memory_space=pltpu.SMEM)
HBM = pl.BlockSpec(memory_space=pltpu.HBM)
PARAMS = pltpu.CompilerParams(vmem_limit_bytes=32 * 1024 * 1024)
FIRST = pltpu.CompilerParams(vmem_limit_bytes=60 * 1024 * 1024)

COEFS = 4
TILE = 8
CORNERS = ((1, 3), (1, 2), (1, 1), (2, 2), (2, 1), (3, 1))


def positions(shape):
    sub = lax.broadcasted_iota(jnp.int32, shape, 0)
    lane = lax.broadcasted_iota(jnp.int32, shape, 1)
    return sub, lane


def edges_kernel(
    load_ref, rows_ref, cols_ref, vias_ref, ground_ref, offset_ref,
    block_ref, next_ref, prev_ref, shift_ref, fields_in, coefs_in, sems,
):
    slabs, planes, cols = block_ref.shape
    fields = load_ref.shape[0] // slabs
    layers, rows, _ = rows_ref.shape
    depth = POWERS
    half = rows // 2
    total_layers = offset_ref.shape[0]
    copies = [
        pltpu.make_async_copy(ref, coefs_in.at[i], sems.at[i])
        for i, ref in enumerate((rows_ref, cols_ref, vias_ref, ground_ref))
    ]
    copies.append(pltpu.make_async_copy(load_ref, fields_in, sems.at[COEFS]))
    for copy in copies:
        copy.start()
    gx, gy, gz = (lax.axis_index(name) for name in ("gx", "gy", "gz"))
    last_row = jnp.where(gx == lax.axis_size("gx") - 1, rows - 1, rows)
    last_col = jnp.where(gy == lax.axis_size("gy") - 1, cols - 1, cols)
    sub, lane = positions((TILE, cols))
    for e in range(shift_ref.shape[0]):
        layer = gz * layers + e - depth
        inside = (layer >= 0) & (layer < total_layers)
        value = jnp.where(inside, offset_ref[jnp.clip(layer, 0, total_layers - 1)], 0)
        shift_ref[e] = jnp.broadcast_to(value, (TILE, cols))
    for copy in copies:
        copy.wait()
    for l in range(layers):
        layer = gz * layers + l
        target = gy * cols + lane + shift_ref[depth + l]
        via_ok = (target >= 0) & (target < cols * lax.axis_size("gy"))
        via_ok = via_ok & (jnp.broadcast_to(layer, lane.shape) < total_layers - 1)
        four = (
            jnp.where(sub == last_row, 0.0, coefs_in[0, l]),
            jnp.where(lane == last_col, 0.0, coefs_in[1, l]),
            jnp.where(via_ok, coefs_in[2, l], 0.0),
            coefs_in[3, l],
        )
        for r in range(rows):
            slab = l * rows + r
            values = [fields_in[pl.ds(f * slabs + slab, TILE, stride=slabs), :] for f in range(0, fields, TILE)]
            value = jnp.zeros((TILE, cols), jnp.float32)
            for c in range(COEFS):
                value = jnp.where(sub == c, jnp.broadcast_to(four[c][r : r + 1, :], (TILE, cols)), value)
            for t, value in enumerate(values + [value]):
                here = slice(t * TILE, t * TILE + TILE)
                block_ref[slab, here, :] = value
                if r < half:
                    prev_ref[l * half + r, here, :] = value
                else:
                    next_ref[l * half + r - half, here, :] = value


def corners_kernel(after_ref, before_ref, up_ref, down_ref, *, layers):
    planes = after_ref.shape[1]
    half = after_ref.shape[0] // layers
    count = len(CORNERS)
    for f in range(0, planes, TILE):
        here = slice(f, f + TILE)
        for i, (dz, dx) in enumerate(CORNERS):
            for ref, l in ((up_ref, layers - dz), (down_ref, dz - 1)):
                ref[i, here, :] = after_ref[l * half + half - dx, here, :]
                ref[count + i, here, :] = before_ref[l * half + dx - 1, here, :]


def slabs_of(e, layers, rows, own, after, before, below, above, corner_below, corner_above):
    depth, half, count = POWERS, rows // 2, len(CORNERS)
    if depth <= e < depth + layers:
        l = e - depth
        found = [(depth + r, own, l * rows + r) for r in range(rows)]
        for i in range(half):
            found.append((i, after, l * half + i))
            found.append((depth + rows + i, before, l * half + i))
        return found
    if e < depth:
        home, corner, first, distance = below, corner_below, 0, depth - e
    else:
        home, corner, first, distance = above, corner_above, depth + layers, e - depth - layers + 1
    found = [(depth + r, home, (e - first) * rows + r) for r in range(rows)]
    for i, (dz, dx) in enumerate(CORNERS):
        if dz == distance:
            found.append((depth - dx, corner, i))
            found.append((depth + rows - 1 + dx, corner, count + i))
    return found


def sides_kernel(*refs, layers, rows, pair):
    sources, edge_ref, out_refs = refs[:7], refs[7], refs[8:]
    high, planes, cols = edge_ref.shape
    depth = POWERS
    group = 2 * depth
    _, lane = positions((TILE, cols))
    early = lax.rem(lane, group) < depth
    gy = jnp.broadcast_to(lax.axis_index("gy"), (TILE, cols))

    @pl.loop(0, planes // TILE)
    def _(f):
        here = pl.ds(pl.multiple_of(f * TILE, TILE), TILE)
        edges = []
        for e in range(high):
            total = jnp.zeros((TILE, cols), jnp.float32)
            for row, ref, slab in slabs_of(e, layers, rows, *sources):
                moved = pltpu.roll(ref[slab, here, :], (group * row + depth) % cols, 1)
                total = jnp.where((lane >= group * row) & (lane < group * row + group), moved, total)
            edge_ref[e, here, :] = total
            edges.append(total)
        for t in range(high // 2):
            one, two = edges[2 * t], edges[2 * t + 1]
            up = jnp.where(early, one, pltpu.roll(two, depth, 1))
            down = jnp.where(early, pltpu.roll(one, cols - depth, 1), two)
            if pair:
                out_refs[0][t, here, :] = jnp.where(gy == 0, up, down)
            else:
                out_refs[0][t, here, :] = up
                out_refs[1][t, here, :] = down


def assemble_kernel(*refs, layers, rows):
    sources, start_ref = refs[:7], refs[7]
    high, _, planes, _ = start_ref.shape

    @pl.loop(0, planes // TILE)
    def _(f):
        here = pl.ds(pl.multiple_of(f * TILE, TILE), TILE)
        for e in range(high):
            for row, ref, slab in slabs_of(e, layers, rows, *sources):
                start_ref[e, row, here, :] = ref[slab, here, :]


def total_kernel(parts_ref, out_ref):
    rows, cols = parts_ref.shape[1:]
    for r in range(0, rows, TILE):
        here = slice(r, r + TILE)
        value = folded([parts_ref[i, here, :] for i in range(parts_ref.shape[0])])
        for i in range(out_ref.shape[0]):
            out_ref[i, here, :] = value


def powers_kernel(*refs, fields, layers, rows, pair):
    gots = 1 if pair else 2
    start_ref, edge_ref, got_refs, shift_ref = refs[0], refs[1], refs[2 : 2 + gots], refs[2 + gots]
    basis_ref, gram_ref, power_ref, coef_ref, strip_ref, strip_coef_ref, border_ref, sum_ref = refs[3 + gots :]
    high, tall, planes, cols = start_ref.shape
    depth = POWERS
    group = 2 * depth
    order = depth * fields
    tiles = range(0, fields, TILE)
    _, lane = positions((TILE, cols))
    gy = lax.axis_index("gy")

    def masks(e):
        shift = shift_ref[e]
        return shift == 0, shift > 0

    def from_above(seen, mask):
        left, centre, right = seen
        return jnp.where(mask[0], centre, jnp.where(mask[1], right, left))

    def from_below(seen, mask):
        left, centre, right = seen
        return jnp.where(mask[0], centre, jnp.where(mask[1], left, right))

    def around(tile):
        return pltpu.roll(tile, 1, 1), tile, pltpu.roll(tile, cols - 1, 1)

    def spread(tile, c):
        return jnp.broadcast_to(tile[c : c + 1, :], (TILE, cols))

    def put_factors(put, tile, row_above, seen, seen_below, mask):
        down, right, upper, ground = (spread(tile, c) for c in range(COEFS))
        up = spread(row_above, 0)
        left = spread(seen[0], 1)
        lower = from_below([spread(x, 2) for x in seen_below], mask)
        diagonal = ground + down + up + right + left + upper + lower
        for i, value in enumerate((down, up, right, left, upper, lower, diagonal)):
            put(i, value * basis_scale)

    def step(factors, theta, seen, up, down, above, below):
        value = (factors[6] - theta) * seen[1]
        value = value - (factors[0] * down + factors[1] * up)
        value = value - (factors[2] * seen[2] + factors[3] * seen[0])
        return value - (factors[4] * above + factors[5] * below)

    thetas = [shift * basis_scale for shift in newton_shifts]

    early = lax.rem(lane, group) < depth
    if pair:
        first_side = jnp.where(gy == 0, 1, 0)
        last_side = first_side + 1
    else:
        first_side, last_side = 0, 2

    @pl.loop(first_side, last_side)
    def _(side):
        left_side = jnp.broadcast_to(side, (TILE, cols)) == 0
        from_edge = early != left_side
        for e in range(high):
            for f in range(0, planes, TILE):
                here = slice(f, f + TILE)
                outer = got_refs[0][e // 2, here, :]
                if not pair:
                    outer = jnp.where(left_side, outer, got_refs[1][e // 2, here, :])
                if e % 2 == 0:
                    outer = jnp.where(left_side, outer, pltpu.roll(outer, depth, 1))
                else:
                    outer = jnp.where(left_side, pltpu.roll(outer, cols - depth, 1), outer)
                strip_ref[side, 0, e, here, :] = jnp.where(from_edge, edge_ref[e, here, :], outer)
        raw = [strip_ref[side, 0, e, fields : fields + TILE, :] for e in range(high)]
        seen = [around(tile) for tile in raw]
        for e in range(1, high - 1):

            def put(i, value, e=e):
                strip_coef_ref[side, i, e] = value

            put_factors(put, raw[e], pltpu.roll(raw[e], group, 1), seen[e], seen[e - 1], masks(e - 1))
        for k in range(1, depth):
            reach = depth - k
            looks = {}

            def look(e, f, k=k, looks=looks):
                if (e, f) not in looks:
                    looks[e, f] = around(strip_ref[side, k - 1, e, f : f + TILE, :])
                return looks[e, f]

            for e in range(depth - reach, depth + layers + reach):
                factors = [strip_coef_ref[side, i, e] for i in range(7)]
                over, under = masks(e), masks(e - 1)
                for f in tiles:
                    here = look(e, f)
                    strip_ref[side, k, e, f : f + TILE, :] = step(
                        factors,
                        thetas[k - 1],
                        here,
                        pltpu.roll(here[1], group, 1),
                        pltpu.roll(here[1], cols - group, 1),
                        from_above(look(e + 1, f), over),
                        from_below(look(e - 1, f), under),
                    )

    gy_lane = jnp.broadcast_to(gy, (TILE, cols))
    on_left = (lax.rem(lane, group) == depth - 1) & (gy_lane > 0)
    on_right = (lax.rem(lane, group) == depth - 2) & (gy_lane < lax.axis_size("gy") - 1)

    @pl.loop(0, high)
    def _(e):
        for k in range(depth):
            for f in range(0, planes if k == 0 else fields, TILE):
                here = slice(f, f + TILE)
                right = jnp.where(on_right, pltpu.roll(strip_ref[1, k, e, here, :], cols - 2, 1), 0.0)
                border_ref[k, e, here, :] = jnp.where(on_left, strip_ref[0, k, e, here, :], right)

    leftmost, rightmost = lane == 0, lane == cols - 1

    def looked(k, e, row, f):
        here = slice(f, f + TILE)
        tile = start_ref[e, row, here, :] if k == 0 else power_ref[k - 1, e, row, here, :]
        turn = lax.rem(2 * cols - group * row - depth + 1, cols)
        outer = pltpu.roll(border_ref[k, e, here, :], turn, 1)
        left, _, right = around(tile)
        return jnp.where(leftmost, outer, left), tile, jnp.where(rightmost, outer, right)

    def by_rows(reach, body):
        @pl.loop(0, rows)
        def _(r):
            body(depth + r, depth - reach, depth + layers + reach)

        for dx in range(1, reach + 1):

            @pl.loop(0, 2)
            def _(side, dx=dx):
                row = jnp.where(side == 0, depth - dx, depth + rows - 1 + dx)
                body(row, depth - reach + dx, depth + layers + reach - dx)

    def factors_of_row(row, first, last):
        seen = {e: looked(0, e, row, fields) for e in range(first - 1, last)}
        for e in range(first, last):

            def put(i, value, e=e):
                coef_ref[i, e, row] = value

            above_row = start_ref[e, row - 1, fields : fields + TILE, :]
            put_factors(put, seen[e][1], above_row, seen[e], seen[e - 1], masks(e - 1))

    by_rows(depth - 1, factors_of_row)

    for k in range(1, depth + 1):

        def advance(row, first, last, k=k):
            source = start_ref if k == 1 else power_ref.at[k - 2]
            below = {f: from_below(looked(k - 1, first - 1, row, f), masks(first - 1)) for f in tiles}
            centre = {f: looked(k - 1, first, row, f) for f in tiles}
            for e in range(first, last):
                factors = [coef_ref[i, e, row] for i in range(7)]
                mask = masks(e)
                for f in tiles:
                    here = slice(f, f + TILE)
                    upper = looked(k - 1, e + 1, row, f)
                    value = step(
                        factors,
                        thetas[k - 1],
                        centre[f],
                        source[e, row - 1, here, :],
                        source[e, row + 1, here, :],
                        from_above(upper, mask),
                        below[f],
                    )
                    below[f], centre[f] = from_below(centre[f], mask), upper
                    if k < depth:
                        power_ref[k - 1, e, row, here, :] = value
                    if first == depth - (depth - k) and depth <= e < depth + layers:
                        slab = (e - depth) * rows + row - depth
                        place = pl.multiple_of(slab * order + (k - 1) * fields + f, TILE)
                        basis_ref[pl.ds(place, TILE), :] = value

        if k < depth:
            by_rows(depth - k, advance)

    def share(r):
        value = None
        for l in range(0, layers, 2):
            places = [pl.multiple_of(((l + i) * rows + r) * order, TILE) for i in range(2)]
            wide = jnp.concatenate([basis_ref[pl.ds(place, order), :] for place in places], axis=1)
            product = lax.dot_general(
                wide, wide, (((1,), (1,)), ((), ())),
                precision=lax.Precision.HIGHEST, preferred_element_type=jnp.float32,
            )
            value = product if value is None else value + product
        return value

    advance(depth, depth, depth + layers)
    sum_ref[...] = jnp.zeros_like(sum_ref)

    @pl.loop(1, rows)
    def _(r):
        product = share(r - 1)
        advance(depth + r, depth, depth + layers)
        sum_ref[...] += product

    total = sum_ref[...] + share(rows - 1)
    padded = jnp.concatenate([total, jnp.zeros((order, cols - order), jnp.float32)], axis=1)
    for i in range(gram_ref.shape[0]):
        gram_ref[i] = padded


def eliminate(tiles, order, step):
    width = tiles[0].shape[1]
    lane = lax.broadcasted_iota(jnp.int32, (8, width), 1)
    sub = lax.broadcasted_iota(jnp.int32, (8, width), 0)
    spread = lambda value: jnp.broadcast_to(value, (8, width))
    for first in range(0, order, step):
        home, base = first // 8, first % 8
        panel = tiles[home]
        entry = {}
        for i in range(step):
            for j in range(i, step):
                entry[i, j] = spread(panel[base + i : base + i + 1, first + j : first + j + 1])
        rows = [spread(panel[base + i : base + i + 1, :]) for i in range(step)]
        inverse = []
        done = []
        for i in range(step):
            row = rows[i]
            if i:
                row = jnp.where((lane >= first) & (lane < first + i), 0.0, row)
            factors = []
            for j in range(i):
                factor = entry[j, i] * inverse[j]
                factors.append(factor)
            for j in range(i):
                source = jnp.where(lane == first + j, 1.0, done[j])
                if i - j > 1:
                    source = jnp.where((lane > first + j) & (lane < first + i), 0.0, source)
                row = row - factors[j] * source
                for m in range(i, step):
                    entry[i, m] = entry[i, m] - factors[j] * entry[j, m]
            inverse.append(1.0 / entry[i, i])
            done.append(row)
        sources = []
        for j in range(step):
            source = jnp.where(lane == first + j, 1.0, done[j])
            if j < step - 1:
                source = jnp.where((lane > first + j) & (lane < first + step), 0.0, source)
            sources.append(source)
        inside = (lane >= first) & (lane < first + step)
        for t in range(home, order // 8):
            if t == home and base + step == 8:
                fresh = tiles[t]
            else:
                columns = [spread(tiles[t][:, first + j : first + j + 1]) for j in range(step)]
                fresh = jnp.where(inside, 0.0, tiles[t])
                for j in range(step):
                    factor = columns[j] * inverse[j]
                    fresh = fresh - factor * sources[j]
                    for m in range(j + 1, step):
                        columns[m] = columns[m] - factor * entry[j, m]
            if t == home:
                fresh = jnp.where(sub < base + step, tiles[t], fresh)
                for j in range(step):
                    fresh = jnp.where(sub == base + j, done[j], fresh)
            tiles[t] = fresh
    return tiles


def finish_kernel(parts_ref, basis_ref, upper_ref, out_ref, *, count, step):
    order = upper_ref.shape[0]
    points = basis_ref.shape[0] // order
    tiles = []
    for t in range(order // 8):
        pieces = [parts_ref[i, 8 * t : 8 * t + 8, :order] for i in range(parts_ref.shape[0])]
        tiles.append(folded(pieces) / count)
    tiles = eliminate(tiles, order, step)
    lane = lax.broadcasted_iota(jnp.int32, (8, order), 1)
    sub = lax.broadcasted_iota(jnp.int32, (8, order), 0)
    inverse = []
    for t in range(order // 8):
        row = sub + 8 * t
        pivot = jnp.sum(jnp.where(lane == row, tiles[t], 0.0), axis=1, keepdims=True)
        scale = 1.0 / jnp.sqrt(pivot)
        upper_ref[8 * t : 8 * t + 8, :] = jnp.where(lane >= row, tiles[t] * scale, 0.0)
        inverse.append(jnp.where(lane < row, tiles[t], jnp.where(lane == row, 1.0, 0.0)) * scale)
    inverse = jnp.concatenate(inverse, axis=0)
    for i in range(points // 2):
        start = 2 * i * order
        wide = jnp.concatenate(
            [basis_ref[start : start + order, :], basis_ref[start + order : start + 2 * order, :]], axis=1
        )
        out = jnp.dot(inverse, wide, precision=lax.Precision.HIGHEST, preferred_element_type=jnp.float32)
        cols = basis_ref.shape[1]
        out_ref[pl.ds(2 * i, order, stride=points), :] = out[:, :cols]
        out_ref[pl.ds(2 * i + 1, order, stride=points), :] = out[:, cols:]


def folded(pieces):
    while len(pieces) > 1:
        half = len(pieces) // 2
        pieces = [pieces[i] + pieces[i + half] for i in range(half)]
    return pieces[0]


def sent(value, steps):
    axes = tuple(steps)
    sizes = [lax.axis_size(name) for name in axes]
    pairs = []
    if len(axes) == 1:
        pairs = [(i, i + steps[axes[0]]) for i in range(sizes[0]) if 0 <= i + steps[axes[0]] < sizes[0]]
        return lax.ppermute(value, axes[0], pairs)
    for i in range(sizes[0]):
        for j in range(sizes[1]):
            m, n = i + steps[axes[0]], j + steps[axes[1]]
            if 0 <= m < sizes[0] and 0 <= n < sizes[1]:
                pairs.append((i * sizes[1] + j, m * sizes[1] + n))
    return lax.ppermute(value, axes, pairs)


def local(load_currents, cond_rows, cond_cols, cond_vias, ground, via_offset):
    fields, layers, rows, cols = load_currents.shape
    depth = POWERS
    assert layers == depth and rows == 2 * depth and cols == 4 * depth * rows and fields % TILE == 0
    float_of = lambda *shape: jax.ShapeDtypeStruct(shape, jnp.float32)
    pair = lax.axis_size("gy") == 2
    planes = fields + TILE
    slabs = layers * rows
    high = layers + 2 * depth
    tall = rows + 2 * depth
    count = len(CORNERS)
    whole, part = float_of(slabs, planes, cols), float_of(slabs // 2, planes, cols)
    block, to_next, to_prev, shifts = pl.pallas_call(
        edges_kernel,
        out_shape=(whole, part, part, jax.ShapeDtypeStruct((high, TILE, cols), jnp.int32)),
        in_specs=[HBM] * 5 + [SMEM],
        out_specs=(VMEM,) * 4,
        scratch_shapes=[
            pltpu.VMEM((fields * slabs, cols), jnp.float32),
            pltpu.VMEM((COEFS, layers, rows, cols), jnp.float32),
            pltpu.SemaphoreType.DMA((COEFS + 1,)),
        ],
        compiler_params=FIRST,
        name="edges",
    )(load_currents.reshape(fields * slabs, cols), cond_rows, cond_cols, cond_vias, ground, via_offset)
    after = sent(to_next, {"gx": 1})
    before = sent(to_prev, {"gx": -1})
    below = sent(block, {"gz": 1})
    above = sent(block, {"gz": -1})
    to_above, to_below = pl.pallas_call(
        functools.partial(corners_kernel, layers=layers),
        out_shape=(float_of(2 * count, planes, cols),) * 2,
        in_specs=[VMEM] * 2,
        out_specs=(VMEM,) * 2,
        compiler_params=PARAMS,
        name="corners",
    )(after, before)
    corner_below = sent(to_above, {"gz": 1})
    corner_above = sent(to_below, {"gz": -1})
    pieces = (block, after, before, below, above, corner_below, corner_above)
    edge, *outer = pl.pallas_call(
        functools.partial(sides_kernel, layers=layers, rows=rows, pair=pair),
        out_shape=(float_of(high, planes, cols),) + (float_of(high // 2, planes, cols),) * (1 if pair else 2),
        in_specs=[VMEM] * 7,
        out_specs=(VMEM,) * (2 if pair else 3),
        compiler_params=PARAMS,
        name="sides",
    )(*pieces)
    if pair:
        got = [lax.ppermute(outer[0], "gy", [(0, 1), (1, 0)])]
    else:
        got = [sent(outer[0], {"gy": 1}), sent(outer[1], {"gy": -1})]
    start = pl.pallas_call(
        functools.partial(assemble_kernel, layers=layers, rows=rows),
        out_shape=float_of(high, tall, planes, cols),
        in_specs=[VMEM] * 7,
        out_specs=VMEM,
        compiler_params=PARAMS,
        cost_estimate=pl.CostEstimate(flops=0, bytes_accessed=2 * high * tall * planes * cols, transcendentals=0),
        name="assemble",
    )(*pieces)
    order = depth * fields
    points = slabs
    plane_devices = lax.axis_size("gy") * lax.axis_size("gz")
    basis, gram = pl.pallas_call(
        functools.partial(powers_kernel, fields=fields, layers=layers, rows=rows, pair=pair),
        out_shape=(float_of(points * order, cols), float_of(plane_devices, order, cols)),
        in_specs=[VMEM] * (3 + len(got)),
        out_specs=(VMEM, VMEM),
        scratch_shapes=[
            pltpu.VMEM((depth - 1, high, tall, fields, cols), jnp.float32),
            pltpu.VMEM((7, high, tall, TILE, cols), jnp.float32),
            pltpu.VMEM((2, depth, high, planes, cols), jnp.float32),
            pltpu.VMEM((2, 7, high, TILE, cols), jnp.float32),
            pltpu.VMEM((depth, high, planes, cols), jnp.float32),
            pltpu.VMEM((order, order), jnp.float32),
        ],
        compiler_params=PARAMS,
        name="powers",
    )(start, edge, *got, shifts)
    points_in_all = points * cols * lax.axis_size("gx") * plane_devices
    gram = lax.all_to_all(gram, ("gy", "gz"), 0, 0)
    gram = pl.pallas_call(
        total_kernel,
        out_shape=float_of(lax.axis_size("gx"), order, cols),
        in_specs=[VMEM],
        out_specs=VMEM,
        compiler_params=PARAMS,
        name="total",
    )(gram)
    gram = lax.all_to_all(gram, "gx", 0, 0)
    upper, basis_q = pl.pallas_call(
        functools.partial(finish_kernel, count=float(points_in_all), step=4),
        out_shape=(float_of(order, order), float_of(order * points, cols)),
        in_specs=[VMEM] * 2,
        out_specs=(VMEM, VMEM),
        compiler_params=PARAMS,
        name="finish",
    )(gram, basis)
    return basis_q.reshape(order, layers, rows, cols), upper


def solution(mesh):
    in_specs = (
        P(None, "gz", "gx", "gy"),
        P("gz", "gx", "gy"),
        P("gz", "gx", "gy"),
        P("gz", "gx", "gy"),
        P("gz", "gx", "gy"),
        P(),
    )
    out_specs = (P(None, "gz", "gx", "gy"), P())
    return jax.shard_map(local, mesh=mesh, in_specs=in_specs, out_specs=out_specs, check_vma=False)
```

```python
import functools

import jax
import jax.numpy as jnp
from jax import lax
from jax.experimental import pallas as pl
from jax.experimental.pallas import tpu as pltpu
from jax.sharding import PartitionSpec as P

POWERS = 4


newton_shifts = (15.4, 0.6, 11.7, 4.3)
basis_scale = 0.125

VMEM = pl.BlockSpec(memory_space=pltpu.VMEM)
SMEM = pl.BlockSpec(memory_space=pltpu.SMEM)
HBM = pl.BlockSpec(memory_space=pltpu.HBM)
PARAMS = pltpu.CompilerParams(vmem_limit_bytes=32 * 1024 * 1024)
FIRST = pltpu.CompilerParams(vmem_limit_bytes=60 * 1024 * 1024)

COEFS = 4
TILE = 8
CORNERS = ((1, 3), (1, 2), (1, 1), (2, 2), (2, 1), (3, 1))


def positions(shape):
    sub = lax.broadcasted_iota(jnp.int32, shape, 0)
    lane = lax.broadcasted_iota(jnp.int32, shape, 1)
    return sub, lane


def edges_kernel(
    load_ref, rows_ref, cols_ref, vias_ref, ground_ref, offset_ref,
    block_ref, first_ref, second_ref, shift_ref, fields_in, coefs_in, sems,
):
    slabs, planes, cols = block_ref.shape
    fields = load_ref.shape[0] // slabs
    layers, rows, _ = rows_ref.shape
    depth = POWERS
    half = rows // 2
    total_layers = offset_ref.shape[0]
    copies = [
        pltpu.make_async_copy(ref, coefs_in.at[i], sems.at[i])
        for i, ref in enumerate((rows_ref, cols_ref, vias_ref, ground_ref))
    ]
    copies.append(pltpu.make_async_copy(load_ref, fields_in, sems.at[COEFS]))
    for copy in copies:
        copy.start()
    gx, gy, gz = (lax.axis_index(name) for name in ("gx", "gy", "gz"))
    last_row = jnp.where(gx == lax.axis_size("gx") - 1, rows - 1, rows)
    last_col = jnp.where(gy == lax.axis_size("gy") - 1, cols - 1, cols)
    sub, lane = positions((TILE, cols))
    for e in range(shift_ref.shape[0]):
        layer = gz * layers + e - depth
        inside = (layer >= 0) & (layer < total_layers)
        value = jnp.where(inside, offset_ref[jnp.clip(layer, 0, total_layers - 1)], 0)
        shift_ref[e] = jnp.broadcast_to(value, (TILE, cols))
    for copy in copies:
        copy.wait()
    for l in range(layers):
        layer = gz * layers + l
        target = gy * cols + lane + shift_ref[depth + l]
        via_ok = (target >= 0) & (target < cols * lax.axis_size("gy"))
        via_ok = via_ok & (jnp.broadcast_to(layer, lane.shape) < total_layers - 1)
        four = (
            jnp.where(sub == last_row, 0.0, coefs_in[0, l]),
            jnp.where(lane == last_col, 0.0, coefs_in[1, l]),
            jnp.where(via_ok, coefs_in[2, l], 0.0),
            coefs_in[3, l],
        )
        for r in range(rows):
            slab = l * rows + r
            values = [fields_in[pl.ds(f * slabs + slab, TILE, stride=slabs), :] for f in range(0, fields, TILE)]
            value = jnp.zeros((TILE, cols), jnp.float32)
            for c in range(COEFS):
                value = jnp.where(sub == c, jnp.broadcast_to(four[c][r : r + 1, :], (TILE, cols)), value)
            for t, value in enumerate(values + [value]):
                here = slice(t * TILE, t * TILE + TILE)
                block_ref[slab, here, :] = value
    even = lax.rem(gx, 2) == 0
    starts = [jnp.where(even, half, 0), jnp.where(even, 0, half)]

    @pl.loop(0, half)
    def _(i):
        for l in range(layers):
            for f in range(0, planes, TILE):
                here = slice(f, f + TILE)
                for ref, start in zip((first_ref, second_ref), starts):
                    ref[l * half + i, here, :] = block_ref[l * rows + start + i, here, :]


def corners_kernel(first_ref, second_ref, after_ref, before_ref, one_ref, two_ref, *, layers):
    planes, cols = after_ref.shape[1:]
    half = after_ref.shape[0] // layers
    count = len(CORNERS)
    even_row = jnp.broadcast_to(lax.rem(lax.axis_index("gx"), 2), (TILE, cols)) == 0
    even_layer = jnp.broadcast_to(lax.rem(lax.axis_index("gz"), 2), (TILE, cols)) == 0

    @pl.loop(0, planes // TILE)
    def _(f):
        here = pl.ds(pl.multiple_of(f * TILE, TILE), TILE)
        after, before = [], []
        for i in range(layers * half):
            first, second = first_ref[i, here, :], second_ref[i, here, :]
            after.append(jnp.where(even_row, second, first))
            before.append(jnp.where(even_row, first, second))
            after_ref[i, here, :] = after[i]
            before_ref[i, here, :] = before[i]
        for i, (dz, dx) in enumerate(CORNERS):
            high, low = (layers - dz) * half, (dz - 1) * half
            for at, source, row in ((i, after, half - dx), (count + i, before, dx - 1)):
                up, down = source[high + row], source[low + row]
                one_ref[at, here, :] = jnp.where(even_layer, up, down)
                two_ref[at, here, :] = jnp.where(even_layer, down, up)


def slabs_of(e, layers, rows, block, after, before, one, two, corner_one, corner_two):
    depth, half, count = POWERS, rows // 2, len(CORNERS)
    cols = block.shape[2]

    def plain(ref, slab):
        return lambda here: ref[slab, here, :]

    def chosen(pair, slab):
        even = jnp.broadcast_to(lax.rem(lax.axis_index("gz"), 2), (TILE, cols)) == 0
        return lambda here: jnp.where(even, pair[0][slab, here, :], pair[1][slab, here, :])

    if depth <= e < depth + layers:
        l = e - depth
        found = [(depth + r, plain(block, l * rows + r)) for r in range(rows)]
        for i in range(half):
            found.append((i, plain(after, l * half + i)))
            found.append((depth + rows + i, plain(before, l * half + i)))
        return found
    if e < depth:
        home, corner, first, distance = (two, one), (corner_two, corner_one), 0, depth - e
    else:
        home, corner, first, distance = (one, two), (corner_one, corner_two), depth + layers, e - depth - layers + 1
    found = [(depth + r, chosen(home, (e - first) * rows + r)) for r in range(rows)]
    for i, (dz, dx) in enumerate(CORNERS):
        if dz == distance:
            found.append((depth - dx, chosen(corner, i)))
            found.append((depth + rows - 1 + dx, chosen(corner, count + i)))
    return found


def sides_kernel(*refs, layers, rows, pair):
    sources, edge_ref, out_refs = refs[:7], refs[7], refs[8:]
    high, planes, cols = edge_ref.shape
    depth = POWERS
    group = 2 * depth
    _, lane = positions((TILE, cols))
    early = lax.rem(lane, group) < depth
    gy = jnp.broadcast_to(lax.axis_index("gy"), (TILE, cols))

    @pl.loop(0, planes // TILE)
    def _(f):
        here = pl.ds(pl.multiple_of(f * TILE, TILE), TILE)
        edges = []
        for e in range(high):
            total = jnp.zeros((TILE, cols), jnp.float32)
            for row, read in slabs_of(e, layers, rows, *sources):
                moved = pltpu.roll(read(here), (group * row + depth) % cols, 1)
                total = jnp.where((lane >= group * row) & (lane < group * row + group), moved, total)
            edge_ref[e, here, :] = total
            edges.append(total)
        for t in range(high // 2):
            one, two = edges[2 * t], edges[2 * t + 1]
            up = jnp.where(early, one, pltpu.roll(two, depth, 1))
            down = jnp.where(early, pltpu.roll(one, cols - depth, 1), two)
            if pair:
                out_refs[0][t, here, :] = jnp.where(gy == 0, up, down)
            else:
                out_refs[0][t, here, :] = up
                out_refs[1][t, here, :] = down


def assemble_kernel(*refs, layers, rows):
    sources, start_ref = refs[:7], refs[7]
    high, _, planes, _ = start_ref.shape

    @pl.loop(0, planes // TILE)
    def _(f):
        here = pl.ds(pl.multiple_of(f * TILE, TILE), TILE)
        for e in range(high):
            for row, read in slabs_of(e, layers, rows, *sources):
                start_ref[e, row, here, :] = read(here)


def powers_kernel(*refs, fields, layers, rows, pair):
    gots = 1 if pair else 2
    start_ref, edge_ref, got_refs, shift_ref = refs[0], refs[1], refs[2 : 2 + gots], refs[2 + gots]
    basis_ref, gram_ref, power_ref, coef_ref, strip_ref, strip_coef_ref, border_ref, sum_ref = refs[3 + gots :]
    high, tall, planes, cols = start_ref.shape
    depth = POWERS
    group = 2 * depth
    order = depth * fields
    tiles = range(0, fields, TILE)
    _, lane = positions((TILE, cols))
    gy = lax.axis_index("gy")

    def masks(e):
        shift = shift_ref[e]
        return shift == 0, shift > 0

    def from_above(seen, mask):
        left, centre, right = seen
        return jnp.where(mask[0], centre, jnp.where(mask[1], right, left))

    def from_below(seen, mask):
        left, centre, right = seen
        return jnp.where(mask[0], centre, jnp.where(mask[1], left, right))

    def around(tile):
        return pltpu.roll(tile, 1, 1), tile, pltpu.roll(tile, cols - 1, 1)

    def spread(tile, c):
        return jnp.broadcast_to(tile[c : c + 1, :], (TILE, cols))

    def put_factors(put, tile, row_above, seen, seen_below, mask):
        down, right, upper, ground = (spread(tile, c) for c in range(COEFS))
        up = spread(row_above, 0)
        left = spread(seen[0], 1)
        lower = from_below([spread(x, 2) for x in seen_below], mask)
        diagonal = ground + down + up + right + left + upper + lower
        for i, value in enumerate((down, up, right, left, upper, lower, diagonal)):
            put(i, value * basis_scale)

    def step(factors, theta, seen, up, down, above, below):
        value = (factors[6] - theta) * seen[1]
        value = value - (factors[0] * down + factors[1] * up)
        value = value - (factors[2] * seen[2] + factors[3] * seen[0])
        return value - (factors[4] * above + factors[5] * below)

    thetas = [shift * basis_scale for shift in newton_shifts]

    early = lax.rem(lane, group) < depth
    if pair:
        first_side = jnp.where(gy == 0, 1, 0)
        last_side = first_side + 1
    else:
        first_side, last_side = 0, 2

    @pl.loop(first_side, last_side)
    def _(side):
        left_side = jnp.broadcast_to(side, (TILE, cols)) == 0
        from_edge = early != left_side
        for e in range(high):
            for f in range(0, planes, TILE):
                here = slice(f, f + TILE)
                outer = got_refs[0][e // 2, here, :]
                if not pair:
                    outer = jnp.where(left_side, outer, got_refs[1][e // 2, here, :])
                if e % 2 == 0:
                    outer = jnp.where(left_side, outer, pltpu.roll(outer, depth, 1))
                else:
                    outer = jnp.where(left_side, pltpu.roll(outer, cols - depth, 1), outer)
                strip_ref[side, 0, e, here, :] = jnp.where(from_edge, edge_ref[e, here, :], outer)
        raw = [strip_ref[side, 0, e, fields : fields + TILE, :] for e in range(high)]
        seen = [around(tile) for tile in raw]
        for e in range(1, high - 1):

            def put(i, value, e=e):
                strip_coef_ref[side, i, e] = value

            put_factors(put, raw[e], pltpu.roll(raw[e], group, 1), seen[e], seen[e - 1], masks(e - 1))
        for k in range(1, depth):
            reach = depth - k
            looks = {}

            def look(e, f, k=k, looks=looks):
                if (e, f) not in looks:
                    looks[e, f] = around(strip_ref[side, k - 1, e, f : f + TILE, :])
                return looks[e, f]

            for e in range(depth - reach, depth + layers + reach):
                factors = [strip_coef_ref[side, i, e] for i in range(7)]
                over, under = masks(e), masks(e - 1)
                for f in tiles:
                    here = look(e, f)
                    strip_ref[side, k, e, f : f + TILE, :] = step(
                        factors,
                        thetas[k - 1],
                        here,
                        pltpu.roll(here[1], group, 1),
                        pltpu.roll(here[1], cols - group, 1),
                        from_above(look(e + 1, f), over),
                        from_below(look(e - 1, f), under),
                    )

    gy_lane = jnp.broadcast_to(gy, (TILE, cols))
    on_left = (lax.rem(lane, group) == depth - 1) & (gy_lane > 0)
    on_right = (lax.rem(lane, group) == depth - 2) & (gy_lane < lax.axis_size("gy") - 1)

    @pl.loop(0, high)
    def _(e):
        for k in range(depth):
            for f in range(0, planes if k == 0 else fields, TILE):
                here = slice(f, f + TILE)
                right = jnp.where(on_right, pltpu.roll(strip_ref[1, k, e, here, :], cols - 2, 1), 0.0)
                border_ref[k, e, here, :] = jnp.where(on_left, strip_ref[0, k, e, here, :], right)

    leftmost, rightmost = lane == 0, lane == cols - 1

    def looked(k, e, row, f):
        here = slice(f, f + TILE)
        tile = start_ref[e, row, here, :] if k == 0 else power_ref[k - 1, e, row, here, :]
        turn = lax.rem(2 * cols - group * row - depth + 1, cols)
        outer = pltpu.roll(border_ref[k, e, here, :], turn, 1)
        left, _, right = around(tile)
        return jnp.where(leftmost, outer, left), tile, jnp.where(rightmost, outer, right)

    def by_rows(reach, body):
        @pl.loop(0, rows)
        def _(r):
            body(depth + r, depth - reach, depth + layers + reach)

        for dx in range(1, reach + 1):

            @pl.loop(0, 2)
            def _(side, dx=dx):
                row = jnp.where(side == 0, depth - dx, depth + rows - 1 + dx)
                body(row, depth - reach + dx, depth + layers + reach - dx)

    def factors_of_row(row, first, last):
        seen = {e: looked(0, e, row, fields) for e in range(first - 1, last)}
        for e in range(first, last):

            def put(i, value, e=e):
                coef_ref[i, e, row] = value

            above_row = start_ref[e, row - 1, fields : fields + TILE, :]
            put_factors(put, seen[e][1], above_row, seen[e], seen[e - 1], masks(e - 1))

    by_rows(depth - 1, factors_of_row)

    for k in range(1, depth + 1):

        def advance(row, first, last, k=k):
            source = start_ref if k == 1 else power_ref.at[k - 2]
            below = {f: from_below(looked(k - 1, first - 1, row, f), masks(first - 1)) for f in tiles}
            centre = {f: looked(k - 1, first, row, f) for f in tiles}
            for e in range(first, last):
                factors = [coef_ref[i, e, row] for i in range(7)]
                mask = masks(e)
                for f in tiles:
                    here = slice(f, f + TILE)
                    upper = looked(k - 1, e + 1, row, f)
                    value = step(
                        factors,
                        thetas[k - 1],
                        centre[f],
                        source[e, row - 1, here, :],
                        source[e, row + 1, here, :],
                        from_above(upper, mask),
                        below[f],
                    )
                    below[f], centre[f] = from_below(centre[f], mask), upper
                    if k < depth:
                        power_ref[k - 1, e, row, here, :] = value
                    if first == depth - (depth - k) and depth <= e < depth + layers:
                        slab = (e - depth) * rows + row - depth
                        place = pl.multiple_of(slab * order + (k - 1) * fields + f, TILE)
                        basis_ref[pl.ds(place, TILE), :] = value

        if k < depth:
            by_rows(depth - k, advance)

    def share(r):
        value = None
        for l in range(0, layers, 2):
            places = [pl.multiple_of(((l + i) * rows + r) * order, TILE) for i in range(2)]
            wide = jnp.concatenate([basis_ref[pl.ds(place, order), :] for place in places], axis=1)
            product = lax.dot_general(
                wide, wide, (((1,), (1,)), ((), ())),
                precision=lax.Precision.HIGHEST, preferred_element_type=jnp.float32,
            )
            value = product if value is None else value + product
        return value

    advance(depth, depth, depth + layers)
    sum_ref[...] = jnp.zeros_like(sum_ref)

    @pl.loop(1, rows)
    def _(r):
        product = share(r - 1)
        advance(depth + r, depth, depth + layers)
        sum_ref[...] += product

    total = sum_ref[...] + share(rows - 1)
    gram_ref[...] = total


def eliminate(tiles, order, step):
    width = tiles[0].shape[1]
    lane = lax.broadcasted_iota(jnp.int32, (8, width), 1)
    sub = lax.broadcasted_iota(jnp.int32, (8, width), 0)
    spread = lambda value: jnp.broadcast_to(value, (8, width))
    for first in range(0, order, step):
        home, base = first // 8, first % 8
        panel = tiles[home]
        entry = {}
        for i in range(step):
            for j in range(i, step):
                entry[i, j] = spread(panel[base + i : base + i + 1, first + j : first + j + 1])
        rows = [spread(panel[base + i : base + i + 1, :]) for i in range(step)]
        inverse = []
        done = []
        for i in range(step):
            row = rows[i]
            if i:
                row = jnp.where((lane >= first) & (lane < first + i), 0.0, row)
            factors = []
            for j in range(i):
                factor = entry[j, i] * inverse[j]
                factors.append(factor)
            for j in range(i):
                source = jnp.where(lane == first + j, 1.0, done[j])
                if i - j > 1:
                    source = jnp.where((lane > first + j) & (lane < first + i), 0.0, source)
                row = row - factors[j] * source
                for m in range(i, step):
                    entry[i, m] = entry[i, m] - factors[j] * entry[j, m]
            inverse.append(1.0 / entry[i, i])
            done.append(row)
        sources = []
        for j in range(step):
            source = jnp.where(lane == first + j, 1.0, done[j])
            if j < step - 1:
                source = jnp.where((lane > first + j) & (lane < first + step), 0.0, source)
            sources.append(source)
        inside = (lane >= first) & (lane < first + step)
        for t in range(home, order // 8):
            if t == home and base + step == 8:
                fresh = tiles[t]
            else:
                columns = [spread(tiles[t][:, first + j : first + j + 1]) for j in range(step)]
                fresh = jnp.where(inside, 0.0, tiles[t])
                for j in range(step):
                    factor = columns[j] * inverse[j]
                    fresh = fresh - factor * sources[j]
                    for m in range(j + 1, step):
                        columns[m] = columns[m] - factor * entry[j, m]
            if t == home:
                fresh = jnp.where(sub < base + step, tiles[t], fresh)
                for j in range(step):
                    fresh = jnp.where(sub == base + j, done[j], fresh)
            tiles[t] = fresh
    return tiles


def finish_kernel(*refs, count, step):
    part_refs, (basis_ref, upper_ref, out_ref) = refs[:-3], refs[-3:]
    order = upper_ref.shape[0]
    points = basis_ref.shape[0] // order
    tiles = []
    for t in range(order // 8):
        pieces = [ref[8 * t : 8 * t + 8, :] for ref in part_refs]
        tiles.append(folded(pieces) / count)
    tiles = eliminate(tiles, order, step)
    lane = lax.broadcasted_iota(jnp.int32, (8, order), 1)
    sub = lax.broadcasted_iota(jnp.int32, (8, order), 0)
    inverse = []
    for t in range(order // 8):
        row = sub + 8 * t
        pivot = jnp.sum(jnp.where(lane == row, tiles[t], 0.0), axis=1, keepdims=True)
        scale = 1.0 / jnp.sqrt(pivot)
        upper_ref[8 * t : 8 * t + 8, :] = jnp.where(lane >= row, tiles[t] * scale, 0.0)
        inverse.append(jnp.where(lane < row, tiles[t], jnp.where(lane == row, 1.0, 0.0)) * scale)
    inverse = jnp.concatenate(inverse, axis=0)
    for i in range(points // 2):
        start = 2 * i * order
        wide = jnp.concatenate(
            [basis_ref[start : start + order, :], basis_ref[start + order : start + 2 * order, :]], axis=1
        )
        out = jnp.dot(inverse, wide, precision=lax.Precision.HIGHEST, preferred_element_type=jnp.float32)
        cols = basis_ref.shape[1]
        out_ref[pl.ds(2 * i, order, stride=points), :] = out[:, :cols]
        out_ref[pl.ds(2 * i + 1, order, stride=points), :] = out[:, cols:]


def folded(pieces):
    while len(pieces) > 1:
        pieces = [pieces[i] + pieces[i + 1] for i in range(0, len(pieces), 2)]
    return pieces[0]


def rounds(axis):
    size, unit, out = lax.axis_size(axis), 1, []
    while unit < size:
        many = 4 if unit * 4 <= size else 2
        out.append([unit * m for m in range(1, many)])
        unit *= many
    return out


def gathered(value, axis, partners):
    size = lax.axis_size(axis)
    return [value] + [lax.ppermute(value, axis, [(i, i ^ m) for i in range(size)]) for m in partners]


def swapped(value, axis, phase):
    pairs = []
    for i in range(phase, lax.axis_size(axis) - 1, 2):
        pairs += [(i, i + 1), (i + 1, i)]
    return lax.ppermute(value, axis, pairs)


def sent(value, steps):
    axes = tuple(steps)
    sizes = [lax.axis_size(name) for name in axes]
    pairs = []
    if len(axes) == 1:
        pairs = [(i, i + steps[axes[0]]) for i in range(sizes[0]) if 0 <= i + steps[axes[0]] < sizes[0]]
        return lax.ppermute(value, axes[0], pairs)
    for i in range(sizes[0]):
        for j in range(sizes[1]):
            m, n = i + steps[axes[0]], j + steps[axes[1]]
            if 0 <= m < sizes[0] and 0 <= n < sizes[1]:
                pairs.append((i * sizes[1] + j, m * sizes[1] + n))
    return lax.ppermute(value, axes, pairs)


def local(load_currents, cond_rows, cond_cols, cond_vias, ground, via_offset):
    fields, layers, rows, cols = load_currents.shape
    depth = POWERS
    assert layers == depth and rows == 2 * depth and cols == 4 * depth * rows and fields % TILE == 0
    float_of = lambda *shape: jax.ShapeDtypeStruct(shape, jnp.float32)
    pair = lax.axis_size("gy") == 2
    planes = fields + TILE
    slabs = layers * rows
    high = layers + 2 * depth
    tall = rows + 2 * depth
    count = len(CORNERS)
    whole, part = float_of(slabs, planes, cols), float_of(slabs // 2, planes, cols)
    block, first, second, shifts = pl.pallas_call(
        edges_kernel,
        out_shape=(whole, part, part, jax.ShapeDtypeStruct((high, TILE, cols), jnp.int32)),
        in_specs=[HBM] * 5 + [SMEM],
        out_specs=(VMEM,) * 4,
        scratch_shapes=[
            pltpu.VMEM((fields * slabs, cols), jnp.float32),
            pltpu.VMEM((COEFS, layers, rows, cols), jnp.float32),
            pltpu.SemaphoreType.DMA((COEFS + 1,)),
        ],
        compiler_params=FIRST,
        name="edges",
    )(load_currents.reshape(fields * slabs, cols), cond_rows, cond_cols, cond_vias, ground, via_offset)
    one = swapped(block, "gz", 0)
    two = swapped(block, "gz", 1)
    after, before, to_first, to_second = pl.pallas_call(
        functools.partial(corners_kernel, layers=layers),
        out_shape=(part, part) + (float_of(2 * count, planes, cols),) * 2,
        in_specs=[VMEM] * 2,
        out_specs=(VMEM,) * 4,
        compiler_params=PARAMS,
        name="corners",
    )(swapped(first, "gx", 0), swapped(second, "gx", 1))
    pieces = (block, after, before, one, two, swapped(to_first, "gz", 0), swapped(to_second, "gz", 1))
    edge, *outer = pl.pallas_call(
        functools.partial(sides_kernel, layers=layers, rows=rows, pair=pair),
        out_shape=(float_of(high, planes, cols),) + (float_of(high // 2, planes, cols),) * (1 if pair else 2),
        in_specs=[VMEM] * 7,
        out_specs=(VMEM,) * (2 if pair else 3),
        compiler_params=PARAMS,
        name="sides",
    )(*pieces)
    if pair:
        got = [lax.ppermute(outer[0], "gy", [(0, 1), (1, 0)])]
    else:
        got = [sent(outer[0], {"gy": 1}), sent(outer[1], {"gy": -1})]
    start = pl.pallas_call(
        functools.partial(assemble_kernel, layers=layers, rows=rows),
        out_shape=float_of(high, tall, planes, cols),
        in_specs=[VMEM] * 7,
        out_specs=VMEM,
        compiler_params=PARAMS,
        cost_estimate=pl.CostEstimate(flops=0, bytes_accessed=2 * high * tall * planes * cols, transcendentals=0),
        name="assemble",
    )(*pieces)
    order = depth * fields
    points = slabs
    basis, gram = pl.pallas_call(
        functools.partial(powers_kernel, fields=fields, layers=layers, rows=rows, pair=pair),
        out_shape=(float_of(points * order, cols), float_of(order, order)),
        in_specs=[VMEM] * (3 + len(got)),
        out_specs=(VMEM, VMEM),
        scratch_shapes=[
            pltpu.VMEM((depth - 1, high, tall, fields, cols), jnp.float32),
            pltpu.VMEM((7, high, tall, TILE, cols), jnp.float32),
            pltpu.VMEM((2, depth, high, planes, cols), jnp.float32),
            pltpu.VMEM((2, 7, high, TILE, cols), jnp.float32),
            pltpu.VMEM((depth, high, planes, cols), jnp.float32),
            pltpu.VMEM((order, order), jnp.float32),
        ],
        compiler_params=PARAMS,
        name="powers",
    )(start, edge, *got, shifts)
    points_in_all = points * cols
    plan = []
    for axis in ("gy", "gx", "gz"):
        points_in_all *= lax.axis_size(axis)
        plan += [(axis, partners) for partners in rounds(axis)]
    parts = [gram]
    for axis, partners in plan:
        parts = gathered(folded(parts), axis, partners)
    upper, basis_q = pl.pallas_call(
        functools.partial(finish_kernel, count=float(points_in_all), step=4),
        out_shape=(float_of(order, order), float_of(order * points, cols)),
        in_specs=[VMEM] * (len(parts) + 1),
        out_specs=(VMEM, VMEM),
        compiler_params=PARAMS,
        name="finish",
    )(*parts, basis)
    return basis_q.reshape(order, layers, rows, cols), upper


def solution(mesh):
    in_specs = (
        P(None, "gz", "gx", "gy"),
        P("gz", "gx", "gy"),
        P("gz", "gx", "gy"),
        P("gz", "gx", "gy"),
        P("gz", "gx", "gy"),
        P(),
    )
    out_specs = (P(None, "gz", "gx", "gy"), P())
    return jax.shard_map(local, mesh=mesh, in_specs=in_specs, out_specs=out_specs, check_vma=False)
```

```python
import functools

import jax
import jax.numpy as jnp
from jax import lax
from jax.experimental import pallas as pl
from jax.experimental.pallas import tpu as pltpu
from jax.sharding import PartitionSpec as P

POWERS = 4


newton_shifts = (15.4, 0.6, 11.7, 4.3)
basis_scale = 0.125

VMEM = pl.BlockSpec(memory_space=pltpu.VMEM)
SMEM = pl.BlockSpec(memory_space=pltpu.SMEM)
HBM = pl.BlockSpec(memory_space=pltpu.HBM)
PARAMS = pltpu.CompilerParams(vmem_limit_bytes=32 * 1024 * 1024)
FIRST = pltpu.CompilerParams(vmem_limit_bytes=60 * 1024 * 1024)

COEFS = 4
TILE = 8
CORNERS = ((1, 3), (1, 2), (1, 1), (2, 2), (2, 1), (3, 1))


def positions(shape):
    sub = lax.broadcasted_iota(jnp.int32, shape, 0)
    lane = lax.broadcasted_iota(jnp.int32, shape, 1)
    return sub, lane


def edges_kernel(
    load_ref, rows_ref, cols_ref, vias_ref, ground_ref, offset_ref,
    block_ref, first_ref, second_ref, shift_ref, fields_in, coefs_in, sems,
):
    slabs, planes, cols = block_ref.shape
    fields = load_ref.shape[0] // slabs
    layers, rows, _ = rows_ref.shape
    depth = POWERS
    half = rows // 2
    total_layers = offset_ref.shape[0]
    copies = [
        pltpu.make_async_copy(ref, coefs_in.at[i], sems.at[i])
        for i, ref in enumerate((rows_ref, cols_ref, vias_ref, ground_ref))
    ]
    copies.append(pltpu.make_async_copy(load_ref, fields_in, sems.at[COEFS]))
    for copy in copies:
        copy.start()
    gx, gy, gz = (lax.axis_index(name) for name in ("gx", "gy", "gz"))
    last_row = jnp.where(gx == lax.axis_size("gx") - 1, rows - 1, rows)
    last_col = jnp.where(gy == lax.axis_size("gy") - 1, cols - 1, cols)
    sub, lane = positions((TILE, cols))
    for e in range(shift_ref.shape[0]):
        layer = gz * layers + e - depth
        inside = (layer >= 0) & (layer < total_layers)
        value = jnp.where(inside, offset_ref[jnp.clip(layer, 0, total_layers - 1)], 0)
        shift_ref[e] = jnp.broadcast_to(value, (TILE, cols))
    for copy in copies:
        copy.wait()
    for l in range(layers):
        layer = gz * layers + l
        target = gy * cols + lane + shift_ref[depth + l]
        via_ok = (target >= 0) & (target < cols * lax.axis_size("gy"))
        via_ok = via_ok & (jnp.broadcast_to(layer, lane.shape) < total_layers - 1)
        four = (
            jnp.where(sub == last_row, 0.0, coefs_in[0, l]),
            jnp.where(lane == last_col, 0.0, coefs_in[1, l]),
            jnp.where(via_ok, coefs_in[2, l], 0.0),
            coefs_in[3, l],
        )
        for r in range(rows):
            slab = l * rows + r
            values = [fields_in[pl.ds(f * slabs + slab, TILE, stride=slabs), :] for f in range(0, fields, TILE)]
            value = jnp.zeros((TILE, cols), jnp.float32)
            for c in range(COEFS):
                value = jnp.where(sub == c, jnp.broadcast_to(four[c][r : r + 1, :], (TILE, cols)), value)
            for t, value in enumerate(values + [value]):
                here = slice(t * TILE, t * TILE + TILE)
                block_ref[slab, here, :] = value
    even = lax.rem(gx, 2) == 0
    starts = [jnp.where(even, half, 0), jnp.where(even, 0, half)]

    @pl.loop(0, half)
    def _(i):
        for l in range(layers):
            for f in range(0, planes, TILE):
                here = slice(f, f + TILE)
                for ref, start in zip((first_ref, second_ref), starts):
                    ref[l * half + i, here, :] = block_ref[l * rows + start + i, here, :]


def corners_kernel(first_ref, second_ref, after_ref, before_ref, one_ref, two_ref, *, layers):
    planes, cols = after_ref.shape[1:]
    half = after_ref.shape[0] // layers
    count = len(CORNERS)
    even_row = jnp.broadcast_to(lax.rem(lax.axis_index("gx"), 2), (TILE, cols)) == 0
    even_layer = jnp.broadcast_to(lax.rem(lax.axis_index("gz"), 2), (TILE, cols)) == 0

    @pl.loop(0, planes // TILE)
    def _(f):
        here = pl.ds(pl.multiple_of(f * TILE, TILE), TILE)
        after, before = [], []
        for i in range(layers * half):
            first, second = first_ref[i, here, :], second_ref[i, here, :]
            after.append(jnp.where(even_row, second, first))
            before.append(jnp.where(even_row, first, second))
            after_ref[i, here, :] = after[i]
            before_ref[i, here, :] = before[i]
        for i, (dz, dx) in enumerate(CORNERS):
            high, low = (layers - dz) * half, (dz - 1) * half
            for at, source, row in ((i, after, half - dx), (count + i, before, dx - 1)):
                up, down = source[high + row], source[low + row]
                one_ref[at, here, :] = jnp.where(even_layer, up, down)
                two_ref[at, here, :] = jnp.where(even_layer, down, up)


def slabs_of(e, layers, rows, block, after, before, one, two, corner_one, corner_two):
    depth, half, count = POWERS, rows // 2, len(CORNERS)
    cols = block.shape[2]

    def plain(ref, slab):
        return lambda here: ref[slab, here, :]

    def chosen(pair, slab):
        even = jnp.broadcast_to(lax.rem(lax.axis_index("gz"), 2), (TILE, cols)) == 0
        return lambda here: jnp.where(even, pair[0][slab, here, :], pair[1][slab, here, :])

    if depth <= e < depth + layers:
        l = e - depth
        found = [(depth + r, plain(block, l * rows + r)) for r in range(rows)]
        for i in range(half):
            found.append((i, plain(after, l * half + i)))
            found.append((depth + rows + i, plain(before, l * half + i)))
        return found
    if e < depth:
        home, corner, first, distance = (two, one), (corner_two, corner_one), 0, depth - e
    else:
        home, corner, first, distance = (one, two), (corner_one, corner_two), depth + layers, e - depth - layers + 1
    found = [(depth + r, chosen(home, (e - first) * rows + r)) for r in range(rows)]
    for i, (dz, dx) in enumerate(CORNERS):
        if dz == distance:
            found.append((depth - dx, chosen(corner, i)))
            found.append((depth + rows - 1 + dx, chosen(corner, count + i)))
    return found


def sides_kernel(*refs, layers, rows, pair):
    sources, edge_ref, out_refs = refs[:7], refs[7], refs[8:]
    high, planes, cols = edge_ref.shape
    depth = POWERS
    group = 2 * depth
    _, lane = positions((TILE, cols))
    early = lax.rem(lane, group) < depth
    gy = jnp.broadcast_to(lax.axis_index("gy"), (TILE, cols))

    @pl.loop(0, planes // TILE)
    def _(f):
        here = pl.ds(pl.multiple_of(f * TILE, TILE), TILE)
        edges = []
        for e in range(high):
            total = jnp.zeros((TILE, cols), jnp.float32)
            for row, read in slabs_of(e, layers, rows, *sources):
                moved = pltpu.roll(read(here), (group * row + depth) % cols, 1)
                total = jnp.where((lane >= group * row) & (lane < group * row + group), moved, total)
            edge_ref[e, here, :] = total
            edges.append(total)
        for t in range(high // 2):
            one, two = edges[2 * t], edges[2 * t + 1]
            up = jnp.where(early, one, pltpu.roll(two, depth, 1))
            down = jnp.where(early, pltpu.roll(one, cols - depth, 1), two)
            if pair:
                out_refs[0][t, here, :] = jnp.where(gy == 0, up, down)
            else:
                out_refs[0][t, here, :] = up
                out_refs[1][t, here, :] = down


def assemble_kernel(*refs, layers, rows):
    sources, start_ref = refs[:7], refs[7]
    high, _, planes, _ = start_ref.shape

    @pl.loop(0, planes // TILE)
    def _(f):
        here = pl.ds(pl.multiple_of(f * TILE, TILE), TILE)
        for e in range(high):
            for row, read in slabs_of(e, layers, rows, *sources):
                start_ref[e, row, here, :] = read(here)


def powers_kernel(*refs, fields, layers, rows, pair):
    gots = 1 if pair else 2
    start_ref, edge_ref, got_refs, shift_ref = refs[0], refs[1], refs[2 : 2 + gots], refs[2 + gots]
    basis_ref, gram_ref, power_ref, coef_ref, strip_ref, strip_coef_ref, border_ref, sum_ref = refs[3 + gots :]
    high, tall, planes, cols = start_ref.shape
    depth = POWERS
    group = 2 * depth
    order = depth * fields
    tiles = range(0, fields, TILE)
    _, lane = positions((TILE, cols))
    gy = lax.axis_index("gy")

    def masks(e):
        shift = shift_ref[e]
        return shift == 0, shift > 0

    def from_above(seen, mask):
        left, centre, right = seen
        return jnp.where(mask[0], centre, jnp.where(mask[1], right, left))

    def from_below(seen, mask):
        left, centre, right = seen
        return jnp.where(mask[0], centre, jnp.where(mask[1], left, right))

    def around(tile):
        return pltpu.roll(tile, 1, 1), tile, pltpu.roll(tile, cols - 1, 1)

    def spread(tile, c):
        return jnp.broadcast_to(tile[c : c + 1, :], (TILE, cols))

    def put_factors(put, tile, row_above, seen, seen_below, mask):
        down, right, upper, ground = (spread(tile, c) for c in range(COEFS))
        up = spread(row_above, 0)
        left = spread(seen[0], 1)
        lower = from_below([spread(x, 2) for x in seen_below], mask)
        diagonal = ground + down + up + right + left + upper + lower
        for i, value in enumerate((down, up, right, left, upper, lower, diagonal)):
            put(i, value * basis_scale)

    def step(factors, theta, seen, up, down, above, below):
        value = (factors[6] - theta) * seen[1]
        value = value - (factors[0] * down + factors[1] * up)
        value = value - (factors[2] * seen[2] + factors[3] * seen[0])
        return value - (factors[4] * above + factors[5] * below)

    thetas = [shift * basis_scale for shift in newton_shifts]

    early = lax.rem(lane, group) < depth
    if pair:
        first_side = jnp.where(gy == 0, 1, 0)
        last_side = first_side + 1
    else:
        first_side, last_side = 0, 2

    @pl.loop(first_side, last_side)
    def _(side):
        left_side = jnp.broadcast_to(side, (TILE, cols)) == 0
        from_edge = early != left_side
        for e in range(high):
            for f in range(0, planes, TILE):
                here = slice(f, f + TILE)
                outer = got_refs[0][e // 2, here, :]
                if not pair:
                    outer = jnp.where(left_side, outer, got_refs[1][e // 2, here, :])
                if e % 2 == 0:
                    outer = jnp.where(left_side, outer, pltpu.roll(outer, depth, 1))
                else:
                    outer = jnp.where(left_side, pltpu.roll(outer, cols - depth, 1), outer)
                strip_ref[side, 0, e, here, :] = jnp.where(from_edge, edge_ref[e, here, :], outer)
        raw = [strip_ref[side, 0, e, fields : fields + TILE, :] for e in range(high)]
        seen = [around(tile) for tile in raw]
        for e in range(1, high - 1):

            def put(i, value, e=e):
                strip_coef_ref[side, i, e] = value

            put_factors(put, raw[e], pltpu.roll(raw[e], group, 1), seen[e], seen[e - 1], masks(e - 1))
        for k in range(1, depth):
            reach = depth - k
            looks = {}

            def look(e, f, k=k, looks=looks):
                if (e, f) not in looks:
                    looks[e, f] = around(strip_ref[side, k - 1, e, f : f + TILE, :])
                return looks[e, f]

            for e in range(depth - reach, depth + layers + reach):
                factors = [strip_coef_ref[side, i, e] for i in range(7)]
                over, under = masks(e), masks(e - 1)
                for f in tiles:
                    here = look(e, f)
                    strip_ref[side, k, e, f : f + TILE, :] = step(
                        factors,
                        thetas[k - 1],
                        here,
                        pltpu.roll(here[1], group, 1),
                        pltpu.roll(here[1], cols - group, 1),
                        from_above(look(e + 1, f), over),
                        from_below(look(e - 1, f), under),
                    )

    gy_lane = jnp.broadcast_to(gy, (TILE, cols))
    on_left = (lax.rem(lane, group) == depth - 1) & (gy_lane > 0)
    on_right = (lax.rem(lane, group) == depth - 2) & (gy_lane < lax.axis_size("gy") - 1)

    @pl.loop(0, high)
    def _(e):
        for k in range(depth):
            for f in range(0, planes if k == 0 else fields, TILE):
                here = slice(f, f + TILE)
                right = jnp.where(on_right, pltpu.roll(strip_ref[1, k, e, here, :], cols - 2, 1), 0.0)
                border_ref[k, e, here, :] = jnp.where(on_left, strip_ref[0, k, e, here, :], right)

    leftmost, rightmost = lane == 0, lane == cols - 1

    def looked(k, e, row, f):
        here = slice(f, f + TILE)
        tile = start_ref[e, row, here, :] if k == 0 else power_ref[k - 1, e, row, here, :]
        turn = (2 * cols - group * row - depth + 1) % cols if isinstance(row, int) else lax.rem(2 * cols - group * row - depth + 1, cols)
        outer = pltpu.roll(border_ref[k, e, here, :], turn, 1)
        left, _, right = around(tile)
        return jnp.where(leftmost, outer, left), tile, jnp.where(rightmost, outer, right)

    def by_rows(reach, body):
        @pl.loop(0, rows, unroll=2)
        def _(r):
            body(depth + r, depth - reach, depth + layers + reach)

        for dx in range(1, reach + 1):
            for row in (depth - dx, depth + rows - 1 + dx):
                body(row, depth - reach + dx, depth + layers + reach - dx)

    def factors_of_row(row, first, last):
        seen = {e: looked(0, e, row, fields) for e in range(first - 1, last)}
        for e in range(first, last):

            def put(i, value, e=e):
                coef_ref[i, e, row] = value

            above_row = start_ref[e, row - 1, fields : fields + TILE, :]
            put_factors(put, seen[e][1], above_row, seen[e], seen[e - 1], masks(e - 1))

    by_rows(depth - 1, factors_of_row)

    for k in range(1, depth + 1):

        def advance(row, first, last, k=k):
            source = start_ref if k == 1 else power_ref.at[k - 2]
            below = {f: from_below(looked(k - 1, first - 1, row, f), masks(first - 1)) for f in tiles}
            centre = {f: looked(k - 1, first, row, f) for f in tiles}
            for e in range(first, last):
                factors = [coef_ref[i, e, row] for i in range(7)]
                mask = masks(e)
                for f in tiles:
                    here = slice(f, f + TILE)
                    upper = looked(k - 1, e + 1, row, f)
                    value = step(
                        factors,
                        thetas[k - 1],
                        centre[f],
                        source[e, row - 1, here, :],
                        source[e, row + 1, here, :],
                        from_above(upper, mask),
                        below[f],
                    )
                    below[f], centre[f] = from_below(centre[f], mask), upper
                    if k < depth:
                        power_ref[k - 1, e, row, here, :] = value
                    if first == k and depth <= e < depth + layers:
                        slab = (e - depth) * rows + row - depth
                        place = pl.multiple_of(slab * order + (k - 1) * fields + f, TILE)
                        basis_ref[pl.ds(place, TILE), :] = value

        if k < depth:
            by_rows(depth - k, advance)

    def share(r):
        value = None
        for l in range(0, layers, 2):
            places = [pl.multiple_of(((l + i) * rows + r) * order, TILE) for i in range(2)]
            wide = jnp.concatenate([basis_ref[pl.ds(place, order), :] for place in places], axis=1)
            product = lax.dot_general(
                wide, wide, (((1,), (1,)), ((), ())),
                precision=lax.Precision.HIGHEST, preferred_element_type=jnp.float32,
            )
            value = product if value is None else value + product
        return value

    advance(depth, depth, depth + layers)
    sum_ref[...] = jnp.zeros_like(sum_ref)

    @pl.loop(1, rows)
    def _(r):
        product = share(r - 1)
        advance(depth + r, depth, depth + layers)
        sum_ref[...] += product

    total = sum_ref[...] + share(rows - 1)
    gram_ref[...] = total


def eliminate(tiles, order, step):
    width = tiles[0].shape[1]
    lane = lax.broadcasted_iota(jnp.int32, (8, width), 1)
    sub = lax.broadcasted_iota(jnp.int32, (8, width), 0)
    spread = lambda value: jnp.broadcast_to(value, (8, width))
    for first in range(0, order, step):
        home, base = first // 8, first % 8
        panel = tiles[home]
        entry = {}
        for i in range(step):
            for j in range(i, step):
                entry[i, j] = spread(panel[base + i : base + i + 1, first + j : first + j + 1])
        rows = [spread(panel[base + i : base + i + 1, :]) for i in range(step)]
        inverse = []
        done = []
        for i in range(step):
            row = rows[i]
            if i:
                row = jnp.where((lane >= first) & (lane < first + i), 0.0, row)
            factors = []
            for j in range(i):
                factor = entry[j, i] * inverse[j]
                factors.append(factor)
            for j in range(i):
                source = jnp.where(lane == first + j, 1.0, done[j])
                if i - j > 1:
                    source = jnp.where((lane > first + j) & (lane < first + i), 0.0, source)
                row = row - factors[j] * source
                for m in range(i, step):
                    entry[i, m] = entry[i, m] - factors[j] * entry[j, m]
            inverse.append(1.0 / entry[i, i])
            done.append(row)
        sources = []
        for j in range(step):
            source = jnp.where(lane == first + j, 1.0, done[j])
            if j < step - 1:
                source = jnp.where((lane > first + j) & (lane < first + step), 0.0, source)
            sources.append(source)
        inside = (lane >= first) & (lane < first + step)
        for t in range(home, order // 8):
            if t == home and base + step == 8:
                fresh = tiles[t]
            else:
                columns = [spread(tiles[t][:, first + j : first + j + 1]) for j in range(step)]
                fresh = jnp.where(inside, 0.0, tiles[t])
                for j in range(step):
                    factor = columns[j] * inverse[j]
                    fresh = fresh - factor * sources[j]
                    for m in range(j + 1, step):
                        columns[m] = columns[m] - factor * entry[j, m]
            if t == home:
                fresh = jnp.where(sub < base + step, tiles[t], fresh)
                for j in range(step):
                    fresh = jnp.where(sub == base + j, done[j], fresh)
            tiles[t] = fresh
    return tiles


def finish_kernel(*refs, count, step):
    part_refs, (basis_ref, upper_ref, out_ref, staged, sems) = refs[:-5], refs[-5:]
    order = upper_ref.shape[0]
    points = basis_ref.shape[0] // order
    tiles = []
    for t in range(order // 8):
        pieces = [ref[8 * t : 8 * t + 8, :] for ref in part_refs]
        tiles.append(folded(pieces) / count)
    tiles = eliminate(tiles, order, step)
    lane = lax.broadcasted_iota(jnp.int32, (8, order), 1)
    sub = lax.broadcasted_iota(jnp.int32, (8, order), 0)
    inverse = []
    for t in range(order // 8):
        row = sub + 8 * t
        pivot = jnp.sum(jnp.where(lane == row, tiles[t], 0.0), axis=1, keepdims=True)
        scale = 1.0 / jnp.sqrt(pivot)
        upper_ref[8 * t : 8 * t + 8, :] = jnp.where(lane >= row, tiles[t] * scale, 0.0)
        inverse.append(jnp.where(lane < row, tiles[t], jnp.where(lane == row, 1.0, 0.0)) * scale)
    inverse = jnp.concatenate(inverse, axis=0)
    cols = basis_ref.shape[1]
    inverse_parts = two_parts(inverse)
    chunk = points // sems.shape[0]
    copies = []
    for i in range(0, points, 2):
        start = i * order
        wide = jnp.concatenate(
            [basis_ref[start : start + order, :], basis_ref[start + order : start + 2 * order, :]], axis=1
        )
        out = product(inverse_parts, two_parts(wide))
        staged[pl.ds(i, order, stride=points), :] = out[:, :cols]
        staged[pl.ds(i + 1, order, stride=points), :] = out[:, cols:]
        if (i + 2) % chunk == 0:
            part = pl.ds(i + 2 - chunk, chunk)
            source = staged.reshape(order, points, cols).at[:, part, :]
            copies.append(pltpu.make_async_copy(source, out_ref.at[:, part, :], sems.at[i // chunk]))
            copies[-1].start()
    for copy in copies:
        copy.wait()


def two_parts(value):
    high = value.astype(jnp.bfloat16)
    return high, (value - high.astype(jnp.float32)).astype(jnp.bfloat16)


def product(left, right):
    dot = functools.partial(jnp.dot, preferred_element_type=jnp.float32)
    return dot(left[0], right[0]) + (dot(left[0], right[1]) + dot(left[1], right[0]))


def folded(pieces):
    while len(pieces) > 1:
        pieces = [pieces[i] + pieces[i + 1] for i in range(0, len(pieces), 2)]
    return pieces[0]


def rounds(axis):
    size, unit, out = lax.axis_size(axis), 1, []
    while unit < size:
        many = 4 if unit * 4 <= size else 2
        out.append([unit * m for m in range(1, many)])
        unit *= many
    return out


def gathered(value, axis, partners):
    size = lax.axis_size(axis)
    return [value] + [lax.ppermute(value, axis, [(i, i ^ m) for i in range(size)]) for m in partners]


def swapped(value, axis, phase):
    pairs = []
    for i in range(phase, lax.axis_size(axis) - 1, 2):
        pairs += [(i, i + 1), (i + 1, i)]
    return lax.ppermute(value, axis, pairs)


def sent(value, steps):
    axes = tuple(steps)
    sizes = [lax.axis_size(name) for name in axes]
    pairs = []
    if len(axes) == 1:
        pairs = [(i, i + steps[axes[0]]) for i in range(sizes[0]) if 0 <= i + steps[axes[0]] < sizes[0]]
        return lax.ppermute(value, axes[0], pairs)
    for i in range(sizes[0]):
        for j in range(sizes[1]):
            m, n = i + steps[axes[0]], j + steps[axes[1]]
            if 0 <= m < sizes[0] and 0 <= n < sizes[1]:
                pairs.append((i * sizes[1] + j, m * sizes[1] + n))
    return lax.ppermute(value, axes, pairs)


def local(load_currents, cond_rows, cond_cols, cond_vias, ground, via_offset):
    fields, layers, rows, cols = load_currents.shape
    depth = POWERS
    assert layers == depth and rows == 2 * depth and cols == 4 * depth * rows and fields % TILE == 0
    float_of = lambda *shape: jax.ShapeDtypeStruct(shape, jnp.float32)
    pair = lax.axis_size("gy") == 2
    planes = fields + TILE
    slabs = layers * rows
    high = layers + 2 * depth
    tall = rows + 2 * depth
    count = len(CORNERS)
    whole, part = float_of(slabs, planes, cols), float_of(slabs // 2, planes, cols)
    block, first, second, shifts = pl.pallas_call(
        edges_kernel,
        out_shape=(whole, part, part, jax.ShapeDtypeStruct((high, TILE, cols), jnp.int32)),
        in_specs=[HBM] * 5 + [SMEM],
        out_specs=(VMEM,) * 4,
        scratch_shapes=[
            pltpu.VMEM((fields * slabs, cols), jnp.float32),
            pltpu.VMEM((COEFS, layers, rows, cols), jnp.float32),
            pltpu.SemaphoreType.DMA((COEFS + 1,)),
        ],
        compiler_params=FIRST,
        name="edges",
    )(load_currents.reshape(fields * slabs, cols), cond_rows, cond_cols, cond_vias, ground, via_offset)
    one = swapped(block, "gz", 0)
    two = swapped(block, "gz", 1)
    after, before, to_first, to_second = pl.pallas_call(
        functools.partial(corners_kernel, layers=layers),
        out_shape=(part, part) + (float_of(2 * count, planes, cols),) * 2,
        in_specs=[VMEM] * 2,
        out_specs=(VMEM,) * 4,
        compiler_params=PARAMS,
        name="corners",
    )(swapped(first, "gx", 0), swapped(second, "gx", 1))
    pieces = (block, after, before, one, two, swapped(to_first, "gz", 0), swapped(to_second, "gz", 1))
    edge, *outer = pl.pallas_call(
        functools.partial(sides_kernel, layers=layers, rows=rows, pair=pair),
        out_shape=(float_of(high, planes, cols),) + (float_of(high // 2, planes, cols),) * (1 if pair else 2),
        in_specs=[VMEM] * 7,
        out_specs=(VMEM,) * (2 if pair else 3),
        compiler_params=PARAMS,
        name="sides",
    )(*pieces)
    if pair:
        got = [lax.ppermute(outer[0], "gy", [(0, 1), (1, 0)])]
    else:
        got = [sent(outer[0], {"gy": 1}), sent(outer[1], {"gy": -1})]
    start = pl.pallas_call(
        functools.partial(assemble_kernel, layers=layers, rows=rows),
        out_shape=float_of(high, tall, planes, cols),
        in_specs=[VMEM] * 7,
        out_specs=VMEM,
        compiler_params=PARAMS,
        cost_estimate=pl.CostEstimate(flops=0, bytes_accessed=2 * high * tall * planes * cols, transcendentals=0),
        name="assemble",
    )(*pieces)
    order = depth * fields
    points = slabs
    basis, gram = pl.pallas_call(
        functools.partial(powers_kernel, fields=fields, layers=layers, rows=rows, pair=pair),
        out_shape=(float_of(points * order, cols), float_of(order, order)),
        in_specs=[VMEM] * (3 + len(got)),
        out_specs=(VMEM, VMEM),
        scratch_shapes=[
            pltpu.VMEM((depth - 1, high, tall, fields, cols), jnp.float32),
            pltpu.VMEM((7, high, tall, TILE, cols), jnp.float32),
            pltpu.VMEM((2, depth, high, planes, cols), jnp.float32),
            pltpu.VMEM((2, 7, high, TILE, cols), jnp.float32),
            pltpu.VMEM((depth, high, planes, cols), jnp.float32),
            pltpu.VMEM((order, order), jnp.float32),
        ],
        compiler_params=PARAMS,
        name="powers",
    )(start, edge, *got, shifts)
    points_in_all = points * cols
    plan = []
    for axis in ("gy", "gx", "gz"):
        points_in_all *= lax.axis_size(axis)
        plan += [(axis, partners) for partners in rounds(axis)]
    parts = [gram]
    for axis, partners in plan:
        parts = gathered(folded(parts), axis, partners)
    upper, basis_q = pl.pallas_call(
        functools.partial(finish_kernel, count=float(points_in_all), step=8),
        out_shape=(float_of(order, order), float_of(order, points, cols)),
        in_specs=[VMEM] * (len(parts) + 1),
        out_specs=(VMEM, HBM),
        scratch_shapes=[pltpu.VMEM((order * points, cols), jnp.float32), pltpu.SemaphoreType.DMA((layers,))],
        compiler_params=PARAMS,
        name="finish",
    )(*parts, basis)
    return basis_q.reshape(order, layers, rows, cols), upper


def solution(mesh):
    in_specs = (
        P(None, "gz", "gx", "gy"),
        P("gz", "gx", "gy"),
        P("gz", "gx", "gy"),
        P("gz", "gx", "gy"),
        P("gz", "gx", "gy"),
        P(),
    )
    out_specs = (P(None, "gz", "gx", "gy"), P())
    return jax.shard_map(local, mesh=mesh, in_specs=in_specs, out_specs=out_specs, check_vma=False)
```

```python
import functools

import jax
import jax.numpy as jnp
from jax import lax
from jax.experimental import pallas as pl
from jax.experimental.pallas import tpu as pltpu
from jax.sharding import PartitionSpec as P

POWERS = 4


newton_shifts = (15.4, 0.6, 11.7, 4.3)
basis_scale = 0.125

VMEM = pl.BlockSpec(memory_space=pltpu.VMEM)
SMEM = pl.BlockSpec(memory_space=pltpu.SMEM)
HBM = pl.BlockSpec(memory_space=pltpu.HBM)
PARAMS = pltpu.CompilerParams(vmem_limit_bytes=32 * 1024 * 1024)
FIRST = pltpu.CompilerParams(vmem_limit_bytes=60 * 1024 * 1024)

COEFS = 4
TILE = 8
CORNERS = ((1, 3), (1, 2), (1, 1), (2, 2), (2, 1), (3, 1))


def positions(shape):
    sub = lax.broadcasted_iota(jnp.int32, shape, 0)
    lane = lax.broadcasted_iota(jnp.int32, shape, 1)
    return sub, lane


def coefs_at(ref, start, i):
    place = start + COEFS * (i // 2) * 2
    tile = ref[place : place + TILE, :]
    return pltpu.roll(tile, COEFS, 0) if i % 2 else tile


def edges_kernel(
    load_ref, rows_ref, cols_ref, vias_ref, ground_ref, offset_ref,
    first_ref, second_ref, tile_ref, flat_ref, shift_ref, fields_in, coefs_in, sems,
):
    slabs, _, cols = tile_ref.shape
    fields = load_ref.shape[0] // slabs
    layers, rows, _ = rows_ref.shape
    depth = POWERS
    half = rows // 2
    total_layers = offset_ref.shape[0]
    copies = [
        pltpu.make_async_copy(ref, coefs_in.at[i], sems.at[i])
        for i, ref in enumerate((rows_ref, cols_ref, vias_ref, ground_ref))
    ]
    copies.append(pltpu.make_async_copy(load_ref, fields_in, sems.at[COEFS]))
    for copy in copies:
        copy.start()
    gx, gy, gz = (lax.axis_index(name) for name in ("gx", "gy", "gz"))
    last_row = jnp.where(gx == lax.axis_size("gx") - 1, rows - 1, rows)
    last_col = jnp.where(gy == lax.axis_size("gy") - 1, cols - 1, cols)
    sub, lane = positions((TILE, cols))
    for e in range(shift_ref.shape[0]):
        layer = gz * layers + e - depth
        inside = (layer >= 0) & (layer < total_layers)
        value = jnp.where(inside, offset_ref[jnp.clip(layer, 0, total_layers - 1)], 0)
        shift_ref[e] = jnp.broadcast_to(value, (TILE, cols))
    for copy in copies:
        copy.wait()

    def joined(one, two):
        return jnp.where(sub < COEFS, one, pltpu.roll(two, COEFS, 0))

    for l in range(layers):
        layer = gz * layers + l
        target = gy * cols + lane + shift_ref[depth + l]
        via_ok = (target >= 0) & (target < cols * lax.axis_size("gy"))
        via_ok = via_ok & (jnp.broadcast_to(layer, lane.shape) < total_layers - 1)
        four = (
            jnp.where(sub == last_row, 0.0, coefs_in[0, l]),
            jnp.where(lane == last_col, 0.0, coefs_in[1, l]),
            jnp.where(via_ok, coefs_in[2, l], 0.0),
            coefs_in[3, l],
        )
        for r in range(rows):
            slab = l * rows + r
            value = jnp.zeros((TILE, cols), jnp.float32)
            for c in range(COEFS):
                value = jnp.where(sub == c, jnp.broadcast_to(four[c][r : r + 1, :], (TILE, cols)), value)
            tile_ref[slab] = value
    for i in range(0, slabs, 2):
        flat_ref[COEFS * i : COEFS * i + TILE, :] = joined(tile_ref[i], tile_ref[i + 1])
    even = lax.rem(gx, 2) == 0
    for ref, start in ((first_ref, jnp.where(even, half, 0)), (second_ref, jnp.where(even, 0, half))):
        for l in range(layers):
            for i in range(half):
                slab = l * rows + start + i
                at = l * half + i
                for f in range(0, fields, TILE):
                    tile = fields_in[pl.ds(f * slabs + slab, TILE, stride=slabs), :]
                    ref[at * fields + f : at * fields + f + TILE, :] = tile
                if i % 2 == 0:
                    place = layers * half * fields + COEFS * at
                    ref[place : place + TILE, :] = joined(tile_ref[slab], tile_ref[slab + 1])


def own_kernel(load_ref, tile_ref, block_ref):
    slabs, planes, _ = block_ref.shape
    for slab in range(slabs):
        for f in range(0, planes - TILE, TILE):
            block_ref[slab, f : f + TILE, :] = load_ref[pl.ds(f * slabs + slab, TILE, stride=slabs), :]
        block_ref[slab, planes - TILE :, :] = tile_ref[slab]


def corners_kernel(first_ref, second_ref, flat_ref, after_ref, before_ref, one_ref, two_ref, *, layers):
    slabs, planes, cols = after_ref.shape
    fields = planes - TILE
    half = slabs // layers
    count = len(CORNERS)
    sub, _ = positions((TILE, cols))
    even_row = jnp.broadcast_to(lax.rem(lax.axis_index("gx"), 2), (TILE, cols)) == 0
    even_layer = jnp.broadcast_to(lax.rem(lax.axis_index("gz"), 2), (TILE, cols)) == 0
    for f in range(0, planes, TILE):
        after, before = [], []
        for i in range(slabs):
            if f < fields:
                first, second = (ref[i * fields + f : i * fields + f + TILE, :] for ref in (first_ref, second_ref))
            else:
                first, second = (coefs_at(ref, slabs * fields, i) for ref in (first_ref, second_ref))
            after.append(jnp.where(even_row, second, first))
            before.append(jnp.where(even_row, first, second))
            after_ref[i, f : f + TILE, :] = after[i]
            before_ref[i, f : f + TILE, :] = before[i]
        ones, twos = [], []
        for source, step in ((after, -1), (before, 1)):
            for dz, dx in CORNERS:
                row = half - dx if step < 0 else dx - 1
                up, down = source[(layers - dz) * half + row], source[(dz - 1) * half + row]
                ones.append(jnp.where(even_layer, up, down))
                twos.append(jnp.where(even_layer, down, up))
        for ref, values in ((one_ref, ones), (two_ref, twos)):
            if f < fields:
                for i, value in enumerate(values):
                    ref[i * fields + f : i * fields + f + TILE, :] = value
            else:
                for i in range(0, 2 * count, 2):
                    place = 2 * count * fields + COEFS * i
                    pair = jnp.where(sub < COEFS, values[i], pltpu.roll(values[i + 1], COEFS, 0))
                    ref[place : place + TILE, :] = pair
    for ref in (one_ref, two_ref):
        place = 2 * count * planes - 2 * count * (TILE - COEFS)
        ref[place : place + flat_ref.shape[0], :] = flat_ref[...]


def slabs_of(e, layers, rows, planes, corners, inner, block, after, before, one, two, corner_one=None, corner_two=None):
    depth, half, count = POWERS, rows // 2, len(CORNERS)
    cols = block.shape[2] if block is not None else corner_one.shape[1]
    fields, slabs = planes - TILE, layers * rows

    def plain(ref, slab):
        return lambda f: ref[slab, f : f + TILE, :]

    def chosen(read, one, two):
        even = jnp.broadcast_to(lax.rem(lax.axis_index("gz"), 2), (TILE, cols)) == 0
        return lambda f: jnp.where(even, read(one, f), read(two, f))

    def home(slab):
        return lambda ref, f: ref[pl.ds(f * slabs + slab, TILE, stride=slabs), :]

    def home_coefs(slab):
        return lambda ref, f: coefs_at(ref, 2 * count * (fields + COEFS), slab)

    def corner(i):
        def read(ref, f):
            if f < fields:
                return ref[i * fields + f : i * fields + f + TILE, :]
            return coefs_at(ref, 2 * count * fields, i)

        return read

    tiles = [f for f in range(0, planes, TILE)]
    found = []
    if depth <= e < depth + layers:
        l = e - depth
        if inner:
            found += [(depth + r, plain(block, l * rows + r), tiles) for r in range(rows)]
            for i in range(half):
                found.append((i, plain(after, l * half + i), tiles))
                found.append((depth + rows + i, plain(before, l * half + i), tiles))
        return found
    if e < depth:
        pair, corner_pair, first, distance = (two, one), (corner_two, corner_one), 0, depth - e
    else:
        pair, corner_pair = (one, two), (corner_one, corner_two)
        first, distance = depth + layers, e - depth - layers + 1
    for r in range(rows):
        slab = (e - first) * rows + r
        if inner:
            found.append((depth + r, chosen(home(slab), *pair), tiles[:-1]))
        if corners:
            found.append((depth + r, chosen(home_coefs(slab), *corner_pair), tiles[-1:]))
    for i, (dz, dx) in enumerate(CORNERS):
        if dz == distance and corners:
            found.append((depth - dx, chosen(corner(i), *corner_pair), tiles))
            found.append((depth + rows - 1 + dx, chosen(corner(count + i), *corner_pair), tiles))
    return found


def inner_kernel(*refs, layers, rows):
    sources, edge_ref = refs[:5], refs[5]
    high, planes, cols = edge_ref.shape
    depth = POWERS
    group = 2 * depth
    _, lane = positions((TILE, cols))
    for e in range(high):
        found = slabs_of(e, layers, rows, planes, False, True, *sources)
        for f in range(0, planes, TILE):
            total = jnp.zeros((TILE, cols), jnp.float32)
            for row, read, tiles in found:
                if f in tiles:
                    moved = pltpu.roll(read(f), (group * row + depth) % cols, 1)
                    total = jnp.where((lane >= group * row) & (lane < group * row + group), moved, total)
            edge_ref[e, f : f + TILE, :] = total


def sides_kernel(inner_ref, one_ref, two_ref, edge_ref, *out_refs, layers, rows, pair):
    high, planes, cols = edge_ref.shape
    depth = POWERS
    group = 2 * depth
    _, lane = positions((TILE, cols))
    early = lax.rem(lane, group) < depth
    gy = jnp.broadcast_to(lax.axis_index("gy"), (TILE, cols))
    for f in range(0, planes, TILE):
        here = slice(f, f + TILE)
        edges = []
        for e in range(high):
            total = inner_ref[e, here, :]
            for row, read, tiles in slabs_of(e, layers, rows, planes, True, False, None, None, None, None, None, one_ref, two_ref):
                if f in tiles:
                    moved = pltpu.roll(read(f), (group * row + depth) % cols, 1)
                    total = jnp.where((lane >= group * row) & (lane < group * row + group), moved, total)
            edge_ref[e, here, :] = total
            edges.append(total)
        for t in range(high // 2):
            one, two = edges[2 * t], edges[2 * t + 1]
            up = jnp.where(early, one, pltpu.roll(two, depth, 1))
            down = jnp.where(early, pltpu.roll(one, cols - depth, 1), two)
            if pair:
                out_refs[0][t, here, :] = jnp.where(gy == 0, up, down)
            else:
                out_refs[0][t, here, :] = up
                out_refs[1][t, here, :] = down


def assemble_kernel(*refs, layers, rows):
    sources, start_ref = refs[:7], refs[7]
    high, _, planes, _ = start_ref.shape
    for e in range(high):
        for row, read, tiles in slabs_of(e, layers, rows, planes, True, True, *sources):
            for f in tiles:
                start_ref[e, row, f : f + TILE, :] = read(f)


def powers_kernel(*refs, fields, layers, rows, pair):
    gots = 1 if pair else 2
    start_ref, edge_ref, got_refs, shift_ref = refs[0], refs[1], refs[2 : 2 + gots], refs[2 + gots]
    basis_ref, gram_ref, power_ref, coef_ref, strip_ref, strip_coef_ref, border_ref, sum_ref = refs[3 + gots :]
    high, tall, planes, cols = start_ref.shape
    depth = POWERS
    group = 2 * depth
    order = depth * fields
    tiles = range(0, fields, TILE)
    _, lane = positions((TILE, cols))
    gy = lax.axis_index("gy")

    def masks(e):
        shift = shift_ref[e]
        return shift == 0, shift > 0

    def from_above(seen, mask):
        left, centre, right = seen
        return jnp.where(mask[0], centre, jnp.where(mask[1], right, left))

    def from_below(seen, mask):
        left, centre, right = seen
        return jnp.where(mask[0], centre, jnp.where(mask[1], left, right))

    def around(tile):
        return pltpu.roll(tile, 1, 1), tile, pltpu.roll(tile, cols - 1, 1)

    def spread(tile, c):
        return jnp.broadcast_to(tile[c : c + 1, :], (TILE, cols))

    def put_factors(put, tile, row_above, seen, seen_below, mask):
        down, right, upper, ground = (spread(tile, c) for c in range(COEFS))
        up = spread(row_above, 0)
        left = spread(seen[0], 1)
        lower = from_below([spread(x, 2) for x in seen_below], mask)
        diagonal = ground + down + up + right + left + upper + lower
        for i, value in enumerate((down, up, right, left, upper, lower, diagonal)):
            put(i, value * basis_scale)

    def step(factors, theta, seen, up, down, above, below):
        value = (factors[6] - theta) * seen[1]
        value = value - (factors[0] * down + factors[1] * up)
        value = value - (factors[2] * seen[2] + factors[3] * seen[0])
        return value - (factors[4] * above + factors[5] * below)

    thetas = [shift * basis_scale for shift in newton_shifts]

    early = lax.rem(lane, group) < depth
    if pair:
        first_side = jnp.where(gy == 0, 1, 0)
        last_side = first_side + 1
    else:
        first_side, last_side = 0, 2

    @pl.loop(first_side, last_side)
    def _(side):
        left_side = jnp.broadcast_to(side, (TILE, cols)) == 0
        from_edge = early != left_side
        for e in range(high):
            for f in range(0, planes, TILE):
                here = slice(f, f + TILE)
                outer = got_refs[0][e // 2, here, :]
                if not pair:
                    outer = jnp.where(left_side, outer, got_refs[1][e // 2, here, :])
                if e % 2 == 0:
                    outer = jnp.where(left_side, outer, pltpu.roll(outer, depth, 1))
                else:
                    outer = jnp.where(left_side, pltpu.roll(outer, cols - depth, 1), outer)
                strip_ref[side, 0, e, here, :] = jnp.where(from_edge, edge_ref[e, here, :], outer)
        raw = [strip_ref[side, 0, e, fields : fields + TILE, :] for e in range(high)]
        seen = [around(tile) for tile in raw]
        for e in range(1, high - 1):

            def put(i, value, e=e):
                strip_coef_ref[side, i, e] = value

            put_factors(put, raw[e], pltpu.roll(raw[e], group, 1), seen[e], seen[e - 1], masks(e - 1))
        for k in range(1, depth):
            reach = depth - k
            looks = {}

            def look(e, f, k=k, looks=looks):
                if (e, f) not in looks:
                    looks[e, f] = around(strip_ref[side, k - 1, e, f : f + TILE, :])
                return looks[e, f]

            for e in range(depth - reach, depth + layers + reach):
                factors = [strip_coef_ref[side, i, e] for i in range(7)]
                over, under = masks(e), masks(e - 1)
                for f in tiles:
                    here = look(e, f)
                    strip_ref[side, k, e, f : f + TILE, :] = step(
                        factors,
                        thetas[k - 1],
                        here,
                        pltpu.roll(here[1], group, 1),
                        pltpu.roll(here[1], cols - group, 1),
                        from_above(look(e + 1, f), over),
                        from_below(look(e - 1, f), under),
                    )

    gy_lane = jnp.broadcast_to(gy, (TILE, cols))
    on_left = (lax.rem(lane, group) == depth - 1) & (gy_lane > 0)
    on_right = (lax.rem(lane, group) == depth - 2) & (gy_lane < lax.axis_size("gy") - 1)

    @pl.loop(0, high)
    def _(e):
        for k in range(depth):
            for f in range(0, planes if k == 0 else fields, TILE):
                here = slice(f, f + TILE)
                right = jnp.where(on_right, pltpu.roll(strip_ref[1, k, e, here, :], cols - 2, 1), 0.0)
                border_ref[k, e, here, :] = jnp.where(on_left, strip_ref[0, k, e, here, :], right)

    leftmost, rightmost = lane == 0, lane == cols - 1

    def looked(k, e, row, f):
        here = slice(f, f + TILE)
        tile = start_ref[e, row, here, :] if k == 0 else power_ref[k - 1, e, row, here, :]
        turn = (2 * cols - group * row - depth + 1) % cols if isinstance(row, int) else lax.rem(2 * cols - group * row - depth + 1, cols)
        outer = pltpu.roll(border_ref[k, e, here, :], turn, 1)
        left, _, right = around(tile)
        return jnp.where(leftmost, outer, left), tile, jnp.where(rightmost, outer, right)

    def by_rows(reach, body):
        @pl.loop(0, rows, unroll=2)
        def _(r):
            body(depth + r, depth - reach, depth + layers + reach)

        for dx in range(1, reach + 1):
            for row in (depth - dx, depth + rows - 1 + dx):
                body(row, depth - reach + dx, depth + layers + reach - dx)

    def factors_of_row(row, first, last):
        seen = {e: looked(0, e, row, fields) for e in range(first - 1, last)}
        for e in range(first, last):

            def put(i, value, e=e):
                coef_ref[i, e, row] = value

            above_row = start_ref[e, row - 1, fields : fields + TILE, :]
            put_factors(put, seen[e][1], above_row, seen[e], seen[e - 1], masks(e - 1))

    by_rows(depth - 1, factors_of_row)

    for k in range(1, depth + 1):

        def advance(row, first, last, k=k):
            source = start_ref if k == 1 else power_ref.at[k - 2]
            below = {f: from_below(looked(k - 1, first - 1, row, f), masks(first - 1)) for f in tiles}
            centre = {f: looked(k - 1, first, row, f) for f in tiles}
            for e in range(first, last):
                factors = [coef_ref[i, e, row] for i in range(7)]
                mask = masks(e)
                for f in tiles:
                    here = slice(f, f + TILE)
                    upper = looked(k - 1, e + 1, row, f)
                    value = step(
                        factors,
                        thetas[k - 1],
                        centre[f],
                        source[e, row - 1, here, :],
                        source[e, row + 1, here, :],
                        from_above(upper, mask),
                        below[f],
                    )
                    below[f], centre[f] = from_below(centre[f], mask), upper
                    if k < depth:
                        power_ref[k - 1, e, row, here, :] = value
                    if first == k and depth <= e < depth + layers:
                        slab = (e - depth) * rows + row - depth
                        place = pl.multiple_of(slab * order + (k - 1) * fields + f, TILE)
                        basis_ref[pl.ds(place, TILE), :] = value

        if k < depth:
            by_rows(depth - k, advance)

    def share(r):
        value = None
        for l in range(0, layers, 2):
            places = [pl.multiple_of(((l + i) * rows + r) * order, TILE) for i in range(2)]
            wide = jnp.concatenate([basis_ref[pl.ds(place, order), :] for place in places], axis=1)
            product = lax.dot_general(
                wide, wide, (((1,), (1,)), ((), ())),
                precision=lax.Precision.HIGHEST, preferred_element_type=jnp.float32,
            )
            value = product if value is None else value + product
        return value

    advance(depth, depth, depth + layers)
    sum_ref[...] = jnp.zeros_like(sum_ref)

    @pl.loop(1, rows)
    def _(r):
        product = share(r - 1)
        advance(depth + r, depth, depth + layers)
        sum_ref[...] += product

    total = sum_ref[...] + share(rows - 1)
    gram_ref[...] = total


def eliminate(tiles, order, step):
    width = tiles[0].shape[1]
    lane = lax.broadcasted_iota(jnp.int32, (8, width), 1)
    sub = lax.broadcasted_iota(jnp.int32, (8, width), 0)
    spread = lambda value: jnp.broadcast_to(value, (8, width))
    for first in range(0, order, step):
        home, base = first // 8, first % 8
        panel = tiles[home]
        entry = {}
        for i in range(step):
            for j in range(i, step):
                entry[i, j] = spread(panel[base + i : base + i + 1, first + j : first + j + 1])
        rows = [spread(panel[base + i : base + i + 1, :]) for i in range(step)]
        inverse = []
        done = []
        for i in range(step):
            row = rows[i]
            if i:
                row = jnp.where((lane >= first) & (lane < first + i), 0.0, row)
            factors = []
            for j in range(i):
                factor = entry[j, i] * inverse[j]
                factors.append(factor)
            for j in range(i):
                source = jnp.where(lane == first + j, 1.0, done[j])
                if i - j > 1:
                    source = jnp.where((lane > first + j) & (lane < first + i), 0.0, source)
                row = row - factors[j] * source
                for m in range(i, step):
                    entry[i, m] = entry[i, m] - factors[j] * entry[j, m]
            inverse.append(1.0 / entry[i, i])
            done.append(row)
        sources = []
        for j in range(step):
            source = jnp.where(lane == first + j, 1.0, done[j])
            if j < step - 1:
                source = jnp.where((lane > first + j) & (lane < first + step), 0.0, source)
            sources.append(source)
        inside = (lane >= first) & (lane < first + step)
        for t in range(home, order // 8):
            if t == home and base + step == 8:
                fresh = tiles[t]
            else:
                columns = [spread(tiles[t][:, first + j : first + j + 1]) for j in range(step)]
                fresh = jnp.where(inside, 0.0, tiles[t])
                for j in range(step):
                    factor = columns[j] * inverse[j]
                    fresh = fresh - factor * sources[j]
                    for m in range(j + 1, step):
                        columns[m] = columns[m] - factor * entry[j, m]
            if t == home:
                fresh = jnp.where(sub < base + step, tiles[t], fresh)
                for j in range(step):
                    fresh = jnp.where(sub == base + j, done[j], fresh)
            tiles[t] = fresh
    return tiles


def finish_kernel(*refs, count, step):
    part_refs, (basis_ref, upper_ref, out_ref, staged, sems) = refs[:-5], refs[-5:]
    order = upper_ref.shape[0]
    points = basis_ref.shape[0] // order
    tiles = []
    for t in range(order // 8):
        pieces = [ref[8 * t : 8 * t + 8, :] for ref in part_refs]
        tiles.append(folded(pieces) / count)
    tiles = eliminate(tiles, order, step)
    lane = lax.broadcasted_iota(jnp.int32, (8, order), 1)
    sub = lax.broadcasted_iota(jnp.int32, (8, order), 0)
    inverse = []
    for t in range(order // 8):
        row = sub + 8 * t
        pivot = jnp.sum(jnp.where(lane == row, tiles[t], 0.0), axis=1, keepdims=True)
        scale = 1.0 / jnp.sqrt(pivot)
        upper_ref[8 * t : 8 * t + 8, :] = jnp.where(lane >= row, tiles[t] * scale, 0.0)
        inverse.append(jnp.where(lane < row, tiles[t], jnp.where(lane == row, 1.0, 0.0)) * scale)
    inverse = jnp.concatenate(inverse, axis=0)
    cols = basis_ref.shape[1]
    inverse_parts = two_parts(inverse)
    chunk = points // sems.shape[0]
    copies = []
    for i in range(0, points, 2):
        start = i * order
        wide = jnp.concatenate(
            [basis_ref[start : start + order, :], basis_ref[start + order : start + 2 * order, :]], axis=1
        )
        out = product(inverse_parts, two_parts(wide))
        staged[pl.ds(i, order, stride=points), :] = out[:, :cols]
        staged[pl.ds(i + 1, order, stride=points), :] = out[:, cols:]
        if (i + 2) % chunk == 0:
            part = pl.ds(i + 2 - chunk, chunk)
            source = staged.reshape(order, points, cols).at[:, part, :]
            copies.append(pltpu.make_async_copy(source, out_ref.at[:, part, :], sems.at[i // chunk]))
            copies[-1].start()
    for copy in copies:
        copy.wait()


def two_parts(value):
    high = value.astype(jnp.bfloat16)
    return high, (value - high.astype(jnp.float32)).astype(jnp.bfloat16)


def product(left, right):
    dot = functools.partial(jnp.dot, preferred_element_type=jnp.float32)
    return dot(left[0], right[0]) + (dot(left[0], right[1]) + dot(left[1], right[0]))


def folded(pieces):
    while len(pieces) > 1:
        pieces = [pieces[i] + pieces[i + 1] for i in range(0, len(pieces), 2)]
    return pieces[0]


def rounds(axis):
    size, unit, out = lax.axis_size(axis), 1, []
    while unit < size:
        many = 4 if unit * 4 <= size else 2
        out.append([unit * m for m in range(1, many)])
        unit *= many
    return out


def gathered(value, axis, partners):
    size = lax.axis_size(axis)
    return [value] + [lax.ppermute(value, axis, [(i, i ^ m) for i in range(size)]) for m in partners]


def swapped(value, axis, phase):
    pairs = []
    for i in range(phase, lax.axis_size(axis) - 1, 2):
        pairs += [(i, i + 1), (i + 1, i)]
    return lax.ppermute(value, axis, pairs)


def sent(value, steps):
    axes = tuple(steps)
    sizes = [lax.axis_size(name) for name in axes]
    pairs = []
    if len(axes) == 1:
        pairs = [(i, i + steps[axes[0]]) for i in range(sizes[0]) if 0 <= i + steps[axes[0]] < sizes[0]]
        return lax.ppermute(value, axes[0], pairs)
    for i in range(sizes[0]):
        for j in range(sizes[1]):
            m, n = i + steps[axes[0]], j + steps[axes[1]]
            if 0 <= m < sizes[0] and 0 <= n < sizes[1]:
                pairs.append((i * sizes[1] + j, m * sizes[1] + n))
    return lax.ppermute(value, axes, pairs)


def local(load_currents, cond_rows, cond_cols, cond_vias, ground, via_offset):
    fields, layers, rows, cols = load_currents.shape
    depth = POWERS
    assert layers == depth and rows == 2 * depth and cols == 4 * depth * rows and fields % TILE == 0
    float_of = lambda *shape: jax.ShapeDtypeStruct(shape, jnp.float32)
    pair = lax.axis_size("gy") == 2
    planes = fields + TILE
    slabs = layers * rows
    high = layers + 2 * depth
    tall = rows + 2 * depth
    count = len(CORNERS)
    part = float_of(slabs // 2, planes, cols)
    flat_rows = (slabs // 2) * (fields + COEFS)
    corner_rows = 2 * count * (fields + COEFS) + slabs * COEFS
    raw = load_currents.reshape(fields * slabs, cols)
    one = swapped(raw, "gz", 0)
    two = swapped(raw, "gz", 1)
    first, second, coef_tiles, coef_rows, shifts = pl.pallas_call(
        edges_kernel,
        out_shape=(
            float_of(flat_rows, cols),
            float_of(flat_rows, cols),
            float_of(slabs, TILE, cols),
            float_of(slabs * COEFS, cols),
            jax.ShapeDtypeStruct((high, TILE, cols), jnp.int32),
        ),
        in_specs=[HBM] * 5 + [SMEM],
        out_specs=(VMEM,) * 5,
        scratch_shapes=[
            pltpu.VMEM((fields * slabs, cols), jnp.float32),
            pltpu.VMEM((COEFS, layers, rows, cols), jnp.float32),
            pltpu.SemaphoreType.DMA((COEFS + 1,)),
        ],
        compiler_params=FIRST,
        name="edges",
    )(raw, cond_rows, cond_cols, cond_vias, ground, via_offset)
    first, second = swapped(first, "gx", 0), swapped(second, "gx", 1)
    block = pl.pallas_call(
        own_kernel,
        out_shape=float_of(slabs, planes, cols),
        in_specs=[VMEM] * 2,
        out_specs=VMEM,
        compiler_params=PARAMS,
        cost_estimate=pl.CostEstimate(flops=0, bytes_accessed=8 * slabs * planes * cols, transcendentals=0),
        name="own",
    )(raw, coef_tiles)
    after, before, to_first, to_second = pl.pallas_call(
        functools.partial(corners_kernel, layers=layers),
        out_shape=(part, part) + (float_of(corner_rows, cols),) * 2,
        in_specs=[VMEM] * 3,
        out_specs=(VMEM,) * 4,
        compiler_params=PARAMS,
        name="corners",
    )(first, second, coef_rows)
    to_first, to_second = swapped(to_first, "gz", 0), swapped(to_second, "gz", 1)
    pieces = (block, after, before, one, two)
    inner = pl.pallas_call(
        functools.partial(inner_kernel, layers=layers, rows=rows),
        out_shape=float_of(high, planes, cols),
        in_specs=[VMEM] * 5,
        out_specs=VMEM,
        compiler_params=PARAMS,
        cost_estimate=pl.CostEstimate(flops=0, bytes_accessed=16 * slabs * planes * cols, transcendentals=0),
        name="inner",
    )(*pieces)
    edge, *outer = pl.pallas_call(
        functools.partial(sides_kernel, layers=layers, rows=rows, pair=pair),
        out_shape=(float_of(high, planes, cols),) + (float_of(high // 2, planes, cols),) * (1 if pair else 2),
        in_specs=[VMEM] * 3,
        out_specs=(VMEM,) * (2 if pair else 3),
        compiler_params=PARAMS,
        name="sides",
    )(inner, to_first, to_second)
    pieces += (to_first, to_second)
    if pair:
        got = [lax.ppermute(outer[0], "gy", [(0, 1), (1, 0)])]
    else:
        got = [sent(outer[0], {"gy": 1}), sent(outer[1], {"gy": -1})]
    start = pl.pallas_call(
        functools.partial(assemble_kernel, layers=layers, rows=rows),
        out_shape=float_of(high, tall, planes, cols),
        in_specs=[VMEM] * 7,
        out_specs=VMEM,
        compiler_params=PARAMS,
        cost_estimate=pl.CostEstimate(flops=0, bytes_accessed=2 * high * tall * planes * cols, transcendentals=0),
        name="assemble",
    )(*pieces)
    order = depth * fields
    points = slabs
    basis, gram = pl.pallas_call(
        functools.partial(powers_kernel, fields=fields, layers=layers, rows=rows, pair=pair),
        out_shape=(float_of(points * order, cols), float_of(order, order)),
        in_specs=[VMEM] * (3 + len(got)),
        out_specs=(VMEM, VMEM),
        scratch_shapes=[
            pltpu.VMEM((depth - 1, high, tall, fields, cols), jnp.float32),
            pltpu.VMEM((7, high, tall, TILE, cols), jnp.float32),
            pltpu.VMEM((2, depth, high, planes, cols), jnp.float32),
            pltpu.VMEM((2, 7, high, TILE, cols), jnp.float32),
            pltpu.VMEM((depth, high, planes, cols), jnp.float32),
            pltpu.VMEM((order, order), jnp.float32),
        ],
        compiler_params=PARAMS,
        name="powers",
    )(start, edge, *got, shifts)
    points_in_all = points * cols
    plan = []
    for axis in ("gy", "gx", "gz"):
        points_in_all *= lax.axis_size(axis)
        plan += [(axis, partners) for partners in rounds(axis)]
    parts = [gram]
    for axis, partners in plan:
        parts = gathered(folded(parts), axis, partners)
    upper, basis_q = pl.pallas_call(
        functools.partial(finish_kernel, count=float(points_in_all), step=8),
        out_shape=(float_of(order, order), float_of(order, points, cols)),
        in_specs=[VMEM] * (len(parts) + 1),
        out_specs=(VMEM, HBM),
        scratch_shapes=[pltpu.VMEM((order * points, cols), jnp.float32), pltpu.SemaphoreType.DMA((layers,))],
        compiler_params=PARAMS,
        name="finish",
    )(*parts, basis)
    return basis_q.reshape(order, layers, rows, cols), upper


def solution(mesh):
    in_specs = (
        P(None, "gz", "gx", "gy"),
        P("gz", "gx", "gy"),
        P("gz", "gx", "gy"),
        P("gz", "gx", "gy"),
        P("gz", "gx", "gy"),
        P(),
    )
    out_specs = (P(None, "gz", "gx", "gy"), P())
    return jax.shard_map(local, mesh=mesh, in_specs=in_specs, out_specs=out_specs, check_vma=False)
```

```python
import functools

import jax
import jax.numpy as jnp
from jax import lax
from jax.experimental import pallas as pl
from jax.experimental.pallas import tpu as pltpu
from jax.sharding import PartitionSpec as P

POWERS = 4


newton_shifts = (15.4, 0.6, 11.7, 4.3)
basis_scale = 0.125

VMEM = pl.BlockSpec(memory_space=pltpu.VMEM)
SMEM = pl.BlockSpec(memory_space=pltpu.SMEM)
HBM = pl.BlockSpec(memory_space=pltpu.HBM)
PARAMS = pltpu.CompilerParams(vmem_limit_bytes=32 * 1024 * 1024)
FIRST = pltpu.CompilerParams(vmem_limit_bytes=60 * 1024 * 1024)

COEFS = 4
TILE = 8
CORNERS = ((1, 3), (1, 2), (1, 1), (2, 2), (2, 1), (3, 1))


def positions(shape):
    sub = lax.broadcasted_iota(jnp.int32, shape, 0)
    lane = lax.broadcasted_iota(jnp.int32, shape, 1)
    return sub, lane


def coefs_at(ref, start, i):
    place = start + COEFS * (i // 2) * 2
    tile = ref[place : place + TILE, :]
    return pltpu.roll(tile, COEFS, 0) if i % 2 else tile


def edges_kernel(
    load_ref, rows_ref, cols_ref, vias_ref, ground_ref, offset_ref,
    first_ref, second_ref, tile_ref, flat_ref, shift_ref, fields_in, coefs_in, sems,
):
    slabs, _, cols = tile_ref.shape
    fields = load_ref.shape[0] // slabs
    layers, rows, _ = rows_ref.shape
    depth = POWERS
    half = rows // 2
    total_layers = offset_ref.shape[0]
    copies = [
        pltpu.make_async_copy(ref, coefs_in.at[i], sems.at[i])
        for i, ref in enumerate((rows_ref, cols_ref, vias_ref, ground_ref))
    ]
    copies.append(pltpu.make_async_copy(load_ref, fields_in, sems.at[COEFS]))
    for copy in copies:
        copy.start()
    gx, gy, gz = (lax.axis_index(name) for name in ("gx", "gy", "gz"))
    last_row = jnp.where(gx == lax.axis_size("gx") - 1, rows - 1, rows)
    last_col = jnp.where(gy == lax.axis_size("gy") - 1, cols - 1, cols)
    sub, lane = positions((TILE, cols))
    for e in range(shift_ref.shape[0]):
        layer = gz * layers + e - depth
        inside = (layer >= 0) & (layer < total_layers)
        value = jnp.where(inside, offset_ref[jnp.clip(layer, 0, total_layers - 1)], 0)
        shift_ref[e] = jnp.broadcast_to(value, (TILE, cols))
    for copy in copies:
        copy.wait()

    def joined(one, two):
        return jnp.where(sub < COEFS, one, pltpu.roll(two, COEFS, 0))

    for l in range(layers):
        layer = gz * layers + l
        target = gy * cols + lane + shift_ref[depth + l]
        via_ok = (target >= 0) & (target < cols * lax.axis_size("gy"))
        via_ok = via_ok & (jnp.broadcast_to(layer, lane.shape) < total_layers - 1)
        four = (
            jnp.where(sub == last_row, 0.0, coefs_in[0, l]),
            jnp.where(lane == last_col, 0.0, coefs_in[1, l]),
            jnp.where(via_ok, coefs_in[2, l], 0.0),
            coefs_in[3, l],
        )
        for r in range(rows):
            slab = l * rows + r
            value = jnp.zeros((TILE, cols), jnp.float32)
            for c in range(COEFS):
                value = jnp.where(sub == c, jnp.broadcast_to(four[c][r : r + 1, :], (TILE, cols)), value)
            tile_ref[slab] = value
    for i in range(0, slabs, 2):
        flat_ref[COEFS * i : COEFS * i + TILE, :] = joined(tile_ref[i], tile_ref[i + 1])
    even = lax.rem(gx, 2) == 0
    for ref, start in ((first_ref, jnp.where(even, half, 0)), (second_ref, jnp.where(even, 0, half))):
        for l in range(layers):
            for i in range(half):
                slab = l * rows + start + i
                at = l * half + i
                for f in range(0, fields, TILE):
                    tile = fields_in[pl.ds(f * slabs + slab, TILE, stride=slabs), :]
                    ref[at * fields + f : at * fields + f + TILE, :] = tile
                if i % 2 == 0:
                    place = layers * half * fields + COEFS * at
                    ref[place : place + TILE, :] = joined(tile_ref[slab], tile_ref[slab + 1])


def own_kernel(load_ref, tile_ref, block_ref):
    slabs, planes, _ = block_ref.shape
    for slab in range(slabs):
        for f in range(0, planes - TILE, TILE):
            block_ref[slab, f : f + TILE, :] = load_ref[pl.ds(f * slabs + slab, TILE, stride=slabs), :]
        block_ref[slab, planes - TILE :, :] = tile_ref[slab]


def corners_kernel(first_ref, second_ref, flat_ref, after_ref, before_ref, one_ref, two_ref, *, layers):
    slabs, planes, cols = after_ref.shape
    fields = planes - TILE
    half = slabs // layers
    count = len(CORNERS)
    sub, _ = positions((TILE, cols))
    even_row = jnp.broadcast_to(lax.rem(lax.axis_index("gx"), 2), (TILE, cols)) == 0
    even_layer = jnp.broadcast_to(lax.rem(lax.axis_index("gz"), 2), (TILE, cols)) == 0
    for f in range(0, planes, TILE):
        after, before = [], []
        for i in range(slabs):
            if f < fields:
                first, second = (ref[i * fields + f : i * fields + f + TILE, :] for ref in (first_ref, second_ref))
            else:
                first, second = (coefs_at(ref, slabs * fields, i) for ref in (first_ref, second_ref))
            after.append(jnp.where(even_row, second, first))
            before.append(jnp.where(even_row, first, second))
            after_ref[i, f : f + TILE, :] = after[i]
            before_ref[i, f : f + TILE, :] = before[i]
        ones, twos = [], []
        for source, step in ((after, -1), (before, 1)):
            for dz, dx in CORNERS:
                row = half - dx if step < 0 else dx - 1
                up, down = source[(layers - dz) * half + row], source[(dz - 1) * half + row]
                ones.append(jnp.where(even_layer, up, down))
                twos.append(jnp.where(even_layer, down, up))
        for ref, values in ((one_ref, ones), (two_ref, twos)):
            if f < fields:
                for i, value in enumerate(values):
                    ref[i * fields + f : i * fields + f + TILE, :] = value
            else:
                for i in range(0, 2 * count, 2):
                    place = 2 * count * fields + COEFS * i
                    pair = jnp.where(sub < COEFS, values[i], pltpu.roll(values[i + 1], COEFS, 0))
                    ref[place : place + TILE, :] = pair
    for ref in (one_ref, two_ref):
        place = 2 * count * planes - 2 * count * (TILE - COEFS)
        ref[place : place + flat_ref.shape[0], :] = flat_ref[...]


def slabs_of(e, layers, rows, planes, corners, inner, block, after, before, one, two, corner_one=None, corner_two=None):
    depth, half, count = POWERS, rows // 2, len(CORNERS)
    cols = block.shape[2] if block is not None else corner_one.shape[1]
    fields, slabs = planes - TILE, layers * rows

    def plain(ref, slab):
        return lambda f: ref[slab, f : f + TILE, :]

    def chosen(read, one, two):
        even = jnp.broadcast_to(lax.rem(lax.axis_index("gz"), 2), (TILE, cols)) == 0
        return lambda f: jnp.where(even, read(one, f), read(two, f))

    def home(slab):
        return lambda ref, f: ref[pl.ds(f * slabs + slab, TILE, stride=slabs), :]

    def home_coefs(slab):
        return lambda ref, f: coefs_at(ref, 2 * count * (fields + COEFS), slab)

    def corner(i):
        def read(ref, f):
            if f < fields:
                return ref[i * fields + f : i * fields + f + TILE, :]
            return coefs_at(ref, 2 * count * fields, i)

        return read

    tiles = [f for f in range(0, planes, TILE)]
    found = []
    if depth <= e < depth + layers:
        l = e - depth
        if inner:
            found += [(depth + r, plain(block, l * rows + r), tiles) for r in range(rows)]
            for i in range(half):
                found.append((i, plain(after, l * half + i), tiles))
                found.append((depth + rows + i, plain(before, l * half + i), tiles))
        return found
    if e < depth:
        pair, corner_pair, first, distance = (two, one), (corner_two, corner_one), 0, depth - e
    else:
        pair, corner_pair = (one, two), (corner_one, corner_two)
        first, distance = depth + layers, e - depth - layers + 1
    for r in range(rows):
        slab = (e - first) * rows + r
        if inner:
            found.append((depth + r, chosen(home(slab), *pair), tiles[:-1]))
        if corners:
            found.append((depth + r, chosen(home_coefs(slab), *corner_pair), tiles[-1:]))
    for i, (dz, dx) in enumerate(CORNERS):
        if dz == distance and corners:
            found.append((depth - dx, chosen(corner(i), *corner_pair), tiles))
            found.append((depth + rows - 1 + dx, chosen(corner(count + i), *corner_pair), tiles))
    return found


def inner_kernel(*refs, layers, rows):
    sources, edge_ref = refs[:5], refs[5]
    high, planes, cols = edge_ref.shape
    depth = POWERS
    group = 2 * depth
    _, lane = positions((TILE, cols))
    for e in range(high):
        found = slabs_of(e, layers, rows, planes, False, True, *sources)
        for f in range(0, planes, TILE):
            total = jnp.zeros((TILE, cols), jnp.float32)
            for row, read, tiles in found:
                if f in tiles:
                    moved = pltpu.roll(read(f), (group * row + depth) % cols, 1)
                    total = jnp.where((lane >= group * row) & (lane < group * row + group), moved, total)
            edge_ref[e, f : f + TILE, :] = total


def sides_kernel(inner_ref, one_ref, two_ref, edge_ref, *out_refs, layers, rows, pair):
    high, planes, cols = edge_ref.shape
    depth = POWERS
    group = 2 * depth
    _, lane = positions((TILE, cols))
    early = lax.rem(lane, group) < depth
    gy = jnp.broadcast_to(lax.axis_index("gy"), (TILE, cols))
    for f in range(0, planes, TILE):
        here = slice(f, f + TILE)
        edges = []
        for e in range(high):
            total = inner_ref[e, here, :]
            for row, read, tiles in slabs_of(e, layers, rows, planes, True, False, None, None, None, None, None, one_ref, two_ref):
                if f in tiles:
                    moved = pltpu.roll(read(f), (group * row + depth) % cols, 1)
                    total = jnp.where((lane >= group * row) & (lane < group * row + group), moved, total)
            edge_ref[e, here, :] = total
            edges.append(total)
        for t in range(high // 2):
            one, two = edges[2 * t], edges[2 * t + 1]
            up = jnp.where(early, one, pltpu.roll(two, depth, 1))
            down = jnp.where(early, pltpu.roll(one, cols - depth, 1), two)
            if pair:
                out_refs[0][t, here, :] = jnp.where(gy == 0, up, down)
            else:
                out_refs[0][t, here, :] = up
                out_refs[1][t, here, :] = down


def assemble_kernel(*refs, layers, rows):
    sources, start_ref = refs[:7], refs[7]
    high, _, planes, _ = start_ref.shape
    for e in range(high):
        for row, read, tiles in slabs_of(e, layers, rows, planes, True, True, *sources):
            for f in tiles:
                start_ref[e, row, f : f + TILE, :] = read(f)


def powers_kernel(*refs, fields, layers, rows, pair):
    gots = 1 if pair else 2
    start_ref, edge_ref, got_refs, shift_ref = refs[0], refs[1], refs[2 : 2 + gots], refs[2 + gots]
    basis_ref, gram_ref, power_ref, coef_ref, strip_ref, strip_coef_ref, border_ref, sum_ref = refs[3 + gots :]
    high, tall, planes, cols = start_ref.shape
    depth = POWERS
    group = 2 * depth
    order = depth * fields
    tiles = range(0, fields, TILE)
    _, lane = positions((TILE, cols))
    gy = lax.axis_index("gy")

    def masks(e):
        shift = shift_ref[e]
        return shift == 0, shift > 0

    def from_above(seen, mask):
        left, centre, right = seen
        return jnp.where(mask[0], centre, jnp.where(mask[1], right, left))

    def from_below(seen, mask):
        left, centre, right = seen
        return jnp.where(mask[0], centre, jnp.where(mask[1], left, right))

    def around(tile):
        return pltpu.roll(tile, 1, 1), tile, pltpu.roll(tile, cols - 1, 1)

    def spread(tile, c):
        return jnp.broadcast_to(tile[c : c + 1, :], (TILE, cols))

    def put_factors(put, tile, row_above, seen, seen_below, mask):
        down, right, upper, ground = (spread(tile, c) for c in range(COEFS))
        up = spread(row_above, 0)
        left = spread(seen[0], 1)
        lower = from_below([spread(x, 2) for x in seen_below], mask)
        diagonal = ground + down + up + right + left + upper + lower
        for i, value in enumerate((down, up, right, left, upper, lower, diagonal)):
            put(i, value * basis_scale)

    def step(factors, theta, seen, up, down, above, below):
        value = (factors[6] - theta) * seen[1]
        value = value - (factors[0] * down + factors[1] * up)
        value = value - (factors[2] * seen[2] + factors[3] * seen[0])
        return value - (factors[4] * above + factors[5] * below)

    thetas = [shift * basis_scale for shift in newton_shifts]

    early = lax.rem(lane, group) < depth
    if pair:
        first_side = jnp.where(gy == 0, 1, 0)
        last_side = first_side + 1
    else:
        first_side, last_side = 0, 2

    @pl.loop(first_side, last_side)
    def _(side):
        left_side = jnp.broadcast_to(side, (TILE, cols)) == 0
        from_edge = early != left_side
        for e in range(high):
            for f in range(0, planes, TILE):
                here = slice(f, f + TILE)
                outer = got_refs[0][e // 2, here, :]
                if not pair:
                    outer = jnp.where(left_side, outer, got_refs[1][e // 2, here, :])
                if e % 2 == 0:
                    outer = jnp.where(left_side, outer, pltpu.roll(outer, depth, 1))
                else:
                    outer = jnp.where(left_side, pltpu.roll(outer, cols - depth, 1), outer)
                strip_ref[side, 0, e, here, :] = jnp.where(from_edge, edge_ref[e, here, :], outer)
        raw = [strip_ref[side, 0, e, fields : fields + TILE, :] for e in range(high)]
        seen = [around(tile) for tile in raw]
        for e in range(1, high - 1):

            def put(i, value, e=e):
                strip_coef_ref[side, i, e] = value

            put_factors(put, raw[e], pltpu.roll(raw[e], group, 1), seen[e], seen[e - 1], masks(e - 1))
        for k in range(1, depth):
            reach = depth - k
            looks = {}

            def look(e, f, k=k, looks=looks):
                if (e, f) not in looks:
                    looks[e, f] = around(strip_ref[side, k - 1, e, f : f + TILE, :])
                return looks[e, f]

            for e in range(depth - reach, depth + layers + reach):
                factors = [strip_coef_ref[side, i, e] for i in range(7)]
                over, under = masks(e), masks(e - 1)
                for f in tiles:
                    here = look(e, f)
                    strip_ref[side, k, e, f : f + TILE, :] = step(
                        factors,
                        thetas[k - 1],
                        here,
                        pltpu.roll(here[1], group, 1),
                        pltpu.roll(here[1], cols - group, 1),
                        from_above(look(e + 1, f), over),
                        from_below(look(e - 1, f), under),
                    )

    gy_lane = jnp.broadcast_to(gy, (TILE, cols))
    on_left = (lax.rem(lane, group) == depth - 1) & (gy_lane > 0)
    on_right = (lax.rem(lane, group) == depth - 2) & (gy_lane < lax.axis_size("gy") - 1)

    @pl.loop(0, high)
    def _(e):
        for k in range(depth):
            for f in range(0, planes if k == 0 else fields, TILE):
                here = slice(f, f + TILE)
                right = jnp.where(on_right, pltpu.roll(strip_ref[1, k, e, here, :], cols - 2, 1), 0.0)
                border_ref[k, e, here, :] = jnp.where(on_left, strip_ref[0, k, e, here, :], right)

    leftmost, rightmost = lane == 0, lane == cols - 1

    def looked(k, e, row, f):
        here = slice(f, f + TILE)
        tile = start_ref[e, row, here, :] if k == 0 else power_ref[k - 1, e, row, here, :]
        turn = (2 * cols - group * row - depth + 1) % cols if isinstance(row, int) else lax.rem(2 * cols - group * row - depth + 1, cols)
        outer = pltpu.roll(border_ref[k, e, here, :], turn, 1)
        left, _, right = around(tile)
        return jnp.where(leftmost, outer, left), tile, jnp.where(rightmost, outer, right)

    def by_rows(reach, body):
        @pl.loop(0, rows, unroll=4)
        def _(r):
            body(depth + r, depth - reach, depth + layers + reach)

        for dx in range(1, reach + 1):
            for row in (depth - dx, depth + rows - 1 + dx):
                body(row, depth - reach + dx, depth + layers + reach - dx)

    def factors_of_row(row, first, last):
        seen = {e: looked(0, e, row, fields) for e in range(first - 1, last)}
        for e in range(first, last):

            def put(i, value, e=e):
                coef_ref[i, e, row] = value

            above_row = start_ref[e, row - 1, fields : fields + TILE, :]
            put_factors(put, seen[e][1], above_row, seen[e], seen[e - 1], masks(e - 1))

    by_rows(depth - 1, factors_of_row)

    for k in range(1, depth + 1):

        def advance(row, first, last, k=k):
            source = start_ref if k == 1 else power_ref.at[k - 2]
            below = {f: from_below(looked(k - 1, first - 1, row, f), masks(first - 1)) for f in tiles}
            centre = {f: looked(k - 1, first, row, f) for f in tiles}
            for e in range(first, last):
                factors = [coef_ref[i, e, row] for i in range(7)]
                mask = masks(e)
                for f in tiles:
                    here = slice(f, f + TILE)
                    upper = looked(k - 1, e + 1, row, f)
                    value = step(
                        factors,
                        thetas[k - 1],
                        centre[f],
                        source[e, row - 1, here, :],
                        source[e, row + 1, here, :],
                        from_above(upper, mask),
                        below[f],
                    )
                    below[f], centre[f] = from_below(centre[f], mask), upper
                    if k < depth:
                        power_ref[k - 1, e, row, here, :] = value
                    if first == k and depth <= e < depth + layers:
                        slab = (e - depth) * rows + row - depth
                        place = pl.multiple_of(slab * order + (k - 1) * fields + f, TILE)
                        basis_ref[pl.ds(place, TILE), :] = value

        if k < depth:
            by_rows(depth - k, advance)

    def share(r):
        value = None
        for l in range(0, layers, 2):
            places = [pl.multiple_of(((l + i) * rows + r) * order, TILE) for i in range(2)]
            wide = jnp.concatenate([basis_ref[pl.ds(place, order), :] for place in places], axis=1)
            product = lax.dot_general(
                wide, wide, (((1,), (1,)), ((), ())),
                precision=lax.Precision.HIGHEST, preferred_element_type=jnp.float32,
            )
            value = product if value is None else value + product
        return value

    advance(depth, depth, depth + layers)
    sum_ref[...] = jnp.zeros_like(sum_ref)

    @pl.loop(1, rows)
    def _(r):
        product = share(r - 1)
        advance(depth + r, depth, depth + layers)
        sum_ref[...] += product

    total = sum_ref[...] + share(rows - 1)
    gram_ref[...] = total


def reciprocal(value):
    guess = pl.reciprocal(value, approx=True)
    for _ in range(2):
        guess = guess * (2.0 - value * guess)
    return guess


def eliminate(tiles, order, step):
    width = tiles[0].shape[1]
    lane = lax.broadcasted_iota(jnp.int32, (8, width), 1)
    sub = lax.broadcasted_iota(jnp.int32, (8, width), 0)
    spread = lambda value: jnp.broadcast_to(value, (8, width))
    for first in range(0, order, step):
        home, base = first // 8, first % 8
        panel = tiles[home]
        entry = {}
        for i in range(step):
            for j in range(i, step):
                entry[i, j] = spread(panel[base + i : base + i + 1, first + j : first + j + 1])
        rows = [spread(panel[base + i : base + i + 1, :]) for i in range(step)]
        inverse = []
        done = []
        for i in range(step):
            row = rows[i]
            if i:
                row = jnp.where((lane >= first) & (lane < first + i), 0.0, row)
            factors = []
            for j in range(i):
                factor = entry[j, i] * inverse[j]
                factors.append(factor)
            for j in range(i):
                source = jnp.where(lane == first + j, 1.0, done[j])
                if i - j > 1:
                    source = jnp.where((lane > first + j) & (lane < first + i), 0.0, source)
                row = row - factors[j] * source
                for m in range(i, step):
                    entry[i, m] = entry[i, m] - factors[j] * entry[j, m]
            inverse.append(reciprocal(entry[i, i]))
            done.append(row)
        sources = []
        for j in range(step):
            source = jnp.where(lane == first + j, 1.0, done[j])
            if j < step - 1:
                source = jnp.where((lane > first + j) & (lane < first + step), 0.0, source)
            sources.append(source)
        inside = (lane >= first) & (lane < first + step)
        for t in range(home, order // 8):
            if t == home and base + step == 8:
                fresh = tiles[t]
            else:
                columns = [spread(tiles[t][:, first + j : first + j + 1]) for j in range(step)]
                fresh = jnp.where(inside, 0.0, tiles[t])
                for j in range(step):
                    factor = columns[j] * inverse[j]
                    fresh = fresh - factor * sources[j]
                    for m in range(j + 1, step):
                        columns[m] = columns[m] - factor * entry[j, m]
            if t == home:
                fresh = jnp.where(sub < base + step, tiles[t], fresh)
                for j in range(step):
                    fresh = jnp.where(sub == base + j, done[j], fresh)
            tiles[t] = fresh
    return tiles


def finish_kernel(*refs, count, step):
    part_refs, (high_ref, low_ref, upper_ref, out_ref, staged, sems) = refs[:-6], refs[-6:]
    order = upper_ref.shape[0]
    points = high_ref.shape[0] // order
    tiles = []
    for t in range(order // 8):
        pieces = [ref[8 * t : 8 * t + 8, :] for ref in part_refs]
        tiles.append(folded(pieces) / count)
    tiles = eliminate(tiles, order, step)
    lane = lax.broadcasted_iota(jnp.int32, (8, order), 1)
    sub = lax.broadcasted_iota(jnp.int32, (8, order), 0)
    inverse = []
    for t in range(order // 8):
        row = sub + 8 * t
        pivot = jnp.sum(jnp.where(lane == row, tiles[t], 0.0), axis=1, keepdims=True)
        scale = 1.0 / jnp.sqrt(pivot)
        upper_ref[8 * t : 8 * t + 8, :] = jnp.where(lane >= row, tiles[t] * scale, 0.0)
        inverse.append(jnp.where(lane < row, tiles[t], jnp.where(lane == row, 1.0, 0.0)) * scale)
    inverse = jnp.concatenate(inverse, axis=0)
    cols = high_ref.shape[1]
    inverse_parts = two_parts(inverse)
    chunk = points // sems.shape[0]
    copies = []
    for i in range(0, points, 2):
        start = i * order
        wide = [
            jnp.concatenate([ref[start : start + order, :], ref[start + order : start + 2 * order, :]], axis=1)
            for ref in (high_ref, low_ref)
        ]
        out = product(inverse_parts, wide)
        staged[pl.ds(i, order, stride=points), :] = out[:, :cols]
        staged[pl.ds(i + 1, order, stride=points), :] = out[:, cols:]
        if (i + 2) % chunk == 0:
            part = pl.ds(i + 2 - chunk, chunk)
            source = staged.reshape(order, points, cols).at[:, part, :]
            copies.append(pltpu.make_async_copy(source, out_ref.at[:, part, :], sems.at[i // chunk]))
            copies[-1].start()
    for copy in copies:
        copy.wait()


def split_kernel(basis_ref, high_ref, low_ref):
    size = 2 * TILE

    @pl.loop(0, basis_ref.shape[0] // size, unroll=8)
    def _(i):
        here = pl.ds(pl.multiple_of(i * size, size), size)
        high_ref[here, :], low_ref[here, :] = two_parts(basis_ref[here, :])


def two_parts(value):
    high = value.astype(jnp.bfloat16)
    return high, (value - high.astype(jnp.float32)).astype(jnp.bfloat16)


def product(left, right):
    dot = functools.partial(jnp.dot, preferred_element_type=jnp.float32)
    return dot(left[0], right[0]) + (dot(left[0], right[1]) + dot(left[1], right[0]))


def folded(pieces):
    while len(pieces) > 1:
        pieces = [pieces[i] + pieces[i + 1] for i in range(0, len(pieces), 2)]
    return pieces[0]


def rounds(axis):
    size = lax.axis_size(axis)
    return [[1 << bit] for bit in range(size.bit_length() - 1)]


def gathered(value, axis, partners):
    size = lax.axis_size(axis)
    return [value] + [lax.ppermute(value, axis, [(i, i ^ m) for i in range(size)]) for m in partners]


def swapped(value, axis, phase):
    pairs = []
    for i in range(phase, lax.axis_size(axis) - 1, 2):
        pairs += [(i, i + 1), (i + 1, i)]
    return lax.ppermute(value, axis, pairs)


def sent(value, steps):
    axes = tuple(steps)
    sizes = [lax.axis_size(name) for name in axes]
    pairs = []
    if len(axes) == 1:
        pairs = [(i, i + steps[axes[0]]) for i in range(sizes[0]) if 0 <= i + steps[axes[0]] < sizes[0]]
        return lax.ppermute(value, axes[0], pairs)
    for i in range(sizes[0]):
        for j in range(sizes[1]):
            m, n = i + steps[axes[0]], j + steps[axes[1]]
            if 0 <= m < sizes[0] and 0 <= n < sizes[1]:
                pairs.append((i * sizes[1] + j, m * sizes[1] + n))
    return lax.ppermute(value, axes, pairs)


def local(load_currents, cond_rows, cond_cols, cond_vias, ground, via_offset):
    fields, layers, rows, cols = load_currents.shape
    depth = POWERS
    assert layers == depth and rows == 2 * depth and cols == 4 * depth * rows and fields % TILE == 0
    float_of = lambda *shape: jax.ShapeDtypeStruct(shape, jnp.float32)
    pair = lax.axis_size("gy") == 2
    planes = fields + TILE
    slabs = layers * rows
    high = layers + 2 * depth
    tall = rows + 2 * depth
    count = len(CORNERS)
    part = float_of(slabs // 2, planes, cols)
    flat_rows = (slabs // 2) * (fields + COEFS)
    corner_rows = 2 * count * (fields + COEFS) + slabs * COEFS
    raw = load_currents.reshape(fields * slabs, cols)
    one = swapped(raw, "gz", 0)
    two = swapped(raw, "gz", 1)
    first, second, coef_tiles, coef_rows, shifts = pl.pallas_call(
        edges_kernel,
        out_shape=(
            float_of(flat_rows, cols),
            float_of(flat_rows, cols),
            float_of(slabs, TILE, cols),
            float_of(slabs * COEFS, cols),
            jax.ShapeDtypeStruct((high, TILE, cols), jnp.int32),
        ),
        in_specs=[HBM] * 5 + [SMEM],
        out_specs=(VMEM,) * 5,
        scratch_shapes=[
            pltpu.VMEM((fields * slabs, cols), jnp.float32),
            pltpu.VMEM((COEFS, layers, rows, cols), jnp.float32),
            pltpu.SemaphoreType.DMA((COEFS + 1,)),
        ],
        compiler_params=FIRST,
        name="edges",
    )(raw, cond_rows, cond_cols, cond_vias, ground, via_offset)
    first, second = swapped(first, "gx", 0), swapped(second, "gx", 1)
    block = pl.pallas_call(
        own_kernel,
        out_shape=float_of(slabs, planes, cols),
        in_specs=[VMEM] * 2,
        out_specs=VMEM,
        compiler_params=PARAMS,
        cost_estimate=pl.CostEstimate(flops=0, bytes_accessed=8 * slabs * planes * cols, transcendentals=0),
        name="own",
    )(raw, coef_tiles)
    after, before, to_first, to_second = pl.pallas_call(
        functools.partial(corners_kernel, layers=layers),
        out_shape=(part, part) + (float_of(corner_rows, cols),) * 2,
        in_specs=[VMEM] * 3,
        out_specs=(VMEM,) * 4,
        compiler_params=PARAMS,
        name="corners",
    )(first, second, coef_rows)
    to_first, to_second = swapped(to_first, "gz", 0), swapped(to_second, "gz", 1)
    pieces = (block, after, before, one, two)
    inner = pl.pallas_call(
        functools.partial(inner_kernel, layers=layers, rows=rows),
        out_shape=float_of(high, planes, cols),
        in_specs=[VMEM] * 5,
        out_specs=VMEM,
        compiler_params=PARAMS,
        cost_estimate=pl.CostEstimate(flops=0, bytes_accessed=16 * slabs * planes * cols, transcendentals=0),
        name="inner",
    )(*pieces)
    edge, *outer = pl.pallas_call(
        functools.partial(sides_kernel, layers=layers, rows=rows, pair=pair),
        out_shape=(float_of(high, planes, cols),) + (float_of(high // 2, planes, cols),) * (1 if pair else 2),
        in_specs=[VMEM] * 3,
        out_specs=(VMEM,) * (2 if pair else 3),
        compiler_params=PARAMS,
        name="sides",
    )(inner, to_first, to_second)
    pieces += (to_first, to_second)
    if pair:
        got = [lax.ppermute(outer[0], "gy", [(0, 1), (1, 0)])]
    else:
        got = [sent(outer[0], {"gy": 1}), sent(outer[1], {"gy": -1})]
    start = pl.pallas_call(
        functools.partial(assemble_kernel, layers=layers, rows=rows),
        out_shape=float_of(high, tall, planes, cols),
        in_specs=[VMEM] * 7,
        out_specs=VMEM,
        compiler_params=PARAMS,
        cost_estimate=pl.CostEstimate(flops=0, bytes_accessed=2 * high * tall * planes * cols, transcendentals=0),
        name="assemble",
    )(*pieces)
    order = depth * fields
    points = slabs
    basis, gram = pl.pallas_call(
        functools.partial(powers_kernel, fields=fields, layers=layers, rows=rows, pair=pair),
        out_shape=(float_of(points * order, cols), float_of(order, order)),
        in_specs=[VMEM] * (3 + len(got)),
        out_specs=(VMEM, VMEM),
        scratch_shapes=[
            pltpu.VMEM((depth - 1, high, tall, fields, cols), jnp.float32),
            pltpu.VMEM((7, high, tall, TILE, cols), jnp.float32),
            pltpu.VMEM((2, depth, high, planes, cols), jnp.float32),
            pltpu.VMEM((2, 7, high, TILE, cols), jnp.float32),
            pltpu.VMEM((depth, high, planes, cols), jnp.float32),
            pltpu.VMEM((order, order), jnp.float32),
        ],
        compiler_params=PARAMS,
        name="powers",
    )(start, edge, *got, shifts)
    half_type = jax.ShapeDtypeStruct((points * order, cols), jnp.bfloat16)
    high_part, low_part = pl.pallas_call(
        split_kernel,
        out_shape=(half_type, half_type),
        in_specs=[VMEM],
        out_specs=(VMEM, VMEM),
        compiler_params=PARAMS,
        cost_estimate=pl.CostEstimate(flops=0, bytes_accessed=8 * points * order * cols, transcendentals=0),
        name="split",
    )(basis)
    points_in_all = points * cols
    plan = []
    for axis in ("gy", "gx", "gz"):
        points_in_all *= lax.axis_size(axis)
        plan += [(axis, partners) for partners in rounds(axis)]
    parts = [gram]
    for axis, partners in plan:
        parts = gathered(folded(parts), axis, partners)
    upper, basis_q = pl.pallas_call(
        functools.partial(finish_kernel, count=float(points_in_all), step=8),
        out_shape=(float_of(order, order), float_of(order, points, cols)),
        in_specs=[VMEM] * (len(parts) + 2),
        out_specs=(VMEM, HBM),
        scratch_shapes=[pltpu.VMEM((order * points, cols), jnp.float32), pltpu.SemaphoreType.DMA((layers,))],
        compiler_params=PARAMS,
        name="finish",
    )(*parts, high_part, low_part)
    return basis_q.reshape(order, layers, rows, cols), upper


def solution(mesh):
    in_specs = (
        P(None, "gz", "gx", "gy"),
        P("gz", "gx", "gy"),
        P("gz", "gx", "gy"),
        P("gz", "gx", "gy"),
        P("gz", "gx", "gy"),
        P(),
    )
    out_specs = (P(None, "gz", "gx", "gy"), P())
    return jax.shard_map(local, mesh=mesh, in_specs=in_specs, out_specs=out_specs, check_vma=False)
```

```python
import functools

import jax
import jax.numpy as jnp
from jax import lax
from jax.experimental import pallas as pl
from jax.experimental.pallas import tpu as pltpu
from jax.sharding import PartitionSpec as P

POWERS = 4


newton_shifts = (15.4, 0.6, 11.7, 4.3)
basis_scale = 0.125

VMEM = pl.BlockSpec(memory_space=pltpu.VMEM)
SMEM = pl.BlockSpec(memory_space=pltpu.SMEM)
HBM = pl.BlockSpec(memory_space=pltpu.HBM)
PARAMS = pltpu.CompilerParams(vmem_limit_bytes=32 * 1024 * 1024)
FIRST = pltpu.CompilerParams(vmem_limit_bytes=60 * 1024 * 1024)

COEFS = 4
TILE = 8
CORNERS = ((1, 3), (1, 2), (1, 1), (2, 2), (2, 1), (3, 1))


def positions(shape):
    sub = lax.broadcasted_iota(jnp.int32, shape, 0)
    lane = lax.broadcasted_iota(jnp.int32, shape, 1)
    return sub, lane


def coefs_at(ref, start, i):
    place = start + COEFS * (i // 2) * 2
    tile = ref[place : place + TILE, :]
    return pltpu.roll(tile, COEFS, 0) if i % 2 else tile


def edges_kernel(
    load_ref, rows_ref, cols_ref, vias_ref, ground_ref, offset_ref,
    first_ref, second_ref, tile_ref, flat_ref, shift_ref, fields_in, coefs_in, sems,
):
    slabs, _, cols = tile_ref.shape
    fields = load_ref.shape[0] // slabs
    layers, rows, _ = rows_ref.shape
    depth = POWERS
    half = rows // 2
    total_layers = offset_ref.shape[0]
    copies = [
        pltpu.make_async_copy(ref, coefs_in.at[i], sems.at[i])
        for i, ref in enumerate((rows_ref, cols_ref, vias_ref, ground_ref))
    ]
    copies.append(pltpu.make_async_copy(load_ref, fields_in, sems.at[COEFS]))
    for copy in copies:
        copy.start()
    gx, gy, gz = (lax.axis_index(name) for name in ("gx", "gy", "gz"))
    last_row = jnp.where(gx == lax.axis_size("gx") - 1, rows - 1, rows)
    last_col = jnp.where(gy == lax.axis_size("gy") - 1, cols - 1, cols)
    sub, lane = positions((TILE, cols))
    for e in range(shift_ref.shape[0]):
        layer = gz * layers + e - depth
        inside = (layer >= 0) & (layer < total_layers)
        value = jnp.where(inside, offset_ref[jnp.clip(layer, 0, total_layers - 1)], 0)
        shift_ref[e] = jnp.broadcast_to(value, (TILE, cols))
    for copy in copies:
        copy.wait()

    def joined(one, two):
        return jnp.where(sub < COEFS, one, pltpu.roll(two, COEFS, 0))

    for l in range(layers):
        layer = gz * layers + l
        target = gy * cols + lane + shift_ref[depth + l]
        via_ok = (target >= 0) & (target < cols * lax.axis_size("gy"))
        via_ok = via_ok & (jnp.broadcast_to(layer, lane.shape) < total_layers - 1)
        four = (
            jnp.where(sub == last_row, 0.0, coefs_in[0, l]),
            jnp.where(lane == last_col, 0.0, coefs_in[1, l]),
            jnp.where(via_ok, coefs_in[2, l], 0.0),
            coefs_in[3, l],
        )
        for r in range(rows):
            slab = l * rows + r
            value = jnp.zeros((TILE, cols), jnp.float32)
            for c in range(COEFS):
                value = jnp.where(sub == c, jnp.broadcast_to(four[c][r : r + 1, :], (TILE, cols)), value)
            tile_ref[slab] = value
    for i in range(0, slabs, 2):
        flat_ref[COEFS * i : COEFS * i + TILE, :] = joined(tile_ref[i], tile_ref[i + 1])
    even = lax.rem(gx, 2) == 0
    for ref, start in ((first_ref, jnp.where(even, half, 0)), (second_ref, jnp.where(even, 0, half))):
        for l in range(layers):
            for i in range(half):
                slab = l * rows + start + i
                at = l * half + i
                for f in range(0, fields, TILE):
                    tile = fields_in[pl.ds(f * slabs + slab, TILE, stride=slabs), :]
                    ref[at * fields + f : at * fields + f + TILE, :] = tile
                if i % 2 == 0:
                    place = layers * half * fields + COEFS * at
                    ref[place : place + TILE, :] = joined(tile_ref[slab], tile_ref[slab + 1])


def own_kernel(load_ref, tile_ref, block_ref):
    slabs, planes, _ = block_ref.shape
    for slab in range(slabs):
        for f in range(0, planes - TILE, TILE):
            block_ref[slab, f : f + TILE, :] = load_ref[pl.ds(f * slabs + slab, TILE, stride=slabs), :]
        block_ref[slab, planes - TILE :, :] = tile_ref[slab]


def corners_kernel(first_ref, second_ref, flat_ref, after_ref, before_ref, one_ref, two_ref, *, layers):
    slabs, planes, cols = after_ref.shape
    fields = planes - TILE
    half = slabs // layers
    count = len(CORNERS)
    sub, _ = positions((TILE, cols))
    even_row = jnp.broadcast_to(lax.rem(lax.axis_index("gx"), 2), (TILE, cols)) == 0
    even_layer = jnp.broadcast_to(lax.rem(lax.axis_index("gz"), 2), (TILE, cols)) == 0
    for f in range(0, planes, TILE):
        after, before = [], []
        for i in range(slabs):
            if f < fields:
                first, second = (ref[i * fields + f : i * fields + f + TILE, :] for ref in (first_ref, second_ref))
            else:
                first, second = (coefs_at(ref, slabs * fields, i) for ref in (first_ref, second_ref))
            after.append(jnp.where(even_row, second, first))
            before.append(jnp.where(even_row, first, second))
            after_ref[i, f : f + TILE, :] = after[i]
            before_ref[i, f : f + TILE, :] = before[i]
        ones, twos = [], []
        for source, step in ((after, -1), (before, 1)):
            for dz, dx in CORNERS:
                row = half - dx if step < 0 else dx - 1
                up, down = source[(layers - dz) * half + row], source[(dz - 1) * half + row]
                ones.append(jnp.where(even_layer, up, down))
                twos.append(jnp.where(even_layer, down, up))
        for ref, values in ((one_ref, ones), (two_ref, twos)):
            if f < fields:
                for i, value in enumerate(values):
                    ref[i * fields + f : i * fields + f + TILE, :] = value
            else:
                for i in range(0, 2 * count, 2):
                    place = 2 * count * fields + COEFS * i
                    pair = jnp.where(sub < COEFS, values[i], pltpu.roll(values[i + 1], COEFS, 0))
                    ref[place : place + TILE, :] = pair
    for ref in (one_ref, two_ref):
        place = 2 * count * planes - 2 * count * (TILE - COEFS)
        ref[place : place + flat_ref.shape[0], :] = flat_ref[...]


def slabs_of(e, layers, rows, planes, corners, inner, block, after, before, one, two, corner_one=None, corner_two=None):
    depth, half, count = POWERS, rows // 2, len(CORNERS)
    cols = block.shape[2] if block is not None else corner_one.shape[1]
    fields, slabs = planes - TILE, layers * rows

    def plain(ref, slab):
        return lambda f: ref[slab, f : f + TILE, :]

    def chosen(read, one, two):
        even = jnp.broadcast_to(lax.rem(lax.axis_index("gz"), 2), (TILE, cols)) == 0
        return lambda f: jnp.where(even, read(one, f), read(two, f))

    def home(slab):
        return lambda ref, f: ref[pl.ds(f * slabs + slab, TILE, stride=slabs), :]

    def home_coefs(slab):
        return lambda ref, f: coefs_at(ref, 2 * count * (fields + COEFS), slab)

    def corner(i):
        def read(ref, f):
            if f < fields:
                return ref[i * fields + f : i * fields + f + TILE, :]
            return coefs_at(ref, 2 * count * fields, i)

        return read

    tiles = [f for f in range(0, planes, TILE)]
    found = []
    if depth <= e < depth + layers:
        l = e - depth
        if inner:
            found += [(depth + r, plain(block, l * rows + r), tiles) for r in range(rows)]
            for i in range(half):
                found.append((i, plain(after, l * half + i), tiles))
                found.append((depth + rows + i, plain(before, l * half + i), tiles))
        return found
    if e < depth:
        pair, corner_pair, first, distance = (two, one), (corner_two, corner_one), 0, depth - e
    else:
        pair, corner_pair = (one, two), (corner_one, corner_two)
        first, distance = depth + layers, e - depth - layers + 1
    for r in range(rows):
        slab = (e - first) * rows + r
        if inner:
            found.append((depth + r, chosen(home(slab), *pair), tiles[:-1]))
        if corners:
            found.append((depth + r, chosen(home_coefs(slab), *corner_pair), tiles[-1:]))
    for i, (dz, dx) in enumerate(CORNERS):
        if dz == distance and corners:
            found.append((depth - dx, chosen(corner(i), *corner_pair), tiles))
            found.append((depth + rows - 1 + dx, chosen(corner(count + i), *corner_pair), tiles))
    return found


def inner_kernel(*refs, layers, rows):
    sources, edge_ref = refs[:5], refs[5]
    high, planes, cols = edge_ref.shape
    depth = POWERS
    group = 2 * depth
    _, lane = positions((TILE, cols))
    for e in range(high):
        found = slabs_of(e, layers, rows, planes, False, True, *sources)
        for f in range(0, planes, TILE):
            total = jnp.zeros((TILE, cols), jnp.float32)
            for row, read, tiles in found:
                if f in tiles:
                    moved = pltpu.roll(read(f), (group * row + depth) % cols, 1)
                    total = jnp.where((lane >= group * row) & (lane < group * row + group), moved, total)
            edge_ref[e, f : f + TILE, :] = total


def sides_kernel(inner_ref, one_ref, two_ref, edge_ref, *out_refs, layers, rows, pair):
    high, planes, cols = edge_ref.shape
    depth = POWERS
    group = 2 * depth
    _, lane = positions((TILE, cols))
    early = lax.rem(lane, group) < depth
    gy = jnp.broadcast_to(lax.axis_index("gy"), (TILE, cols))
    for f in range(0, planes, TILE):
        here = slice(f, f + TILE)
        edges = []
        for e in range(high):
            total = inner_ref[e, here, :]
            for row, read, tiles in slabs_of(e, layers, rows, planes, True, False, None, None, None, None, None, one_ref, two_ref):
                if f in tiles:
                    moved = pltpu.roll(read(f), (group * row + depth) % cols, 1)
                    total = jnp.where((lane >= group * row) & (lane < group * row + group), moved, total)
            edge_ref[e, here, :] = total
            edges.append(total)
        for t in range(high // 2):
            one, two = edges[2 * t], edges[2 * t + 1]
            up = jnp.where(early, one, pltpu.roll(two, depth, 1))
            down = jnp.where(early, pltpu.roll(one, cols - depth, 1), two)
            if pair:
                out_refs[0][t, here, :] = jnp.where(gy == 0, up, down)
            else:
                out_refs[0][t, here, :] = up
                out_refs[1][t, here, :] = down


def assemble_kernel(*refs, layers, rows):
    sources, start_ref = refs[:7], refs[7]
    high, _, planes, _ = start_ref.shape
    for e in range(high):
        for row, read, tiles in slabs_of(e, layers, rows, planes, True, True, *sources):
            for f in tiles:
                start_ref[e, row, f : f + TILE, :] = read(f)


def powers_kernel(*refs, fields, layers, rows, pair):
    gots = 1 if pair else 2
    start_ref, edge_ref, got_refs, shift_ref = refs[0], refs[1], refs[2 : 2 + gots], refs[2 + gots]
    basis_ref, keep_ref, send_ref, power_ref, coef_ref, strip_ref, strip_coef_ref, border_ref, sum_ref = refs[3 + gots :]
    high, tall, planes, cols = start_ref.shape
    depth = POWERS
    group = 2 * depth
    order = depth * fields
    tiles = range(0, fields, TILE)
    _, lane = positions((TILE, cols))
    gy = lax.axis_index("gy")

    def masks(e):
        shift = shift_ref[e]
        return shift == 0, shift > 0

    def from_above(seen, mask):
        left, centre, right = seen
        return jnp.where(mask[0], centre, jnp.where(mask[1], right, left))

    def from_below(seen, mask):
        left, centre, right = seen
        return jnp.where(mask[0], centre, jnp.where(mask[1], left, right))

    def around(tile):
        return pltpu.roll(tile, 1, 1), tile, pltpu.roll(tile, cols - 1, 1)

    def spread(tile, c):
        return jnp.broadcast_to(tile[c : c + 1, :], (TILE, cols))

    def put_factors(put, tile, row_above, seen, seen_below, mask):
        down, right, upper, ground = (spread(tile, c) for c in range(COEFS))
        up = spread(row_above, 0)
        left = spread(seen[0], 1)
        lower = from_below([spread(x, 2) for x in seen_below], mask)
        diagonal = ground + down + up + right + left + upper + lower
        for i, value in enumerate((down, up, right, left, upper, lower, diagonal)):
            put(i, value * basis_scale)

    def step(factors, theta, seen, up, down, above, below):
        value = (factors[6] - theta) * seen[1]
        value = value - (factors[0] * down + factors[1] * up)
        value = value - (factors[2] * seen[2] + factors[3] * seen[0])
        return value - (factors[4] * above + factors[5] * below)

    thetas = [shift * basis_scale for shift in newton_shifts]

    early = lax.rem(lane, group) < depth
    if pair:
        first_side = jnp.where(gy == 0, 1, 0)
        last_side = first_side + 1
    else:
        first_side, last_side = 0, 2

    @pl.loop(first_side, last_side)
    def _(side):
        left_side = jnp.broadcast_to(side, (TILE, cols)) == 0
        from_edge = early != left_side
        for e in range(high):
            for f in range(0, planes, TILE):
                here = slice(f, f + TILE)
                outer = got_refs[0][e // 2, here, :]
                if not pair:
                    outer = jnp.where(left_side, outer, got_refs[1][e // 2, here, :])
                if e % 2 == 0:
                    outer = jnp.where(left_side, outer, pltpu.roll(outer, depth, 1))
                else:
                    outer = jnp.where(left_side, pltpu.roll(outer, cols - depth, 1), outer)
                strip_ref[side, 0, e, here, :] = jnp.where(from_edge, edge_ref[e, here, :], outer)
        raw = [strip_ref[side, 0, e, fields : fields + TILE, :] for e in range(high)]
        seen = [around(tile) for tile in raw]
        for e in range(1, high - 1):

            def put(i, value, e=e):
                strip_coef_ref[side, i, e] = value

            put_factors(put, raw[e], pltpu.roll(raw[e], group, 1), seen[e], seen[e - 1], masks(e - 1))
        for k in range(1, depth):
            reach = depth - k
            looks = {}

            def look(e, f, k=k, looks=looks):
                if (e, f) not in looks:
                    looks[e, f] = around(strip_ref[side, k - 1, e, f : f + TILE, :])
                return looks[e, f]

            for e in range(depth - reach, depth + layers + reach):
                factors = [strip_coef_ref[side, i, e] for i in range(7)]
                over, under = masks(e), masks(e - 1)
                for f in tiles:
                    here = look(e, f)
                    strip_ref[side, k, e, f : f + TILE, :] = step(
                        factors,
                        thetas[k - 1],
                        here,
                        pltpu.roll(here[1], group, 1),
                        pltpu.roll(here[1], cols - group, 1),
                        from_above(look(e + 1, f), over),
                        from_below(look(e - 1, f), under),
                    )

    gy_lane = jnp.broadcast_to(gy, (TILE, cols))
    on_left = (lax.rem(lane, group) == depth - 1) & (gy_lane > 0)
    on_right = (lax.rem(lane, group) == depth - 2) & (gy_lane < lax.axis_size("gy") - 1)

    @pl.loop(0, high)
    def _(e):
        for k in range(depth):
            for f in range(0, planes if k == 0 else fields, TILE):
                here = slice(f, f + TILE)
                right = jnp.where(on_right, pltpu.roll(strip_ref[1, k, e, here, :], cols - 2, 1), 0.0)
                border_ref[k, e, here, :] = jnp.where(on_left, strip_ref[0, k, e, here, :], right)

    leftmost, rightmost = lane == 0, lane == cols - 1

    def looked(k, e, row, f):
        here = slice(f, f + TILE)
        tile = start_ref[e, row, here, :] if k == 0 else power_ref[k - 1, e, row, here, :]
        turn = (2 * cols - group * row - depth + 1) % cols if isinstance(row, int) else lax.rem(2 * cols - group * row - depth + 1, cols)
        outer = pltpu.roll(border_ref[k, e, here, :], turn, 1)
        left, _, right = around(tile)
        return jnp.where(leftmost, outer, left), tile, jnp.where(rightmost, outer, right)

    def by_rows(reach, body):
        @pl.loop(0, rows, unroll=4)
        def _(r):
            body(depth + r, depth - reach, depth + layers + reach)

        for dx in range(1, reach + 1):
            for row in (depth - dx, depth + rows - 1 + dx):
                body(row, depth - reach + dx, depth + layers + reach - dx)

    def factors_of_row(row, first, last):
        seen = {e: looked(0, e, row, fields) for e in range(first - 1, last)}
        for e in range(first, last):

            def put(i, value, e=e):
                coef_ref[i, e, row] = value

            above_row = start_ref[e, row - 1, fields : fields + TILE, :]
            put_factors(put, seen[e][1], above_row, seen[e], seen[e - 1], masks(e - 1))

    by_rows(depth - 1, factors_of_row)

    for k in range(1, depth + 1):

        def advance(row, first, last, k=k):
            source = start_ref if k == 1 else power_ref.at[k - 2]
            below = {f: from_below(looked(k - 1, first - 1, row, f), masks(first - 1)) for f in tiles}
            centre = {f: looked(k - 1, first, row, f) for f in tiles}
            for e in range(first, last):
                factors = [coef_ref[i, e, row] for i in range(7)]
                mask = masks(e)
                for f in tiles:
                    here = slice(f, f + TILE)
                    upper = looked(k - 1, e + 1, row, f)
                    value = step(
                        factors,
                        thetas[k - 1],
                        centre[f],
                        source[e, row - 1, here, :],
                        source[e, row + 1, here, :],
                        from_above(upper, mask),
                        below[f],
                    )
                    below[f], centre[f] = from_below(centre[f], mask), upper
                    if k < depth:
                        power_ref[k - 1, e, row, here, :] = value
                    if first == k and depth <= e < depth + layers:
                        slab = (e - depth) * rows + row - depth
                        place = pl.multiple_of(slab * order + (k - 1) * fields + f, TILE)
                        basis_ref[pl.ds(place, TILE), :] = value

        if k < depth:
            by_rows(depth - k, advance)

    def share(r):
        value = None
        for l in range(0, layers, 2):
            places = [pl.multiple_of(((l + i) * rows + r) * order, TILE) for i in range(2)]
            wide = jnp.concatenate([basis_ref[pl.ds(place, order), :] for place in places], axis=1)
            product = lax.dot_general(
                wide, wide, (((1,), (1,)), ((), ())),
                precision=lax.Precision.HIGHEST, preferred_element_type=jnp.float32,
            )
            value = product if value is None else value + product
        return value

    advance(depth, depth, depth + layers)
    sum_ref[...] = jnp.zeros_like(sum_ref)

    @pl.loop(1, rows)
    def _(r):
        product = share(r - 1)
        advance(depth + r, depth, depth + layers)
        sum_ref[...] += product

    total = sum_ref[...] + share(rows - 1)
    sum_ref[...] = total
    half = order // 2
    odd = lax.rem(lax.axis_index("gz"), 2)
    keep_ref[...] = sum_ref[pl.ds(pl.multiple_of(odd * half, TILE), half), :]
    send_ref[...] = sum_ref[pl.ds(pl.multiple_of((1 - odd) * half, TILE), half), :]


def eliminate(tiles, order, step):
    width = tiles[0].shape[1]
    lane = lax.broadcasted_iota(jnp.int32, (8, width), 1)
    sub = lax.broadcasted_iota(jnp.int32, (8, width), 0)
    spread = lambda value: jnp.broadcast_to(value, (8, width))
    for first in range(0, order, step):
        home, base = first // 8, first % 8
        panel = tiles[home]
        entry = {}
        for i in range(step):
            for j in range(i, step):
                entry[i, j] = spread(panel[base + i : base + i + 1, first + j : first + j + 1])
        rows = [spread(panel[base + i : base + i + 1, :]) for i in range(step)]
        inverse = []
        done = []
        for i in range(step):
            row = rows[i]
            if i:
                row = jnp.where((lane >= first) & (lane < first + i), 0.0, row)
            factors = []
            for j in range(i):
                factor = entry[j, i] * inverse[j]
                factors.append(factor)
            for j in range(i):
                source = jnp.where(lane == first + j, 1.0, done[j])
                if i - j > 1:
                    source = jnp.where((lane > first + j) & (lane < first + i), 0.0, source)
                row = row - factors[j] * source
                for m in range(i, step):
                    entry[i, m] = entry[i, m] - factors[j] * entry[j, m]
            inverse.append(1.0 / entry[i, i])
            done.append(row)
        sources = []
        for j in range(step):
            source = jnp.where(lane == first + j, 1.0, done[j])
            if j < step - 1:
                source = jnp.where((lane > first + j) & (lane < first + step), 0.0, source)
            sources.append(source)
        inside = (lane >= first) & (lane < first + step)
        for t in range(home, order // 8):
            if t == home and base + step == 8:
                fresh = tiles[t]
            else:
                columns = [spread(tiles[t][:, first + j : first + j + 1]) for j in range(step)]
                fresh = jnp.where(inside, 0.0, tiles[t])
                for j in range(step):
                    factor = columns[j] * inverse[j]
                    fresh = fresh - factor * sources[j]
                    for m in range(j + 1, step):
                        columns[m] = columns[m] - factor * entry[j, m]
            if t == home:
                fresh = jnp.where(sub < base + step, tiles[t], fresh)
                for j in range(step):
                    fresh = jnp.where(sub == base + j, done[j], fresh)
            tiles[t] = fresh
    return tiles


def finish_kernel(*refs, count, step):
    own_ref, other_ref, high_ref, low_ref, upper_ref, out_ref, staged, sems = refs
    order = upper_ref.shape[0]
    points = high_ref.shape[0] // order
    even = jnp.broadcast_to(lax.rem(lax.axis_index("gz"), 2), (TILE, order)) == 0
    halves = [[], []]
    for r in range(0, order // 2, TILE):
        own, other = own_ref[r : r + TILE, :] / count, other_ref[r : r + TILE, :] / count
        halves[0].append(jnp.where(even, own, other))
        halves[1].append(jnp.where(even, other, own))
    tiles = eliminate(halves[0] + halves[1], order, step)
    lane = lax.broadcasted_iota(jnp.int32, (8, order), 1)
    sub = lax.broadcasted_iota(jnp.int32, (8, order), 0)
    inverse = []
    for t in range(order // 8):
        row = sub + 8 * t
        pivot = jnp.sum(jnp.where(lane == row, tiles[t], 0.0), axis=1, keepdims=True)
        scale = 1.0 / jnp.sqrt(pivot)
        upper_ref[8 * t : 8 * t + 8, :] = jnp.where(lane >= row, tiles[t] * scale, 0.0)
        inverse.append(jnp.where(lane < row, tiles[t], jnp.where(lane == row, 1.0, 0.0)) * scale)
    inverse = jnp.concatenate(inverse, axis=0)
    cols = high_ref.shape[1]
    inverse_parts = two_parts(inverse)
    chunk = points // sems.shape[0]
    copies = []
    for i in range(0, points, 2):
        start = i * order
        wide = [
            jnp.concatenate([ref[start : start + order, :], ref[start + order : start + 2 * order, :]], axis=1)
            for ref in (high_ref, low_ref)
        ]
        out = product(inverse_parts, wide)
        staged[pl.ds(i, order, stride=points), :] = out[:, :cols]
        staged[pl.ds(i + 1, order, stride=points), :] = out[:, cols:]
        if (i + 2) % chunk == 0:
            part = pl.ds(i + 2 - chunk, chunk)
            source = staged.reshape(order, points, cols).at[:, part, :]
            copies.append(pltpu.make_async_copy(source, out_ref.at[:, part, :], sems.at[i // chunk]))
            copies[-1].start()
    for copy in copies:
        copy.wait()


def split_kernel(basis_ref, high_ref, low_ref):
    size = 2 * TILE

    @pl.loop(0, basis_ref.shape[0] // size, unroll=8)
    def _(i):
        here = pl.ds(pl.multiple_of(i * size, size), size)
        high_ref[here, :], low_ref[here, :] = two_parts(basis_ref[here, :])


def two_parts(value):
    high = value.astype(jnp.bfloat16)
    return high, (value - high.astype(jnp.float32)).astype(jnp.bfloat16)


def product(left, right):
    dot = functools.partial(jnp.dot, preferred_element_type=jnp.float32)
    return dot(left[0], right[0]) + (dot(left[0], right[1]) + dot(left[1], right[0]))


def doubled(value, steps_of):
    axes = ("gx", "gy", "gz")
    sizes = [lax.axis_size(name) for name in axes]
    assert all(size & (size - 1) == 0 for size in sizes)

    def index(place):
        return (place[0] * sizes[1] + place[1]) * sizes[2] + place[2]

    for r in range(len(steps_of[0])):
        pairs = []
        for x in range(sizes[0]):
            for y in range(sizes[1]):
                for z in range(sizes[2]):
                    axis, mask = steps_of[z % 2][r]
                    partner = [x, y, z]
                    partner[axes.index(axis)] ^= mask
                    pairs.append((index((x, y, z)), index(partner)))
        value = value + lax.ppermute(value, axes, pairs)
    return value


def swapped(value, axis, phase):
    pairs = []
    for i in range(phase, lax.axis_size(axis) - 1, 2):
        pairs += [(i, i + 1), (i + 1, i)]
    return lax.ppermute(value, axis, pairs)


def sent(value, steps):
    axes = tuple(steps)
    sizes = [lax.axis_size(name) for name in axes]
    pairs = []
    if len(axes) == 1:
        pairs = [(i, i + steps[axes[0]]) for i in range(sizes[0]) if 0 <= i + steps[axes[0]] < sizes[0]]
        return lax.ppermute(value, axes[0], pairs)
    for i in range(sizes[0]):
        for j in range(sizes[1]):
            m, n = i + steps[axes[0]], j + steps[axes[1]]
            if 0 <= m < sizes[0] and 0 <= n < sizes[1]:
                pairs.append((i * sizes[1] + j, m * sizes[1] + n))
    return lax.ppermute(value, axes, pairs)


def local(load_currents, cond_rows, cond_cols, cond_vias, ground, via_offset):
    fields, layers, rows, cols = load_currents.shape
    depth = POWERS
    assert layers == depth and rows == 2 * depth and cols == 4 * depth * rows and fields % TILE == 0
    float_of = lambda *shape: jax.ShapeDtypeStruct(shape, jnp.float32)
    pair = lax.axis_size("gy") == 2
    planes = fields + TILE
    slabs = layers * rows
    high = layers + 2 * depth
    tall = rows + 2 * depth
    count = len(CORNERS)
    part = float_of(slabs // 2, planes, cols)
    flat_rows = (slabs // 2) * (fields + COEFS)
    corner_rows = 2 * count * (fields + COEFS) + slabs * COEFS
    raw = load_currents.reshape(fields * slabs, cols)
    one = swapped(raw, "gz", 0)
    two = swapped(raw, "gz", 1)
    first, second, coef_tiles, coef_rows, shifts = pl.pallas_call(
        edges_kernel,
        out_shape=(
            float_of(flat_rows, cols),
            float_of(flat_rows, cols),
            float_of(slabs, TILE, cols),
            float_of(slabs * COEFS, cols),
            jax.ShapeDtypeStruct((high, TILE, cols), jnp.int32),
        ),
        in_specs=[HBM] * 5 + [SMEM],
        out_specs=(VMEM,) * 5,
        scratch_shapes=[
            pltpu.VMEM((fields * slabs, cols), jnp.float32),
            pltpu.VMEM((COEFS, layers, rows, cols), jnp.float32),
            pltpu.SemaphoreType.DMA((COEFS + 1,)),
        ],
        compiler_params=FIRST,
        name="edges",
    )(raw, cond_rows, cond_cols, cond_vias, ground, via_offset)
    first, second = swapped(first, "gx", 0), swapped(second, "gx", 1)
    block = pl.pallas_call(
        own_kernel,
        out_shape=float_of(slabs, planes, cols),
        in_specs=[VMEM] * 2,
        out_specs=VMEM,
        compiler_params=PARAMS,
        cost_estimate=pl.CostEstimate(flops=0, bytes_accessed=8 * slabs * planes * cols, transcendentals=0),
        name="own",
    )(raw, coef_tiles)
    after, before, to_first, to_second = pl.pallas_call(
        functools.partial(corners_kernel, layers=layers),
        out_shape=(part, part) + (float_of(corner_rows, cols),) * 2,
        in_specs=[VMEM] * 3,
        out_specs=(VMEM,) * 4,
        compiler_params=PARAMS,
        name="corners",
    )(first, second, coef_rows)
    to_first, to_second = swapped(to_first, "gz", 0), swapped(to_second, "gz", 1)
    pieces = (block, after, before, one, two)
    inner = pl.pallas_call(
        functools.partial(inner_kernel, layers=layers, rows=rows),
        out_shape=float_of(high, planes, cols),
        in_specs=[VMEM] * 5,
        out_specs=VMEM,
        compiler_params=PARAMS,
        cost_estimate=pl.CostEstimate(flops=0, bytes_accessed=16 * slabs * planes * cols, transcendentals=0),
        name="inner",
    )(*pieces)
    edge, *outer = pl.pallas_call(
        functools.partial(sides_kernel, layers=layers, rows=rows, pair=pair),
        out_shape=(float_of(high, planes, cols),) + (float_of(high // 2, planes, cols),) * (1 if pair else 2),
        in_specs=[VMEM] * 3,
        out_specs=(VMEM,) * (2 if pair else 3),
        compiler_params=PARAMS,
        name="sides",
    )(inner, to_first, to_second)
    pieces += (to_first, to_second)
    if pair:
        got = [lax.ppermute(outer[0], "gy", [(0, 1), (1, 0)])]
    else:
        got = [sent(outer[0], {"gy": 1}), sent(outer[1], {"gy": -1})]
    start = pl.pallas_call(
        functools.partial(assemble_kernel, layers=layers, rows=rows),
        out_shape=float_of(high, tall, planes, cols),
        in_specs=[VMEM] * 7,
        out_specs=VMEM,
        compiler_params=PARAMS,
        cost_estimate=pl.CostEstimate(flops=0, bytes_accessed=2 * high * tall * planes * cols, transcendentals=0),
        name="assemble",
    )(*pieces)
    order = depth * fields
    points = slabs
    basis, keep, send = pl.pallas_call(
        functools.partial(powers_kernel, fields=fields, layers=layers, rows=rows, pair=pair),
        out_shape=(float_of(points * order, cols),) + (float_of(order // 2, order),) * 2,
        in_specs=[VMEM] * (3 + len(got)),
        out_specs=(VMEM,) * 3,
        scratch_shapes=[
            pltpu.VMEM((depth - 1, high, tall, fields, cols), jnp.float32),
            pltpu.VMEM((7, high, tall, TILE, cols), jnp.float32),
            pltpu.VMEM((2, depth, high, planes, cols), jnp.float32),
            pltpu.VMEM((2, 7, high, TILE, cols), jnp.float32),
            pltpu.VMEM((depth, high, planes, cols), jnp.float32),
            pltpu.VMEM((order, order), jnp.float32),
        ],
        compiler_params=PARAMS,
        name="powers",
    )(start, edge, *got, shifts)
    half_type = jax.ShapeDtypeStruct((points * order, cols), jnp.bfloat16)
    high_part, low_part = pl.pallas_call(
        split_kernel,
        out_shape=(half_type, half_type),
        in_specs=[VMEM],
        out_specs=(VMEM, VMEM),
        compiler_params=PARAMS,
        cost_estimate=pl.CostEstimate(flops=0, bytes_accessed=8 * points * order * cols, transcendentals=0),
        name="split",
    )(basis)
    points_in_all = points * cols
    steps = []
    for axis in ("gx", "gy", "gz"):
        size = lax.axis_size(axis)
        points_in_all *= size
        steps += [(axis, 1 << bit) for bit in range(axis == "gz", size.bit_length() - 1)]
    assert lax.axis_size("gz") % 2 == 0
    across = [(i, i ^ 1) for i in range(lax.axis_size("gz"))]
    own = keep + lax.ppermute(send, "gz", across)
    own = doubled(own, (steps, steps[len(steps) // 2 :] + steps[: len(steps) // 2]))
    other = lax.ppermute(own, "gz", across)
    upper, basis_q = pl.pallas_call(
        functools.partial(finish_kernel, count=float(points_in_all), step=8),
        out_shape=(float_of(order, order), float_of(order, points, cols)),
        in_specs=[VMEM] * 4,
        out_specs=(VMEM, HBM),
        scratch_shapes=[pltpu.VMEM((order * points, cols), jnp.float32), pltpu.SemaphoreType.DMA((layers,))],
        compiler_params=PARAMS,
        name="finish",
    )(own, other, high_part, low_part)
    return basis_q.reshape(order, layers, rows, cols), upper


def solution(mesh):
    in_specs = (
        P(None, "gz", "gx", "gy"),
        P("gz", "gx", "gy"),
        P("gz", "gx", "gy"),
        P("gz", "gx", "gy"),
        P("gz", "gx", "gy"),
        P(),
    )
    out_specs = (P(None, "gz", "gx", "gy"), P())
    return jax.shard_map(local, mesh=mesh, in_specs=in_specs, out_specs=out_specs, check_vma=False)
```

```python
import functools

import jax
import jax.numpy as jnp
from jax import lax
from jax.experimental import pallas as pl
from jax.experimental.pallas import tpu as pltpu
from jax.sharding import PartitionSpec as P

POWERS = 4


newton_shifts = (15.4, 0.6, 11.7, 4.3)
basis_scale = 0.125

VMEM = pl.BlockSpec(memory_space=pltpu.VMEM)
SMEM = pl.BlockSpec(memory_space=pltpu.SMEM)
HBM = pl.BlockSpec(memory_space=pltpu.HBM)
PARAMS = pltpu.CompilerParams(vmem_limit_bytes=32 * 1024 * 1024)
FIRST = pltpu.CompilerParams(vmem_limit_bytes=60 * 1024 * 1024)

COEFS = 4
TILE = 8
CORNERS = ((1, 3), (1, 2), (1, 1), (2, 2), (2, 1), (3, 1))


def positions(shape):
    sub = lax.broadcasted_iota(jnp.int32, shape, 0)
    lane = lax.broadcasted_iota(jnp.int32, shape, 1)
    return sub, lane


def coefs_at(ref, start, i):
    place = start + COEFS * (i // 2) * 2
    tile = ref[place : place + TILE, :]
    return pltpu.roll(tile, COEFS, 0) if i % 2 else tile


def edges_kernel(
    load_ref, rows_ref, cols_ref, vias_ref, ground_ref, offset_ref,
    first_ref, second_ref, tile_ref, flat_ref, shift_ref, fields_in, coefs_in, sems,
):
    slabs, _, cols = tile_ref.shape
    fields = load_ref.shape[0] // slabs
    layers, rows, _ = rows_ref.shape
    depth = POWERS
    half = rows // 2
    total_layers = offset_ref.shape[0]
    copies = [
        pltpu.make_async_copy(ref, coefs_in.at[i], sems.at[i])
        for i, ref in enumerate((rows_ref, cols_ref, vias_ref, ground_ref))
    ]
    copies.append(pltpu.make_async_copy(load_ref, fields_in, sems.at[COEFS]))
    for copy in copies:
        copy.start()
    gx, gy, gz = (lax.axis_index(name) for name in ("gx", "gy", "gz"))
    last_row = jnp.where(gx == lax.axis_size("gx") - 1, rows - 1, rows)
    last_col = jnp.where(gy == lax.axis_size("gy") - 1, cols - 1, cols)
    sub, lane = positions((TILE, cols))
    for e in range(shift_ref.shape[0]):
        layer = gz * layers + e - depth
        inside = (layer >= 0) & (layer < total_layers)
        value = jnp.where(inside, offset_ref[jnp.clip(layer, 0, total_layers - 1)], 0)
        shift_ref[e] = jnp.broadcast_to(value, (TILE, cols))
    for copy in copies:
        copy.wait()

    def joined(one, two):
        return jnp.where(sub < COEFS, one, pltpu.roll(two, COEFS, 0))

    for l in range(layers):
        layer = gz * layers + l
        target = gy * cols + lane + shift_ref[depth + l]
        via_ok = (target >= 0) & (target < cols * lax.axis_size("gy"))
        via_ok = via_ok & (jnp.broadcast_to(layer, lane.shape) < total_layers - 1)
        four = (
            jnp.where(sub == last_row, 0.0, coefs_in[0, l]),
            jnp.where(lane == last_col, 0.0, coefs_in[1, l]),
            jnp.where(via_ok, coefs_in[2, l], 0.0),
            coefs_in[3, l],
        )
        for r in range(rows):
            slab = l * rows + r
            value = jnp.zeros((TILE, cols), jnp.float32)
            for c in range(COEFS):
                value = jnp.where(sub == c, jnp.broadcast_to(four[c][r : r + 1, :], (TILE, cols)), value)
            tile_ref[slab] = value
    for i in range(0, slabs, 2):
        flat_ref[COEFS * i : COEFS * i + TILE, :] = joined(tile_ref[i], tile_ref[i + 1])
    even = lax.rem(gx, 2) == 0
    for ref, start in ((first_ref, jnp.where(even, half, 0)), (second_ref, jnp.where(even, 0, half))):
        for l in range(layers):
            for i in range(half):
                slab = l * rows + start + i
                at = l * half + i
                for f in range(0, fields, TILE):
                    tile = fields_in[pl.ds(f * slabs + slab, TILE, stride=slabs), :]
                    ref[at * fields + f : at * fields + f + TILE, :] = tile
                if i % 2 == 0:
                    place = layers * half * fields + COEFS * at
                    ref[place : place + TILE, :] = joined(tile_ref[slab], tile_ref[slab + 1])


def own_kernel(load_ref, tile_ref, block_ref):
    slabs, planes, _ = block_ref.shape
    for slab in range(slabs):
        for f in range(0, planes - TILE, TILE):
            block_ref[slab, f : f + TILE, :] = load_ref[pl.ds(f * slabs + slab, TILE, stride=slabs), :]
        block_ref[slab, planes - TILE :, :] = tile_ref[slab]


def corners_kernel(first_ref, second_ref, flat_ref, after_ref, before_ref, one_ref, two_ref, *, layers):
    slabs, planes, cols = after_ref.shape
    fields = planes - TILE
    half = slabs // layers
    count = len(CORNERS)
    sub, _ = positions((TILE, cols))
    even_row = jnp.broadcast_to(lax.rem(lax.axis_index("gx"), 2), (TILE, cols)) == 0
    even_layer = jnp.broadcast_to(lax.rem(lax.axis_index("gz"), 2), (TILE, cols)) == 0
    for f in range(0, planes, TILE):
        after, before = [], []
        for i in range(slabs):
            if f < fields:
                first, second = (ref[i * fields + f : i * fields + f + TILE, :] for ref in (first_ref, second_ref))
            else:
                first, second = (coefs_at(ref, slabs * fields, i) for ref in (first_ref, second_ref))
            after.append(jnp.where(even_row, second, first))
            before.append(jnp.where(even_row, first, second))
            after_ref[i, f : f + TILE, :] = after[i]
            before_ref[i, f : f + TILE, :] = before[i]
        ones, twos = [], []
        for source, step in ((after, -1), (before, 1)):
            for dz, dx in CORNERS:
                row = half - dx if step < 0 else dx - 1
                up, down = source[(layers - dz) * half + row], source[(dz - 1) * half + row]
                ones.append(jnp.where(even_layer, up, down))
                twos.append(jnp.where(even_layer, down, up))
        for ref, values in ((one_ref, ones), (two_ref, twos)):
            if f < fields:
                for i, value in enumerate(values):
                    ref[i * fields + f : i * fields + f + TILE, :] = value
            else:
                for i in range(0, 2 * count, 2):
                    place = 2 * count * fields + COEFS * i
                    pair = jnp.where(sub < COEFS, values[i], pltpu.roll(values[i + 1], COEFS, 0))
                    ref[place : place + TILE, :] = pair
    for ref in (one_ref, two_ref):
        place = 2 * count * planes - 2 * count * (TILE - COEFS)
        ref[place : place + flat_ref.shape[0], :] = flat_ref[...]


def slabs_of(e, layers, rows, planes, corners, inner, block, after, before, one, two, corner_one=None, corner_two=None):
    depth, half, count = POWERS, rows // 2, len(CORNERS)
    cols = block.shape[2] if block is not None else corner_one.shape[1]
    fields, slabs = planes - TILE, layers * rows

    def plain(ref, slab):
        return lambda f: ref[slab, f : f + TILE, :]

    def chosen(read, one, two):
        even = jnp.broadcast_to(lax.rem(lax.axis_index("gz"), 2), (TILE, cols)) == 0
        return lambda f: jnp.where(even, read(one, f), read(two, f))

    def home(slab):
        return lambda ref, f: ref[pl.ds(f * slabs + slab, TILE, stride=slabs), :]

    def home_coefs(slab):
        return lambda ref, f: coefs_at(ref, 2 * count * (fields + COEFS), slab)

    def corner(i):
        def read(ref, f):
            if f < fields:
                return ref[i * fields + f : i * fields + f + TILE, :]
            return coefs_at(ref, 2 * count * fields, i)

        return read

    tiles = [f for f in range(0, planes, TILE)]
    found = []
    if depth <= e < depth + layers:
        l = e - depth
        if inner:
            found += [(depth + r, plain(block, l * rows + r), tiles) for r in range(rows)]
            for i in range(half):
                found.append((i, plain(after, l * half + i), tiles))
                found.append((depth + rows + i, plain(before, l * half + i), tiles))
        return found
    if e < depth:
        pair, corner_pair, first, distance = (two, one), (corner_two, corner_one), 0, depth - e
    else:
        pair, corner_pair = (one, two), (corner_one, corner_two)
        first, distance = depth + layers, e - depth - layers + 1
    for r in range(rows):
        slab = (e - first) * rows + r
        if inner:
            found.append((depth + r, chosen(home(slab), *pair), tiles[:-1]))
        if corners:
            found.append((depth + r, chosen(home_coefs(slab), *corner_pair), tiles[-1:]))
    for i, (dz, dx) in enumerate(CORNERS):
        if dz == distance and corners:
            found.append((depth - dx, chosen(corner(i), *corner_pair), tiles))
            found.append((depth + rows - 1 + dx, chosen(corner(count + i), *corner_pair), tiles))
    return found


def inner_kernel(*refs, layers, rows):
    sources, edge_ref = refs[:5], refs[5]
    high, planes, cols = edge_ref.shape
    depth = POWERS
    group = 2 * depth
    _, lane = positions((TILE, cols))
    for e in range(high):
        found = slabs_of(e, layers, rows, planes, False, True, *sources)
        for f in range(0, planes, TILE):
            total = jnp.zeros((TILE, cols), jnp.float32)
            for row, read, tiles in found:
                if f in tiles:
                    moved = pltpu.roll(read(f), (group * row + depth) % cols, 1)
                    total = jnp.where((lane >= group * row) & (lane < group * row + group), moved, total)
            edge_ref[e, f : f + TILE, :] = total


def sides_kernel(inner_ref, one_ref, two_ref, edge_ref, *out_refs, layers, rows, pair):
    high, planes, cols = edge_ref.shape
    depth = POWERS
    group = 2 * depth
    _, lane = positions((TILE, cols))
    early = lax.rem(lane, group) < depth
    gy = jnp.broadcast_to(lax.axis_index("gy"), (TILE, cols))
    for f in range(0, planes, TILE):
        here = slice(f, f + TILE)
        edges = []
        for e in range(high):
            total = inner_ref[e, here, :]
            for row, read, tiles in slabs_of(e, layers, rows, planes, True, False, None, None, None, None, None, one_ref, two_ref):
                if f in tiles:
                    moved = pltpu.roll(read(f), (group * row + depth) % cols, 1)
                    total = jnp.where((lane >= group * row) & (lane < group * row + group), moved, total)
            edge_ref[e, here, :] = total
            edges.append(total)
        for t in range(high // 2):
            one, two = edges[2 * t], edges[2 * t + 1]
            up = jnp.where(early, one, pltpu.roll(two, depth, 1))
            down = jnp.where(early, pltpu.roll(one, cols - depth, 1), two)
            if pair:
                out_refs[0][t, here, :] = jnp.where(gy == 0, up, down)
            else:
                out_refs[0][t, here, :] = up
                out_refs[1][t, here, :] = down


def assemble_kernel(*refs, layers, rows):
    sources, start_ref = refs[:7], refs[7]
    high, _, planes, _ = start_ref.shape
    for e in range(high):
        for row, read, tiles in slabs_of(e, layers, rows, planes, True, True, *sources):
            for f in tiles:
                start_ref[e, row, f : f + TILE, :] = read(f)


def powers_kernel(*refs, fields, layers, rows, pair):
    gots = 1 if pair else 2
    start_ref, edge_ref, got_refs, shift_ref = refs[0], refs[1], refs[2 : 2 + gots], refs[2 + gots]
    basis_ref, gram_ref, power_ref, coef_ref, strip_ref, strip_coef_ref, border_ref, sum_ref = refs[3 + gots :]
    high, tall, planes, cols = start_ref.shape
    depth = POWERS
    group = 2 * depth
    order = depth * fields
    tiles = range(0, fields, TILE)
    _, lane = positions((TILE, cols))
    gy = lax.axis_index("gy")

    def masks(e):
        shift = shift_ref[e]
        return shift == 0, shift > 0

    def from_above(seen, mask):
        left, centre, right = seen
        return jnp.where(mask[0], centre, jnp.where(mask[1], right, left))

    def from_below(seen, mask):
        left, centre, right = seen
        return jnp.where(mask[0], centre, jnp.where(mask[1], left, right))

    def around(tile):
        return pltpu.roll(tile, 1, 1), tile, pltpu.roll(tile, cols - 1, 1)

    def spread(tile, c):
        return jnp.broadcast_to(tile[c : c + 1, :], (TILE, cols))

    def put_factors(put, tile, row_above, seen, seen_below, mask):
        down, right, upper, ground = (spread(tile, c) for c in range(COEFS))
        up = spread(row_above, 0)
        left = spread(seen[0], 1)
        lower = from_below([spread(x, 2) for x in seen_below], mask)
        diagonal = ground + down + up + right + left + upper + lower
        for i, value in enumerate((down, up, right, left, upper, lower, diagonal)):
            put(i, value * basis_scale)

    def step(factors, theta, seen, up, down, above, below):
        value = (factors[6] - theta) * seen[1]
        value = value - (factors[0] * down + factors[1] * up)
        value = value - (factors[2] * seen[2] + factors[3] * seen[0])
        return value - (factors[4] * above + factors[5] * below)

    thetas = [shift * basis_scale for shift in newton_shifts]

    early = lax.rem(lane, group) < depth
    if pair:
        first_side = jnp.where(gy == 0, 1, 0)
        last_side = first_side + 1
    else:
        first_side, last_side = 0, 2

    @pl.loop(first_side, last_side)
    def _(side):
        left_side = jnp.broadcast_to(side, (TILE, cols)) == 0
        from_edge = early != left_side
        for e in range(high):
            for f in range(0, planes, TILE):
                here = slice(f, f + TILE)
                outer = got_refs[0][e // 2, here, :]
                if not pair:
                    outer = jnp.where(left_side, outer, got_refs[1][e // 2, here, :])
                if e % 2 == 0:
                    outer = jnp.where(left_side, outer, pltpu.roll(outer, depth, 1))
                else:
                    outer = jnp.where(left_side, pltpu.roll(outer, cols - depth, 1), outer)
                strip_ref[side, 0, e, here, :] = jnp.where(from_edge, edge_ref[e, here, :], outer)
        raw = [strip_ref[side, 0, e, fields : fields + TILE, :] for e in range(high)]
        seen = [around(tile) for tile in raw]
        for e in range(1, high - 1):

            def put(i, value, e=e):
                strip_coef_ref[side, i, e] = value

            put_factors(put, raw[e], pltpu.roll(raw[e], group, 1), seen[e], seen[e - 1], masks(e - 1))
        for k in range(1, depth):
            reach = depth - k
            looks = {}

            def look(e, f, k=k, looks=looks):
                if (e, f) not in looks:
                    looks[e, f] = around(strip_ref[side, k - 1, e, f : f + TILE, :])
                return looks[e, f]

            for e in range(depth - reach, depth + layers + reach):
                factors = [strip_coef_ref[side, i, e] for i in range(7)]
                over, under = masks(e), masks(e - 1)
                for f in tiles:
                    here = look(e, f)
                    strip_ref[side, k, e, f : f + TILE, :] = step(
                        factors,
                        thetas[k - 1],
                        here,
                        pltpu.roll(here[1], group, 1),
                        pltpu.roll(here[1], cols - group, 1),
                        from_above(look(e + 1, f), over),
                        from_below(look(e - 1, f), under),
                    )

    gy_lane = jnp.broadcast_to(gy, (TILE, cols))
    on_left = (lax.rem(lane, group) == depth - 1) & (gy_lane > 0)
    on_right = (lax.rem(lane, group) == depth - 2) & (gy_lane < lax.axis_size("gy") - 1)

    @pl.loop(0, high)
    def _(e):
        for k in range(depth):
            for f in range(0, planes if k == 0 else fields, TILE):
                here = slice(f, f + TILE)
                right = jnp.where(on_right, pltpu.roll(strip_ref[1, k, e, here, :], cols - 2, 1), 0.0)
                border_ref[k, e, here, :] = jnp.where(on_left, strip_ref[0, k, e, here, :], right)

    leftmost, rightmost = lane == 0, lane == cols - 1

    def looked(k, e, row, f):
        here = slice(f, f + TILE)
        tile = start_ref[e, row, here, :] if k == 0 else power_ref[k - 1, e, row, here, :]
        turn = (2 * cols - group * row - depth + 1) % cols if isinstance(row, int) else lax.rem(2 * cols - group * row - depth + 1, cols)
        outer = pltpu.roll(border_ref[k, e, here, :], turn, 1)
        left, _, right = around(tile)
        return jnp.where(leftmost, outer, left), tile, jnp.where(rightmost, outer, right)

    def by_rows(reach, body):
        @pl.loop(0, rows, unroll=4)
        def _(r):
            body(depth + r, depth - reach, depth + layers + reach)

        for dx in range(1, reach + 1):
            for row in (depth - dx, depth + rows - 1 + dx):
                body(row, depth - reach + dx, depth + layers + reach - dx)

    def factors_of_row(row, first, last):
        seen = {e: looked(0, e, row, fields) for e in range(first - 1, last)}
        for e in range(first, last):

            def put(i, value, e=e):
                coef_ref[i, e, row] = value

            above_row = start_ref[e, row - 1, fields : fields + TILE, :]
            put_factors(put, seen[e][1], above_row, seen[e], seen[e - 1], masks(e - 1))

    by_rows(depth - 1, factors_of_row)

    for k in range(1, depth + 1):

        def advance(row, first, last, k=k):
            source = start_ref if k == 1 else power_ref.at[k - 2]
            below = {f: from_below(looked(k - 1, first - 1, row, f), masks(first - 1)) for f in tiles}
            centre = {f: looked(k - 1, first, row, f) for f in tiles}
            for e in range(first, last):
                factors = [coef_ref[i, e, row] for i in range(7)]
                mask = masks(e)
                for f in tiles:
                    here = slice(f, f + TILE)
                    upper = looked(k - 1, e + 1, row, f)
                    value = step(
                        factors,
                        thetas[k - 1],
                        centre[f],
                        source[e, row - 1, here, :],
                        source[e, row + 1, here, :],
                        from_above(upper, mask),
                        below[f],
                    )
                    below[f], centre[f] = from_below(centre[f], mask), upper
                    if k < depth:
                        power_ref[k - 1, e, row, here, :] = value
                    if first == k and depth <= e < depth + layers:
                        slab = (e - depth) * rows + row - depth
                        place = pl.multiple_of(slab * order + (k - 1) * fields + f, TILE)
                        basis_ref[pl.ds(place, TILE), :] = value

        if k < depth:
            by_rows(depth - k, advance)

    def share(r):
        value = None
        for l in range(0, layers, 2):
            places = [pl.multiple_of(((l + i) * rows + r) * order, TILE) for i in range(2)]
            wide = jnp.concatenate([basis_ref[pl.ds(place, order), :] for place in places], axis=1)
            product = lax.dot_general(
                wide, wide, (((1,), (1,)), ((), ())),
                precision=lax.Precision.HIGHEST, preferred_element_type=jnp.float32,
            )
            value = product if value is None else value + product
        return value

    advance(depth, depth, depth + layers)
    sum_ref[...] = jnp.zeros_like(sum_ref)

    @pl.loop(1, rows)
    def _(r):
        product = share(r - 1)
        advance(depth + r, depth, depth + layers)
        sum_ref[...] += product

    total = sum_ref[...] + share(rows - 1)
    gram_ref[...] = total


def eliminate(tiles, order, step):
    width = tiles[0].shape[1]
    lane = lax.broadcasted_iota(jnp.int32, (8, width), 1)
    sub = lax.broadcasted_iota(jnp.int32, (8, width), 0)
    spread = lambda value: jnp.broadcast_to(value, (8, width))
    for first in range(0, order, step):
        home, base = first // 8, first % 8
        panel = tiles[home]
        entry = {}
        for i in range(step):
            for j in range(i, step):
                entry[i, j] = spread(panel[base + i : base + i + 1, first + j : first + j + 1])
        rows = [spread(panel[base + i : base + i + 1, :]) for i in range(step)]
        inverse = []
        done = []
        for i in range(step):
            row = rows[i]
            if i:
                row = jnp.where((lane >= first) & (lane < first + i), 0.0, row)
            factors = []
            for j in range(i):
                factor = entry[j, i] * inverse[j]
                factors.append(factor)
            for j in range(i):
                source = jnp.where(lane == first + j, 1.0, done[j])
                if i - j > 1:
                    source = jnp.where((lane > first + j) & (lane < first + i), 0.0, source)
                row = row - factors[j] * source
                for m in range(i, step):
                    entry[i, m] = entry[i, m] - factors[j] * entry[j, m]
            inverse.append(1.0 / entry[i, i])
            done.append(row)
        sources = []
        for j in range(step):
            source = jnp.where(lane == first + j, 1.0, done[j])
            if j < step - 1:
                source = jnp.where((lane > first + j) & (lane < first + step), 0.0, source)
            sources.append(source)
        inside = (lane >= first) & (lane < first + step)
        for t in range(home, order // 8):
            if t == home and base + step == 8:
                fresh = tiles[t]
            else:
                columns = [spread(tiles[t][:, first + j : first + j + 1]) for j in range(step)]
                fresh = jnp.where(inside, 0.0, tiles[t])
                for j in range(step):
                    factor = columns[j] * inverse[j]
                    fresh = fresh - factor * sources[j]
                    for m in range(j + 1, step):
                        columns[m] = columns[m] - factor * entry[j, m]
            if t == home:
                fresh = jnp.where(sub < base + step, tiles[t], fresh)
                for j in range(step):
                    fresh = jnp.where(sub == base + j, done[j], fresh)
            tiles[t] = fresh
    return tiles


def finish_kernel(*refs, count, step):
    own_ref, other_ref, high_ref, low_ref, upper_ref, out_ref, staged, sems = refs
    order = upper_ref.shape[0]
    points = high_ref.shape[0] // order
    even = jnp.broadcast_to(lax.rem(lax.axis_index("gz"), 2), (TILE, order)) == 0
    tiles = []
    for r in range(0, order, TILE):
        tiles.append(jnp.where(even, other_ref[r : r + TILE, :], own_ref[r : r + TILE, :]) / count)
    tiles = eliminate(tiles, order, step)
    lane = lax.broadcasted_iota(jnp.int32, (8, order), 1)
    sub = lax.broadcasted_iota(jnp.int32, (8, order), 0)
    inverse = []
    for t in range(order // 8):
        row = sub + 8 * t
        pivot = jnp.sum(jnp.where(lane == row, tiles[t], 0.0), axis=1, keepdims=True)
        scale = 1.0 / jnp.sqrt(pivot)
        upper_ref[8 * t : 8 * t + 8, :] = jnp.where(lane >= row, tiles[t] * scale, 0.0)
        inverse.append(jnp.where(lane < row, tiles[t], jnp.where(lane == row, 1.0, 0.0)) * scale)
    inverse = jnp.concatenate(inverse, axis=0)
    cols = high_ref.shape[1]
    inverse_parts = two_parts(inverse)
    chunk = points // sems.shape[0]
    copies = []
    for i in range(0, points, 2):
        start = i * order
        wide = [
            jnp.concatenate([ref[start : start + order, :], ref[start + order : start + 2 * order, :]], axis=1)
            for ref in (high_ref, low_ref)
        ]
        out = product(inverse_parts, wide)
        staged[pl.ds(i, order, stride=points), :] = out[:, :cols]
        staged[pl.ds(i + 1, order, stride=points), :] = out[:, cols:]
        if (i + 2) % chunk == 0:
            part = pl.ds(i + 2 - chunk, chunk)
            source = staged.reshape(order, points, cols).at[:, part, :]
            copies.append(pltpu.make_async_copy(source, out_ref.at[:, part, :], sems.at[i // chunk]))
            copies[-1].start()
    for copy in copies:
        copy.wait()


def split_kernel(basis_ref, high_ref, low_ref):
    size = 2 * TILE

    @pl.loop(0, basis_ref.shape[0] // size, unroll=8)
    def _(i):
        here = pl.ds(pl.multiple_of(i * size, size), size)
        high_ref[here, :], low_ref[here, :] = two_parts(basis_ref[here, :])


def two_parts(value):
    high = value.astype(jnp.bfloat16)
    return high, (value - high.astype(jnp.float32)).astype(jnp.bfloat16)


def product(left, right):
    dot = functools.partial(jnp.dot, preferred_element_type=jnp.float32)
    return dot(left[0], right[0]) + (dot(left[0], right[1]) + dot(left[1], right[0]))


def doubled(value, steps):
    axes = ("gx", "gy", "gz")
    sizes = [lax.axis_size(name) for name in axes]
    assert all(size & (size - 1) == 0 for size in sizes)

    def index(place):
        return (place[0] * sizes[1] + place[1]) * sizes[2] + place[2]

    for axis, mask in steps:
        pairs = []
        for x in range(sizes[0]):
            for y in range(sizes[1]):
                for z in range(1, sizes[2], 2):
                    partner = [x, y, z]
                    partner[axes.index(axis)] ^= mask
                    pairs.append((index((x, y, z)), index(partner)))
        value = value + lax.ppermute(value, axes, pairs)
    return value


def swapped(value, axis, phase):
    pairs = []
    for i in range(phase, lax.axis_size(axis) - 1, 2):
        pairs += [(i, i + 1), (i + 1, i)]
    return lax.ppermute(value, axis, pairs)


def sent(value, steps):
    axes = tuple(steps)
    sizes = [lax.axis_size(name) for name in axes]
    pairs = []
    if len(axes) == 1:
        pairs = [(i, i + steps[axes[0]]) for i in range(sizes[0]) if 0 <= i + steps[axes[0]] < sizes[0]]
        return lax.ppermute(value, axes[0], pairs)
    for i in range(sizes[0]):
        for j in range(sizes[1]):
            m, n = i + steps[axes[0]], j + steps[axes[1]]
            if 0 <= m < sizes[0] and 0 <= n < sizes[1]:
                pairs.append((i * sizes[1] + j, m * sizes[1] + n))
    return lax.ppermute(value, axes, pairs)


def local(load_currents, cond_rows, cond_cols, cond_vias, ground, via_offset):
    fields, layers, rows, cols = load_currents.shape
    depth = POWERS
    assert layers == depth and rows == 2 * depth and cols == 4 * depth * rows and fields % TILE == 0
    float_of = lambda *shape: jax.ShapeDtypeStruct(shape, jnp.float32)
    pair = lax.axis_size("gy") == 2
    planes = fields + TILE
    slabs = layers * rows
    high = layers + 2 * depth
    tall = rows + 2 * depth
    count = len(CORNERS)
    part = float_of(slabs // 2, planes, cols)
    flat_rows = (slabs // 2) * (fields + COEFS)
    corner_rows = 2 * count * (fields + COEFS) + slabs * COEFS
    raw = load_currents.reshape(fields * slabs, cols)
    one = swapped(raw, "gz", 0)
    two = swapped(raw, "gz", 1)
    first, second, coef_tiles, coef_rows, shifts = pl.pallas_call(
        edges_kernel,
        out_shape=(
            float_of(flat_rows, cols),
            float_of(flat_rows, cols),
            float_of(slabs, TILE, cols),
            float_of(slabs * COEFS, cols),
            jax.ShapeDtypeStruct((high, TILE, cols), jnp.int32),
        ),
        in_specs=[HBM] * 5 + [SMEM],
        out_specs=(VMEM,) * 5,
        scratch_shapes=[
            pltpu.VMEM((fields * slabs, cols), jnp.float32),
            pltpu.VMEM((COEFS, layers, rows, cols), jnp.float32),
            pltpu.SemaphoreType.DMA((COEFS + 1,)),
        ],
        compiler_params=FIRST,
        name="edges",
    )(raw, cond_rows, cond_cols, cond_vias, ground, via_offset)
    first, second = swapped(first, "gx", 0), swapped(second, "gx", 1)
    block = pl.pallas_call(
        own_kernel,
        out_shape=float_of(slabs, planes, cols),
        in_specs=[VMEM] * 2,
        out_specs=VMEM,
        compiler_params=PARAMS,
        cost_estimate=pl.CostEstimate(flops=0, bytes_accessed=8 * slabs * planes * cols, transcendentals=0),
        name="own",
    )(raw, coef_tiles)
    after, before, to_first, to_second = pl.pallas_call(
        functools.partial(corners_kernel, layers=layers),
        out_shape=(part, part) + (float_of(corner_rows, cols),) * 2,
        in_specs=[VMEM] * 3,
        out_specs=(VMEM,) * 4,
        compiler_params=PARAMS,
        name="corners",
    )(first, second, coef_rows)
    to_first, to_second = swapped(to_first, "gz", 0), swapped(to_second, "gz", 1)
    pieces = (block, after, before, one, two)
    inner = pl.pallas_call(
        functools.partial(inner_kernel, layers=layers, rows=rows),
        out_shape=float_of(high, planes, cols),
        in_specs=[VMEM] * 5,
        out_specs=VMEM,
        compiler_params=PARAMS,
        cost_estimate=pl.CostEstimate(flops=0, bytes_accessed=16 * slabs * planes * cols, transcendentals=0),
        name="inner",
    )(*pieces)
    edge, *outer = pl.pallas_call(
        functools.partial(sides_kernel, layers=layers, rows=rows, pair=pair),
        out_shape=(float_of(high, planes, cols),) + (float_of(high // 2, planes, cols),) * (1 if pair else 2),
        in_specs=[VMEM] * 3,
        out_specs=(VMEM,) * (2 if pair else 3),
        compiler_params=PARAMS,
        name="sides",
    )(inner, to_first, to_second)
    pieces += (to_first, to_second)
    if pair:
        got = [lax.ppermute(outer[0], "gy", [(0, 1), (1, 0)])]
    else:
        got = [sent(outer[0], {"gy": 1}), sent(outer[1], {"gy": -1})]
    start = pl.pallas_call(
        functools.partial(assemble_kernel, layers=layers, rows=rows),
        out_shape=float_of(high, tall, planes, cols),
        in_specs=[VMEM] * 7,
        out_specs=VMEM,
        compiler_params=PARAMS,
        cost_estimate=pl.CostEstimate(flops=0, bytes_accessed=2 * high * tall * planes * cols, transcendentals=0),
        name="assemble",
    )(*pieces)
    order = depth * fields
    points = slabs
    basis, gram = pl.pallas_call(
        functools.partial(powers_kernel, fields=fields, layers=layers, rows=rows, pair=pair),
        out_shape=(float_of(points * order, cols), float_of(order, order)),
        in_specs=[VMEM] * (3 + len(got)),
        out_specs=(VMEM,) * 2,
        scratch_shapes=[
            pltpu.VMEM((depth - 1, high, tall, fields, cols), jnp.float32),
            pltpu.VMEM((7, high, tall, TILE, cols), jnp.float32),
            pltpu.VMEM((2, depth, high, planes, cols), jnp.float32),
            pltpu.VMEM((2, 7, high, TILE, cols), jnp.float32),
            pltpu.VMEM((depth, high, planes, cols), jnp.float32),
            pltpu.VMEM((order, order), jnp.float32),
        ],
        compiler_params=PARAMS,
        name="powers",
    )(start, edge, *got, shifts)
    half_type = jax.ShapeDtypeStruct((points * order, cols), jnp.bfloat16)
    high_part, low_part = pl.pallas_call(
        split_kernel,
        out_shape=(half_type, half_type),
        in_specs=[VMEM],
        out_specs=(VMEM, VMEM),
        compiler_params=PARAMS,
        cost_estimate=pl.CostEstimate(flops=0, bytes_accessed=8 * points * order * cols, transcendentals=0),
        name="split",
    )(basis)
    points_in_all = points * cols
    steps = []
    for axis in ("gx", "gy", "gz"):
        size = lax.axis_size(axis)
        points_in_all *= size
        steps += [(axis, 1 << bit) for bit in range(axis == "gz", size.bit_length() - 1)]
    assert lax.axis_size("gz") % 2 == 0
    to_odd = [(i, i + 1) for i in range(0, lax.axis_size("gz"), 2)]
    own = doubled(gram + lax.ppermute(gram, "gz", to_odd), steps)
    other = lax.ppermute(own, "gz", [(j, i) for i, j in to_odd])
    upper, basis_q = pl.pallas_call(
        functools.partial(finish_kernel, count=float(points_in_all), step=8),
        out_shape=(float_of(order, order), float_of(order, points, cols)),
        in_specs=[VMEM] * 4,
        out_specs=(VMEM, HBM),
        scratch_shapes=[pltpu.VMEM((order * points, cols), jnp.float32), pltpu.SemaphoreType.DMA((layers,))],
        compiler_params=PARAMS,
        name="finish",
    )(own, other, high_part, low_part)
    return basis_q.reshape(order, layers, rows, cols), upper


def solution(mesh):
    in_specs = (
        P(None, "gz", "gx", "gy"),
        P("gz", "gx", "gy"),
        P("gz", "gx", "gy"),
        P("gz", "gx", "gy"),
        P("gz", "gx", "gy"),
        P(),
    )
    out_specs = (P(None, "gz", "gx", "gy"), P())
    return jax.shard_map(local, mesh=mesh, in_specs=in_specs, out_specs=out_specs, check_vma=False)
```

```python
import functools

import jax
import jax.numpy as jnp
from jax import lax
from jax.experimental import pallas as pl
from jax.experimental.pallas import tpu as pltpu
from jax.sharding import PartitionSpec as P

POWERS = 4


newton_shifts = (15.4, 0.6, 11.7, 4.3)
basis_scale = 0.125

VMEM = pl.BlockSpec(memory_space=pltpu.VMEM)
SMEM = pl.BlockSpec(memory_space=pltpu.SMEM)
HBM = pl.BlockSpec(memory_space=pltpu.HBM)
PARAMS = pltpu.CompilerParams(vmem_limit_bytes=32 * 1024 * 1024)
FIRST = pltpu.CompilerParams(vmem_limit_bytes=60 * 1024 * 1024)

COEFS = 4
TILE = 8
CORNERS = ((1, 3), (1, 2), (1, 1), (2, 2), (2, 1), (3, 1))


def positions(shape):
    sub = lax.broadcasted_iota(jnp.int32, shape, 0)
    lane = lax.broadcasted_iota(jnp.int32, shape, 1)
    return sub, lane


def coefs_at(ref, start, i):
    place = start + COEFS * (i // 2) * 2
    tile = ref[place : place + TILE, :]
    return pltpu.roll(tile, COEFS, 0) if i % 2 else tile


def edges_kernel(
    load_ref, rows_ref, cols_ref, vias_ref, ground_ref, offset_ref,
    first_ref, second_ref, tile_ref, flat_ref, shift_ref, fields_in, coefs_in, sems,
):
    slabs, _, cols = tile_ref.shape
    fields = load_ref.shape[0] // slabs
    layers, rows, _ = rows_ref.shape
    depth = POWERS
    half = rows // 2
    total_layers = offset_ref.shape[0]
    copies = [
        pltpu.make_async_copy(ref, coefs_in.at[i], sems.at[i])
        for i, ref in enumerate((rows_ref, cols_ref, vias_ref, ground_ref))
    ]
    copies.append(pltpu.make_async_copy(load_ref, fields_in, sems.at[COEFS]))
    for copy in copies:
        copy.start()
    gx, gy, gz = (lax.axis_index(name) for name in ("gx", "gy", "gz"))
    last_row = jnp.where(gx == lax.axis_size("gx") - 1, rows - 1, rows)
    last_col = jnp.where(gy == lax.axis_size("gy") - 1, cols - 1, cols)
    sub, lane = positions((TILE, cols))
    for e in range(shift_ref.shape[0]):
        layer = gz * layers + e - depth
        inside = (layer >= 0) & (layer < total_layers)
        value = jnp.where(inside, offset_ref[jnp.clip(layer, 0, total_layers - 1)], 0)
        shift_ref[e] = jnp.broadcast_to(value, (TILE, cols))
    for copy in copies:
        copy.wait()

    def joined(one, two):
        return jnp.where(sub < COEFS, one, pltpu.roll(two, COEFS, 0))

    for l in range(layers):
        layer = gz * layers + l
        target = gy * cols + lane + shift_ref[depth + l]
        via_ok = (target >= 0) & (target < cols * lax.axis_size("gy"))
        via_ok = via_ok & (jnp.broadcast_to(layer, lane.shape) < total_layers - 1)
        four = (
            jnp.where(sub == last_row, 0.0, coefs_in[0, l]),
            jnp.where(lane == last_col, 0.0, coefs_in[1, l]),
            jnp.where(via_ok, coefs_in[2, l], 0.0),
            coefs_in[3, l],
        )
        for r in range(rows):
            slab = l * rows + r
            value = jnp.zeros((TILE, cols), jnp.float32)
            for c in range(COEFS):
                value = jnp.where(sub == c, jnp.broadcast_to(four[c][r : r + 1, :], (TILE, cols)), value)
            tile_ref[slab] = value
    for i in range(0, slabs, 2):
        flat_ref[COEFS * i : COEFS * i + TILE, :] = joined(tile_ref[i], tile_ref[i + 1])
    even = lax.rem(gx, 2) == 0
    for ref, start in ((first_ref, jnp.where(even, half, 0)), (second_ref, jnp.where(even, 0, half))):
        for l in range(layers):
            for i in range(half):
                slab = l * rows + start + i
                at = l * half + i
                for f in range(0, fields, TILE):
                    tile = fields_in[pl.ds(f * slabs + slab, TILE, stride=slabs), :]
                    ref[at * fields + f : at * fields + f + TILE, :] = tile
                if i % 2 == 0:
                    place = layers * half * fields + COEFS * at
                    ref[place : place + TILE, :] = joined(tile_ref[slab], tile_ref[slab + 1])


def own_kernel(load_ref, tile_ref, block_ref):
    slabs, planes, _ = block_ref.shape
    for slab in range(slabs):
        for f in range(0, planes - TILE, TILE):
            block_ref[slab, f : f + TILE, :] = load_ref[pl.ds(f * slabs + slab, TILE, stride=slabs), :]
        block_ref[slab, planes - TILE :, :] = tile_ref[slab]


def corners_kernel(first_ref, second_ref, flat_ref, after_ref, before_ref, one_ref, two_ref, *, layers):
    slabs, planes, cols = after_ref.shape
    fields = planes - TILE
    half = slabs // layers
    count = len(CORNERS)
    sub, _ = positions((TILE, cols))
    even_row = jnp.broadcast_to(lax.rem(lax.axis_index("gx"), 2), (TILE, cols)) == 0
    even_layer = jnp.broadcast_to(lax.rem(lax.axis_index("gz"), 2), (TILE, cols)) == 0
    row_block = jnp.broadcast_to(lax.axis_index("gx"), (TILE, cols))
    has_prev, has_next = row_block > 0, row_block < lax.axis_size("gx") - 1
    for f in range(0, planes, TILE):
        after, before = [], []
        for i in range(slabs):
            if f < fields:
                first, second = (ref[i * fields + f : i * fields + f + TILE, :] for ref in (first_ref, second_ref))
            else:
                first, second = (coefs_at(ref, slabs * fields, i) for ref in (first_ref, second_ref))
            after.append(jnp.where(has_prev, jnp.where(even_row, second, first), 0.0))
            before.append(jnp.where(has_next, jnp.where(even_row, first, second), 0.0))
            after_ref[i, f : f + TILE, :] = after[i]
            before_ref[i, f : f + TILE, :] = before[i]
        ones, twos = [], []
        for source, step in ((after, -1), (before, 1)):
            for dz, dx in CORNERS:
                row = half - dx if step < 0 else dx - 1
                up, down = source[(layers - dz) * half + row], source[(dz - 1) * half + row]
                ones.append(jnp.where(even_layer, up, down))
                twos.append(jnp.where(even_layer, down, up))
        for ref, values in ((one_ref, ones), (two_ref, twos)):
            if f < fields:
                for i, value in enumerate(values):
                    ref[i * fields + f : i * fields + f + TILE, :] = value
            else:
                for i in range(0, 2 * count, 2):
                    place = 2 * count * fields + COEFS * i
                    pair = jnp.where(sub < COEFS, values[i], pltpu.roll(values[i + 1], COEFS, 0))
                    ref[place : place + TILE, :] = pair
    for ref in (one_ref, two_ref):
        place = 2 * count * planes - 2 * count * (TILE - COEFS)
        ref[place : place + flat_ref.shape[0], :] = flat_ref[...]


def slabs_of(e, layers, rows, planes, corners, inner, block, after, before, one, two, corner_one=None, corner_two=None):
    depth, half, count = POWERS, rows // 2, len(CORNERS)
    cols = block.shape[2] if block is not None else corner_one.shape[1]
    fields, slabs = planes - TILE, layers * rows

    def plain(ref, slab):
        return lambda f: ref[slab, f : f + TILE, :]

    def chosen(read, one, two):
        place = jnp.broadcast_to(lax.axis_index("gz"), (TILE, cols))
        even = lax.rem(place, 2) == 0
        there = place > 0 if e < depth else place < lax.axis_size("gz") - 1
        return lambda f: jnp.where(there, jnp.where(even, read(one, f), read(two, f)), 0.0)

    def home(slab):
        return lambda ref, f: ref[pl.ds(f * slabs + slab, TILE, stride=slabs), :]

    def home_coefs(slab):
        return lambda ref, f: coefs_at(ref, 2 * count * (fields + COEFS), slab)

    def corner(i):
        def read(ref, f):
            if f < fields:
                return ref[i * fields + f : i * fields + f + TILE, :]
            return coefs_at(ref, 2 * count * fields, i)

        return read

    tiles = [f for f in range(0, planes, TILE)]
    found = []
    if depth <= e < depth + layers:
        l = e - depth
        if inner:
            found += [(depth + r, plain(block, l * rows + r), tiles) for r in range(rows)]
            for i in range(half):
                found.append((i, plain(after, l * half + i), tiles))
                found.append((depth + rows + i, plain(before, l * half + i), tiles))
        return found
    if e < depth:
        pair, corner_pair, first, distance = (two, one), (corner_two, corner_one), 0, depth - e
    else:
        pair, corner_pair = (one, two), (corner_one, corner_two)
        first, distance = depth + layers, e - depth - layers + 1
    for r in range(rows):
        slab = (e - first) * rows + r
        if inner:
            found.append((depth + r, chosen(home(slab), *pair), tiles[:-1]))
        if corners:
            found.append((depth + r, chosen(home_coefs(slab), *corner_pair), tiles[-1:]))
    for i, (dz, dx) in enumerate(CORNERS):
        if dz == distance and corners:
            found.append((depth - dx, chosen(corner(i), *corner_pair), tiles))
            found.append((depth + rows - 1 + dx, chosen(corner(count + i), *corner_pair), tiles))
    return found


def inner_kernel(*refs, layers, rows):
    sources, edge_ref = refs[:5], refs[5]
    high, planes, cols = edge_ref.shape
    depth = POWERS
    group = 2 * depth
    _, lane = positions((TILE, cols))
    for e in range(high):
        found = slabs_of(e, layers, rows, planes, False, True, *sources)
        for f in range(0, planes, TILE):
            total = jnp.zeros((TILE, cols), jnp.float32)
            for row, read, tiles in found:
                if f in tiles:
                    moved = pltpu.roll(read(f), (group * row + depth) % cols, 1)
                    total = jnp.where((lane >= group * row) & (lane < group * row + group), moved, total)
            edge_ref[e, f : f + TILE, :] = total


def sides_kernel(inner_ref, one_ref, two_ref, edge_ref, *out_refs, layers, rows, pair):
    high, planes, cols = edge_ref.shape
    depth = POWERS
    group = 2 * depth
    _, lane = positions((TILE, cols))
    early = lax.rem(lane, group) < depth
    gy = jnp.broadcast_to(lax.axis_index("gy"), (TILE, cols))
    for f in range(0, planes, TILE):
        here = slice(f, f + TILE)
        edges = []
        for e in range(high):
            total = inner_ref[e, here, :]
            for row, read, tiles in slabs_of(e, layers, rows, planes, True, False, None, None, None, None, None, one_ref, two_ref):
                if f in tiles:
                    moved = pltpu.roll(read(f), (group * row + depth) % cols, 1)
                    total = jnp.where((lane >= group * row) & (lane < group * row + group), moved, total)
            edge_ref[e, here, :] = total
            edges.append(total)
        for t in range(high // 2):
            one, two = edges[2 * t], edges[2 * t + 1]
            up = jnp.where(early, one, pltpu.roll(two, depth, 1))
            down = jnp.where(early, pltpu.roll(one, cols - depth, 1), two)
            if pair:
                out_refs[0][t, here, :] = jnp.where(gy == 0, up, down)
            else:
                out_refs[0][t, here, :] = up
                out_refs[1][t, here, :] = down


def assemble_kernel(*refs, layers, rows):
    sources, start_ref = refs[:7], refs[7]
    high, _, planes, _ = start_ref.shape
    for e in range(high):
        for row, read, tiles in slabs_of(e, layers, rows, planes, True, True, *sources):
            for f in tiles:
                start_ref[e, row, f : f + TILE, :] = read(f)


def powers_kernel(*refs, fields, layers, rows, pair):
    gots = 1 if pair else 2
    start_ref, edge_ref, got_refs, shift_ref = refs[0], refs[1], refs[2 : 2 + gots], refs[2 + gots]
    basis_ref, keep_ref, send_ref, power_ref, coef_ref, strip_ref, strip_coef_ref, border_ref, sum_ref = refs[3 + gots :]
    high, tall, planes, cols = start_ref.shape
    depth = POWERS
    group = 2 * depth
    order = depth * fields
    tiles = range(0, fields, TILE)
    _, lane = positions((TILE, cols))
    gy = lax.axis_index("gy")

    def masks(e):
        shift = shift_ref[e]
        return shift == 0, shift > 0

    def from_above(seen, mask):
        left, centre, right = seen
        return jnp.where(mask[0], centre, jnp.where(mask[1], right, left))

    def from_below(seen, mask):
        left, centre, right = seen
        return jnp.where(mask[0], centre, jnp.where(mask[1], left, right))

    def around(tile):
        return pltpu.roll(tile, 1, 1), tile, pltpu.roll(tile, cols - 1, 1)

    def spread(tile, c):
        return jnp.broadcast_to(tile[c : c + 1, :], (TILE, cols))

    def put_factors(put, tile, row_above, seen, seen_below, mask):
        down, right, upper, ground = (spread(tile, c) for c in range(COEFS))
        up = spread(row_above, 0)
        left = spread(seen[0], 1)
        lower = from_below([spread(x, 2) for x in seen_below], mask)
        diagonal = ground + down + up + right + left + upper + lower
        for i, value in enumerate((down, up, right, left, upper, lower, diagonal)):
            put(i, value * basis_scale)

    def step(factors, theta, seen, up, down, above, below):
        value = (factors[6] - theta) * seen[1]
        value = value - (factors[0] * down + factors[1] * up)
        value = value - (factors[2] * seen[2] + factors[3] * seen[0])
        return value - (factors[4] * above + factors[5] * below)

    thetas = [shift * basis_scale for shift in newton_shifts]

    early = lax.rem(lane, group) < depth
    if pair:
        first_side = jnp.where(gy == 0, 1, 0)
        last_side = first_side + 1
    else:
        first_side, last_side = 0, 2

    @pl.loop(first_side, last_side)
    def _(side):
        left_side = jnp.broadcast_to(side, (TILE, cols)) == 0
        from_edge = early != left_side
        for e in range(high):
            for f in range(0, planes, TILE):
                here = slice(f, f + TILE)
                outer = got_refs[0][e // 2, here, :]
                if not pair:
                    outer = jnp.where(left_side, outer, got_refs[1][e // 2, here, :])
                if e % 2 == 0:
                    outer = jnp.where(left_side, outer, pltpu.roll(outer, depth, 1))
                else:
                    outer = jnp.where(left_side, pltpu.roll(outer, cols - depth, 1), outer)
                strip_ref[side, 0, e, here, :] = jnp.where(from_edge, edge_ref[e, here, :], outer)
        raw = [strip_ref[side, 0, e, fields : fields + TILE, :] for e in range(high)]
        seen = [around(tile) for tile in raw]
        for e in range(1, high - 1):

            def put(i, value, e=e):
                strip_coef_ref[side, i, e] = value

            put_factors(put, raw[e], pltpu.roll(raw[e], group, 1), seen[e], seen[e - 1], masks(e - 1))
        for k in range(1, depth):
            reach = depth - k
            looks = {}

            def look(e, f, k=k, looks=looks):
                if (e, f) not in looks:
                    looks[e, f] = around(strip_ref[side, k - 1, e, f : f + TILE, :])
                return looks[e, f]

            for e in range(depth - reach, depth + layers + reach):
                factors = [strip_coef_ref[side, i, e] for i in range(7)]
                over, under = masks(e), masks(e - 1)
                for f in tiles:
                    here = look(e, f)
                    strip_ref[side, k, e, f : f + TILE, :] = step(
                        factors,
                        thetas[k - 1],
                        here,
                        pltpu.roll(here[1], group, 1),
                        pltpu.roll(here[1], cols - group, 1),
                        from_above(look(e + 1, f), over),
                        from_below(look(e - 1, f), under),
                    )

    gy_lane = jnp.broadcast_to(gy, (TILE, cols))
    on_left = (lax.rem(lane, group) == depth - 1) & (gy_lane > 0)
    on_right = (lax.rem(lane, group) == depth - 2) & (gy_lane < lax.axis_size("gy") - 1)

    @pl.loop(0, high)
    def _(e):
        for k in range(depth):
            for f in range(0, planes if k == 0 else fields, TILE):
                here = slice(f, f + TILE)
                right = jnp.where(on_right, pltpu.roll(strip_ref[1, k, e, here, :], cols - 2, 1), 0.0)
                border_ref[k, e, here, :] = jnp.where(on_left, strip_ref[0, k, e, here, :], right)

    leftmost, rightmost = lane == 0, lane == cols - 1

    def looked(k, e, row, f):
        here = slice(f, f + TILE)
        tile = start_ref[e, row, here, :] if k == 0 else power_ref[k - 1, e, row, here, :]
        turn = (2 * cols - group * row - depth + 1) % cols if isinstance(row, int) else lax.rem(2 * cols - group * row - depth + 1, cols)
        outer = pltpu.roll(border_ref[k, e, here, :], turn, 1)
        left, _, right = around(tile)
        return jnp.where(leftmost, outer, left), tile, jnp.where(rightmost, outer, right)

    def by_rows(reach, body):
        @pl.loop(0, rows, unroll=4)
        def _(r):
            body(depth + r, depth - reach, depth + layers + reach)

        for dx in range(1, reach + 1):
            for row in (depth - dx, depth + rows - 1 + dx):
                body(row, depth - reach + dx, depth + layers + reach - dx)

    def factors_of_row(row, first, last):
        seen = {e: looked(0, e, row, fields) for e in range(first - 1, last)}
        for e in range(first, last):

            def put(i, value, e=e):
                coef_ref[i, e, row] = value

            above_row = start_ref[e, row - 1, fields : fields + TILE, :]
            put_factors(put, seen[e][1], above_row, seen[e], seen[e - 1], masks(e - 1))

    by_rows(depth - 1, factors_of_row)

    for k in range(1, depth + 1):

        def advance(row, first, last, k=k):
            source = start_ref if k == 1 else power_ref.at[k - 2]
            below = {f: from_below(looked(k - 1, first - 1, row, f), masks(first - 1)) for f in tiles}
            centre = {f: looked(k - 1, first, row, f) for f in tiles}
            for e in range(first, last):
                factors = [coef_ref[i, e, row] for i in range(7)]
                mask = masks(e)
                for f in tiles:
                    here = slice(f, f + TILE)
                    upper = looked(k - 1, e + 1, row, f)
                    value = step(
                        factors,
                        thetas[k - 1],
                        centre[f],
                        source[e, row - 1, here, :],
                        source[e, row + 1, here, :],
                        from_above(upper, mask),
                        below[f],
                    )
                    below[f], centre[f] = from_below(centre[f], mask), upper
                    if k < depth:
                        power_ref[k - 1, e, row, here, :] = value
                    if first == k and depth <= e < depth + layers:
                        slab = (e - depth) * rows + row - depth
                        place = pl.multiple_of(slab * order + (k - 1) * fields + f, TILE)
                        basis_ref[pl.ds(place, TILE), :] = value

        if k < depth:
            by_rows(depth - k, advance)

    def share(r):
        value = None
        for l in range(0, layers, 2):
            places = [pl.multiple_of(((l + i) * rows + r) * order, TILE) for i in range(2)]
            wide = jnp.concatenate([basis_ref[pl.ds(place, order), :] for place in places], axis=1)
            product = lax.dot_general(
                wide, wide, (((1,), (1,)), ((), ())),
                precision=lax.Precision.HIGHEST, preferred_element_type=jnp.float32,
            )
            value = product if value is None else value + product
        return value

    advance(depth, depth, depth + layers)
    sum_ref[...] = jnp.zeros_like(sum_ref)

    @pl.loop(1, rows)
    def _(r):
        product = share(r - 1)
        advance(depth + r, depth, depth + layers)
        sum_ref[...] += product

    total = sum_ref[...] + share(rows - 1)
    sum_ref[...] = total
    half = order // 2
    odd = lax.rem(lax.axis_index("gz"), 2)
    keep_ref[...] = sum_ref[pl.ds(pl.multiple_of(odd * half, TILE), half), :]
    send_ref[...] = sum_ref[pl.ds(pl.multiple_of((1 - odd) * half, TILE), half), :]


def eliminate(tiles, order, step):
    width = tiles[0].shape[1]
    lane = lax.broadcasted_iota(jnp.int32, (8, width), 1)
    sub = lax.broadcasted_iota(jnp.int32, (8, width), 0)
    spread = lambda value: jnp.broadcast_to(value, (8, width))
    for first in range(0, order, step):
        home, base = first // 8, first % 8
        panel = tiles[home]
        entry = {}
        for i in range(step):
            for j in range(i, step):
                entry[i, j] = spread(panel[base + i : base + i + 1, first + j : first + j + 1])
        rows = [spread(panel[base + i : base + i + 1, :]) for i in range(step)]
        inverse = []
        done = []
        for i in range(step):
            row = rows[i]
            if i:
                row = jnp.where((lane >= first) & (lane < first + i), 0.0, row)
            factors = []
            for j in range(i):
                factor = entry[j, i] * inverse[j]
                factors.append(factor)
            for j in range(i):
                source = jnp.where(lane == first + j, 1.0, done[j])
                if i - j > 1:
                    source = jnp.where((lane > first + j) & (lane < first + i), 0.0, source)
                row = row - factors[j] * source
                for m in range(i, step):
                    entry[i, m] = entry[i, m] - factors[j] * entry[j, m]
            inverse.append(1.0 / entry[i, i])
            done.append(row)
        sources = []
        for j in range(step):
            source = jnp.where(lane == first + j, 1.0, done[j])
            if j < step - 1:
                source = jnp.where((lane > first + j) & (lane < first + step), 0.0, source)
            sources.append(source)
        inside = (lane >= first) & (lane < first + step)
        for t in range(home, order // 8):
            if t == home and base + step == 8:
                fresh = tiles[t]
            else:
                columns = [spread(tiles[t][:, first + j : first + j + 1]) for j in range(step)]
                fresh = jnp.where(inside, 0.0, tiles[t])
                for j in range(step):
                    factor = columns[j] * inverse[j]
                    fresh = fresh - factor * sources[j]
                    for m in range(j + 1, step):
                        columns[m] = columns[m] - factor * entry[j, m]
            if t == home:
                fresh = jnp.where(sub < base + step, tiles[t], fresh)
                for j in range(step):
                    fresh = jnp.where(sub == base + j, done[j], fresh)
            tiles[t] = fresh
    return tiles


def finish_kernel(*refs, count, step):
    own_ref, other_ref, high_ref, low_ref, upper_ref, out_ref, staged, sems = refs
    order = upper_ref.shape[0]
    points = high_ref.shape[0] // order
    even = jnp.broadcast_to(lax.rem(lax.axis_index("gz"), 2), (TILE, order)) == 0
    halves = [[], []]
    for r in range(0, order // 2, TILE):
        own, other = own_ref[r : r + TILE, :] / count, other_ref[r : r + TILE, :] / count
        halves[0].append(jnp.where(even, own, other))
        halves[1].append(jnp.where(even, other, own))
    tiles = eliminate(halves[0] + halves[1], order, step)
    lane = lax.broadcasted_iota(jnp.int32, (8, order), 1)
    sub = lax.broadcasted_iota(jnp.int32, (8, order), 0)
    inverse = []
    for t in range(order // 8):
        row = sub + 8 * t
        pivot = jnp.sum(jnp.where(lane == row, tiles[t], 0.0), axis=1, keepdims=True)
        scale = 1.0 / jnp.sqrt(pivot)
        upper_ref[8 * t : 8 * t + 8, :] = jnp.where(lane >= row, tiles[t] * scale, 0.0)
        inverse.append(jnp.where(lane < row, tiles[t], jnp.where(lane == row, 1.0, 0.0)) * scale)
    inverse = jnp.concatenate(inverse, axis=0)
    cols = high_ref.shape[1]
    inverse_parts = two_parts(inverse)
    chunk = points // sems.shape[0]
    copies = []
    for i in range(0, points, 2):
        start = i * order
        wide = [
            jnp.concatenate([ref[start : start + order, :], ref[start + order : start + 2 * order, :]], axis=1)
            for ref in (high_ref, low_ref)
        ]
        out = product(inverse_parts, wide)
        staged[pl.ds(i, order, stride=points), :] = out[:, :cols]
        staged[pl.ds(i + 1, order, stride=points), :] = out[:, cols:]
        if (i + 2) % chunk == 0:
            part = pl.ds(i + 2 - chunk, chunk)
            source = staged.reshape(order, points, cols).at[:, part, :]
            copies.append(pltpu.make_async_copy(source, out_ref.at[:, part, :], sems.at[i // chunk]))
            copies[-1].start()
    for copy in copies:
        copy.wait()


def split_kernel(basis_ref, high_ref, low_ref):
    size = 2 * TILE

    @pl.loop(0, basis_ref.shape[0] // size, unroll=8)
    def _(i):
        here = pl.ds(pl.multiple_of(i * size, size), size)
        high_ref[here, :], low_ref[here, :] = two_parts(basis_ref[here, :])


def two_parts(value):
    high = value.astype(jnp.bfloat16)
    return high, (value - high.astype(jnp.float32)).astype(jnp.bfloat16)


def product(left, right):
    dot = functools.partial(jnp.dot, preferred_element_type=jnp.float32)
    return dot(left[0], right[0]) + (dot(left[0], right[1]) + dot(left[1], right[0]))


def doubled(value, steps_of):
    axes = ("gx", "gy", "gz")
    sizes = [lax.axis_size(name) for name in axes]
    assert all(size & (size - 1) == 0 for size in sizes)

    def index(place):
        return (place[0] * sizes[1] + place[1]) * sizes[2] + place[2]

    for r in range(len(steps_of[0])):
        pairs = []
        for x in range(sizes[0]):
            for y in range(sizes[1]):
                for z in range(sizes[2]):
                    axis, mask = steps_of[z % 2][r]
                    partner = [x, y, z]
                    partner[axes.index(axis)] ^= mask
                    pairs.append((index((x, y, z)), index(partner)))
        value = value + lax.ppermute(value, axes, pairs)
    return value


def swapped(value, axis, phase):
    pairs = []
    for i in range(phase, lax.axis_size(axis) - 1, 2):
        pairs += [(i, i + 1), (i + 1, i)]
    paired = {i for i, _ in pairs}
    pairs += [(i, i) for i in range(lax.axis_size(axis)) if i not in paired]
    return lax.ppermute(value, axis, pairs)


def sent(value, steps):
    axes = tuple(steps)
    sizes = [lax.axis_size(name) for name in axes]
    pairs = []
    if len(axes) == 1:
        pairs = [(i, i + steps[axes[0]]) for i in range(sizes[0]) if 0 <= i + steps[axes[0]] < sizes[0]]
        return lax.ppermute(value, axes[0], pairs)
    for i in range(sizes[0]):
        for j in range(sizes[1]):
            m, n = i + steps[axes[0]], j + steps[axes[1]]
            if 0 <= m < sizes[0] and 0 <= n < sizes[1]:
                pairs.append((i * sizes[1] + j, m * sizes[1] + n))
    return lax.ppermute(value, axes, pairs)


def local(load_currents, cond_rows, cond_cols, cond_vias, ground, via_offset):
    fields, layers, rows, cols = load_currents.shape
    depth = POWERS
    assert layers == depth and rows == 2 * depth and cols == 4 * depth * rows and fields % TILE == 0
    float_of = lambda *shape: jax.ShapeDtypeStruct(shape, jnp.float32)
    pair = lax.axis_size("gy") == 2
    planes = fields + TILE
    slabs = layers * rows
    high = layers + 2 * depth
    tall = rows + 2 * depth
    count = len(CORNERS)
    part = float_of(slabs // 2, planes, cols)
    flat_rows = (slabs // 2) * (fields + COEFS)
    corner_rows = 2 * count * (fields + COEFS) + slabs * COEFS
    raw = load_currents.reshape(fields * slabs, cols)
    one = swapped(raw, "gz", 0)
    two = swapped(raw, "gz", 1)
    first, second, coef_tiles, coef_rows, shifts = pl.pallas_call(
        edges_kernel,
        out_shape=(
            float_of(flat_rows, cols),
            float_of(flat_rows, cols),
            float_of(slabs, TILE, cols),
            float_of(slabs * COEFS, cols),
            jax.ShapeDtypeStruct((high, TILE, cols), jnp.int32),
        ),
        in_specs=[HBM] * 5 + [SMEM],
        out_specs=(VMEM,) * 5,
        scratch_shapes=[
            pltpu.VMEM((fields * slabs, cols), jnp.float32),
            pltpu.VMEM((COEFS, layers, rows, cols), jnp.float32),
            pltpu.SemaphoreType.DMA((COEFS + 1,)),
        ],
        compiler_params=FIRST,
        name="edges",
    )(raw, cond_rows, cond_cols, cond_vias, ground, via_offset)
    first, second = swapped(first, "gx", 0), swapped(second, "gx", 1)
    block = pl.pallas_call(
        own_kernel,
        out_shape=float_of(slabs, planes, cols),
        in_specs=[VMEM] * 2,
        out_specs=VMEM,
        compiler_params=PARAMS,
        cost_estimate=pl.CostEstimate(flops=0, bytes_accessed=8 * slabs * planes * cols, transcendentals=0),
        name="own",
    )(raw, coef_tiles)
    after, before, to_first, to_second = pl.pallas_call(
        functools.partial(corners_kernel, layers=layers),
        out_shape=(part, part) + (float_of(corner_rows, cols),) * 2,
        in_specs=[VMEM] * 3,
        out_specs=(VMEM,) * 4,
        compiler_params=PARAMS,
        name="corners",
    )(first, second, coef_rows)
    to_first, to_second = swapped(to_first, "gz", 0), swapped(to_second, "gz", 1)
    pieces = (block, after, before, one, two)
    inner = pl.pallas_call(
        functools.partial(inner_kernel, layers=layers, rows=rows),
        out_shape=float_of(high, planes, cols),
        in_specs=[VMEM] * 5,
        out_specs=VMEM,
        compiler_params=PARAMS,
        cost_estimate=pl.CostEstimate(flops=0, bytes_accessed=16 * slabs * planes * cols, transcendentals=0),
        name="inner",
    )(*pieces)
    edge, *outer = pl.pallas_call(
        functools.partial(sides_kernel, layers=layers, rows=rows, pair=pair),
        out_shape=(float_of(high, planes, cols),) + (float_of(high // 2, planes, cols),) * (1 if pair else 2),
        in_specs=[VMEM] * 3,
        out_specs=(VMEM,) * (2 if pair else 3),
        compiler_params=PARAMS,
        name="sides",
    )(inner, to_first, to_second)
    pieces += (to_first, to_second)
    if pair:
        got = [lax.ppermute(outer[0], "gy", [(0, 1), (1, 0)])]
    else:
        got = [sent(outer[0], {"gy": 1}), sent(outer[1], {"gy": -1})]
    start = pl.pallas_call(
        functools.partial(assemble_kernel, layers=layers, rows=rows),
        out_shape=float_of(high, tall, planes, cols),
        in_specs=[VMEM] * 7,
        out_specs=VMEM,
        compiler_params=PARAMS,
        cost_estimate=pl.CostEstimate(flops=0, bytes_accessed=2 * high * tall * planes * cols, transcendentals=0),
        name="assemble",
    )(*pieces)
    order = depth * fields
    points = slabs
    basis, keep, send = pl.pallas_call(
        functools.partial(powers_kernel, fields=fields, layers=layers, rows=rows, pair=pair),
        out_shape=(float_of(points * order, cols),) + (float_of(order // 2, order),) * 2,
        in_specs=[VMEM] * (3 + len(got)),
        out_specs=(VMEM,) * 3,
        scratch_shapes=[
            pltpu.VMEM((depth - 1, high, tall, fields, cols), jnp.float32),
            pltpu.VMEM((7, high, tall, TILE, cols), jnp.float32),
            pltpu.VMEM((2, depth, high, planes, cols), jnp.float32),
            pltpu.VMEM((2, 7, high, TILE, cols), jnp.float32),
            pltpu.VMEM((depth, high, planes, cols), jnp.float32),
            pltpu.VMEM((order, order), jnp.float32),
        ],
        compiler_params=PARAMS,
        name="powers",
    )(start, edge, *got, shifts)
    half_type = jax.ShapeDtypeStruct((points * order, cols), jnp.bfloat16)
    high_part, low_part = pl.pallas_call(
        split_kernel,
        out_shape=(half_type, half_type),
        in_specs=[VMEM],
        out_specs=(VMEM, VMEM),
        compiler_params=PARAMS,
        cost_estimate=pl.CostEstimate(flops=0, bytes_accessed=8 * points * order * cols, transcendentals=0),
        name="split",
    )(basis)
    points_in_all = points * cols
    steps = []
    for axis in ("gx", "gy", "gz"):
        size = lax.axis_size(axis)
        points_in_all *= size
        steps += [(axis, 1 << bit) for bit in range(axis == "gz", size.bit_length() - 1)]
    assert lax.axis_size("gz") % 2 == 0
    across = [(i, i ^ 1) for i in range(lax.axis_size("gz"))]
    own = keep + lax.ppermute(send, "gz", across)
    own = doubled(own, (steps, steps[len(steps) // 2 :] + steps[: len(steps) // 2]))
    other = lax.ppermute(own, "gz", across)
    upper, basis_q = pl.pallas_call(
        functools.partial(finish_kernel, count=float(points_in_all), step=8),
        out_shape=(float_of(order, order), float_of(order, points, cols)),
        in_specs=[VMEM] * 4,
        out_specs=(VMEM, HBM),
        scratch_shapes=[pltpu.VMEM((order * points, cols), jnp.float32), pltpu.SemaphoreType.DMA((layers,))],
        compiler_params=PARAMS,
        name="finish",
    )(own, other, high_part, low_part)
    return basis_q.reshape(order, layers, rows, cols), upper


def solution(mesh):
    in_specs = (
        P(None, "gz", "gx", "gy"),
        P("gz", "gx", "gy"),
        P("gz", "gx", "gy"),
        P("gz", "gx", "gy"),
        P("gz", "gx", "gy"),
        P(),
    )
    out_specs = (P(None, "gz", "gx", "gy"), P())
    return jax.shard_map(local, mesh=mesh, in_specs=in_specs, out_specs=out_specs, check_vma=False)
```

```python
import functools

import jax
import jax.numpy as jnp
from jax import lax
from jax.experimental import pallas as pl
from jax.experimental.pallas import tpu as pltpu
from jax.sharding import PartitionSpec as P

POWERS = 4


newton_shifts = (15.4, 0.6, 11.7, 4.3)
basis_scale = 0.125

VMEM = pl.BlockSpec(memory_space=pltpu.VMEM)
SMEM = pl.BlockSpec(memory_space=pltpu.SMEM)
HBM = pl.BlockSpec(memory_space=pltpu.HBM)
PARAMS = pltpu.CompilerParams(vmem_limit_bytes=32 * 1024 * 1024)
FIRST = pltpu.CompilerParams(vmem_limit_bytes=60 * 1024 * 1024)

COEFS = 4
TILE = 8
CORNERS = ((1, 3), (1, 2), (1, 1), (2, 2), (2, 1), (3, 1))


def positions(shape):
    sub = lax.broadcasted_iota(jnp.int32, shape, 0)
    lane = lax.broadcasted_iota(jnp.int32, shape, 1)
    return sub, lane


def coefs_at(ref, start, i):
    place = start + COEFS * (i // 2) * 2
    tile = ref[place : place + TILE, :]
    return pltpu.roll(tile, COEFS, 0) if i % 2 else tile


def edges_kernel(
    load_ref, rows_ref, cols_ref, vias_ref, ground_ref, offset_ref,
    first_ref, second_ref, tile_ref, flat_ref, shift_ref, fields_in, coefs_in, sems,
):
    slabs, _, cols = tile_ref.shape
    fields = load_ref.shape[0] // slabs
    layers, rows, _ = rows_ref.shape
    depth = POWERS
    half = rows // 2
    total_layers = offset_ref.shape[0]
    copies = [
        pltpu.make_async_copy(ref, coefs_in.at[i], sems.at[i])
        for i, ref in enumerate((rows_ref, cols_ref, vias_ref, ground_ref))
    ]
    copies.append(pltpu.make_async_copy(load_ref, fields_in, sems.at[COEFS]))
    for copy in copies:
        copy.start()
    gx, gy, gz = (lax.axis_index(name) for name in ("gx", "gy", "gz"))
    last_row = jnp.where(gx == lax.axis_size("gx") - 1, rows - 1, rows)
    last_col = jnp.where(gy == lax.axis_size("gy") - 1, cols - 1, cols)
    sub, lane = positions((TILE, cols))
    for e in range(shift_ref.shape[0]):
        layer = gz * layers + e - depth
        inside = (layer >= 0) & (layer < total_layers)
        value = jnp.where(inside, offset_ref[jnp.clip(layer, 0, total_layers - 1)], 0)
        shift_ref[e] = jnp.broadcast_to(value, (TILE, cols))
    for copy in copies:
        copy.wait()

    def joined(one, two):
        return jnp.where(sub < COEFS, one, pltpu.roll(two, COEFS, 0))

    for l in range(layers):
        layer = gz * layers + l
        target = gy * cols + lane + shift_ref[depth + l]
        via_ok = (target >= 0) & (target < cols * lax.axis_size("gy"))
        via_ok = via_ok & (jnp.broadcast_to(layer, lane.shape) < total_layers - 1)
        four = (
            jnp.where(sub == last_row, 0.0, coefs_in[0, l]),
            jnp.where(lane == last_col, 0.0, coefs_in[1, l]),
            jnp.where(via_ok, coefs_in[2, l], 0.0),
            coefs_in[3, l],
        )
        for r in range(rows):
            slab = l * rows + r
            value = jnp.zeros((TILE, cols), jnp.float32)
            for c in range(COEFS):
                value = jnp.where(sub == c, jnp.broadcast_to(four[c][r : r + 1, :], (TILE, cols)), value)
            tile_ref[slab] = value
    for i in range(0, slabs, 2):
        flat_ref[COEFS * i : COEFS * i + TILE, :] = joined(tile_ref[i], tile_ref[i + 1])
    even = lax.rem(gx, 2) == 0
    for ref, start in ((first_ref, jnp.where(even, half, 0)), (second_ref, jnp.where(even, 0, half))):
        for l in range(layers):
            for i in range(half):
                slab = l * rows + start + i
                at = l * half + i
                for f in range(0, fields, TILE):
                    tile = fields_in[pl.ds(f * slabs + slab, TILE, stride=slabs), :]
                    ref[at * fields + f : at * fields + f + TILE, :] = tile
                if i % 2 == 0:
                    place = layers * half * fields + COEFS * at
                    ref[place : place + TILE, :] = joined(tile_ref[slab], tile_ref[slab + 1])


def own_kernel(load_ref, tile_ref, block_ref):
    slabs, planes, _ = block_ref.shape
    for slab in range(slabs):
        for f in range(0, planes - TILE, TILE):
            block_ref[slab, f : f + TILE, :] = load_ref[pl.ds(f * slabs + slab, TILE, stride=slabs), :]
        block_ref[slab, planes - TILE :, :] = tile_ref[slab]


def corners_kernel(first_ref, second_ref, flat_ref, after_ref, before_ref, one_ref, two_ref, *, layers):
    slabs, planes, cols = after_ref.shape
    fields = planes - TILE
    half = slabs // layers
    count = len(CORNERS)
    sub, _ = positions((TILE, cols))
    even_row = jnp.broadcast_to(lax.rem(lax.axis_index("gx"), 2), (TILE, cols)) == 0
    even_layer = jnp.broadcast_to(lax.rem(lax.axis_index("gz"), 2), (TILE, cols)) == 0
    row_block = jnp.broadcast_to(lax.axis_index("gx"), (TILE, cols))
    has_prev, has_next = row_block > 0, row_block < lax.axis_size("gx") - 1
    for f in range(0, planes, TILE):
        after, before = [], []
        for i in range(slabs):
            if f < fields:
                first, second = (ref[i * fields + f : i * fields + f + TILE, :] for ref in (first_ref, second_ref))
            else:
                first, second = (coefs_at(ref, slabs * fields, i) for ref in (first_ref, second_ref))
            after.append(jnp.where(has_prev, jnp.where(even_row, second, first), 0.0))
            before.append(jnp.where(has_next, jnp.where(even_row, first, second), 0.0))
            after_ref[i, f : f + TILE, :] = after[i]
            before_ref[i, f : f + TILE, :] = before[i]
        ones, twos = [], []
        for source, step in ((after, -1), (before, 1)):
            for dz, dx in CORNERS:
                row = half - dx if step < 0 else dx - 1
                up, down = source[(layers - dz) * half + row], source[(dz - 1) * half + row]
                ones.append(jnp.where(even_layer, up, down))
                twos.append(jnp.where(even_layer, down, up))
        for ref, values in ((one_ref, ones), (two_ref, twos)):
            if f < fields:
                for i, value in enumerate(values):
                    ref[i * fields + f : i * fields + f + TILE, :] = value
            else:
                for i in range(0, 2 * count, 2):
                    place = 2 * count * fields + COEFS * i
                    pair = jnp.where(sub < COEFS, values[i], pltpu.roll(values[i + 1], COEFS, 0))
                    ref[place : place + TILE, :] = pair
    for ref in (one_ref, two_ref):
        place = 2 * count * planes - 2 * count * (TILE - COEFS)
        ref[place : place + flat_ref.shape[0], :] = flat_ref[...]


def slabs_of(e, layers, rows, planes, corners, inner, block, after, before, one, two, corner_one=None, corner_two=None):
    depth, half, count = POWERS, rows // 2, len(CORNERS)
    cols = block.shape[2] if block is not None else corner_one.shape[1]
    fields, slabs = planes - TILE, layers * rows

    def plain(ref, slab):
        return lambda f: ref[slab, f : f + TILE, :]

    def chosen(read, one, two):
        place = jnp.broadcast_to(lax.axis_index("gz"), (TILE, cols))
        even = lax.rem(place, 2) == 0
        there = place > 0 if e < depth else place < lax.axis_size("gz") - 1
        return lambda f: jnp.where(there, jnp.where(even, read(one, f), read(two, f)), 0.0)

    def home(slab):
        return lambda ref, f: ref[pl.ds(f * slabs + slab, TILE, stride=slabs), :]

    def home_coefs(slab):
        return lambda ref, f: coefs_at(ref, 2 * count * (fields + COEFS), slab)

    def corner(i):
        def read(ref, f):
            if f < fields:
                return ref[i * fields + f : i * fields + f + TILE, :]
            return coefs_at(ref, 2 * count * fields, i)

        return read

    tiles = [f for f in range(0, planes, TILE)]
    found = []
    if depth <= e < depth + layers:
        l = e - depth
        if inner:
            found += [(depth + r, plain(block, l * rows + r), tiles) for r in range(rows)]
            for i in range(half):
                found.append((i, plain(after, l * half + i), tiles))
                found.append((depth + rows + i, plain(before, l * half + i), tiles))
        return found
    if e < depth:
        pair, corner_pair, first, distance = (two, one), (corner_two, corner_one), 0, depth - e
    else:
        pair, corner_pair = (one, two), (corner_one, corner_two)
        first, distance = depth + layers, e - depth - layers + 1
    for r in range(rows):
        slab = (e - first) * rows + r
        if inner:
            found.append((depth + r, chosen(home(slab), *pair), tiles[:-1]))
        if corners:
            found.append((depth + r, chosen(home_coefs(slab), *corner_pair), tiles[-1:]))
    for i, (dz, dx) in enumerate(CORNERS):
        if dz == distance and corners:
            found.append((depth - dx, chosen(corner(i), *corner_pair), tiles))
            found.append((depth + rows - 1 + dx, chosen(corner(count + i), *corner_pair), tiles))
    return found


def inner_kernel(*refs, layers, rows):
    sources, edge_ref = refs[:5], refs[5]
    high, planes, cols = edge_ref.shape
    depth = POWERS
    group = 2 * depth
    _, lane = positions((TILE, cols))
    for e in range(high):
        found = slabs_of(e, layers, rows, planes, False, True, *sources)
        for f in range(0, planes, TILE):
            total = jnp.zeros((TILE, cols), jnp.float32)
            for row, read, tiles in found:
                if f in tiles:
                    moved = pltpu.roll(read(f), (group * row + depth) % cols, 1)
                    total = jnp.where((lane >= group * row) & (lane < group * row + group), moved, total)
            edge_ref[e, f : f + TILE, :] = total


def sides_kernel(inner_ref, one_ref, two_ref, edge_ref, *out_refs, layers, rows, pair):
    high, planes, cols = edge_ref.shape
    depth = POWERS
    group = 2 * depth
    _, lane = positions((TILE, cols))
    early = lax.rem(lane, group) < depth
    gy = jnp.broadcast_to(lax.axis_index("gy"), (TILE, cols))
    for f in range(0, planes, TILE):
        here = slice(f, f + TILE)
        edges = []
        for e in range(high):
            total = inner_ref[e, here, :]
            for row, read, tiles in slabs_of(e, layers, rows, planes, True, False, None, None, None, None, None, one_ref, two_ref):
                if f in tiles:
                    moved = pltpu.roll(read(f), (group * row + depth) % cols, 1)
                    total = jnp.where((lane >= group * row) & (lane < group * row + group), moved, total)
            edge_ref[e, here, :] = total
            edges.append(total)
        for t in range(high // 2):
            one, two = edges[2 * t], edges[2 * t + 1]
            up = jnp.where(early, one, pltpu.roll(two, depth, 1))
            down = jnp.where(early, pltpu.roll(one, cols - depth, 1), two)
            if pair:
                out_refs[0][t, here, :] = jnp.where(gy == 0, up, down)
            else:
                out_refs[0][t, here, :] = up
                out_refs[1][t, here, :] = down


def assemble_kernel(*refs, layers, rows):
    sources, start_ref = refs[:7], refs[7]
    high, _, planes, _ = start_ref.shape
    for e in range(high):
        for row, read, tiles in slabs_of(e, layers, rows, planes, True, True, *sources):
            for f in tiles:
                start_ref[e, row, f : f + TILE, :] = read(f)


def powers_kernel(*refs, fields, layers, rows, pair):
    gots = 1 if pair else 2
    start_ref, edge_ref, got_refs, shift_ref = refs[0], refs[1], refs[2 : 2 + gots], refs[2 + gots]
    basis_ref, gram_ref, power_ref, coef_ref, strip_ref, strip_coef_ref, border_ref, sum_ref = refs[3 + gots :]
    high, tall, planes, cols = start_ref.shape
    depth = POWERS
    group = 2 * depth
    order = depth * fields
    tiles = range(0, fields, TILE)
    _, lane = positions((TILE, cols))
    gy = lax.axis_index("gy")

    def masks(e):
        shift = shift_ref[e]
        return shift == 0, shift > 0

    def from_above(seen, mask):
        left, centre, right = seen
        return jnp.where(mask[0], centre, jnp.where(mask[1], right, left))

    def from_below(seen, mask):
        left, centre, right = seen
        return jnp.where(mask[0], centre, jnp.where(mask[1], left, right))

    def around(tile):
        return pltpu.roll(tile, 1, 1), tile, pltpu.roll(tile, cols - 1, 1)

    def spread(tile, c):
        return jnp.broadcast_to(tile[c : c + 1, :], (TILE, cols))

    def put_factors(put, tile, row_above, seen, seen_below, mask):
        down, right, upper, ground = (spread(tile, c) for c in range(COEFS))
        up = spread(row_above, 0)
        left = spread(seen[0], 1)
        lower = from_below([spread(x, 2) for x in seen_below], mask)
        diagonal = ground + down + up + right + left + upper + lower
        for i, value in enumerate((down, up, right, left, upper, lower, diagonal)):
            put(i, value * basis_scale)

    def step(factors, theta, seen, up, down, above, below):
        value = (factors[6] - theta) * seen[1]
        value = value - (factors[0] * down + factors[1] * up)
        value = value - (factors[2] * seen[2] + factors[3] * seen[0])
        return value - (factors[4] * above + factors[5] * below)

    thetas = [shift * basis_scale for shift in newton_shifts]

    early = lax.rem(lane, group) < depth
    if pair:
        first_side = jnp.where(gy == 0, 1, 0)
        last_side = first_side + 1
    else:
        first_side, last_side = 0, 2

    @pl.loop(first_side, last_side)
    def _(side):
        left_side = jnp.broadcast_to(side, (TILE, cols)) == 0
        from_edge = early != left_side
        for e in range(high):
            for f in range(0, planes, TILE):
                here = slice(f, f + TILE)
                outer = got_refs[0][e // 2, here, :]
                if not pair:
                    outer = jnp.where(left_side, outer, got_refs[1][e // 2, here, :])
                if e % 2 == 0:
                    outer = jnp.where(left_side, outer, pltpu.roll(outer, depth, 1))
                else:
                    outer = jnp.where(left_side, pltpu.roll(outer, cols - depth, 1), outer)
                strip_ref[side, 0, e, here, :] = jnp.where(from_edge, edge_ref[e, here, :], outer)
        raw = [strip_ref[side, 0, e, fields : fields + TILE, :] for e in range(high)]
        seen = [around(tile) for tile in raw]
        for e in range(1, high - 1):

            def put(i, value, e=e):
                strip_coef_ref[side, i, e] = value

            put_factors(put, raw[e], pltpu.roll(raw[e], group, 1), seen[e], seen[e - 1], masks(e - 1))
        for k in range(1, depth):
            reach = depth - k
            looks = {}

            def look(e, f, k=k, looks=looks):
                if (e, f) not in looks:
                    looks[e, f] = around(strip_ref[side, k - 1, e, f : f + TILE, :])
                return looks[e, f]

            for e in range(depth - reach, depth + layers + reach):
                factors = [strip_coef_ref[side, i, e] for i in range(7)]
                over, under = masks(e), masks(e - 1)
                for f in tiles:
                    here = look(e, f)
                    strip_ref[side, k, e, f : f + TILE, :] = step(
                        factors,
                        thetas[k - 1],
                        here,
                        pltpu.roll(here[1], group, 1),
                        pltpu.roll(here[1], cols - group, 1),
                        from_above(look(e + 1, f), over),
                        from_below(look(e - 1, f), under),
                    )

    gy_lane = jnp.broadcast_to(gy, (TILE, cols))
    on_left = (lax.rem(lane, group) == depth - 1) & (gy_lane > 0)
    on_right = (lax.rem(lane, group) == depth - 2) & (gy_lane < lax.axis_size("gy") - 1)

    @pl.loop(0, high)
    def _(e):
        for k in range(depth):
            for f in range(0, planes if k == 0 else fields, TILE):
                here = slice(f, f + TILE)
                right = jnp.where(on_right, pltpu.roll(strip_ref[1, k, e, here, :], cols - 2, 1), 0.0)
                border_ref[k, e, here, :] = jnp.where(on_left, strip_ref[0, k, e, here, :], right)

    leftmost, rightmost = lane == 0, lane == cols - 1

    def looked(k, e, row, f):
        here = slice(f, f + TILE)
        tile = start_ref[e, row, here, :] if k == 0 else power_ref[k - 1, e, row, here, :]
        turn = (2 * cols - group * row - depth + 1) % cols if isinstance(row, int) else lax.rem(2 * cols - group * row - depth + 1, cols)
        outer = pltpu.roll(border_ref[k, e, here, :], turn, 1)
        left, _, right = around(tile)
        return jnp.where(leftmost, outer, left), tile, jnp.where(rightmost, outer, right)

    def by_rows(reach, body):
        @pl.loop(0, rows, unroll=4)
        def _(r):
            body(depth + r, depth - reach, depth + layers + reach)

        for dx in range(1, reach + 1):
            for row in (depth - dx, depth + rows - 1 + dx):
                body(row, depth - reach + dx, depth + layers + reach - dx)

    def factors_of_row(row, first, last):
        seen = {e: looked(0, e, row, fields) for e in range(first - 1, last)}
        for e in range(first, last):

            def put(i, value, e=e):
                coef_ref[i, e, row] = value

            above_row = start_ref[e, row - 1, fields : fields + TILE, :]
            put_factors(put, seen[e][1], above_row, seen[e], seen[e - 1], masks(e - 1))

    by_rows(depth - 1, factors_of_row)

    for k in range(1, depth + 1):

        def advance(row, first, last, k=k):
            source = start_ref if k == 1 else power_ref.at[k - 2]
            below = {f: from_below(looked(k - 1, first - 1, row, f), masks(first - 1)) for f in tiles}
            centre = {f: looked(k - 1, first, row, f) for f in tiles}
            for e in range(first, last):
                factors = [coef_ref[i, e, row] for i in range(7)]
                mask = masks(e)
                for f in tiles:
                    here = slice(f, f + TILE)
                    upper = looked(k - 1, e + 1, row, f)
                    value = step(
                        factors,
                        thetas[k - 1],
                        centre[f],
                        source[e, row - 1, here, :],
                        source[e, row + 1, here, :],
                        from_above(upper, mask),
                        below[f],
                    )
                    below[f], centre[f] = from_below(centre[f], mask), upper
                    if k < depth:
                        power_ref[k - 1, e, row, here, :] = value
                    if first == k and depth <= e < depth + layers:
                        slab = (e - depth) * rows + row - depth
                        place = pl.multiple_of(slab * order + (k - 1) * fields + f, TILE)
                        basis_ref[pl.ds(place, TILE), :] = value

        if k < depth:
            by_rows(depth - k, advance)

    def share(r):
        value = None
        for l in range(0, layers, 2):
            places = [pl.multiple_of(((l + i) * rows + r) * order, TILE) for i in range(2)]
            wide = jnp.concatenate([basis_ref[pl.ds(place, order), :] for place in places], axis=1)
            product = lax.dot_general(
                wide, wide, (((1,), (1,)), ((), ())),
                precision=lax.Precision.HIGHEST, preferred_element_type=jnp.float32,
            )
            value = product if value is None else value + product
        return value

    advance(depth, depth, depth + layers)
    sum_ref[...] = jnp.zeros_like(sum_ref)

    @pl.loop(1, rows)
    def _(r):
        product = share(r - 1)
        advance(depth + r, depth, depth + layers)
        sum_ref[...] += product

    total = sum_ref[...] + share(rows - 1)
    gram_ref[...] = total


def eliminate(tiles, order, step):
    width = tiles[0].shape[1]
    lane = lax.broadcasted_iota(jnp.int32, (8, width), 1)
    sub = lax.broadcasted_iota(jnp.int32, (8, width), 0)
    spread = lambda value: jnp.broadcast_to(value, (8, width))
    for first in range(0, order, step):
        home, base = first // 8, first % 8
        panel = tiles[home]
        along = [spread(panel[:, first + j : first + j + 1]) for j in range(step)]
        entry = {}
        for i in range(step):
            for j in range(i, step):
                entry[i, j] = spread(along[j][base + i : base + i + 1, :])
        rows = [spread(panel[base + i : base + i + 1, :]) for i in range(step)]
        inverse = []
        done = []
        for i in range(step):
            row = rows[i]
            if i:
                row = jnp.where((lane >= first) & (lane < first + i), 0.0, row)
            factors = []
            for j in range(i):
                factor = entry[j, i] * inverse[j]
                factors.append(factor)
            for j in range(i):
                source = jnp.where(lane == first + j, 1.0, done[j])
                if i - j > 1:
                    source = jnp.where((lane > first + j) & (lane < first + i), 0.0, source)
                row = row - factors[j] * source
                for m in range(i, step):
                    entry[i, m] = entry[i, m] - factors[j] * entry[j, m]
            inverse.append(1.0 / entry[i, i])
            done.append(row)
        sources = []
        for j in range(step):
            source = jnp.where(lane == first + j, 1.0, done[j])
            if j < step - 1:
                source = jnp.where((lane > first + j) & (lane < first + step), 0.0, source)
            sources.append(source)
        inside = (lane >= first) & (lane < first + step)
        for t in range(home, order // 8):
            if t == home and base + step == 8:
                fresh = tiles[t]
            else:
                columns = [spread(tiles[t][:, first + j : first + j + 1]) for j in range(step)]
                fresh = jnp.where(inside, 0.0, tiles[t])
                for j in range(step):
                    factor = columns[j] * inverse[j]
                    fresh = fresh - factor * sources[j]
                    for m in range(j + 1, step):
                        columns[m] = columns[m] - factor * entry[j, m]
            if t == home:
                fresh = jnp.where(sub < base + step, tiles[t], fresh)
                for j in range(step):
                    fresh = jnp.where(sub == base + j, done[j], fresh)
            tiles[t] = fresh
    return tiles


def finish_kernel(*refs, count, step):
    own_ref, other_ref, high_ref, low_ref, upper_ref, out_ref, staged, sems = refs
    order = upper_ref.shape[0]
    points = high_ref.shape[0] // order
    even = jnp.broadcast_to(lax.rem(lax.axis_index("gz"), 2), (TILE, order)) == 0
    tiles = []
    for r in range(0, order, TILE):
        tiles.append(jnp.where(even, other_ref[r : r + TILE, :], own_ref[r : r + TILE, :]) / count)
    tiles = eliminate(tiles, order, step)
    lane = lax.broadcasted_iota(jnp.int32, (8, order), 1)
    sub = lax.broadcasted_iota(jnp.int32, (8, order), 0)
    inverse = []
    for t in range(order // 8):
        row = sub + 8 * t
        pivot = jnp.sum(jnp.where(lane == row, tiles[t], 0.0), axis=1, keepdims=True)
        scale = 1.0 / jnp.sqrt(pivot)
        upper_ref[8 * t : 8 * t + 8, :] = jnp.where(lane >= row, tiles[t] * scale, 0.0)
        inverse.append(jnp.where(lane < row, tiles[t], jnp.where(lane == row, 1.0, 0.0)) * scale)
    inverse = jnp.concatenate(inverse, axis=0)
    cols = high_ref.shape[1]
    inverse_parts = two_parts(inverse)
    chunk = points // sems.shape[0]
    copies = []
    for i in range(0, points, 2):
        start = i * order
        wide = [
            jnp.concatenate([ref[start : start + order, :], ref[start + order : start + 2 * order, :]], axis=1)
            for ref in (high_ref, low_ref)
        ]
        out = product(inverse_parts, wide)
        staged[pl.ds(i, order, stride=points), :] = out[:, :cols]
        staged[pl.ds(i + 1, order, stride=points), :] = out[:, cols:]
        if (i + 2) % chunk == 0:
            part = pl.ds(i + 2 - chunk, chunk)
            source = staged.reshape(order, points, cols).at[:, part, :]
            copies.append(pltpu.make_async_copy(source, out_ref.at[:, part, :], sems.at[i // chunk]))
            copies[-1].start()
    for copy in copies:
        copy.wait()


def split_kernel(basis_ref, high_ref, low_ref):
    size = 2 * TILE

    @pl.loop(0, basis_ref.shape[0] // size, unroll=8)
    def _(i):
        here = pl.ds(pl.multiple_of(i * size, size), size)
        high_ref[here, :], low_ref[here, :] = two_parts(basis_ref[here, :])


def two_parts(value):
    high = value.astype(jnp.bfloat16)
    return high, (value - high.astype(jnp.float32)).astype(jnp.bfloat16)


def product(left, right):
    dot = functools.partial(jnp.dot, preferred_element_type=jnp.float32)
    return dot(left[0], right[0]) + (dot(left[0], right[1]) + dot(left[1], right[0]))


def doubled(value, steps):
    axes = ("gx", "gy", "gz")
    sizes = [lax.axis_size(name) for name in axes]
    assert all(size & (size - 1) == 0 for size in sizes)

    def index(place):
        return (place[0] * sizes[1] + place[1]) * sizes[2] + place[2]

    for axis, mask in steps:
        pairs = []
        for x in range(sizes[0]):
            for y in range(sizes[1]):
                for z in range(sizes[2]):
                    partner = [x, y, z]
                    partner[axes.index(axis)] ^= mask * (z % 2)
                    pairs.append((index((x, y, z)), index(partner)))
        value = value + lax.ppermute(value, axes, pairs)
    return value


def swapped(value, axis, phase):
    pairs = []
    for i in range(phase, lax.axis_size(axis) - 1, 2):
        pairs += [(i, i + 1), (i + 1, i)]
    paired = {i for i, _ in pairs}
    pairs += [(i, i) for i in range(lax.axis_size(axis)) if i not in paired]
    return lax.ppermute(value, axis, pairs)


def sent(value, steps):
    axes = tuple(steps)
    sizes = [lax.axis_size(name) for name in axes]
    pairs = []
    if len(axes) == 1:
        pairs = [(i, i + steps[axes[0]]) for i in range(sizes[0]) if 0 <= i + steps[axes[0]] < sizes[0]]
        return lax.ppermute(value, axes[0], pairs)
    for i in range(sizes[0]):
        for j in range(sizes[1]):
            m, n = i + steps[axes[0]], j + steps[axes[1]]
            if 0 <= m < sizes[0] and 0 <= n < sizes[1]:
                pairs.append((i * sizes[1] + j, m * sizes[1] + n))
    return lax.ppermute(value, axes, pairs)


def local(load_currents, cond_rows, cond_cols, cond_vias, ground, via_offset):
    fields, layers, rows, cols = load_currents.shape
    depth = POWERS
    assert layers == depth and rows == 2 * depth and cols == 4 * depth * rows and fields % TILE == 0
    float_of = lambda *shape: jax.ShapeDtypeStruct(shape, jnp.float32)
    pair = lax.axis_size("gy") == 2
    planes = fields + TILE
    slabs = layers * rows
    high = layers + 2 * depth
    tall = rows + 2 * depth
    count = len(CORNERS)
    part = float_of(slabs // 2, planes, cols)
    flat_rows = (slabs // 2) * (fields + COEFS)
    corner_rows = 2 * count * (fields + COEFS) + slabs * COEFS
    raw = load_currents.reshape(fields * slabs, cols)
    one = swapped(raw, "gz", 0)
    two = swapped(raw, "gz", 1)
    first, second, coef_tiles, coef_rows, shifts = pl.pallas_call(
        edges_kernel,
        out_shape=(
            float_of(flat_rows, cols),
            float_of(flat_rows, cols),
            float_of(slabs, TILE, cols),
            float_of(slabs * COEFS, cols),
            jax.ShapeDtypeStruct((high, TILE, cols), jnp.int32),
        ),
        in_specs=[HBM] * 5 + [SMEM],
        out_specs=(VMEM,) * 5,
        scratch_shapes=[
            pltpu.VMEM((fields * slabs, cols), jnp.float32),
            pltpu.VMEM((COEFS, layers, rows, cols), jnp.float32),
            pltpu.SemaphoreType.DMA((COEFS + 1,)),
        ],
        compiler_params=FIRST,
        name="edges",
    )(raw, cond_rows, cond_cols, cond_vias, ground, via_offset)
    first, second = swapped(first, "gx", 0), swapped(second, "gx", 1)
    block = pl.pallas_call(
        own_kernel,
        out_shape=float_of(slabs, planes, cols),
        in_specs=[VMEM] * 2,
        out_specs=VMEM,
        compiler_params=PARAMS,
        cost_estimate=pl.CostEstimate(flops=0, bytes_accessed=8 * slabs * planes * cols, transcendentals=0),
        name="own",
    )(raw, coef_tiles)
    after, before, to_first, to_second = pl.pallas_call(
        functools.partial(corners_kernel, layers=layers),
        out_shape=(part, part) + (float_of(corner_rows, cols),) * 2,
        in_specs=[VMEM] * 3,
        out_specs=(VMEM,) * 4,
        compiler_params=PARAMS,
        name="corners",
    )(first, second, coef_rows)
    to_first, to_second = swapped(to_first, "gz", 0), swapped(to_second, "gz", 1)
    pieces = (block, after, before, one, two)
    inner = pl.pallas_call(
        functools.partial(inner_kernel, layers=layers, rows=rows),
        out_shape=float_of(high, planes, cols),
        in_specs=[VMEM] * 5,
        out_specs=VMEM,
        compiler_params=PARAMS,
        cost_estimate=pl.CostEstimate(flops=0, bytes_accessed=16 * slabs * planes * cols, transcendentals=0),
        name="inner",
    )(*pieces)
    edge, *outer = pl.pallas_call(
        functools.partial(sides_kernel, layers=layers, rows=rows, pair=pair),
        out_shape=(float_of(high, planes, cols),) + (float_of(high // 2, planes, cols),) * (1 if pair else 2),
        in_specs=[VMEM] * 3,
        out_specs=(VMEM,) * (2 if pair else 3),
        compiler_params=PARAMS,
        name="sides",
    )(inner, to_first, to_second)
    pieces += (to_first, to_second)
    if pair:
        got = [lax.ppermute(outer[0], "gy", [(0, 1), (1, 0)])]
    else:
        got = [sent(outer[0], {"gy": 1}), sent(outer[1], {"gy": -1})]
    start = pl.pallas_call(
        functools.partial(assemble_kernel, layers=layers, rows=rows),
        out_shape=float_of(high, tall, planes, cols),
        in_specs=[VMEM] * 7,
        out_specs=VMEM,
        compiler_params=PARAMS,
        cost_estimate=pl.CostEstimate(flops=0, bytes_accessed=2 * high * tall * planes * cols, transcendentals=0),
        name="assemble",
    )(*pieces)
    order = depth * fields
    points = slabs
    basis, gram = pl.pallas_call(
        functools.partial(powers_kernel, fields=fields, layers=layers, rows=rows, pair=pair),
        out_shape=(float_of(points * order, cols), float_of(order, order)),
        in_specs=[VMEM] * (3 + len(got)),
        out_specs=(VMEM,) * 2,
        scratch_shapes=[
            pltpu.VMEM((depth - 1, high, tall, fields, cols), jnp.float32),
            pltpu.VMEM((7, high, tall, TILE, cols), jnp.float32),
            pltpu.VMEM((2, depth, high, planes, cols), jnp.float32),
            pltpu.VMEM((2, 7, high, TILE, cols), jnp.float32),
            pltpu.VMEM((depth, high, planes, cols), jnp.float32),
            pltpu.VMEM((order, order), jnp.float32),
        ],
        compiler_params=PARAMS,
        name="powers",
    )(start, edge, *got, shifts)
    half_type = jax.ShapeDtypeStruct((points * order, cols), jnp.bfloat16)
    high_part, low_part = pl.pallas_call(
        split_kernel,
        out_shape=(half_type, half_type),
        in_specs=[VMEM],
        out_specs=(VMEM, VMEM),
        compiler_params=PARAMS,
        cost_estimate=pl.CostEstimate(flops=0, bytes_accessed=8 * points * order * cols, transcendentals=0),
        name="split",
    )(basis)
    points_in_all = points * cols
    steps = []
    for axis in ("gx", "gy", "gz"):
        size = lax.axis_size(axis)
        points_in_all *= size
        steps += [(axis, 1 << bit) for bit in range(axis == "gz", size.bit_length() - 1)]
    assert lax.axis_size("gz") % 2 == 0
    own = doubled(gram + swapped(gram, "gz", 0), steps)
    other = swapped(own, "gz", 0)
    upper, basis_q = pl.pallas_call(
        functools.partial(finish_kernel, count=float(points_in_all), step=8),
        out_shape=(float_of(order, order), float_of(order, points, cols)),
        in_specs=[VMEM] * 4,
        out_specs=(VMEM, HBM),
        scratch_shapes=[pltpu.VMEM((order * points, cols), jnp.float32), pltpu.SemaphoreType.DMA((layers,))],
        compiler_params=PARAMS,
        name="finish",
    )(own, other, high_part, low_part)
    return basis_q.reshape(order, layers, rows, cols), upper


def solution(mesh):
    in_specs = (
        P(None, "gz", "gx", "gy"),
        P("gz", "gx", "gy"),
        P("gz", "gx", "gy"),
        P("gz", "gx", "gy"),
        P("gz", "gx", "gy"),
        P(),
    )
    out_specs = (P(None, "gz", "gx", "gy"), P())
    return jax.shard_map(local, mesh=mesh, in_specs=in_specs, out_specs=out_specs, check_vma=False)
```

```python
import functools

import jax
import jax.numpy as jnp
from jax import lax
from jax.experimental import pallas as pl
from jax.experimental.pallas import tpu as pltpu
from jax.sharding import PartitionSpec as P

POWERS = 4


newton_shifts = (15.4, 0.6, 11.7, 4.3)
basis_scale = 0.125

VMEM = pl.BlockSpec(memory_space=pltpu.VMEM)
SMEM = pl.BlockSpec(memory_space=pltpu.SMEM)
HBM = pl.BlockSpec(memory_space=pltpu.HBM)
PARAMS = pltpu.CompilerParams(vmem_limit_bytes=32 * 1024 * 1024)
FIRST = pltpu.CompilerParams(vmem_limit_bytes=60 * 1024 * 1024)

COEFS = 4
TILE = 8
CORNERS = ((1, 3), (1, 2), (1, 1), (2, 2), (2, 1), (3, 1))


def positions(shape):
    sub = lax.broadcasted_iota(jnp.int32, shape, 0)
    lane = lax.broadcasted_iota(jnp.int32, shape, 1)
    return sub, lane


def coefs_at(ref, start, i):
    place = start + COEFS * (i // 2) * 2
    tile = ref[place : place + TILE, :]
    return pltpu.roll(tile, COEFS, 0) if i % 2 else tile


def edges_kernel(
    load_ref, rows_ref, cols_ref, vias_ref, ground_ref, offset_ref,
    first_ref, second_ref, tile_ref, flat_ref, shift_ref, fields_in, coefs_in, sems,
):
    slabs, _, cols = tile_ref.shape
    fields = load_ref.shape[0] // slabs
    layers, rows, _ = rows_ref.shape
    depth = POWERS
    half = rows // 2
    total_layers = offset_ref.shape[0]
    copies = [
        pltpu.make_async_copy(ref, coefs_in.at[i], sems.at[i])
        for i, ref in enumerate((rows_ref, cols_ref, vias_ref, ground_ref))
    ]
    copies.append(pltpu.make_async_copy(load_ref, fields_in, sems.at[COEFS]))
    for copy in copies:
        copy.start()
    gx, gy, gz = (lax.axis_index(name) for name in ("gx", "gy", "gz"))
    last_row = jnp.where(gx == lax.axis_size("gx") - 1, rows - 1, rows)
    last_col = jnp.where(gy == lax.axis_size("gy") - 1, cols - 1, cols)
    sub, lane = positions((TILE, cols))
    for e in range(shift_ref.shape[0]):
        layer = gz * layers + e - depth
        inside = (layer >= 0) & (layer < total_layers)
        value = jnp.where(inside, offset_ref[jnp.clip(layer, 0, total_layers - 1)], 0)
        shift_ref[e] = jnp.broadcast_to(value, (TILE, cols))
    for copy in copies:
        copy.wait()

    def joined(one, two):
        return jnp.where(sub < COEFS, one, pltpu.roll(two, COEFS, 0))

    for l in range(layers):
        layer = gz * layers + l
        target = gy * cols + lane + shift_ref[depth + l]
        via_ok = (target >= 0) & (target < cols * lax.axis_size("gy"))
        via_ok = via_ok & (jnp.broadcast_to(layer, lane.shape) < total_layers - 1)
        four = (
            jnp.where(sub == last_row, 0.0, coefs_in[0, l]),
            jnp.where(lane == last_col, 0.0, coefs_in[1, l]),
            jnp.where(via_ok, coefs_in[2, l], 0.0),
            coefs_in[3, l],
        )
        for r in range(rows):
            slab = l * rows + r
            value = jnp.zeros((TILE, cols), jnp.float32)
            for c in range(COEFS):
                value = jnp.where(sub == c, jnp.broadcast_to(four[c][r : r + 1, :], (TILE, cols)), value)
            tile_ref[slab] = value
    for i in range(0, slabs, 2):
        flat_ref[COEFS * i : COEFS * i + TILE, :] = joined(tile_ref[i], tile_ref[i + 1])
    even = lax.rem(gx, 2) == 0
    for ref, start in ((first_ref, jnp.where(even, half, 0)), (second_ref, jnp.where(even, 0, half))):
        for l in range(layers):
            for i in range(half):
                slab = l * rows + start + i
                at = l * half + i
                for f in range(0, fields, TILE):
                    tile = fields_in[pl.ds(f * slabs + slab, TILE, stride=slabs), :]
                    ref[at * fields + f : at * fields + f + TILE, :] = tile
                if i % 2 == 0:
                    place = layers * half * fields + COEFS * at
                    ref[place : place + TILE, :] = joined(tile_ref[slab], tile_ref[slab + 1])


def own_kernel(load_ref, tile_ref, block_ref):
    slabs, planes, _ = block_ref.shape
    for slab in range(slabs):
        for f in range(0, planes - TILE, TILE):
            block_ref[slab, f : f + TILE, :] = load_ref[pl.ds(f * slabs + slab, TILE, stride=slabs), :]
        block_ref[slab, planes - TILE :, :] = tile_ref[slab]


def corners_kernel(first_ref, second_ref, flat_ref, after_ref, before_ref, one_ref, two_ref, *, layers):
    slabs, planes, cols = after_ref.shape
    fields = planes - TILE
    half = slabs // layers
    count = len(CORNERS)
    sub, _ = positions((TILE, cols))
    even_row = jnp.broadcast_to(lax.rem(lax.axis_index("gx"), 2), (TILE, cols)) == 0
    even_layer = jnp.broadcast_to(lax.rem(lax.axis_index("gz"), 2), (TILE, cols)) == 0
    row_block = jnp.broadcast_to(lax.axis_index("gx"), (TILE, cols))
    has_prev, has_next = row_block > 0, row_block < lax.axis_size("gx") - 1
    for f in range(0, planes, TILE):
        after, before = [], []
        for i in range(slabs):
            if f < fields:
                first, second = (ref[i * fields + f : i * fields + f + TILE, :] for ref in (first_ref, second_ref))
            else:
                first, second = (coefs_at(ref, slabs * fields, i) for ref in (first_ref, second_ref))
            after.append(jnp.where(has_prev, jnp.where(even_row, second, first), 0.0))
            before.append(jnp.where(has_next, jnp.where(even_row, first, second), 0.0))
            after_ref[i, f : f + TILE, :] = after[i]
            before_ref[i, f : f + TILE, :] = before[i]
        ones, twos = [], []
        for source, step in ((after, -1), (before, 1)):
            for dz, dx in CORNERS:
                row = half - dx if step < 0 else dx - 1
                up, down = source[(layers - dz) * half + row], source[(dz - 1) * half + row]
                ones.append(jnp.where(even_layer, up, down))
                twos.append(jnp.where(even_layer, down, up))
        for ref, values in ((one_ref, ones), (two_ref, twos)):
            if f < fields:
                for i, value in enumerate(values):
                    ref[i * fields + f : i * fields + f + TILE, :] = value
            else:
                for i in range(0, 2 * count, 2):
                    place = 2 * count * fields + COEFS * i
                    pair = jnp.where(sub < COEFS, values[i], pltpu.roll(values[i + 1], COEFS, 0))
                    ref[place : place + TILE, :] = pair
    for ref in (one_ref, two_ref):
        place = 2 * count * planes - 2 * count * (TILE - COEFS)
        ref[place : place + flat_ref.shape[0], :] = flat_ref[...]


def slabs_of(e, layers, rows, planes, corners, inner, block, after, before, one, two, corner_one=None, corner_two=None):
    depth, half, count = POWERS, rows // 2, len(CORNERS)
    cols = block.shape[2] if block is not None else corner_one.shape[1]
    fields, slabs = planes - TILE, layers * rows

    def plain(ref, slab):
        return lambda f: ref[slab, f : f + TILE, :]

    def chosen(read, one, two):
        place = jnp.broadcast_to(lax.axis_index("gz"), (TILE, cols))
        even = lax.rem(place, 2) == 0
        there = place > 0 if e < depth else place < lax.axis_size("gz") - 1
        return lambda f: jnp.where(there, jnp.where(even, read(one, f), read(two, f)), 0.0)

    def home(slab):
        return lambda ref, f: ref[pl.ds(f * slabs + slab, TILE, stride=slabs), :]

    def home_coefs(slab):
        return lambda ref, f: coefs_at(ref, 2 * count * (fields + COEFS), slab)

    def corner(i):
        def read(ref, f):
            if f < fields:
                return ref[i * fields + f : i * fields + f + TILE, :]
            return coefs_at(ref, 2 * count * fields, i)

        return read

    tiles = [f for f in range(0, planes, TILE)]
    found = []
    if depth <= e < depth + layers:
        l = e - depth
        if inner:
            found += [(depth + r, plain(block, l * rows + r), tiles) for r in range(rows)]
            for i in range(half):
                found.append((i, plain(after, l * half + i), tiles))
                found.append((depth + rows + i, plain(before, l * half + i), tiles))
        return found
    if e < depth:
        pair, corner_pair, first, distance = (two, one), (corner_two, corner_one), 0, depth - e
    else:
        pair, corner_pair = (one, two), (corner_one, corner_two)
        first, distance = depth + layers, e - depth - layers + 1
    for r in range(rows):
        slab = (e - first) * rows + r
        if inner:
            found.append((depth + r, chosen(home(slab), *pair), tiles[:-1]))
        if corners:
            found.append((depth + r, chosen(home_coefs(slab), *corner_pair), tiles[-1:]))
    for i, (dz, dx) in enumerate(CORNERS):
        if dz == distance and corners:
            found.append((depth - dx, chosen(corner(i), *corner_pair), tiles))
            found.append((depth + rows - 1 + dx, chosen(corner(count + i), *corner_pair), tiles))
    return found


def inner_kernel(*refs, layers, rows):
    sources, edge_ref = refs[:5], refs[5]
    high, planes, cols = edge_ref.shape
    depth = POWERS
    group = 2 * depth
    _, lane = positions((TILE, cols))
    for e in range(high):
        found = slabs_of(e, layers, rows, planes, False, True, *sources)
        for f in range(0, planes, TILE):
            total = jnp.zeros((TILE, cols), jnp.float32)
            for row, read, tiles in found:
                if f in tiles:
                    moved = pltpu.roll(read(f), (group * row + depth) % cols, 1)
                    total = jnp.where((lane >= group * row) & (lane < group * row + group), moved, total)
            edge_ref[e, f : f + TILE, :] = total


def sides_kernel(inner_ref, one_ref, two_ref, edge_ref, *out_refs, layers, rows, pair):
    high, planes, cols = edge_ref.shape
    depth = POWERS
    group = 2 * depth
    _, lane = positions((TILE, cols))
    early = lax.rem(lane, group) < depth
    gy = jnp.broadcast_to(lax.axis_index("gy"), (TILE, cols))
    for f in range(0, planes, TILE):
        here = slice(f, f + TILE)
        edges = []
        for e in range(high):
            total = inner_ref[e, here, :]
            for row, read, tiles in slabs_of(e, layers, rows, planes, True, False, None, None, None, None, None, one_ref, two_ref):
                if f in tiles:
                    moved = pltpu.roll(read(f), (group * row + depth) % cols, 1)
                    total = jnp.where((lane >= group * row) & (lane < group * row + group), moved, total)
            edge_ref[e, here, :] = total
            edges.append(total)
        for t in range(high // 2):
            one, two = edges[2 * t], edges[2 * t + 1]
            up = jnp.where(early, one, pltpu.roll(two, depth, 1))
            down = jnp.where(early, pltpu.roll(one, cols - depth, 1), two)
            if pair:
                out_refs[0][t, here, :] = jnp.where(gy == 0, up, down)
            else:
                out_refs[0][t, here, :] = up
                out_refs[1][t, here, :] = down


def assemble_kernel(*refs, layers, rows):
    sources, start_ref = refs[:7], refs[7]
    high, _, planes, _ = start_ref.shape
    for e in range(high):
        for row, read, tiles in slabs_of(e, layers, rows, planes, True, True, *sources):
            for f in tiles:
                start_ref[e, row, f : f + TILE, :] = read(f)


def powers_kernel(*refs, fields, layers, rows, pair):
    gots = 1 if pair else 2
    start_ref, edge_ref, got_refs, shift_ref = refs[0], refs[1], refs[2 : 2 + gots], refs[2 + gots]
    basis_ref, keep_ref, send_ref, power_ref, coef_ref, strip_ref, strip_coef_ref, border_ref, sum_ref = refs[3 + gots :]
    high, tall, planes, cols = start_ref.shape
    depth = POWERS
    group = 2 * depth
    order = depth * fields
    tiles = range(0, fields, TILE)
    _, lane = positions((TILE, cols))
    gy = lax.axis_index("gy")

    def masks(e):
        shift = shift_ref[e]
        return shift == 0, shift > 0

    def from_above(seen, mask):
        left, centre, right = seen
        return jnp.where(mask[0], centre, jnp.where(mask[1], right, left))

    def from_below(seen, mask):
        left, centre, right = seen
        return jnp.where(mask[0], centre, jnp.where(mask[1], left, right))

    def around(tile):
        return pltpu.roll(tile, 1, 1), tile, pltpu.roll(tile, cols - 1, 1)

    def spread(tile, c):
        return jnp.broadcast_to(tile[c : c + 1, :], (TILE, cols))

    def put_factors(put, tile, row_above, seen, seen_below, mask):
        down, right, upper, ground = (spread(tile, c) for c in range(COEFS))
        up = spread(row_above, 0)
        left = spread(seen[0], 1)
        lower = from_below([spread(x, 2) for x in seen_below], mask)
        diagonal = ground + down + up + right + left + upper + lower
        for i, value in enumerate((down, up, right, left, upper, lower, diagonal)):
            put(i, value * basis_scale)

    def step(factors, theta, seen, up, down, above, below):
        value = (factors[6] - theta) * seen[1]
        value = value - (factors[0] * down + factors[1] * up)
        value = value - (factors[2] * seen[2] + factors[3] * seen[0])
        return value - (factors[4] * above + factors[5] * below)

    thetas = [shift * basis_scale for shift in newton_shifts]

    early = lax.rem(lane, group) < depth
    if pair:
        first_side = jnp.where(gy == 0, 1, 0)
        last_side = first_side + 1
    else:
        first_side, last_side = 0, 2

    @pl.loop(first_side, last_side)
    def _(side):
        left_side = jnp.broadcast_to(side, (TILE, cols)) == 0
        from_edge = early != left_side
        for e in range(high):
            for f in range(0, planes, TILE):
                here = slice(f, f + TILE)
                outer = got_refs[0][e // 2, here, :]
                if not pair:
                    outer = jnp.where(left_side, outer, got_refs[1][e // 2, here, :])
                if e % 2 == 0:
                    outer = jnp.where(left_side, outer, pltpu.roll(outer, depth, 1))
                else:
                    outer = jnp.where(left_side, pltpu.roll(outer, cols - depth, 1), outer)
                strip_ref[side, 0, e, here, :] = jnp.where(from_edge, edge_ref[e, here, :], outer)
        raw = [strip_ref[side, 0, e, fields : fields + TILE, :] for e in range(high)]
        seen = [around(tile) for tile in raw]
        for e in range(1, high - 1):

            def put(i, value, e=e):
                strip_coef_ref[side, i, e] = value

            put_factors(put, raw[e], pltpu.roll(raw[e], group, 1), seen[e], seen[e - 1], masks(e - 1))
        for k in range(1, depth):
            reach = depth - k
            looks = {}

            def look(e, f, k=k, looks=looks):
                if (e, f) not in looks:
                    looks[e, f] = around(strip_ref[side, k - 1, e, f : f + TILE, :])
                return looks[e, f]

            for e in range(depth - reach, depth + layers + reach):
                factors = [strip_coef_ref[side, i, e] for i in range(7)]
                over, under = masks(e), masks(e - 1)
                for f in tiles:
                    here = look(e, f)
                    strip_ref[side, k, e, f : f + TILE, :] = step(
                        factors,
                        thetas[k - 1],
                        here,
                        pltpu.roll(here[1], group, 1),
                        pltpu.roll(here[1], cols - group, 1),
                        from_above(look(e + 1, f), over),
                        from_below(look(e - 1, f), under),
                    )

    gy_lane = jnp.broadcast_to(gy, (TILE, cols))
    on_left = (lax.rem(lane, group) == depth - 1) & (gy_lane > 0)
    on_right = (lax.rem(lane, group) == depth - 2) & (gy_lane < lax.axis_size("gy") - 1)

    @pl.loop(0, high)
    def _(e):
        for k in range(depth):
            for f in range(0, planes if k == 0 else fields, TILE):
                here = slice(f, f + TILE)
                right = jnp.where(on_right, pltpu.roll(strip_ref[1, k, e, here, :], cols - 2, 1), 0.0)
                border_ref[k, e, here, :] = jnp.where(on_left, strip_ref[0, k, e, here, :], right)

    leftmost, rightmost = lane == 0, lane == cols - 1

    def looked(k, e, row, f):
        here = slice(f, f + TILE)
        tile = start_ref[e, row, here, :] if k == 0 else power_ref[k - 1, e, row, here, :]
        turn = (2 * cols - group * row - depth + 1) % cols if isinstance(row, int) else lax.rem(2 * cols - group * row - depth + 1, cols)
        outer = pltpu.roll(border_ref[k, e, here, :], turn, 1)
        left, _, right = around(tile)
        return jnp.where(leftmost, outer, left), tile, jnp.where(rightmost, outer, right)

    def by_rows(reach, body):
        @pl.loop(0, rows, unroll=4)
        def _(r):
            body(depth + r, depth - reach, depth + layers + reach)

        for dx in range(1, reach + 1):
            for row in (depth - dx, depth + rows - 1 + dx):
                body(row, depth - reach + dx, depth + layers + reach - dx)

    def factors_of_row(row, first, last):
        seen = {e: looked(0, e, row, fields) for e in range(first - 1, last)}
        for e in range(first, last):

            def put(i, value, e=e):
                coef_ref[i, e, row] = value

            above_row = start_ref[e, row - 1, fields : fields + TILE, :]
            put_factors(put, seen[e][1], above_row, seen[e], seen[e - 1], masks(e - 1))

    by_rows(depth - 1, factors_of_row)

    for k in range(1, depth + 1):

        def advance(row, first, last, k=k):
            source = start_ref if k == 1 else power_ref.at[k - 2]
            below = {f: from_below(looked(k - 1, first - 1, row, f), masks(first - 1)) for f in tiles}
            centre = {f: looked(k - 1, first, row, f) for f in tiles}
            for e in range(first, last):
                factors = [coef_ref[i, e, row] for i in range(7)]
                mask = masks(e)
                for f in tiles:
                    here = slice(f, f + TILE)
                    upper = looked(k - 1, e + 1, row, f)
                    value = step(
                        factors,
                        thetas[k - 1],
                        centre[f],
                        source[e, row - 1, here, :],
                        source[e, row + 1, here, :],
                        from_above(upper, mask),
                        below[f],
                    )
                    below[f], centre[f] = from_below(centre[f], mask), upper
                    if k < depth:
                        power_ref[k - 1, e, row, here, :] = value
                    if first == k and depth <= e < depth + layers:
                        slab = (e - depth) * rows + row - depth
                        place = pl.multiple_of(slab * order + (k - 1) * fields + f, TILE)
                        basis_ref[pl.ds(place, TILE), :] = value

        if k < depth:
            by_rows(depth - k, advance)

    def share(r):
        value = None
        for l in range(0, layers, 2):
            places = [pl.multiple_of(((l + i) * rows + r) * order, TILE) for i in range(2)]
            wide = jnp.concatenate([basis_ref[pl.ds(place, order), :] for place in places], axis=1)
            product = lax.dot_general(
                wide, wide, (((1,), (1,)), ((), ())),
                precision=lax.Precision.HIGHEST, preferred_element_type=jnp.float32,
            )
            value = product if value is None else value + product
        return value

    advance(depth, depth, depth + layers)
    sum_ref[...] = jnp.zeros_like(sum_ref)

    @pl.loop(1, rows)
    def _(r):
        product = share(r - 1)
        advance(depth + r, depth, depth + layers)
        sum_ref[...] += product

    total = sum_ref[...] + share(rows - 1)
    sum_ref[...] = total
    half = order // 2
    odd = lax.rem(lax.axis_index("gz"), 2)
    keep_ref[...] = sum_ref[pl.ds(pl.multiple_of(odd * half, TILE), half), :]
    send_ref[...] = sum_ref[pl.ds(pl.multiple_of((1 - odd) * half, TILE), half), :]


def eliminate(tiles, order, step):
    width = tiles[0].shape[1]
    lane = lax.broadcasted_iota(jnp.int32, (8, width), 1)
    sub = lax.broadcasted_iota(jnp.int32, (8, width), 0)
    spread = lambda value: jnp.broadcast_to(value, (8, width))
    for first in range(0, order, step):
        home, base = first // 8, first % 8
        panel = tiles[home]
        entry = {}
        for i in range(step):
            for j in range(i, step):
                entry[i, j] = spread(panel[base + i : base + i + 1, first + j : first + j + 1])
        rows = [spread(panel[base + i : base + i + 1, :]) for i in range(step)]
        inverse = []
        done = []
        for i in range(step):
            row = rows[i]
            if i:
                row = jnp.where((lane >= first) & (lane < first + i), 0.0, row)
            factors = []
            for j in range(i):
                factor = entry[j, i] * inverse[j]
                factors.append(factor)
            for j in range(i):
                source = jnp.where(lane == first + j, 1.0, done[j])
                if i - j > 1:
                    source = jnp.where((lane > first + j) & (lane < first + i), 0.0, source)
                row = row - factors[j] * source
                for m in range(i, step):
                    entry[i, m] = entry[i, m] - factors[j] * entry[j, m]
            inverse.append(1.0 / entry[i, i])
            done.append(row)
        sources = []
        for j in range(step):
            source = jnp.where(lane == first + j, 1.0, done[j])
            if j < step - 1:
                source = jnp.where((lane > first + j) & (lane < first + step), 0.0, source)
            sources.append(source)
        inside = (lane >= first) & (lane < first + step)
        for t in range(home, order // 8):
            if t == home and base + step == 8:
                fresh = tiles[t]
            else:
                columns = [spread(tiles[t][:, first + j : first + j + 1]) for j in range(step)]
                fresh = jnp.where(inside, 0.0, tiles[t])
                for j in range(step):
                    factor = columns[j] * inverse[j]
                    fresh = fresh - factor * sources[j]
                    for m in range(j + 1, step):
                        columns[m] = columns[m] - factor * entry[j, m]
            if t == home:
                fresh = jnp.where(sub < base + step, tiles[t], fresh)
                for j in range(step):
                    fresh = jnp.where(sub == base + j, done[j], fresh)
            tiles[t] = fresh
    return tiles


def finish_kernel(*refs, count, step):
    own_ref, other_ref, high_ref, low_ref, upper_ref, out_ref, staged, sems = refs
    order = upper_ref.shape[0]
    points = high_ref.shape[0] // order
    even = jnp.broadcast_to(lax.rem(lax.axis_index("gz"), 2), (TILE, order)) == 0
    halves = [[], []]
    for r in range(0, order // 2, TILE):
        own, other = own_ref[r : r + TILE, :] / count, other_ref[r : r + TILE, :] / count
        halves[0].append(jnp.where(even, own, other))
        halves[1].append(jnp.where(even, other, own))
    tiles = eliminate(halves[0] + halves[1], order, step)
    lane = lax.broadcasted_iota(jnp.int32, (8, order), 1)
    sub = lax.broadcasted_iota(jnp.int32, (8, order), 0)
    inverse = []
    for t in range(order // 8):
        row = sub + 8 * t
        pivot = jnp.sum(jnp.where(lane == row, tiles[t], 0.0), axis=1, keepdims=True)
        scale = 1.0 / jnp.sqrt(pivot)
        upper_ref[8 * t : 8 * t + 8, :] = jnp.where(lane >= row, tiles[t] * scale, 0.0)
        inverse.append(jnp.where(lane < row, tiles[t], jnp.where(lane == row, 1.0, 0.0)) * scale)
    inverse = jnp.concatenate(inverse, axis=0)
    cols = high_ref.shape[1]
    inverse_parts = two_parts(inverse)
    chunk = points // sems.shape[0]
    copies = []
    for i in range(0, points, 2):
        start = i * order
        wide = [
            jnp.concatenate([ref[start : start + order, :], ref[start + order : start + 2 * order, :]], axis=1)
            for ref in (high_ref, low_ref)
        ]
        out = product(inverse_parts, wide)
        staged[pl.ds(i, order, stride=points), :] = out[:, :cols]
        staged[pl.ds(i + 1, order, stride=points), :] = out[:, cols:]
        if (i + 2) % chunk == 0:
            part = pl.ds(i + 2 - chunk, chunk)
            source = staged.reshape(order, points, cols).at[:, part, :]
            copies.append(pltpu.make_async_copy(source, out_ref.at[:, part, :], sems.at[i // chunk]))
            copies[-1].start()
    for copy in copies:
        copy.wait()


def split_kernel(basis_ref, high_ref, low_ref):
    size = 2 * TILE

    @pl.loop(0, basis_ref.shape[0] // size, unroll=8)
    def _(i):
        here = pl.ds(pl.multiple_of(i * size, size), size)
        high_ref[here, :], low_ref[here, :] = two_parts(basis_ref[here, :])


def two_parts(value):
    high = value.astype(jnp.bfloat16)
    return high, (value - high.astype(jnp.float32)).astype(jnp.bfloat16)


def product(left, right):
    dot = functools.partial(jnp.dot, preferred_element_type=jnp.float32)
    return dot(left[0], right[0]) + (dot(left[0], right[1]) + dot(left[1], right[0]))


def summed(value, rounds_of):
    axes = ("gx", "gy", "gz")
    sizes = [lax.axis_size(name) for name in axes]
    assert all(size & (size - 1) == 0 for size in sizes)

    def index(place):
        return (place[0] * sizes[1] + place[1]) * sizes[2] + place[2]

    for r in range(len(rounds_of[0])):
        got = []
        for chosen in range(1, 1 << len(rounds_of[0][r])):
            pairs = []
            for x in range(sizes[0]):
                for y in range(sizes[1]):
                    for z in range(sizes[2]):
                        partner = [x, y, z]
                        for bit, (axis, mask) in enumerate(rounds_of[z % 2][r]):
                            if chosen >> bit & 1:
                                partner[axes.index(axis)] ^= mask
                        pairs.append((index((x, y, z)), index(partner)))
            got.append(lax.ppermute(value, axes, pairs))
        value = value + got[0]
        if len(got) == 3:
            value = value + (got[1] + got[2])
    return value


def swapped(value, axis, phase):
    pairs = []
    for i in range(phase, lax.axis_size(axis) - 1, 2):
        pairs += [(i, i + 1), (i + 1, i)]
    paired = {i for i, _ in pairs}
    pairs += [(i, i) for i in range(lax.axis_size(axis)) if i not in paired]
    return lax.ppermute(value, axis, pairs)


def sent(value, steps):
    axes = tuple(steps)
    sizes = [lax.axis_size(name) for name in axes]
    pairs = []
    if len(axes) == 1:
        pairs = [(i, i + steps[axes[0]]) for i in range(sizes[0]) if 0 <= i + steps[axes[0]] < sizes[0]]
        return lax.ppermute(value, axes[0], pairs)
    for i in range(sizes[0]):
        for j in range(sizes[1]):
            m, n = i + steps[axes[0]], j + steps[axes[1]]
            if 0 <= m < sizes[0] and 0 <= n < sizes[1]:
                pairs.append((i * sizes[1] + j, m * sizes[1] + n))
    return lax.ppermute(value, axes, pairs)


def local(load_currents, cond_rows, cond_cols, cond_vias, ground, via_offset):
    fields, layers, rows, cols = load_currents.shape
    depth = POWERS
    assert layers == depth and rows == 2 * depth and cols == 4 * depth * rows and fields % TILE == 0
    float_of = lambda *shape: jax.ShapeDtypeStruct(shape, jnp.float32)
    pair = lax.axis_size("gy") == 2
    planes = fields + TILE
    slabs = layers * rows
    high = layers + 2 * depth
    tall = rows + 2 * depth
    count = len(CORNERS)
    part = float_of(slabs // 2, planes, cols)
    flat_rows = (slabs // 2) * (fields + COEFS)
    corner_rows = 2 * count * (fields + COEFS) + slabs * COEFS
    raw = load_currents.reshape(fields * slabs, cols)
    one = swapped(raw, "gz", 0)
    two = swapped(raw, "gz", 1)
    first, second, coef_tiles, coef_rows, shifts = pl.pallas_call(
        edges_kernel,
        out_shape=(
            float_of(flat_rows, cols),
            float_of(flat_rows, cols),
            float_of(slabs, TILE, cols),
            float_of(slabs * COEFS, cols),
            jax.ShapeDtypeStruct((high, TILE, cols), jnp.int32),
        ),
        in_specs=[HBM] * 5 + [SMEM],
        out_specs=(VMEM,) * 5,
        scratch_shapes=[
            pltpu.VMEM((fields * slabs, cols), jnp.float32),
            pltpu.VMEM((COEFS, layers, rows, cols), jnp.float32),
            pltpu.SemaphoreType.DMA((COEFS + 1,)),
        ],
        compiler_params=FIRST,
        name="edges",
    )(raw, cond_rows, cond_cols, cond_vias, ground, via_offset)
    first, second = swapped(first, "gx", 0), swapped(second, "gx", 1)
    block = pl.pallas_call(
        own_kernel,
        out_shape=float_of(slabs, planes, cols),
        in_specs=[VMEM] * 2,
        out_specs=VMEM,
        compiler_params=PARAMS,
        cost_estimate=pl.CostEstimate(flops=0, bytes_accessed=8 * slabs * planes * cols, transcendentals=0),
        name="own",
    )(raw, coef_tiles)
    after, before, to_first, to_second = pl.pallas_call(
        functools.partial(corners_kernel, layers=layers),
        out_shape=(part, part) + (float_of(corner_rows, cols),) * 2,
        in_specs=[VMEM] * 3,
        out_specs=(VMEM,) * 4,
        compiler_params=PARAMS,
        name="corners",
    )(first, second, coef_rows)
    to_first, to_second = swapped(to_first, "gz", 0), swapped(to_second, "gz", 1)
    pieces = (block, after, before, one, two)
    inner = pl.pallas_call(
        functools.partial(inner_kernel, layers=layers, rows=rows),
        out_shape=float_of(high, planes, cols),
        in_specs=[VMEM] * 5,
        out_specs=VMEM,
        compiler_params=PARAMS,
        cost_estimate=pl.CostEstimate(flops=0, bytes_accessed=16 * slabs * planes * cols, transcendentals=0),
        name="inner",
    )(*pieces)
    edge, *outer = pl.pallas_call(
        functools.partial(sides_kernel, layers=layers, rows=rows, pair=pair),
        out_shape=(float_of(high, planes, cols),) + (float_of(high // 2, planes, cols),) * (1 if pair else 2),
        in_specs=[VMEM] * 3,
        out_specs=(VMEM,) * (2 if pair else 3),
        compiler_params=PARAMS,
        name="sides",
    )(inner, to_first, to_second)
    pieces += (to_first, to_second)
    if pair:
        got = [lax.ppermute(outer[0], "gy", [(0, 1), (1, 0)])]
    else:
        got = [sent(outer[0], {"gy": 1}), sent(outer[1], {"gy": -1})]
    start = pl.pallas_call(
        functools.partial(assemble_kernel, layers=layers, rows=rows),
        out_shape=float_of(high, tall, planes, cols),
        in_specs=[VMEM] * 7,
        out_specs=VMEM,
        compiler_params=PARAMS,
        cost_estimate=pl.CostEstimate(flops=0, bytes_accessed=2 * high * tall * planes * cols, transcendentals=0),
        name="assemble",
    )(*pieces)
    order = depth * fields
    points = slabs
    basis, keep, send = pl.pallas_call(
        functools.partial(powers_kernel, fields=fields, layers=layers, rows=rows, pair=pair),
        out_shape=(float_of(points * order, cols),) + (float_of(order // 2, order),) * 2,
        in_specs=[VMEM] * (3 + len(got)),
        out_specs=(VMEM,) * 3,
        scratch_shapes=[
            pltpu.VMEM((depth - 1, high, tall, fields, cols), jnp.float32),
            pltpu.VMEM((7, high, tall, TILE, cols), jnp.float32),
            pltpu.VMEM((2, depth, high, planes, cols), jnp.float32),
            pltpu.VMEM((2, 7, high, TILE, cols), jnp.float32),
            pltpu.VMEM((depth, high, planes, cols), jnp.float32),
            pltpu.VMEM((order, order), jnp.float32),
        ],
        compiler_params=PARAMS,
        name="powers",
    )(start, edge, *got, shifts)
    half_type = jax.ShapeDtypeStruct((points * order, cols), jnp.bfloat16)
    high_part, low_part = pl.pallas_call(
        split_kernel,
        out_shape=(half_type, half_type),
        in_specs=[VMEM],
        out_specs=(VMEM, VMEM),
        compiler_params=PARAMS,
        cost_estimate=pl.CostEstimate(flops=0, bytes_accessed=8 * points * order * cols, transcendentals=0),
        name="split",
    )(basis)
    points_in_all = points * cols
    steps = []
    for axis in ("gx", "gy", "gz"):
        size = lax.axis_size(axis)
        points_in_all *= size
        steps += [(axis, 1 << bit) for bit in range(axis == "gz", size.bit_length() - 1)]
    assert lax.axis_size("gz") % 2 == 0
    across = [(i, i ^ 1) for i in range(lax.axis_size("gz"))]
    own = keep + lax.ppermute(send, "gz", across)
    turns = [steps[i : i + 2] for i in range(0, len(steps), 2)]
    turn = len(turns) // 2 if len(steps) % 2 == 0 else 0
    own = summed(own, (turns, turns[turn:] + turns[:turn]))
    other = lax.ppermute(own, "gz", across)
    upper, basis_q = pl.pallas_call(
        functools.partial(finish_kernel, count=float(points_in_all), step=8),
        out_shape=(float_of(order, order), float_of(order, points, cols)),
        in_specs=[VMEM] * 4,
        out_specs=(VMEM, HBM),
        scratch_shapes=[pltpu.VMEM((order * points, cols), jnp.float32), pltpu.SemaphoreType.DMA((layers,))],
        compiler_params=PARAMS,
        name="finish",
    )(own, other, high_part, low_part)
    return basis_q.reshape(order, layers, rows, cols), upper


def solution(mesh):
    in_specs = (
        P(None, "gz", "gx", "gy"),
        P("gz", "gx", "gy"),
        P("gz", "gx", "gy"),
        P("gz", "gx", "gy"),
        P("gz", "gx", "gy"),
        P(),
    )
    out_specs = (P(None, "gz", "gx", "gy"), P())
    return jax.shard_map(local, mesh=mesh, in_specs=in_specs, out_specs=out_specs, check_vma=False)
```

```python
import functools

import jax
import jax.numpy as jnp
from jax import lax
from jax.experimental import pallas as pl
from jax.experimental.pallas import tpu as pltpu
from jax.sharding import PartitionSpec as P

POWERS = 4


newton_shifts = (15.4, 0.6, 11.7, 4.3)
basis_scale = 0.125

VMEM = pl.BlockSpec(memory_space=pltpu.VMEM)
SMEM = pl.BlockSpec(memory_space=pltpu.SMEM)
HBM = pl.BlockSpec(memory_space=pltpu.HBM)
PARAMS = pltpu.CompilerParams(vmem_limit_bytes=32 * 1024 * 1024)
FIRST = pltpu.CompilerParams(vmem_limit_bytes=60 * 1024 * 1024)

COEFS = 4
TILE = 8
CORNERS = ((1, 3), (1, 2), (1, 1), (2, 2), (2, 1), (3, 1))


def positions(shape):
    sub = lax.broadcasted_iota(jnp.int32, shape, 0)
    lane = lax.broadcasted_iota(jnp.int32, shape, 1)
    return sub, lane


def coefs_at(ref, start, i):
    place = start + COEFS * (i // 2) * 2
    tile = ref[place : place + TILE, :]
    return pltpu.roll(tile, COEFS, 0) if i % 2 else tile


def edges_kernel(
    load_ref, rows_ref, cols_ref, vias_ref, ground_ref, offset_ref,
    first_ref, second_ref, tile_ref, flat_ref, shift_ref, fields_in, coefs_in, sems,
):
    slabs, _, cols = tile_ref.shape
    fields = load_ref.shape[0] // slabs
    layers, rows, _ = rows_ref.shape
    depth = POWERS
    half = rows // 2
    total_layers = offset_ref.shape[0]
    copies = [
        pltpu.make_async_copy(ref, coefs_in.at[i], sems.at[i])
        for i, ref in enumerate((rows_ref, cols_ref, vias_ref, ground_ref))
    ]
    copies.append(pltpu.make_async_copy(load_ref, fields_in, sems.at[COEFS]))
    for copy in copies:
        copy.start()
    gx, gy, gz = (lax.axis_index(name) for name in ("gx", "gy", "gz"))
    last_row = jnp.where(gx == lax.axis_size("gx") - 1, rows - 1, rows)
    last_col = jnp.where(gy == lax.axis_size("gy") - 1, cols - 1, cols)
    sub, lane = positions((TILE, cols))
    for e in range(shift_ref.shape[0]):
        layer = gz * layers + e - depth
        inside = (layer >= 0) & (layer < total_layers)
        value = jnp.where(inside, offset_ref[jnp.clip(layer, 0, total_layers - 1)], 0)
        shift_ref[e] = jnp.broadcast_to(value, (TILE, cols))
    for copy in copies:
        copy.wait()

    def joined(one, two):
        return jnp.where(sub < COEFS, one, pltpu.roll(two, COEFS, 0))

    for l in range(layers):
        layer = gz * layers + l
        target = gy * cols + lane + shift_ref[depth + l]
        via_ok = (target >= 0) & (target < cols * lax.axis_size("gy"))
        via_ok = via_ok & (jnp.broadcast_to(layer, lane.shape) < total_layers - 1)
        four = (
            jnp.where(sub == last_row, 0.0, coefs_in[0, l]),
            jnp.where(lane == last_col, 0.0, coefs_in[1, l]),
            jnp.where(via_ok, coefs_in[2, l], 0.0),
            coefs_in[3, l],
        )
        for r in range(rows):
            slab = l * rows + r
            value = jnp.zeros((TILE, cols), jnp.float32)
            for c in range(COEFS):
                value = jnp.where(sub == c, jnp.broadcast_to(four[c][r : r + 1, :], (TILE, cols)), value)
            tile_ref[slab] = value
    for i in range(0, slabs, 2):
        flat_ref[COEFS * i : COEFS * i + TILE, :] = joined(tile_ref[i], tile_ref[i + 1])
    even = lax.rem(gx, 2) == 0
    for ref, start in ((first_ref, jnp.where(even, half, 0)), (second_ref, jnp.where(even, 0, half))):
        for l in range(layers):
            for i in range(half):
                slab = l * rows + start + i
                at = l * half + i
                for f in range(0, fields, TILE):
                    tile = fields_in[pl.ds(f * slabs + slab, TILE, stride=slabs), :]
                    ref[at * fields + f : at * fields + f + TILE, :] = tile
                if i % 2 == 0:
                    place = layers * half * fields + COEFS * at
                    ref[place : place + TILE, :] = joined(tile_ref[slab], tile_ref[slab + 1])


def own_kernel(load_ref, tile_ref, block_ref):
    slabs, planes, _ = block_ref.shape
    for slab in range(slabs):
        for f in range(0, planes - TILE, TILE):
            block_ref[slab, f : f + TILE, :] = load_ref[pl.ds(f * slabs + slab, TILE, stride=slabs), :]
        block_ref[slab, planes - TILE :, :] = tile_ref[slab]


def corners_kernel(first_ref, second_ref, flat_ref, after_ref, before_ref, one_ref, two_ref, *, layers):
    slabs, planes, cols = after_ref.shape
    fields = planes - TILE
    half = slabs // layers
    count = len(CORNERS)
    sub, _ = positions((TILE, cols))
    even_row = jnp.broadcast_to(lax.rem(lax.axis_index("gx"), 2), (TILE, cols)) == 0
    even_layer = jnp.broadcast_to(lax.rem(lax.axis_index("gz"), 2), (TILE, cols)) == 0
    row_block = jnp.broadcast_to(lax.axis_index("gx"), (TILE, cols))
    has_prev, has_next = row_block > 0, row_block < lax.axis_size("gx") - 1
    for f in range(0, planes, TILE):
        after, before = [], []
        for i in range(slabs):
            if f < fields:
                first, second = (ref[i * fields + f : i * fields + f + TILE, :] for ref in (first_ref, second_ref))
            else:
                first, second = (coefs_at(ref, slabs * fields, i) for ref in (first_ref, second_ref))
            after.append(jnp.where(has_prev, jnp.where(even_row, second, first), 0.0))
            before.append(jnp.where(has_next, jnp.where(even_row, first, second), 0.0))
            after_ref[i, f : f + TILE, :] = after[i]
            before_ref[i, f : f + TILE, :] = before[i]
        ones, twos = [], []
        for source, step in ((after, -1), (before, 1)):
            for dz, dx in CORNERS:
                row = half - dx if step < 0 else dx - 1
                up, down = source[(layers - dz) * half + row], source[(dz - 1) * half + row]
                ones.append(jnp.where(even_layer, up, down))
                twos.append(jnp.where(even_layer, down, up))
        for ref, values in ((one_ref, ones), (two_ref, twos)):
            if f < fields:
                for i, value in enumerate(values):
                    ref[i * fields + f : i * fields + f + TILE, :] = value
            else:
                for i in range(0, 2 * count, 2):
                    place = 2 * count * fields + COEFS * i
                    pair = jnp.where(sub < COEFS, values[i], pltpu.roll(values[i + 1], COEFS, 0))
                    ref[place : place + TILE, :] = pair
    for ref in (one_ref, two_ref):
        place = 2 * count * planes - 2 * count * (TILE - COEFS)
        ref[place : place + flat_ref.shape[0], :] = flat_ref[...]


def slabs_of(e, layers, rows, planes, corners, inner, block, after, before, one, two, corner_one=None, corner_two=None):
    depth, half, count = POWERS, rows // 2, len(CORNERS)
    cols = block.shape[2] if block is not None else corner_one.shape[1]
    fields, slabs = planes - TILE, layers * rows

    def plain(ref, slab):
        return lambda f: ref[slab, f : f + TILE, :]

    def chosen(read, one, two):
        place = jnp.broadcast_to(lax.axis_index("gz"), (TILE, cols))
        even = lax.rem(place, 2) == 0
        there = place > 0 if e < depth else place < lax.axis_size("gz") - 1
        return lambda f: jnp.where(there, jnp.where(even, read(one, f), read(two, f)), 0.0)

    def home(slab):
        return lambda ref, f: ref[pl.ds(f * slabs + slab, TILE, stride=slabs), :]

    def home_coefs(slab):
        return lambda ref, f: coefs_at(ref, 2 * count * (fields + COEFS), slab)

    def corner(i):
        def read(ref, f):
            if f < fields:
                return ref[i * fields + f : i * fields + f + TILE, :]
            return coefs_at(ref, 2 * count * fields, i)

        return read

    tiles = [f for f in range(0, planes, TILE)]
    found = []
    if depth <= e < depth + layers:
        l = e - depth
        if inner:
            found += [(depth + r, plain(block, l * rows + r), tiles) for r in range(rows)]
            for i in range(half):
                found.append((i, plain(after, l * half + i), tiles))
                found.append((depth + rows + i, plain(before, l * half + i), tiles))
        return found
    if e < depth:
        pair, corner_pair, first, distance = (two, one), (corner_two, corner_one), 0, depth - e
    else:
        pair, corner_pair = (one, two), (corner_one, corner_two)
        first, distance = depth + layers, e - depth - layers + 1
    for r in range(rows):
        slab = (e - first) * rows + r
        if inner:
            found.append((depth + r, chosen(home(slab), *pair), tiles[:-1]))
        if corners:
            found.append((depth + r, chosen(home_coefs(slab), *corner_pair), tiles[-1:]))
    for i, (dz, dx) in enumerate(CORNERS):
        if dz == distance and corners:
            found.append((depth - dx, chosen(corner(i), *corner_pair), tiles))
            found.append((depth + rows - 1 + dx, chosen(corner(count + i), *corner_pair), tiles))
    return found


def inner_kernel(*refs, layers, rows):
    sources, edge_ref = refs[:5], refs[5]
    high, planes, cols = edge_ref.shape
    depth = POWERS
    group = 2 * depth
    _, lane = positions((TILE, cols))
    for e in range(high):
        found = slabs_of(e, layers, rows, planes, False, True, *sources)
        for f in range(0, planes, TILE):
            total = jnp.zeros((TILE, cols), jnp.float32)
            for row, read, tiles in found:
                if f in tiles:
                    moved = pltpu.roll(read(f), (group * row + depth) % cols, 1)
                    total = jnp.where((lane >= group * row) & (lane < group * row + group), moved, total)
            edge_ref[e, f : f + TILE, :] = total


def sides_kernel(inner_ref, one_ref, two_ref, edge_ref, *out_refs, layers, rows, pair):
    high, planes, cols = edge_ref.shape
    depth = POWERS
    group = 2 * depth
    _, lane = positions((TILE, cols))
    early = lax.rem(lane, group) < depth
    gy = jnp.broadcast_to(lax.axis_index("gy"), (TILE, cols))
    for f in range(0, planes, TILE):
        here = slice(f, f + TILE)
        edges = []
        for e in range(high):
            total = inner_ref[e, here, :]
            for row, read, tiles in slabs_of(e, layers, rows, planes, True, False, None, None, None, None, None, one_ref, two_ref):
                if f in tiles:
                    moved = pltpu.roll(read(f), (group * row + depth) % cols, 1)
                    total = jnp.where((lane >= group * row) & (lane < group * row + group), moved, total)
            edge_ref[e, here, :] = total
            edges.append(total)
        for t in range(high // 2):
            one, two = edges[2 * t], edges[2 * t + 1]
            up = jnp.where(early, one, pltpu.roll(two, depth, 1))
            down = jnp.where(early, pltpu.roll(one, cols - depth, 1), two)
            if pair:
                out_refs[0][t, here, :] = jnp.where(gy == 0, up, down)
            else:
                out_refs[0][t, here, :] = up
                out_refs[1][t, here, :] = down


def assemble_kernel(*refs, layers, rows):
    sources, start_ref = refs[:7], refs[7]
    high, _, planes, _ = start_ref.shape
    for e in range(high):
        for row, read, tiles in slabs_of(e, layers, rows, planes, True, True, *sources):
            for f in tiles:
                start_ref[e, row, f : f + TILE, :] = read(f)


def powers_kernel(*refs, fields, layers, rows, pair):
    gots = 1 if pair else 2
    start_ref, edge_ref, got_refs, shift_ref = refs[0], refs[1], refs[2 : 2 + gots], refs[2 + gots]
    basis_ref, keep_ref, send_ref, power_ref, coef_ref, strip_ref, strip_coef_ref, border_ref, sum_ref = refs[3 + gots :]
    high, tall, planes, cols = start_ref.shape
    depth = POWERS
    group = 2 * depth
    order = depth * fields
    tiles = range(0, fields, TILE)
    _, lane = positions((TILE, cols))
    gy = lax.axis_index("gy")

    def masks(e):
        shift = shift_ref[e]
        return shift == 0, shift > 0

    def from_above(seen, mask):
        left, centre, right = seen
        return jnp.where(mask[0], centre, jnp.where(mask[1], right, left))

    def from_below(seen, mask):
        left, centre, right = seen
        return jnp.where(mask[0], centre, jnp.where(mask[1], left, right))

    def around(tile):
        return pltpu.roll(tile, 1, 1), tile, pltpu.roll(tile, cols - 1, 1)

    def spread(tile, c):
        return jnp.broadcast_to(tile[c : c + 1, :], (TILE, cols))

    def put_factors(put, tile, row_above, seen, seen_below, mask):
        down, right, upper, ground = (spread(tile, c) for c in range(COEFS))
        up = spread(row_above, 0)
        left = spread(seen[0], 1)
        lower = from_below([spread(x, 2) for x in seen_below], mask)
        diagonal = ground + down + up + right + left + upper + lower
        for i, value in enumerate((down, up, right, left, upper, lower, diagonal)):
            put(i, value * basis_scale)

    def step(factors, theta, seen, up, down, above, below):
        value = (factors[6] - theta) * seen[1]
        value = value - (factors[0] * down + factors[1] * up)
        value = value - (factors[2] * seen[2] + factors[3] * seen[0])
        return value - (factors[4] * above + factors[5] * below)

    thetas = [shift * basis_scale for shift in newton_shifts]

    early = lax.rem(lane, group) < depth
    if pair:
        first_side = jnp.where(gy == 0, 1, 0)
        last_side = first_side + 1
    else:
        first_side, last_side = 0, 2

    @pl.loop(first_side, last_side)
    def _(side):
        left_side = jnp.broadcast_to(side, (TILE, cols)) == 0
        from_edge = early != left_side
        for e in range(high):
            for f in range(0, planes, TILE):
                here = slice(f, f + TILE)
                outer = got_refs[0][e // 2, here, :]
                if not pair:
                    outer = jnp.where(left_side, outer, got_refs[1][e // 2, here, :])
                if e % 2 == 0:
                    outer = jnp.where(left_side, outer, pltpu.roll(outer, depth, 1))
                else:
                    outer = jnp.where(left_side, pltpu.roll(outer, cols - depth, 1), outer)
                strip_ref[side, 0, e, here, :] = jnp.where(from_edge, edge_ref[e, here, :], outer)
        raw = [strip_ref[side, 0, e, fields : fields + TILE, :] for e in range(high)]
        seen = [around(tile) for tile in raw]
        for e in range(1, high - 1):

            def put(i, value, e=e):
                strip_coef_ref[side, i, e] = value

            put_factors(put, raw[e], pltpu.roll(raw[e], group, 1), seen[e], seen[e - 1], masks(e - 1))
        for k in range(1, depth):
            reach = depth - k
            looks = {}

            def look(e, f, k=k, looks=looks):
                if (e, f) not in looks:
                    looks[e, f] = around(strip_ref[side, k - 1, e, f : f + TILE, :])
                return looks[e, f]

            for e in range(depth - reach, depth + layers + reach):
                factors = [strip_coef_ref[side, i, e] for i in range(7)]
                over, under = masks(e), masks(e - 1)
                for f in tiles:
                    here = look(e, f)
                    strip_ref[side, k, e, f : f + TILE, :] = step(
                        factors,
                        thetas[k - 1],
                        here,
                        pltpu.roll(here[1], group, 1),
                        pltpu.roll(here[1], cols - group, 1),
                        from_above(look(e + 1, f), over),
                        from_below(look(e - 1, f), under),
                    )

    gy_lane = jnp.broadcast_to(gy, (TILE, cols))
    on_left = (lax.rem(lane, group) == depth - 1) & (gy_lane > 0)
    on_right = (lax.rem(lane, group) == depth - 2) & (gy_lane < lax.axis_size("gy") - 1)

    @pl.loop(0, high)
    def _(e):
        for k in range(depth):
            for f in range(0, planes if k == 0 else fields, TILE):
                here = slice(f, f + TILE)
                right = jnp.where(on_right, pltpu.roll(strip_ref[1, k, e, here, :], cols - 2, 1), 0.0)
                border_ref[k, e, here, :] = jnp.where(on_left, strip_ref[0, k, e, here, :], right)

    leftmost, rightmost = lane == 0, lane == cols - 1

    def looked(k, e, row, f):
        here = slice(f, f + TILE)
        tile = start_ref[e, row, here, :] if k == 0 else power_ref[k - 1, e, row, here, :]
        turn = (2 * cols - group * row - depth + 1) % cols
        outer = pltpu.roll(border_ref[k, e, here, :], turn, 1)
        left, _, right = around(tile)
        return jnp.where(leftmost, outer, left), tile, jnp.where(rightmost, outer, right)

    def by_rows(reach, body):
        for r in range(rows):
            body(depth + r, depth - reach, depth + layers + reach)

        for dx in range(1, reach + 1):
            for row in (depth - dx, depth + rows - 1 + dx):
                body(row, depth - reach + dx, depth + layers + reach - dx)

    def factors_of_row(row, first, last):
        seen = {e: looked(0, e, row, fields) for e in range(first - 1, last)}
        for e in range(first, last):

            def put(i, value, e=e):
                coef_ref[i, e, row] = value

            above_row = start_ref[e, row - 1, fields : fields + TILE, :]
            put_factors(put, seen[e][1], above_row, seen[e], seen[e - 1], masks(e - 1))

    by_rows(depth - 1, factors_of_row)

    for k in range(1, depth + 1):

        def advance(row, first, last, k=k):
            source = start_ref if k == 1 else power_ref.at[k - 2]
            below = {f: from_below(looked(k - 1, first - 1, row, f), masks(first - 1)) for f in tiles}
            centre = {f: looked(k - 1, first, row, f) for f in tiles}
            for e in range(first, last):
                factors = [coef_ref[i, e, row] for i in range(7)]
                mask = masks(e)
                for f in tiles:
                    here = slice(f, f + TILE)
                    upper = looked(k - 1, e + 1, row, f)
                    value = step(
                        factors,
                        thetas[k - 1],
                        centre[f],
                        source[e, row - 1, here, :],
                        source[e, row + 1, here, :],
                        from_above(upper, mask),
                        below[f],
                    )
                    below[f], centre[f] = from_below(centre[f], mask), upper
                    if k < depth:
                        power_ref[k - 1, e, row, here, :] = value
                    if first == k and depth <= e < depth + layers:
                        slab = (e - depth) * rows + row - depth
                        place = slab * order + (k - 1) * fields + f
                        basis_ref[place : place + TILE, :] = value

        if k < depth:
            by_rows(depth - k, advance)

    def share(r):
        value = None
        for l in range(0, layers, 2):
            places = [((l + i) * rows + r) * order for i in range(2)]
            wide = jnp.concatenate([basis_ref[place : place + order, :] for place in places], axis=1)
            product = lax.dot_general(
                wide, wide, (((1,), (1,)), ((), ())),
                precision=lax.Precision.HIGHEST, preferred_element_type=jnp.float32,
            )
            value = product if value is None else value + product
        return value

    advance(depth, depth, depth + layers)
    for r in range(1, rows):
        total = share(r - 1) if r == 1 else total + share(r - 1)
        advance(depth + r, depth, depth + layers)
    total = total + share(rows - 1)
    sum_ref[...] = total
    half = order // 2
    odd = lax.rem(lax.axis_index("gz"), 2)
    keep_ref[...] = sum_ref[pl.ds(pl.multiple_of(odd * half, TILE), half), :]
    send_ref[...] = sum_ref[pl.ds(pl.multiple_of((1 - odd) * half, TILE), half), :]


def eliminate(tiles, order, step):
    width = tiles[0].shape[1]
    lane = lax.broadcasted_iota(jnp.int32, (8, width), 1)
    sub = lax.broadcasted_iota(jnp.int32, (8, width), 0)
    spread = lambda value: jnp.broadcast_to(value, (8, width))
    for first in range(0, order, step):
        home, base = first // 8, first % 8
        panel = tiles[home]
        entry = {}
        for i in range(step):
            for j in range(i, step):
                entry[i, j] = spread(panel[base + i : base + i + 1, first + j : first + j + 1])
        rows = [spread(panel[base + i : base + i + 1, :]) for i in range(step)]
        inverse = []
        done = []
        for i in range(step):
            row = rows[i]
            if i:
                row = jnp.where((lane >= first) & (lane < first + i), 0.0, row)
            factors = []
            for j in range(i):
                factor = entry[j, i] * inverse[j]
                factors.append(factor)
            for j in range(i):
                source = jnp.where(lane == first + j, 1.0, done[j])
                if i - j > 1:
                    source = jnp.where((lane > first + j) & (lane < first + i), 0.0, source)
                row = row - factors[j] * source
                for m in range(i, step):
                    entry[i, m] = entry[i, m] - factors[j] * entry[j, m]
            inverse.append(1.0 / entry[i, i])
            done.append(row)
        sources = []
        for j in range(step):
            source = jnp.where(lane == first + j, 1.0, done[j])
            if j < step - 1:
                source = jnp.where((lane > first + j) & (lane < first + step), 0.0, source)
            sources.append(source)
        inside = (lane >= first) & (lane < first + step)
        for t in range(home, order // 8):
            if t == home and base + step == 8:
                fresh = tiles[t]
            else:
                columns = [spread(tiles[t][:, first + j : first + j + 1]) for j in range(step)]
                fresh = jnp.where(inside, 0.0, tiles[t])
                for j in range(step):
                    factor = columns[j] * inverse[j]
                    fresh = fresh - factor * sources[j]
                    for m in range(j + 1, step):
                        columns[m] = columns[m] - factor * entry[j, m]
            if t == home:
                fresh = jnp.where(sub < base + step, tiles[t], fresh)
                for j in range(step):
                    fresh = jnp.where(sub == base + j, done[j], fresh)
            tiles[t] = fresh
    return tiles


def finish_kernel(*refs, count, step):
    own_ref, other_ref, high_ref, low_ref, upper_ref, out_ref, staged, sems = refs
    order = upper_ref.shape[0]
    points = high_ref.shape[0] // order
    even = jnp.broadcast_to(lax.rem(lax.axis_index("gz"), 2), (TILE, order)) == 0
    halves = [[], []]
    for r in range(0, order // 2, TILE):
        own, other = own_ref[r : r + TILE, :] / count, other_ref[r : r + TILE, :] / count
        halves[0].append(jnp.where(even, own, other))
        halves[1].append(jnp.where(even, other, own))
    tiles = eliminate(halves[0] + halves[1], order, step)
    lane = lax.broadcasted_iota(jnp.int32, (8, order), 1)
    sub = lax.broadcasted_iota(jnp.int32, (8, order), 0)
    inverse = []
    for t in range(order // 8):
        row = sub + 8 * t
        pivot = jnp.sum(jnp.where(lane == row, tiles[t], 0.0), axis=1, keepdims=True)
        scale = 1.0 / jnp.sqrt(pivot)
        upper_ref[8 * t : 8 * t + 8, :] = jnp.where(lane >= row, tiles[t] * scale, 0.0)
        inverse.append(jnp.where(lane < row, tiles[t], jnp.where(lane == row, 1.0, 0.0)) * scale)
    inverse = jnp.concatenate(inverse, axis=0)
    cols = high_ref.shape[1]
    inverse_parts = two_parts(inverse)
    chunk = points // sems.shape[0]
    copies = []
    for i in range(0, points, 2):
        start = i * order
        wide = [
            jnp.concatenate([ref[start : start + order, :], ref[start + order : start + 2 * order, :]], axis=1)
            for ref in (high_ref, low_ref)
        ]
        out = product(inverse_parts, wide)
        staged[pl.ds(i, order, stride=points), :] = out[:, :cols]
        staged[pl.ds(i + 1, order, stride=points), :] = out[:, cols:]
        if (i + 2) % chunk == 0:
            part = pl.ds(i + 2 - chunk, chunk)
            source = staged.reshape(order, points, cols).at[:, part, :]
            copies.append(pltpu.make_async_copy(source, out_ref.at[:, part, :], sems.at[i // chunk]))
            copies[-1].start()
    for copy in copies:
        copy.wait()


def split_kernel(basis_ref, high_ref, low_ref):
    size = 2 * TILE

    @pl.loop(0, basis_ref.shape[0] // size, unroll=8)
    def _(i):
        here = pl.ds(pl.multiple_of(i * size, size), size)
        high_ref[here, :], low_ref[here, :] = two_parts(basis_ref[here, :])


def two_parts(value):
    high = value.astype(jnp.bfloat16)
    return high, (value - high.astype(jnp.float32)).astype(jnp.bfloat16)


def product(left, right):
    dot = functools.partial(jnp.dot, preferred_element_type=jnp.float32)
    return dot(left[0], right[0]) + (dot(left[0], right[1]) + dot(left[1], right[0]))


def summed(value, rounds_of):
    axes = ("gx", "gy", "gz")
    sizes = [lax.axis_size(name) for name in axes]
    assert all(size & (size - 1) == 0 for size in sizes)

    def index(place):
        return (place[0] * sizes[1] + place[1]) * sizes[2] + place[2]

    for r in range(len(rounds_of[0])):
        got = []
        for chosen in range(1, 1 << len(rounds_of[0][r])):
            pairs = []
            for x in range(sizes[0]):
                for y in range(sizes[1]):
                    for z in range(sizes[2]):
                        partner = [x, y, z]
                        for bit, (axis, mask) in enumerate(rounds_of[z % 2][r]):
                            if chosen >> bit & 1:
                                partner[axes.index(axis)] ^= mask
                        pairs.append((index((x, y, z)), index(partner)))
            got.append(lax.ppermute(value, axes, pairs))
        value = value + got[0]
        if len(got) == 3:
            value = value + (got[1] + got[2])
    return value


def swapped(value, axis, phase):
    pairs = []
    for i in range(phase, lax.axis_size(axis) - 1, 2):
        pairs += [(i, i + 1), (i + 1, i)]
    paired = {i for i, _ in pairs}
    pairs += [(i, i) for i in range(lax.axis_size(axis)) if i not in paired]
    return lax.ppermute(value, axis, pairs)


def sent(value, steps):
    axes = tuple(steps)
    sizes = [lax.axis_size(name) for name in axes]
    pairs = []
    if len(axes) == 1:
        pairs = [(i, i + steps[axes[0]]) for i in range(sizes[0]) if 0 <= i + steps[axes[0]] < sizes[0]]
        return lax.ppermute(value, axes[0], pairs)
    for i in range(sizes[0]):
        for j in range(sizes[1]):
            m, n = i + steps[axes[0]], j + steps[axes[1]]
            if 0 <= m < sizes[0] and 0 <= n < sizes[1]:
                pairs.append((i * sizes[1] + j, m * sizes[1] + n))
    return lax.ppermute(value, axes, pairs)


def local(load_currents, cond_rows, cond_cols, cond_vias, ground, via_offset):
    fields, layers, rows, cols = load_currents.shape
    depth = POWERS
    assert layers == depth and rows == 2 * depth and cols == 4 * depth * rows and fields % TILE == 0
    float_of = lambda *shape: jax.ShapeDtypeStruct(shape, jnp.float32)
    pair = lax.axis_size("gy") == 2
    planes = fields + TILE
    slabs = layers * rows
    high = layers + 2 * depth
    tall = rows + 2 * depth
    count = len(CORNERS)
    part = float_of(slabs // 2, planes, cols)
    flat_rows = (slabs // 2) * (fields + COEFS)
    corner_rows = 2 * count * (fields + COEFS) + slabs * COEFS
    raw = load_currents.reshape(fields * slabs, cols)
    one = swapped(raw, "gz", 0)
    two = swapped(raw, "gz", 1)
    first, second, coef_tiles, coef_rows, shifts = pl.pallas_call(
        edges_kernel,
        out_shape=(
            float_of(flat_rows, cols),
            float_of(flat_rows, cols),
            float_of(slabs, TILE, cols),
            float_of(slabs * COEFS, cols),
            jax.ShapeDtypeStruct((high, TILE, cols), jnp.int32),
        ),
        in_specs=[HBM] * 5 + [SMEM],
        out_specs=(VMEM,) * 5,
        scratch_shapes=[
            pltpu.VMEM((fields * slabs, cols), jnp.float32),
            pltpu.VMEM((COEFS, layers, rows, cols), jnp.float32),
            pltpu.SemaphoreType.DMA((COEFS + 1,)),
        ],
        compiler_params=FIRST,
        name="edges",
    )(raw, cond_rows, cond_cols, cond_vias, ground, via_offset)
    first, second = swapped(first, "gx", 0), swapped(second, "gx", 1)
    block = pl.pallas_call(
        own_kernel,
        out_shape=float_of(slabs, planes, cols),
        in_specs=[VMEM] * 2,
        out_specs=VMEM,
        compiler_params=PARAMS,
        cost_estimate=pl.CostEstimate(flops=0, bytes_accessed=8 * slabs * planes * cols, transcendentals=0),
        name="own",
    )(raw, coef_tiles)
    after, before, to_first, to_second = pl.pallas_call(
        functools.partial(corners_kernel, layers=layers),
        out_shape=(part, part) + (float_of(corner_rows, cols),) * 2,
        in_specs=[VMEM] * 3,
        out_specs=(VMEM,) * 4,
        compiler_params=PARAMS,
        name="corners",
    )(first, second, coef_rows)
    to_first, to_second = swapped(to_first, "gz", 0), swapped(to_second, "gz", 1)
    pieces = (block, after, before, one, two)
    inner = pl.pallas_call(
        functools.partial(inner_kernel, layers=layers, rows=rows),
        out_shape=float_of(high, planes, cols),
        in_specs=[VMEM] * 5,
        out_specs=VMEM,
        compiler_params=PARAMS,
        cost_estimate=pl.CostEstimate(flops=0, bytes_accessed=16 * slabs * planes * cols, transcendentals=0),
        name="inner",
    )(*pieces)
    edge, *outer = pl.pallas_call(
        functools.partial(sides_kernel, layers=layers, rows=rows, pair=pair),
        out_shape=(float_of(high, planes, cols),) + (float_of(high // 2, planes, cols),) * (1 if pair else 2),
        in_specs=[VMEM] * 3,
        out_specs=(VMEM,) * (2 if pair else 3),
        compiler_params=PARAMS,
        name="sides",
    )(inner, to_first, to_second)
    pieces += (to_first, to_second)
    if pair:
        got = [lax.ppermute(outer[0], "gy", [(0, 1), (1, 0)])]
    else:
        got = [sent(outer[0], {"gy": 1}), sent(outer[1], {"gy": -1})]
    start = pl.pallas_call(
        functools.partial(assemble_kernel, layers=layers, rows=rows),
        out_shape=float_of(high, tall, planes, cols),
        in_specs=[VMEM] * 7,
        out_specs=VMEM,
        compiler_params=PARAMS,
        cost_estimate=pl.CostEstimate(flops=0, bytes_accessed=2 * high * tall * planes * cols, transcendentals=0),
        name="assemble",
    )(*pieces)
    order = depth * fields
    points = slabs
    basis, keep, send = pl.pallas_call(
        functools.partial(powers_kernel, fields=fields, layers=layers, rows=rows, pair=pair),
        out_shape=(float_of(points * order, cols),) + (float_of(order // 2, order),) * 2,
        in_specs=[VMEM] * (3 + len(got)),
        out_specs=(VMEM,) * 3,
        scratch_shapes=[
            pltpu.VMEM((depth - 1, high, tall, fields, cols), jnp.float32),
            pltpu.VMEM((7, high, tall, TILE, cols), jnp.float32),
            pltpu.VMEM((2, depth, high, planes, cols), jnp.float32),
            pltpu.VMEM((2, 7, high, TILE, cols), jnp.float32),
            pltpu.VMEM((depth, high, planes, cols), jnp.float32),
            pltpu.VMEM((order, order), jnp.float32),
        ],
        compiler_params=PARAMS,
        name="powers",
    )(start, edge, *got, shifts)
    half_type = jax.ShapeDtypeStruct((points * order, cols), jnp.bfloat16)
    high_part, low_part = pl.pallas_call(
        split_kernel,
        out_shape=(half_type, half_type),
        in_specs=[VMEM],
        out_specs=(VMEM, VMEM),
        compiler_params=PARAMS,
        cost_estimate=pl.CostEstimate(flops=0, bytes_accessed=8 * points * order * cols, transcendentals=0),
        name="split",
    )(basis)
    points_in_all = points * cols
    steps = []
    for axis in ("gx", "gy", "gz"):
        size = lax.axis_size(axis)
        points_in_all *= size
        steps += [(axis, 1 << bit) for bit in range(axis == "gz", size.bit_length() - 1)]
    assert lax.axis_size("gz") % 2 == 0
    across = [(i, i ^ 1) for i in range(lax.axis_size("gz"))]
    own = keep + lax.ppermute(send, "gz", across)
    turns = [steps[i : i + 2] for i in range(0, len(steps), 2)]
    turn = len(turns) // 2 if len(steps) % 2 == 0 else 0
    own = summed(own, (turns, turns[turn:] + turns[:turn]))
    other = lax.ppermute(own, "gz", across)
    upper, basis_q = pl.pallas_call(
        functools.partial(finish_kernel, count=float(points_in_all), step=8),
        out_shape=(float_of(order, order), float_of(order, points, cols)),
        in_specs=[VMEM] * 4,
        out_specs=(VMEM, HBM),
        scratch_shapes=[pltpu.VMEM((order * points, cols), jnp.float32), pltpu.SemaphoreType.DMA((layers,))],
        compiler_params=PARAMS,
        name="finish",
    )(own, other, high_part, low_part)
    return basis_q.reshape(order, layers, rows, cols), upper


def solution(mesh):
    in_specs = (
        P(None, "gz", "gx", "gy"),
        P("gz", "gx", "gy"),
        P("gz", "gx", "gy"),
        P("gz", "gx", "gy"),
        P("gz", "gx", "gy"),
        P(),
    )
    out_specs = (P(None, "gz", "gx", "gy"), P())
    return jax.shard_map(local, mesh=mesh, in_specs=in_specs, out_specs=out_specs, check_vma=False)
```

```python
import functools

import jax
import jax.numpy as jnp
from jax import lax
from jax.experimental import pallas as pl
from jax.experimental.pallas import tpu as pltpu
from jax.sharding import PartitionSpec as P

POWERS = 4


newton_shifts = (15.4, 0.6, 11.7, 4.3)
basis_scale = 0.125

VMEM = pl.BlockSpec(memory_space=pltpu.VMEM)
SMEM = pl.BlockSpec(memory_space=pltpu.SMEM)
HBM = pl.BlockSpec(memory_space=pltpu.HBM)
PARAMS = pltpu.CompilerParams(vmem_limit_bytes=32 * 1024 * 1024)
FIRST = pltpu.CompilerParams(vmem_limit_bytes=60 * 1024 * 1024)

COEFS = 4
TILE = 8
CORNERS = ((1, 3), (1, 2), (1, 1), (2, 2), (2, 1), (3, 1))


def positions(shape):
    sub = lax.broadcasted_iota(jnp.int32, shape, 0)
    lane = lax.broadcasted_iota(jnp.int32, shape, 1)
    return sub, lane


def coefs_at(ref, start, i):
    place = start + COEFS * (i // 2) * 2
    tile = ref[place : place + TILE, :]
    return pltpu.roll(tile, COEFS, 0) if i % 2 else tile


def edges_kernel(
    load_ref, rows_ref, cols_ref, vias_ref, ground_ref, offset_ref,
    first_ref, second_ref, tile_ref, flat_ref, shift_ref, fields_in, coefs_in, sems,
):
    slabs, _, cols = tile_ref.shape
    fields = load_ref.shape[0] // slabs
    layers, rows, _ = rows_ref.shape
    depth = POWERS
    half = rows // 2
    total_layers = offset_ref.shape[0]
    copies = [
        pltpu.make_async_copy(ref, coefs_in.at[i], sems.at[i])
        for i, ref in enumerate((rows_ref, cols_ref, vias_ref, ground_ref))
    ]
    copies.append(pltpu.make_async_copy(load_ref, fields_in, sems.at[COEFS]))
    for copy in copies:
        copy.start()
    gx, gy, gz = (lax.axis_index(name) for name in ("gx", "gy", "gz"))
    last_row = jnp.where(gx == lax.axis_size("gx") - 1, rows - 1, rows)
    last_col = jnp.where(gy == lax.axis_size("gy") - 1, cols - 1, cols)
    sub, lane = positions((TILE, cols))
    for e in range(shift_ref.shape[0]):
        layer = gz * layers + e - depth
        inside = (layer >= 0) & (layer < total_layers)
        value = jnp.where(inside, offset_ref[jnp.clip(layer, 0, total_layers - 1)], 0)
        shift_ref[e] = jnp.broadcast_to(value, (TILE, cols))
    for copy in copies:
        copy.wait()

    def joined(one, two):
        return jnp.where(sub < COEFS, one, pltpu.roll(two, COEFS, 0))

    for l in range(layers):
        layer = gz * layers + l
        target = gy * cols + lane + shift_ref[depth + l]
        via_ok = (target >= 0) & (target < cols * lax.axis_size("gy"))
        via_ok = via_ok & (jnp.broadcast_to(layer, lane.shape) < total_layers - 1)
        four = (
            jnp.where(sub == last_row, 0.0, coefs_in[0, l]),
            jnp.where(lane == last_col, 0.0, coefs_in[1, l]),
            jnp.where(via_ok, coefs_in[2, l], 0.0),
            coefs_in[3, l],
        )
        for r in range(rows):
            slab = l * rows + r
            value = jnp.zeros((TILE, cols), jnp.float32)
            for c in range(COEFS):
                value = jnp.where(sub == c, jnp.broadcast_to(four[c][r : r + 1, :], (TILE, cols)), value)
            tile_ref[slab] = value
    for i in range(0, slabs, 2):
        flat_ref[COEFS * i : COEFS * i + TILE, :] = joined(tile_ref[i], tile_ref[i + 1])
    even = lax.rem(gx, 2) == 0
    for ref, start in ((first_ref, jnp.where(even, half, 0)), (second_ref, jnp.where(even, 0, half))):
        for l in range(layers):
            for i in range(half):
                slab = l * rows + start + i
                at = l * half + i
                for f in range(0, fields, TILE):
                    tile = fields_in[pl.ds(f * slabs + slab, TILE, stride=slabs), :]
                    ref[at * fields + f : at * fields + f + TILE, :] = tile
                if i % 2 == 0:
                    place = layers * half * fields + COEFS * at
                    ref[place : place + TILE, :] = joined(tile_ref[slab], tile_ref[slab + 1])


def own_kernel(load_ref, tile_ref, block_ref):
    slabs, planes, _ = block_ref.shape
    for slab in range(slabs):
        for f in range(0, planes - TILE, TILE):
            block_ref[slab, f : f + TILE, :] = load_ref[pl.ds(f * slabs + slab, TILE, stride=slabs), :]
        block_ref[slab, planes - TILE :, :] = tile_ref[slab]


def corners_kernel(first_ref, second_ref, flat_ref, after_ref, before_ref, one_ref, two_ref, *, layers):
    slabs, planes, cols = after_ref.shape
    fields = planes - TILE
    half = slabs // layers
    count = len(CORNERS)
    sub, _ = positions((TILE, cols))
    even_row = jnp.broadcast_to(lax.rem(lax.axis_index("gx"), 2), (TILE, cols)) == 0
    even_layer = jnp.broadcast_to(lax.rem(lax.axis_index("gz"), 2), (TILE, cols)) == 0
    row_block = jnp.broadcast_to(lax.axis_index("gx"), (TILE, cols))
    has_prev, has_next = row_block > 0, row_block < lax.axis_size("gx") - 1
    for f in range(0, planes, TILE):
        after, before = [], []
        for i in range(slabs):
            if f < fields:
                first, second = (ref[i * fields + f : i * fields + f + TILE, :] for ref in (first_ref, second_ref))
            else:
                first, second = (coefs_at(ref, slabs * fields, i) for ref in (first_ref, second_ref))
            after.append(jnp.where(has_prev, jnp.where(even_row, second, first), 0.0))
            before.append(jnp.where(has_next, jnp.where(even_row, first, second), 0.0))
            after_ref[i, f : f + TILE, :] = after[i]
            before_ref[i, f : f + TILE, :] = before[i]
        ones, twos = [], []
        for source, step in ((after, -1), (before, 1)):
            for dz, dx in CORNERS:
                row = half - dx if step < 0 else dx - 1
                up, down = source[(layers - dz) * half + row], source[(dz - 1) * half + row]
                ones.append(jnp.where(even_layer, up, down))
                twos.append(jnp.where(even_layer, down, up))
        for ref, values in ((one_ref, ones), (two_ref, twos)):
            if f < fields:
                for i, value in enumerate(values):
                    ref[i * fields + f : i * fields + f + TILE, :] = value
            else:
                for i in range(0, 2 * count, 2):
                    place = 2 * count * fields + COEFS * i
                    pair = jnp.where(sub < COEFS, values[i], pltpu.roll(values[i + 1], COEFS, 0))
                    ref[place : place + TILE, :] = pair
    for ref in (one_ref, two_ref):
        place = 2 * count * planes - 2 * count * (TILE - COEFS)
        ref[place : place + flat_ref.shape[0], :] = flat_ref[...]


def slabs_of(e, layers, rows, planes, corners, inner, block, after, before, one, two, corner_one=None, corner_two=None):
    depth, half, count = POWERS, rows // 2, len(CORNERS)
    cols = block.shape[2] if block is not None else corner_one.shape[1]
    fields, slabs = planes - TILE, layers * rows

    def plain(ref, slab):
        return lambda f: ref[slab, f : f + TILE, :]

    def chosen(read, one, two):
        place = jnp.broadcast_to(lax.axis_index("gz"), (TILE, cols))
        even = lax.rem(place, 2) == 0
        there = place > 0 if e < depth else place < lax.axis_size("gz") - 1
        return lambda f: jnp.where(there, jnp.where(even, read(one, f), read(two, f)), 0.0)

    def home(slab):
        return lambda ref, f: ref[pl.ds(f * slabs + slab, TILE, stride=slabs), :]

    def home_coefs(slab):
        return lambda ref, f: coefs_at(ref, 2 * count * (fields + COEFS), slab)

    def corner(i):
        def read(ref, f):
            if f < fields:
                return ref[i * fields + f : i * fields + f + TILE, :]
            return coefs_at(ref, 2 * count * fields, i)

        return read

    tiles = [f for f in range(0, planes, TILE)]
    found = []
    if depth <= e < depth + layers:
        l = e - depth
        if inner:
            found += [(depth + r, plain(block, l * rows + r), tiles) for r in range(rows)]
            for i in range(half):
                found.append((i, plain(after, l * half + i), tiles))
                found.append((depth + rows + i, plain(before, l * half + i), tiles))
        return found
    if e < depth:
        pair, corner_pair, first, distance = (two, one), (corner_two, corner_one), 0, depth - e
    else:
        pair, corner_pair = (one, two), (corner_one, corner_two)
        first, distance = depth + layers, e - depth - layers + 1
    for r in range(rows):
        slab = (e - first) * rows + r
        if inner:
            found.append((depth + r, chosen(home(slab), *pair), tiles[:-1]))
        if corners:
            found.append((depth + r, chosen(home_coefs(slab), *corner_pair), tiles[-1:]))
    for i, (dz, dx) in enumerate(CORNERS):
        if dz == distance and corners:
            found.append((depth - dx, chosen(corner(i), *corner_pair), tiles))
            found.append((depth + rows - 1 + dx, chosen(corner(count + i), *corner_pair), tiles))
    return found


def inner_kernel(*refs, layers, rows):
    sources, edge_ref = refs[:5], refs[5]
    high, planes, cols = edge_ref.shape
    depth = POWERS
    group = 2 * depth
    _, lane = positions((TILE, cols))
    for e in range(high):
        found = slabs_of(e, layers, rows, planes, False, True, *sources)
        for f in range(0, planes, TILE):
            total = jnp.zeros((TILE, cols), jnp.float32)
            for row, read, tiles in found:
                if f in tiles:
                    moved = pltpu.roll(read(f), (group * row + depth) % cols, 1)
                    total = jnp.where((lane >= group * row) & (lane < group * row + group), moved, total)
            edge_ref[e, f : f + TILE, :] = total


def sides_kernel(inner_ref, one_ref, two_ref, edge_ref, *out_refs, layers, rows, pair):
    high, planes, cols = edge_ref.shape
    depth = POWERS
    group = 2 * depth
    _, lane = positions((TILE, cols))
    early = lax.rem(lane, group) < depth
    gy = jnp.broadcast_to(lax.axis_index("gy"), (TILE, cols))
    for f in range(0, planes, TILE):
        here = slice(f, f + TILE)
        edges = []
        for e in range(high):
            total = inner_ref[e, here, :]
            for row, read, tiles in slabs_of(e, layers, rows, planes, True, False, None, None, None, None, None, one_ref, two_ref):
                if f in tiles:
                    moved = pltpu.roll(read(f), (group * row + depth) % cols, 1)
                    total = jnp.where((lane >= group * row) & (lane < group * row + group), moved, total)
            edge_ref[e, here, :] = total
            edges.append(total)
        for t in range(high // 2):
            one, two = edges[2 * t], edges[2 * t + 1]
            up = jnp.where(early, one, pltpu.roll(two, depth, 1))
            down = jnp.where(early, pltpu.roll(one, cols - depth, 1), two)
            if pair:
                out_refs[0][t, here, :] = jnp.where(gy == 0, up, down)
            else:
                out_refs[0][t, here, :] = up
                out_refs[1][t, here, :] = down


def assemble_kernel(*refs, layers, rows):
    sources, start_ref = refs[:7], refs[7]
    high, _, planes, _ = start_ref.shape
    for e in range(high):
        for row, read, tiles in slabs_of(e, layers, rows, planes, True, True, *sources):
            for f in tiles:
                start_ref[e, row, f : f + TILE, :] = read(f)


def powers_kernel(*refs, fields, layers, rows, pair):
    gots = 1 if pair else 2
    start_ref, edge_ref, got_refs, shift_ref = refs[0], refs[1], refs[2 : 2 + gots], refs[2 + gots]
    basis_ref, keep_ref, send_ref, power_ref, coef_ref, strip_ref, strip_coef_ref, border_ref, sum_ref = refs[3 + gots :]
    high, tall, planes, cols = start_ref.shape
    depth = POWERS
    group = 2 * depth
    order = depth * fields
    tiles = range(0, fields, TILE)
    _, lane = positions((TILE, cols))
    gy = lax.axis_index("gy")

    def masks(e):
        shift = shift_ref[e]
        return shift == 0, shift > 0

    def from_above(seen, mask):
        left, centre, right = seen
        return jnp.where(mask[0], centre, jnp.where(mask[1], right, left))

    def from_below(seen, mask):
        left, centre, right = seen
        return jnp.where(mask[0], centre, jnp.where(mask[1], left, right))

    def around(tile):
        return pltpu.roll(tile, 1, 1), tile, pltpu.roll(tile, cols - 1, 1)

    def spread(tile, c):
        return jnp.broadcast_to(tile[c : c + 1, :], (TILE, cols))

    def put_factors(put, tile, row_above, seen, seen_below, mask):
        down, right, upper, ground = (spread(tile, c) for c in range(COEFS))
        up = spread(row_above, 0)
        left = spread(seen[0], 1)
        lower = from_below([spread(x, 2) for x in seen_below], mask)
        diagonal = ground + down + up + right + left + upper + lower
        for i, value in enumerate((down, up, right, left, upper, lower, diagonal)):
            put(i, value * basis_scale)

    def step(factors, theta, seen, up, down, above, below):
        value = (factors[6] - theta) * seen[1]
        value = value - (factors[0] * down + factors[1] * up)
        value = value - (factors[2] * seen[2] + factors[3] * seen[0])
        return value - (factors[4] * above + factors[5] * below)

    thetas = [shift * basis_scale for shift in newton_shifts]

    early = lax.rem(lane, group) < depth
    def advance_strip(side):
        left_side = jnp.broadcast_to(side, (TILE, cols)) == 0
        from_edge = early != left_side
        for e in range(high):
            for f in range(0, planes, TILE):
                here = slice(f, f + TILE)
                outer = got_refs[0][e // 2, here, :]
                if not pair:
                    outer = jnp.where(left_side, outer, got_refs[1][e // 2, here, :])
                if e % 2 == 0:
                    outer = jnp.where(left_side, outer, pltpu.roll(outer, depth, 1))
                else:
                    outer = jnp.where(left_side, pltpu.roll(outer, cols - depth, 1), outer)
                strip_ref[side, 0, e, here, :] = jnp.where(from_edge, edge_ref[e, here, :], outer)
        raw = [strip_ref[side, 0, e, fields : fields + TILE, :] for e in range(high)]
        seen = [around(tile) for tile in raw]
        for e in range(1, high - 1):

            def put(i, value, e=e):
                strip_coef_ref[side, i, e] = value

            put_factors(put, raw[e], pltpu.roll(raw[e], group, 1), seen[e], seen[e - 1], masks(e - 1))
        for k in range(1, depth):
            reach = depth - k
            looks = {}

            def look(e, f, k=k, looks=looks):
                if (e, f) not in looks:
                    looks[e, f] = around(strip_ref[side, k - 1, e, f : f + TILE, :])
                return looks[e, f]

            for e in range(depth - reach, depth + layers + reach):
                factors = [strip_coef_ref[side, i, e] for i in range(7)]
                over, under = masks(e), masks(e - 1)
                for f in tiles:
                    here = look(e, f)
                    strip_ref[side, k, e, f : f + TILE, :] = step(
                        factors,
                        thetas[k - 1],
                        here,
                        pltpu.roll(here[1], group, 1),
                        pltpu.roll(here[1], cols - group, 1),
                        from_above(look(e + 1, f), over),
                        from_below(look(e - 1, f), under),
                    )

    if pair:
        advance_strip(jnp.where(gy == 0, 1, 0))
    else:
        pl.loop(0, 2)(advance_strip)

    gy_lane = jnp.broadcast_to(gy, (TILE, cols))
    on_left = (lax.rem(lane, group) == depth - 1) & (gy_lane > 0)
    on_right = (lax.rem(lane, group) == depth - 2) & (gy_lane < lax.axis_size("gy") - 1)

    for e in range(high):
        for k in range(depth):
            for f in range(0, planes if k == 0 else fields, TILE):
                here = slice(f, f + TILE)
                right = jnp.where(on_right, pltpu.roll(strip_ref[1, k, e, here, :], cols - 2, 1), 0.0)
                border_ref[k, e, here, :] = jnp.where(on_left, strip_ref[0, k, e, here, :], right)

    leftmost, rightmost = lane == 0, lane == cols - 1

    def looked(k, e, row, f):
        here = slice(f, f + TILE)
        tile = start_ref[e, row, here, :] if k == 0 else power_ref[k - 1, e, row, here, :]
        turn = (2 * cols - group * row - depth + 1) % cols
        outer = pltpu.roll(border_ref[k, e, here, :], turn, 1)
        left, _, right = around(tile)
        return jnp.where(leftmost, outer, left), tile, jnp.where(rightmost, outer, right)

    def by_rows(reach, body):
        for r in range(rows):
            body(depth + r, depth - reach, depth + layers + reach)

        for dx in range(1, reach + 1):
            for row in (depth - dx, depth + rows - 1 + dx):
                body(row, depth - reach + dx, depth + layers + reach - dx)

    def factors_of_row(row, first, last):
        seen = {e: looked(0, e, row, fields) for e in range(first - 1, last)}
        for e in range(first, last):

            def put(i, value, e=e):
                coef_ref[i, e, row] = value

            above_row = start_ref[e, row - 1, fields : fields + TILE, :]
            put_factors(put, seen[e][1], above_row, seen[e], seen[e - 1], masks(e - 1))

    by_rows(depth - 1, factors_of_row)

    for k in range(1, depth + 1):

        def advance(row, first, last, k=k):
            source = start_ref if k == 1 else power_ref.at[k - 2]
            below = {f: from_below(looked(k - 1, first - 1, row, f), masks(first - 1)) for f in tiles}
            centre = {f: looked(k - 1, first, row, f) for f in tiles}
            for e in range(first, last):
                factors = [coef_ref[i, e, row] for i in range(7)]
                mask = masks(e)
                for f in tiles:
                    here = slice(f, f + TILE)
                    upper = looked(k - 1, e + 1, row, f)
                    value = step(
                        factors,
                        thetas[k - 1],
                        centre[f],
                        source[e, row - 1, here, :],
                        source[e, row + 1, here, :],
                        from_above(upper, mask),
                        below[f],
                    )
                    below[f], centre[f] = from_below(centre[f], mask), upper
                    if k < depth:
                        power_ref[k - 1, e, row, here, :] = value
                    if first == k and depth <= e < depth + layers:
                        slab = (e - depth) * rows + row - depth
                        place = slab * order + (k - 1) * fields + f
                        basis_ref[place : place + TILE, :] = value

        if k < depth:
            by_rows(depth - k, advance)

    def share(r):
        value = None
        for l in range(0, layers, 2):
            places = [((l + i) * rows + r) * order for i in range(2)]
            wide = jnp.concatenate([basis_ref[place : place + order, :] for place in places], axis=1)
            product = lax.dot_general(
                wide, wide, (((1,), (1,)), ((), ())),
                precision=lax.Precision.HIGHEST, preferred_element_type=jnp.float32,
            )
            value = product if value is None else value + product
        return value

    advance(depth, depth, depth + layers)
    for r in range(1, rows):
        total = share(r - 1) if r == 1 else total + share(r - 1)
        advance(depth + r, depth, depth + layers)
    total = total + share(rows - 1)
    sum_ref[...] = total
    half = order // 2
    odd = lax.rem(lax.axis_index("gz"), 2)
    keep_ref[...] = sum_ref[pl.ds(pl.multiple_of(odd * half, TILE), half), :]
    send_ref[...] = sum_ref[pl.ds(pl.multiple_of((1 - odd) * half, TILE), half), :]


def eliminate(tiles, order, step):
    width = tiles[0].shape[1]
    lane = lax.broadcasted_iota(jnp.int32, (8, width), 1)
    sub = lax.broadcasted_iota(jnp.int32, (8, width), 0)
    spread = lambda value: jnp.broadcast_to(value, (8, width))
    for first in range(0, order, step):
        home, base = first // 8, first % 8
        panel = tiles[home]
        entry = {}
        for i in range(step):
            for j in range(i, step):
                entry[i, j] = spread(panel[base + i : base + i + 1, first + j : first + j + 1])
        rows = [spread(panel[base + i : base + i + 1, :]) for i in range(step)]
        inverse = []
        done = []
        for i in range(step):
            row = rows[i]
            if i:
                row = jnp.where((lane >= first) & (lane < first + i), 0.0, row)
            factors = []
            for j in range(i):
                factor = entry[j, i] * inverse[j]
                factors.append(factor)
            for j in range(i):
                source = jnp.where(lane == first + j, 1.0, done[j])
                if i - j > 1:
                    source = jnp.where((lane > first + j) & (lane < first + i), 0.0, source)
                row = row - factors[j] * source
                for m in range(i, step):
                    entry[i, m] = entry[i, m] - factors[j] * entry[j, m]
            inverse.append(1.0 / entry[i, i])
            done.append(row)
        sources = []
        for j in range(step):
            source = jnp.where(lane == first + j, 1.0, done[j])
            if j < step - 1:
                source = jnp.where((lane > first + j) & (lane < first + step), 0.0, source)
            sources.append(source)
        inside = (lane >= first) & (lane < first + step)
        for t in range(home, order // 8):
            if t == home and base + step == 8:
                fresh = tiles[t]
            else:
                columns = [spread(tiles[t][:, first + j : first + j + 1]) for j in range(step)]
                fresh = jnp.where(inside, 0.0, tiles[t])
                for j in range(step):
                    factor = columns[j] * inverse[j]
                    fresh = fresh - factor * sources[j]
                    for m in range(j + 1, step):
                        columns[m] = columns[m] - factor * entry[j, m]
            if t == home:
                fresh = jnp.where(sub < base + step, tiles[t], fresh)
                for j in range(step):
                    fresh = jnp.where(sub == base + j, done[j], fresh)
            tiles[t] = fresh
    return tiles


def finish_kernel(*refs, count, step):
    own_ref, other_ref, high_ref, low_ref, upper_ref, out_ref, staged, sems = refs
    order = upper_ref.shape[0]
    points = high_ref.shape[0] // order
    even = jnp.broadcast_to(lax.rem(lax.axis_index("gz"), 2), (TILE, order)) == 0
    halves = [[], []]
    for r in range(0, order // 2, TILE):
        own, other = own_ref[r : r + TILE, :] / count, other_ref[r : r + TILE, :] / count
        halves[0].append(jnp.where(even, own, other))
        halves[1].append(jnp.where(even, other, own))
    tiles = eliminate(halves[0] + halves[1], order, step)
    lane = lax.broadcasted_iota(jnp.int32, (8, order), 1)
    sub = lax.broadcasted_iota(jnp.int32, (8, order), 0)
    inverse = []
    for t in range(order // 8):
        row = sub + 8 * t
        pivot = jnp.sum(jnp.where(lane == row, tiles[t], 0.0), axis=1, keepdims=True)
        scale = 1.0 / jnp.sqrt(pivot)
        upper_ref[8 * t : 8 * t + 8, :] = jnp.where(lane >= row, tiles[t] * scale, 0.0)
        inverse.append(jnp.where(lane < row, tiles[t], jnp.where(lane == row, 1.0, 0.0)) * scale)
    inverse = jnp.concatenate(inverse, axis=0)
    cols = high_ref.shape[1]
    inverse_parts = two_parts(inverse)
    chunk = points // sems.shape[0]
    copies = []
    for i in range(0, points, 2):
        start = i * order
        wide = [
            jnp.concatenate([ref[start : start + order, :], ref[start + order : start + 2 * order, :]], axis=1)
            for ref in (high_ref, low_ref)
        ]
        out = product(inverse_parts, wide)
        staged[pl.ds(i, order, stride=points), :] = out[:, :cols]
        staged[pl.ds(i + 1, order, stride=points), :] = out[:, cols:]
        if (i + 2) % chunk == 0:
            part = pl.ds(i + 2 - chunk, chunk)
            source = staged.reshape(order, points, cols).at[:, part, :]
            copies.append(pltpu.make_async_copy(source, out_ref.at[:, part, :], sems.at[i // chunk]))
            copies[-1].start()
    for copy in copies:
        copy.wait()


def split_kernel(basis_ref, high_ref, low_ref):
    size = 2 * TILE

    @pl.loop(0, basis_ref.shape[0] // size, unroll=8)
    def _(i):
        here = pl.ds(pl.multiple_of(i * size, size), size)
        high_ref[here, :], low_ref[here, :] = two_parts(basis_ref[here, :])


def two_parts(value):
    high = value.astype(jnp.bfloat16)
    return high, (value - high.astype(jnp.float32)).astype(jnp.bfloat16)


def product(left, right):
    dot = functools.partial(jnp.dot, preferred_element_type=jnp.float32)
    return dot(left[0], right[0]) + (dot(left[0], right[1]) + dot(left[1], right[0]))


def summed(value, rounds_of):
    axes = ("gx", "gy", "gz")
    sizes = [lax.axis_size(name) for name in axes]
    assert all(size & (size - 1) == 0 for size in sizes)

    def index(place):
        return (place[0] * sizes[1] + place[1]) * sizes[2] + place[2]

    for r in range(len(rounds_of[0])):
        got = []
        for chosen in range(1, 1 << len(rounds_of[0][r])):
            pairs = []
            for x in range(sizes[0]):
                for y in range(sizes[1]):
                    for z in range(sizes[2]):
                        partner = [x, y, z]
                        for bit, (axis, mask) in enumerate(rounds_of[z % 2][r]):
                            if chosen >> bit & 1:
                                partner[axes.index(axis)] ^= mask
                        pairs.append((index((x, y, z)), index(partner)))
            got.append(lax.ppermute(value, axes, pairs))
        value = value + got[0]
        if len(got) == 3:
            value = value + (got[1] + got[2])
    return value


def swapped(value, axis, phase):
    pairs = []
    for i in range(phase, lax.axis_size(axis) - 1, 2):
        pairs += [(i, i + 1), (i + 1, i)]
    paired = {i for i, _ in pairs}
    pairs += [(i, i) for i in range(lax.axis_size(axis)) if i not in paired]
    return lax.ppermute(value, axis, pairs)


def sent(value, steps):
    axes = tuple(steps)
    sizes = [lax.axis_size(name) for name in axes]
    pairs = []
    if len(axes) == 1:
        pairs = [(i, i + steps[axes[0]]) for i in range(sizes[0]) if 0 <= i + steps[axes[0]] < sizes[0]]
        return lax.ppermute(value, axes[0], pairs)
    for i in range(sizes[0]):
        for j in range(sizes[1]):
            m, n = i + steps[axes[0]], j + steps[axes[1]]
            if 0 <= m < sizes[0] and 0 <= n < sizes[1]:
                pairs.append((i * sizes[1] + j, m * sizes[1] + n))
    return lax.ppermute(value, axes, pairs)


def local(load_currents, cond_rows, cond_cols, cond_vias, ground, via_offset):
    fields, layers, rows, cols = load_currents.shape
    depth = POWERS
    assert layers == depth and rows == 2 * depth and cols == 4 * depth * rows and fields % TILE == 0
    float_of = lambda *shape: jax.ShapeDtypeStruct(shape, jnp.float32)
    pair = lax.axis_size("gy") == 2
    planes = fields + TILE
    slabs = layers * rows
    high = layers + 2 * depth
    tall = rows + 2 * depth
    count = len(CORNERS)
    part = float_of(slabs // 2, planes, cols)
    flat_rows = (slabs // 2) * (fields + COEFS)
    corner_rows = 2 * count * (fields + COEFS) + slabs * COEFS
    raw = load_currents.reshape(fields * slabs, cols)
    one = swapped(raw, "gz", 0)
    two = swapped(raw, "gz", 1)
    first, second, coef_tiles, coef_rows, shifts = pl.pallas_call(
        edges_kernel,
        out_shape=(
            float_of(flat_rows, cols),
            float_of(flat_rows, cols),
            float_of(slabs, TILE, cols),
            float_of(slabs * COEFS, cols),
            jax.ShapeDtypeStruct((high, TILE, cols), jnp.int32),
        ),
        in_specs=[HBM] * 5 + [SMEM],
        out_specs=(VMEM,) * 5,
        scratch_shapes=[
            pltpu.VMEM((fields * slabs, cols), jnp.float32),
            pltpu.VMEM((COEFS, layers, rows, cols), jnp.float32),
            pltpu.SemaphoreType.DMA((COEFS + 1,)),
        ],
        compiler_params=FIRST,
        name="edges",
    )(raw, cond_rows, cond_cols, cond_vias, ground, via_offset)
    first, second = swapped(first, "gx", 0), swapped(second, "gx", 1)
    block = pl.pallas_call(
        own_kernel,
        out_shape=float_of(slabs, planes, cols),
        in_specs=[VMEM] * 2,
        out_specs=VMEM,
        compiler_params=PARAMS,
        cost_estimate=pl.CostEstimate(flops=0, bytes_accessed=8 * slabs * planes * cols, transcendentals=0),
        name="own",
    )(raw, coef_tiles)
    after, before, to_first, to_second = pl.pallas_call(
        functools.partial(corners_kernel, layers=layers),
        out_shape=(part, part) + (float_of(corner_rows, cols),) * 2,
        in_specs=[VMEM] * 3,
        out_specs=(VMEM,) * 4,
        compiler_params=PARAMS,
        name="corners",
    )(first, second, coef_rows)
    to_first, to_second = swapped(to_first, "gz", 0), swapped(to_second, "gz", 1)
    pieces = (block, after, before, one, two)
    inner = pl.pallas_call(
        functools.partial(inner_kernel, layers=layers, rows=rows),
        out_shape=float_of(high, planes, cols),
        in_specs=[VMEM] * 5,
        out_specs=VMEM,
        compiler_params=PARAMS,
        cost_estimate=pl.CostEstimate(flops=0, bytes_accessed=16 * slabs * planes * cols, transcendentals=0),
        name="inner",
    )(*pieces)
    edge, *outer = pl.pallas_call(
        functools.partial(sides_kernel, layers=layers, rows=rows, pair=pair),
        out_shape=(float_of(high, planes, cols),) + (float_of(high // 2, planes, cols),) * (1 if pair else 2),
        in_specs=[VMEM] * 3,
        out_specs=(VMEM,) * (2 if pair else 3),
        compiler_params=PARAMS,
        name="sides",
    )(inner, to_first, to_second)
    pieces += (to_first, to_second)
    if pair:
        got = [lax.ppermute(outer[0], "gy", [(0, 1), (1, 0)])]
    else:
        got = [sent(outer[0], {"gy": 1}), sent(outer[1], {"gy": -1})]
    start = pl.pallas_call(
        functools.partial(assemble_kernel, layers=layers, rows=rows),
        out_shape=float_of(high, tall, planes, cols),
        in_specs=[VMEM] * 7,
        out_specs=VMEM,
        compiler_params=PARAMS,
        cost_estimate=pl.CostEstimate(flops=0, bytes_accessed=2 * high * tall * planes * cols, transcendentals=0),
        name="assemble",
    )(*pieces)
    order = depth * fields
    points = slabs
    basis, keep, send = pl.pallas_call(
        functools.partial(powers_kernel, fields=fields, layers=layers, rows=rows, pair=pair),
        out_shape=(float_of(points * order, cols),) + (float_of(order // 2, order),) * 2,
        in_specs=[VMEM] * (3 + len(got)),
        out_specs=(VMEM,) * 3,
        scratch_shapes=[
            pltpu.VMEM((depth - 1, high, tall, fields, cols), jnp.float32),
            pltpu.VMEM((7, high, tall, TILE, cols), jnp.float32),
            pltpu.VMEM((2, depth, high, planes, cols), jnp.float32),
            pltpu.VMEM((2, 7, high, TILE, cols), jnp.float32),
            pltpu.VMEM((depth, high, planes, cols), jnp.float32),
            pltpu.VMEM((order, order), jnp.float32),
        ],
        compiler_params=PARAMS,
        name="powers",
    )(start, edge, *got, shifts)
    half_type = jax.ShapeDtypeStruct((points * order, cols), jnp.bfloat16)
    high_part, low_part = pl.pallas_call(
        split_kernel,
        out_shape=(half_type, half_type),
        in_specs=[VMEM],
        out_specs=(VMEM, VMEM),
        compiler_params=PARAMS,
        cost_estimate=pl.CostEstimate(flops=0, bytes_accessed=8 * points * order * cols, transcendentals=0),
        name="split",
    )(basis)
    points_in_all = points * cols
    steps = []
    for axis in ("gx", "gy", "gz"):
        size = lax.axis_size(axis)
        points_in_all *= size
        steps += [(axis, 1 << bit) for bit in range(axis == "gz", size.bit_length() - 1)]
    assert lax.axis_size("gz") % 2 == 0
    across = [(i, i ^ 1) for i in range(lax.axis_size("gz"))]
    own = keep + lax.ppermute(send, "gz", across)
    turns = [steps[i : i + 2] for i in range(0, len(steps), 2)]
    turn = len(turns) // 2 if len(steps) % 2 == 0 else 0
    own = summed(own, (turns, turns[turn:] + turns[:turn]))
    other = lax.ppermute(own, "gz", across)
    upper, basis_q = pl.pallas_call(
        functools.partial(finish_kernel, count=float(points_in_all), step=8),
        out_shape=(float_of(order, order), float_of(order, points, cols)),
        in_specs=[VMEM] * 4,
        out_specs=(VMEM, HBM),
        scratch_shapes=[pltpu.VMEM((order * points, cols), jnp.float32), pltpu.SemaphoreType.DMA((layers,))],
        compiler_params=PARAMS,
        name="finish",
    )(own, other, high_part, low_part)
    return basis_q.reshape(order, layers, rows, cols), upper


def solution(mesh):
    in_specs = (
        P(None, "gz", "gx", "gy"),
        P("gz", "gx", "gy"),
        P("gz", "gx", "gy"),
        P("gz", "gx", "gy"),
        P("gz", "gx", "gy"),
        P(),
    )
    out_specs = (P(None, "gz", "gx", "gy"), P())
    return jax.shard_map(local, mesh=mesh, in_specs=in_specs, out_specs=out_specs, check_vma=False)
```
